32 devices in a mesh: seq: 4 (over y, x), dp: 8 (over z, core).
Axes of the slice: x: 2, y: 2, z: 4, core: 2. Of those that a mesh axis runs over, the one named last changes fastest.
Arguments:
- hidden: bfloat16 [3, 16, 256, 1024], P(None, 'dp', 'seq'), may hold values from -6 to 6
- encoder: bfloat16 [16, 256, 1024], P('dp', 'seq'), may hold values from -6 to 6
- lengths: int32 [16], P('dp'), may hold values from 1 to 256, as said below
- enc_lengths: int32 [16], P('dp'), may hold values from 1 to 256, as said below
- w_query: bfloat16 [1024, 1024], P('dp'), may hold values from -0.1875 to 0.1875
- w_key: bfloat16 [1024, 1024], P('dp'), may hold values from -0.1875 to 0.1875
- w_value: bfloat16 [1024, 1024], P('dp'), may hold values from -0.1875 to 0.1875
- w_attn_out: bfloat16 [1024, 1024], P('dp'), may hold values from -0.75 to 0.75
- w_relative: bfloat16 [1024, 512], P('dp'), may hold values from -0.1875 to 0.1875
- w_cross_query: bfloat16 [1024, 1024], P('dp'), may hold values from -0.1875 to 0.1875
- w_cross_key: bfloat16 [1024, 1024], P('dp'), may hold values from -0.1875 to 0.1875
- w_cross_value: bfloat16 [1024, 1024], P('dp'), may hold values from -0.1875 to 0.1875
- w_cross_out: bfloat16 [1024, 1024], P('dp'), may hold values from -0.75 to 0.75
- w_up: bfloat16 [1024, 4096], P('dp'), may hold values from -0.1875 to 0.1875
- w_down: bfloat16 [4096, 1024], P('dp'), may hold values from -0.09375 to 0.09375
- gain_attn: bfloat16 [1024], P('dp'), may hold values from 0.099609375 to 1.8984375
- gain_cross: bfloat16 [1024], P('dp'), may hold values from 0.099609375 to 1.8984375
- gain_ffn: bfloat16 [1024], P('dp'), may hold values from 0.099609375 to 1.8984375
- cotangent: bfloat16 [3, 16, 256, 1024], P(None, 'dp', 'seq'), may hold values from -6 to 6
Outputs:
- output: bfloat16 [3, 16, 256, 1024], P(None, 'dp', 'seq')
- hidden_grad: float32 [3, 16, 256, 1024], P(None, 'dp', 'seq')
- encoder_grad: float32 [16, 256, 1024], P('dp', 'seq')
- query_grad: float32 [1024, 1024], P(('seq', 'dp'))
- key_grad: float32 [1024, 1024], P(('seq', 'dp'))
- value_grad: float32 [1024, 1024], P(('seq', 'dp'))
- attn_out_grad: float32 [1024, 1024], P(('seq', 'dp'))
- relative_grad: float32 [1024, 512], P(('seq', 'dp'))
- cross_query_grad: float32 [1024, 1024], P(('seq', 'dp'))
- cross_key_grad: float32 [1024, 1024], P(('seq', 'dp'))
- cross_value_grad: float32 [1024, 1024], P(('seq', 'dp'))
- cross_out_grad: float32 [1024, 1024], P(('seq', 'dp'))
- up_grad: float32 [1024, 4096], P(('seq', 'dp'))
- down_grad: float32 [4096, 1024], P(('seq', 'dp'))
- gain_attn_grad: float32 [1024], P(('seq', 'dp'))
- gain_cross_grad: float32 [1024], P(('seq', 'dp'))
- gain_ffn_grad: float32 [1024], P(('seq', 'dp'))
The draws below stay inside these ranges and needn't reach their ends.
Inputs may be any that keep to these rules, and one draw needn't show every extreme that they name: `lengths`: among the 2 rows of each index of dp, one has length 256. `enc_lengths`: among the 2 rows of each index of dp, one has encoder length 256.
All inputs are finite; a program needn't handle non-finite values.
Results may differ from the reference program's by a relative error of at most 0.02.
Values may be sent and summed in bfloat16 or wider, within the bound.
A program may use at most 320 MiB of HBM per device.

```python
import math
import jax
import jax.numpy as jnp
from jax import lax

D = 1024
HEADS = 16
HEAD_DIM = 64
FF = 4096
BUCKETS = 32
STREAMS = 3
SEQ_LEN = 256
ENC_LEN = 256
ROWS_DEV = 2
ROWS = 16


def draw_lengths(key, part):
    key = jax.random.fold_in(key, 7)
    length_key, pick_key = jax.random.split(key)
    drawn = jax.random.randint(length_key, (ROWS,), 1, SEQ_LEN + 1)
    chosen = jax.random.randint(pick_key, (ROWS // ROWS_DEV, 1), 0, ROWS_DEV)
    full_row = (jnp.arange(ROWS_DEV)[None, :] == chosen).reshape(ROWS)
    return jnp.where(full_row, SEQ_LEN, drawn).astype(jnp.int32)


def draw_enc_lengths(key, part):
    key = jax.random.fold_in(key, 11)
    length_key, pick_key = jax.random.split(key)
    drawn = jax.random.randint(length_key, (ROWS,), 1, ENC_LEN + 1)
    chosen = jax.random.randint(pick_key, (ROWS // ROWS_DEV, 1), 0, ROWS_DEV)
    full_row = (jnp.arange(ROWS_DEV)[None, :] == chosen).reshape(ROWS)
    return jnp.where(full_row, ENC_LEN, drawn).astype(jnp.int32)


def levels(key, extent, cuts, low, largest):
    gain, own = 1.0, jax.random.fold_in(key, 6)
    for axis_at, shards_of in cuts:
        steps = jnp.exp(jax.random.uniform(jax.random.fold_in(own, axis_at), (shards_of,), jnp.float32, low / len(cuts), largest / len(cuts)))
        gain = gain * jnp.repeat(steps, extent[axis_at] // shards_of).reshape([-1 if axis == axis_at else 1 for axis in range(len(extent))])
    return gain


def scatter_about(key, extent, scale, limit, shards=(), kind=jnp.bfloat16):
    values = scale * jax.random.normal(key, extent, jnp.float32)
    if shards:
        values = values * levels(key, extent, shards, -0.22, 0.18)
    return jnp.clip(values, -limit, limit).astype(kind)


def setup_inputs(seed: int = 0) -> dict:
    streams_of = jax.random.split(jax.random.key(seed), 20)
    hidden = scatter_about(streams_of[0], (STREAMS, ROWS, SEQ_LEN, D), 1.0, 6.0, ((1, 8), (2, 4)))
    encoder = scatter_about(streams_of[1], (ROWS, ENC_LEN, D), 1.0, 6.0, ((0, 8), (1, 4)))
    lengths = draw_lengths(jax.random.fold_in(streams_of[19], 71), 0)
    enc_lengths = draw_enc_lengths(jax.random.fold_in(streams_of[19], 71), 0)
    w_query = scatter_about(streams_of[4], (D, D), D ** -0.5, 0.1875, ((0, 8),))
    w_key = scatter_about(streams_of[5], (D, D), D ** -0.5, 0.1875, ((0, 8),))
    w_value = scatter_about(streams_of[6], (D, D), D ** -0.5, 0.1875, ((0, 8),))
    w_attn_out = scatter_about(streams_of[7], (D, D), (D // 16) ** -0.5, 0.75, ((0, 8),))
    w_relative = scatter_about(streams_of[8], (D, HEADS * BUCKETS), D ** -0.5, 0.1875, ((0, 8),))
    w_cross_query = scatter_about(streams_of[9], (D, D), D ** -0.5, 0.1875, ((0, 8),))
    w_cross_key = scatter_about(streams_of[10], (D, D), D ** -0.5, 0.1875, ((0, 8),))
    w_cross_value = scatter_about(streams_of[11], (D, D), D ** -0.5, 0.1875, ((0, 8),))
    w_cross_out = scatter_about(streams_of[12], (D, D), (D // 16) ** -0.5, 0.75, ((0, 8),))
    w_up = scatter_about(streams_of[13], (D, FF), D ** -0.5, 0.1875, ((0, 8),))
    w_down = scatter_about(streams_of[14], (FF, D), FF ** -0.5, 0.09375, ((0, 8),))
    gain_attn = jnp.clip(1.0 + 0.18 * jax.random.normal(streams_of[15], (D,), jnp.float32), 0.099609375, 1.8984375).astype(jnp.bfloat16)
    gain_cross = jnp.clip(1.0 + 0.18 * jax.random.normal(streams_of[16], (D,), jnp.float32), 0.099609375, 1.8984375).astype(jnp.bfloat16)
    gain_ffn = jnp.clip(1.0 + 0.18 * jax.random.normal(streams_of[17], (D,), jnp.float32), 0.099609375, 1.8984375).astype(jnp.bfloat16)
    cotangent = scatter_about(streams_of[18], (STREAMS, ROWS, SEQ_LEN, D), 1.0, 6.0, ((1, 8), (2, 4)))
    return dict(hidden=hidden, encoder=encoder, lengths=lengths, enc_lengths=enc_lengths, w_query=w_query, w_key=w_key, w_value=w_value, w_attn_out=w_attn_out, w_relative=w_relative, w_cross_query=w_cross_query, w_cross_key=w_cross_key, w_cross_value=w_cross_value, w_cross_out=w_cross_out, w_up=w_up, w_down=w_down, gain_attn=gain_attn, gain_cross=gain_cross, gain_ffn=gain_ffn, cotangent=cotangent)


eps_norm = 1e-05
bucket_edges = [step_index for step_index in range(1, 16)] + [int(math.ceil(16 * 8 ** ((step_index - 16) / 16))) for step_index in range(16, 32)]

@jax.custom_vjp
def low(v):
    return lax.optimization_barrier(v.astype(jnp.bfloat16)).astype(jnp.float32)

@jax.custom_vjp
def low_back(v):
    return v

def low_keep(v):
    return (low(v), None)

def low_pass(kept, grad):
    return (grad,)

def back_keep(v):
    return (v, None)

def back_low(kept, grad):
    return (low(grad),)
low.defvjp(low_keep, low_pass)
low_back.defvjp(back_keep, back_low)

def matmul(left, right):
    return jnp.einsum('...d,de->...e', left, right, precision=lax.Precision.HIGHEST)

def layer_norm(values, gain_vec):
    row_mean = lax.optimization_barrier(jnp.mean(values, axis=-1, keepdims=True))
    centred = values - row_mean
    row_var = lax.optimization_barrier(jnp.mean(centred * centred, axis=-1, keepdims=True))
    return centred * lax.rsqrt(row_var + eps_norm) * gain_vec

def bucket_hot(query_pos, key_pos, hot_type):
    distance = jnp.maximum(query_pos[:, None] - key_pos[None, :], 0)
    edges = jnp.array(bucket_edges, jnp.int32)
    bucket = lax.optimization_barrier(jnp.sum((distance[:, :, None] >= edges[None, None, :]).astype(jnp.int32), axis=2))
    return (bucket[:, :, None] == jnp.arange(BUCKETS, dtype=jnp.int32)[None, None, :]).astype(hot_type)

def score_masks(query_pos, key_pos, row_lengths, streams):
    stream_index = jnp.arange(streams)[:, None, None, None, None]
    main_mask = key_pos[None, :] <= query_pos[:, None]
    ahead_mask = key_pos[None, :] < query_pos[:, None]
    causal = jnp.where(stream_index == 0, main_mask[None, None, None], ahead_mask[None, None, None])
    live_keys = (key_pos[None, :] < row_lengths[:, None])[None, :, None, None, :]
    own_ok = jnp.arange(streams)[:, None, None, None] > 0
    return (causal & live_keys, own_ok)

def stream_softmax(main_scores, own_scores):
    peak_score = jnp.maximum(lax.optimization_barrier(jnp.max(main_scores, axis=-1)), own_scores)
    main_exp = jnp.exp(main_scores - peak_score[..., None])
    own_exp = jnp.exp(own_scores - peak_score)
    denominator = lax.optimization_barrier(jnp.sum(main_exp, axis=-1)) + own_exp
    return (main_exp / denominator[..., None], own_exp / denominator)

def cross_softmax(scores):
    peak_score = lax.optimization_barrier(jnp.max(scores, axis=-1, keepdims=True))
    exps = jnp.exp(scores - peak_score)
    return exps / lax.optimization_barrier(jnp.sum(exps, axis=-1, keepdims=True))

def attention(query, keys, values, rel_proj, row_lengths):
    streams, seq_len = (query.shape[0], query.shape[2])
    positions = jnp.arange(seq_len, dtype=jnp.int32)
    hot = bucket_hot(positions, positions, jnp.float32)
    allowed, own_ok = score_masks(positions, positions, row_lengths, streams)
    raw_scores = jnp.einsum('jgthe,gshe->jghts', query, keys[0], precision=lax.Precision.HIGHEST)
    rel_bias = jnp.einsum('jgthb,tsb->jghts', rel_proj, hot, precision=lax.Precision.HIGHEST)
    main_scores = jnp.where(allowed, low_back(raw_scores + rel_bias), -1000000000.0)
    own_raw = jnp.einsum('jgthe,jgthe->jgth', query, keys, precision=lax.Precision.HIGHEST) + rel_proj[..., 0]
    own_scores = jnp.where(own_ok, jnp.transpose(own_raw, (0, 1, 3, 2)), -1000000000.0)
    main_prob, own_prob = stream_softmax(main_scores, own_scores)
    context = jnp.einsum('jghts,gshe->jgthe', low(main_prob), values[0], precision=lax.Precision.HIGHEST)
    return context + jnp.transpose(own_prob, (0, 1, 3, 2))[..., None] * values

def cross_attention(cross_query, enc_keys, enc_values, enc_row_lengths):
    enc_len = enc_keys.shape[1]
    live = (jnp.arange(enc_len, dtype=jnp.int32)[None, :] < enc_row_lengths[:, None])[None, :, None, None, :]
    raw_scores = jnp.einsum('jgthe,gshe->jghts', cross_query, enc_keys, precision=lax.Precision.HIGHEST)
    scores = jnp.where(live, low_back(raw_scores), -1000000000.0)
    prob = cross_softmax(scores)
    return jnp.einsum('jghts,gshe->jgthe', low(prob), enc_values, precision=lax.Precision.HIGHEST)

def layer(hidden_group, enc_group, row_lengths, enc_row_lengths, weights):
    w_query, w_key, w_value, w_attn_out, w_relative, w_cross_query, w_cross_key, w_cross_value, w_cross_out, w_up, w_down, gain_attn, gain_cross, gain_ffn = weights
    streams, group, seq_len = (hidden_group.shape[0], hidden_group.shape[1], hidden_group.shape[2])
    enc_len = enc_group.shape[1]
    head_shape = (streams, group, seq_len, HEADS, HEAD_DIM)
    enc_shape = (group, enc_len, HEADS, HEAD_DIM)
    query = low_back(low(matmul(hidden_group, w_query) * 0.125)).reshape(head_shape)
    keys = low_back(low(matmul(hidden_group, w_key))).reshape(head_shape)
    values = low_back(low(matmul(hidden_group, w_value))).reshape(head_shape)
    rel_proj = low_back(low(matmul(hidden_group, w_relative))).reshape(streams, group, seq_len, HEADS, BUCKETS)
    context = attention(query, keys, values, rel_proj, row_lengths).reshape(streams, group, seq_len, D)
    context = low_back(low(context))
    attn_out = low_back(matmul(context, w_attn_out))
    normed = layer_norm(hidden_group + attn_out, gain_attn)
    cross_query = low_back(low(matmul(low(normed), w_cross_query) * 0.125)).reshape(head_shape)
    enc_keys = low_back(low(matmul(enc_group, w_cross_key))).reshape(enc_shape)
    enc_values = low_back(low(matmul(enc_group, w_cross_value))).reshape(enc_shape)
    cross_context = cross_attention(cross_query, enc_keys, enc_values, enc_row_lengths).reshape(streams, group, seq_len, D)
    cross_context = low_back(low(cross_context))
    cross_out = low_back(matmul(cross_context, w_cross_out))
    crossed = layer_norm(normed + cross_out, gain_cross)
    upward = low_back(matmul(low(crossed), w_up))
    down = low_back(matmul(low(jax.nn.gelu(upward, approximate=False)), w_down))
    return layer_norm(crossed + down, gain_ffn)

def reference(hidden, encoder, lengths, enc_lengths, w_query, w_key, w_value, w_attn_out, w_relative, w_cross_query, w_cross_key, w_cross_value, w_cross_out, w_up, w_down, gain_attn, gain_cross, gain_ffn, cotangent):
    row_count = hidden.shape[1]
    groups = row_count // ROWS_DEV

    def by_group(array):
        return array.astype(jnp.float32).reshape(STREAMS, groups, ROWS_DEV, SEQ_LEN, D).transpose(1, 0, 2, 3, 4)
    hidden_all = by_group(hidden)
    cot_all = by_group(cotangent)
    enc_all = encoder.astype(jnp.float32).reshape(groups, ROWS_DEV, ENC_LEN, D)
    length_all = lengths.reshape(groups, ROWS_DEV)
    enc_length_all = enc_lengths.reshape(groups, ROWS_DEV)
    weight_list = tuple((weight_arg.astype(jnp.float32) for weight_arg in (w_query, w_key, w_value, w_attn_out, w_relative, w_cross_query, w_cross_key, w_cross_value, w_cross_out, w_up, w_down, gain_attn, gain_cross, gain_ffn)))

    def forward(hidden_in, enc_in, *weight_in):

        def one_group(group_item):
            hidden_group, enc_group, row_lengths, enc_row_lengths = group_item
            return layer(hidden_group, enc_group, row_lengths, enc_row_lengths, weight_in)
        return lax.map(jax.checkpoint(one_group), (hidden_in, enc_in, length_all, enc_length_all))
    result, pullback = jax.vjp(forward, hidden_all, enc_all, *weight_list)
    gradients = pullback(cot_all)

    def from_group(array):
        return array.transpose(1, 0, 2, 3, 4).reshape(STREAMS, row_count, SEQ_LEN, D)
    encoder_grad = gradients[1].reshape(row_count, ENC_LEN, D)
    return (from_group(result).astype(jnp.bfloat16), from_group(gradients[0]), encoder_grad, gradients[2], gradients[3], gradients[4], gradients[5], gradients[6], gradients[7], gradients[8], gradients[9], gradients[10], gradients[11], gradients[12], gradients[13], gradients[14], gradients[15])
```

```python
import math

import jax
import jax.numpy as jnp
from jax import lax
from jax.experimental import pallas as pl
from jax.experimental.pallas import tpu as pltpu
from jax.sharding import PartitionSpec as P

MESH = pl.DeviceIdType.MESH

HEADS = 16
HEAD_DIM = 64
BUCKETS = 32


eps_norm = 1e-05
bucket_edges = [step_index for step_index in range(1, 16)] + [
    int(math.ceil(16 * 8 ** ((step_index - 16) / 16))) for step_index in range(16, 32)
]


def layer_norm(values, gain_vec):
    row_mean = jnp.mean(values, axis=-1, keepdims=True)
    centred = values - row_mean
    row_var = jnp.mean(centred * centred, axis=-1, keepdims=True)
    return centred * lax.rsqrt(row_var + eps_norm) * gain_vec


def bucket_hot(query_pos, key_pos, hot_type):
    distance = jnp.maximum(query_pos[:, None] - key_pos[None, :], 0)
    edges = jnp.array(bucket_edges, jnp.int32)
    bucket = jnp.sum((distance[:, :, None] >= edges[None, None, :]).astype(jnp.int32), axis=2)
    return (bucket[:, :, None] == jnp.arange(BUCKETS, dtype=jnp.int32)[None, None, :]).astype(
        hot_type
    )


def score_masks(query_pos, key_pos, row_lengths, streams):
    stream_index = jnp.arange(streams)[:, None, None, None, None]
    main_mask = key_pos[None, :] <= query_pos[:, None]
    ahead_mask = key_pos[None, :] < query_pos[:, None]
    causal = jnp.where(stream_index == 0, main_mask[None, None, None], ahead_mask[None, None, None])
    live_keys = (key_pos[None, :] < row_lengths[:, None])[None, :, None, None, :]
    own_ok = jnp.arange(streams)[:, None, None, None] > 0
    return (causal & live_keys, own_ok)


def stream_softmax(main_scores, own_scores):
    peak_score = jnp.maximum(jnp.max(main_scores, axis=-1), own_scores)
    main_exp = jnp.exp(main_scores - peak_score[..., None])
    own_exp = jnp.exp(own_scores - peak_score)
    denominator = jnp.sum(main_exp, axis=-1) + own_exp
    return (main_exp / denominator[..., None], own_exp / denominator)


def cross_softmax(scores):
    peak_score = jnp.max(scores, axis=-1, keepdims=True)
    exps = jnp.exp(scores - peak_score)
    return exps / jnp.sum(exps, axis=-1, keepdims=True)


def exact_gelu(values):
    return jax.nn.gelu(values, approximate=False)


def flatten_rows(array):
    return array.reshape(-1, array.shape[-1])


def project(array, weight):
    result = jnp.dot(flatten_rows(array), weight, preferred_element_type=jnp.float32)
    return result.reshape(array.shape[:-1] + (weight.shape[1],))


def project_back(grad_rows, weight):
    result = jnp.einsum(
        "ne,de->nd", flatten_rows(grad_rows), weight, preferred_element_type=jnp.float32
    )
    return result.reshape(grad_rows.shape[:-1] + (weight.shape[0],))


def weight_grad(array, grad_rows):
    return jnp.einsum(
        "nd,ne->de",
        flatten_rows(array),
        flatten_rows(grad_rows),
        preferred_element_type=jnp.float32,
    )


def turned(array):
    return jnp.transpose(array, (0, 1, 3, 2))


def remote(src, dst, send, recv, to):
    return pltpu.make_async_remote_copy(
        src_ref=src, dst_ref=dst, send_sem=send, recv_sem=recv, device_id=to, device_id_type=MESH
    )


def place():
    s = lax.axis_index("seq")
    d = lax.axis_index("dp")
    z, c = d // 2, lax.rem(d, 2)
    sx = s + 1 - 2 * lax.rem(s, 2)
    sy = lax.rem(s + 2, 4)
    return s, z, c, sx, sy


def greet(nz):
    s, z, c, sx, sy = place()
    barrier = pltpu.get_barrier_semaphore()
    dests = [(s, 2 * z + 1 - c), (sx, 2 * z + c), (sy, 2 * z + c)]
    for dz in range(1, nz):
        dests.append((s, 2 * lax.rem(z + dz, nz) + c))
    for dest in dests:
        pl.semaphore_signal(barrier, inc=1, device_id=dest, device_id_type=MESH)
    pl.semaphore_wait(barrier, len(dests))


def gather_weights_kernel(count, nz, *refs):
    shards, wholes = refs[:count], refs[count : 2 * count]
    local_sem, send, recv = refs[2 * count :]
    s, z, c, sx, sy = place()
    own = 2 * z + c
    core = (s, 2 * z + 1 - c)
    beside_x, beside_y = (sx, own), (sy, own)
    greet(nz)
    started = []

    def put(copy):
        copy.start()
        started.append(copy)

    def rows_of(i, q, half):
        quarter = shards[i].shape[0] // 4
        if half is None:
            return pl.ds(q * quarter, quarter)
        return pl.ds(q * quarter + half * (quarter // 2), quarter // 2)

    split = [shards[i].shape[0] % 128 == 0 for i in range(count)]
    def along_z(i):
        here = pltpu.make_async_copy(shards[i], wholes[i].at[own], local_sem.at[i])
        here.start()
        started.append(here)
        for dz in range(1, nz):
            to = (s, 2 * lax.rem(z + dz, nz) + c)
            if split[i]:
                src, dst = shards[i].at[rows_of(i, s, None)], wholes[i].at[own, rows_of(i, s, None)]
            else:
                src, dst = shards[i], wholes[i].at[own]
            put(remote(src, dst, send.at[i, dz, 0], recv.at[i, dz, 0], to))
        put(remote(shards[i], wholes[i].at[own], send.at[i, 0, 0], recv.at[i, 0, 0], core))

    def moved(i, dz, kind, q, half, to):
        block = 2 * lax.rem(z + nz - dz, nz) + c
        part = wholes[i].at[block, rows_of(i, q, half)] if split[i] else wholes[i].at[block]
        return remote(part, part, send.at[i, dz, kind], recv.at[i, dz, kind], to)

    def to_core(i, dz, kind, q, half):
        put(moved(i, dz, kind, q, half, core))

    def first(i):
        for dz in range(1, nz):
            moved(i, dz, 0, s, None, core).wait_recv()
            if split[i]:
                put(moved(i, dz, 1, s, None, beside_x))
                put(moved(i, dz, 2, s, None, beside_y))
            to_core(i, dz, 5, s, None)

    def second(i):
        if not split[i]:
            return
        for dz in range(1, nz):
            moved(i, dz, 1, sx, None, core).wait_recv()
            put(moved(i, dz, 4, sx, 0, beside_y))
            to_core(i, dz, 6, sx, None)
            moved(i, dz, 2, sy, None, core).wait_recv()
            put(moved(i, dz, 3, sy, 1, beside_x))
            to_core(i, dz, 7, sy, None)

    def third(i):
        if not split[i]:
            return
        for dz in range(1, nz):
            moved(i, dz, 4, 3 - s, 0, core).wait_recv()
            to_core(i, dz, 8, 3 - s, 0)
            moved(i, dz, 3, 3 - s, 1, core).wait_recv()
            to_core(i, dz, 9, 3 - s, 1)

    def last(i):
        other = 1 - c
        block = wholes[i].at[2 * z + other]
        remote(block, block, send.at[i, 0, 0], recv.at[i, 0, 0], core).wait_recv()
        for dz in range(1, nz):
            block = wholes[i].at[2 * lax.rem(z + nz - dz, nz) + other]
            kinds = [(5, s, None)]
            if split[i]:
                kinds += [(6, sx, None), (7, sy, None), (8, 3 - s, 0), (9, 3 - s, 1)]
            for kind, q, half in kinds:
                part = block.at[rows_of(i, q, half)] if split[i] else block
                remote(part, part, send.at[i, dz, kind], recv.at[i, dz, kind], core).wait_recv()

    ahead = 3
    for i in range(min(ahead, count)):
        along_z(i)
    for i in range(count + 2):
        if i < count:
            first(i)
        if ahead + i < count:
            along_z(ahead + i)
        if 1 <= i <= count:
            second(i - 1)
        if i >= 2:
            third(i - 2)
    for i in range(count):
        last(i)
    for copy in started:
        if hasattr(copy, "wait_send") and copy.is_remote:
            copy.wait_send()
        else:
            copy.wait()


def gather_weights(shards, ndp):
    nz = ndp // 2
    count = len(shards)
    return pl.pallas_call(
        lambda *refs: gather_weights_kernel(count, nz, *refs),
        out_shape=[jax.ShapeDtypeStruct((ndp,) + w.shape, w.dtype) for w in shards],
        in_specs=[pl.BlockSpec(memory_space=pl.ANY)] * count,
        out_specs=[pl.BlockSpec(memory_space=pl.ANY)] * count,
        scratch_shapes=[
            pltpu.SemaphoreType.DMA((count,)),
            pltpu.SemaphoreType.DMA((count, nz, 10)),
            pltpu.SemaphoreType.DMA((count, nz, 10)),
        ],
        compiler_params=pltpu.CompilerParams(collective_id=0, has_side_effects=True),
        name="gather_weights",
    )(*shards)


def reduce_grads_kernel(plan, nz, n_x, n_g, n_out, *refs):
    at = 0
    xs, at = refs[at : at + n_x], at + n_x
    gs, at = refs[at : at + n_g], at + n_g
    gain_part, at = refs[at], at + 1
    outs, at = refs[at : at + n_out], at + n_out
    gain_out, at = refs[at], at + 1
    kinds = []
    for _ in range(3):
        kinds.append(refs[at : at + 5])
        at += 5
    send, recv = refs[at : at + 2]
    s, z, c, sx, sy = place()
    own = 2 * z + c
    x, y = lax.rem(s, 2), s // 2
    core = (s, 2 * z + 1 - c)
    beside_x, beside_y = (sx, own), (sy, own)
    greet(nz)
    count = len(plan)

    def buffers(k):
        kind, slot = plan[k][0], plan[k][1]
        part, held0, held1, held2, held3 = kinds[kind]
        if kind == 2:
            return gain_part, held0.at[slot], held1.at[slot], held2.at[slot], held3.at[slot]
        return (part.at[slot % 2], held0.at[slot], held1.at[slot], held2.at[slot], held3.at[slot])

    def core_copy(k):
        part, held0 = buffers(k)[:2]
        return remote(part.at[:, :, :, 1 - c], held0, send.at[k, 0], recv.at[k, 0], core)

    def first_copy(k):
        _, held0, held1 = buffers(k)[:3]
        if k % 2 == 0:
            return remote(held0.at[:, 1 - x], held1, send.at[k, 1], recv.at[k, 1], beside_x)
        return remote(held0.at[1 - y], held1, send.at[k, 1], recv.at[k, 1], beside_y)

    def second_copy(k):
        held1, held2 = buffers(k)[2:4]
        if k % 2 == 0:
            return remote(held1.at[1 - y], held2, send.at[k, 2], recv.at[k, 2], beside_y)
        return remote(held1.at[1 - x], held2, send.at[k, 2], recv.at[k, 2], beside_x)

    def z_copy(k, dz):
        held2, held3 = buffers(k)[3:5]
        zt = lax.rem(z + dz, nz)
        return remote(
            held2.at[zt], held3.at[dz - 1], send.at[k, 2 + dz], recv.at[k, 2 + dz], (s, 2 * zt + c)
        )

    def added(held, mine):
        held[...] = (held[...].astype(jnp.float32) + mine.astype(jnp.float32)).astype(held.dtype)

    def make(k):
        kind, slot, xi, gi, _, col, wide = plan[k]
        if kind < 2:
            part = buffers(k)[0]
            left, right = xs[xi], gs[gi]
            block = part.shape[4]
            if slot >= 2:
                core_copy(before[k]).wait_send()
            group = 256 // block
            for i in range(left.shape[1] // 256):
                product = lax.dot_general(
                    left[:, i * 256 : (i + 1) * 256],
                    right[:, col : col + wide],
                    (((0,), (0,)), ((), ())),
                    preferred_element_type=jnp.float32,
                )
                index = i * group
                i_s, rest = divmod(index, 2 * nz)
                zs = rest // 2
                part[i_s // 2, i_s % 2, zs : zs + group // 2] = product.reshape(group // 2, 2, block, wide).astype(
                    part.dtype
                )
        core_copy(k).start()

    def after_core(k):
        part, held0 = buffers(k)[:2]
        core_copy(k).wait_recv()
        added(held0, part[:, :, :, c])
        first_copy(k).start()

    def after_first(k):
        _, held0, held1 = buffers(k)[:3]
        first_copy(k).wait_recv()
        added(held1, held0[:, x] if k % 2 == 0 else held0[y])
        second_copy(k).start()

    def after_second(k):
        held1, held2 = buffers(k)[2:4]
        second_copy(k).wait_recv()
        added(held2, held1[y] if k % 2 == 0 else held1[x])
        for dz in range(1, nz):
            z_copy(k, dz).start()

    def finish(k):
        held2, held3 = buffers(k)[3:5]
        total = held2[z].astype(jnp.float32)
        for dz in range(1, nz):
            z_copy(k, dz).wait_recv()
            total = total + held3[dz - 1].astype(jnp.float32)
        kind, _, _, _, oi, col, wide = plan[k]
        if kind == 2:
            gain_out[...] = total
        else:
            outs[oi][:, col : col + wide] = total

    before = {}
    recent = {}
    for k in range(count):
        kind, slot = plan[k][0], plan[k][1]
        before[k] = recent.get((kind, slot - 2))
        recent[(kind, slot)] = k
    followed = set(v for v in before.values() if v is not None)

    for t in range(count + 7):
        if t >= 7:
            finish(t - 7)
        if 5 <= t < count + 5:
            after_second(t - 5)
        if 3 <= t < count + 3:
            after_first(t - 3)
        if t < count:
            make(t)
        if 1 <= t < count + 1:
            after_core(t - 1)
    for k in range(count):
        if k not in followed:
            core_copy(k).wait_send()
        first_copy(k).wait_send()
        second_copy(k).wait_send()
        for dz in range(1, nz):
            z_copy(k, dz).wait_send()


def reduce_grads(xs, gs, pairs, gain_part, nz):
    plan, slots = [], [0, 0, 0]
    blocks, columns = [], []
    ndev = 8 * nz
    for oi, (xi, gi) in enumerate(pairs):
        rows, wide = xs[xi].shape[1], gs[gi].shape[1]
        columns.append((rows // ndev, wide))
        kind = 0 if rows // ndev <= 32 else 1
        step = (512, 256)[kind]
        for col in range(0, wide, step):
            plan.append((kind, slots[kind], xi, gi, oi, col, step))
            slots[kind] += 1
    plan.append((2, 0, 0, 0, 0, 0, 128))
    rb = min(rows for rows, _ in columns)
    shapes = [((rb, 512), jnp.bfloat16, slots[0]), ((max(rows for rows, _ in columns), 256), jnp.bfloat16, slots[1])]
    scratch = []
    for (tail, kind_type, n) in shapes + [((8, 128), jnp.float32, 1)]:
        scratch.append(
            pltpu.VMEM((2, 2, 2, nz, 2) + tail if kind_type == jnp.bfloat16 else (8, 128), kind_type)
        )
        scratch.append(pltpu.VMEM((n, 2, 2, nz) + tail, kind_type))
        scratch.append(pltpu.VMEM((n, 2, nz) + tail, kind_type))
        scratch.append(pltpu.VMEM((n, nz) + tail, kind_type))
        scratch.append(pltpu.VMEM((n, nz - 1) + tail, kind_type))
    n = len(plan)
    vmem = pl.BlockSpec(memory_space=pltpu.VMEM)
    outs = [jax.ShapeDtypeStruct(shape, jnp.float32) for shape in columns]
    outs.append(jax.ShapeDtypeStruct((8, 128), jnp.float32))
    return pl.pallas_call(
        lambda *refs: reduce_grads_kernel(plan, nz, len(xs), len(gs), len(columns), *refs),
        out_shape=outs,
        in_specs=[vmem] * (len(xs) + len(gs) + 1),
        out_specs=[vmem] * len(outs),
        scratch_shapes=scratch
        + [pltpu.SemaphoreType.DMA((n, 2 + nz)), pltpu.SemaphoreType.DMA((n, 2 + nz))],
        compiler_params=pltpu.CompilerParams(
            collective_id=1, has_side_effects=True, vmem_limit_bytes=62 * 2**20
        ),
        name="reduce_grads",
    )(*xs, *gs, gain_part)


def local(
    hidden,
    encoder,
    lengths,
    enc_lengths,
    w_query,
    w_key,
    w_value,
    w_attn_out,
    w_relative,
    w_cross_query,
    w_cross_key,
    w_cross_value,
    w_cross_out,
    w_up,
    w_down,
    gain_attn,
    gain_cross,
    gain_ffn,
    cotangent,
):
    ndp = lax.axis_size("dp")
    devices = ndp * lax.axis_size("seq")
    weights = (
        w_key,
        w_value,
        w_query,
        w_relative,
        w_attn_out,
        w_cross_key,
        w_cross_value,
        w_cross_query,
        w_cross_out,
        w_up,
        w_down,
    )
    gains = jnp.stack([gain_attn, gain_cross, gain_ffn])
    kernels = lax.axis_size("seq") == 4 and w_query.shape[0] % 128 == 0
    if kernels:
        gains = jnp.pad(gains, ((0, 13), (0, 0)))
        *whole, whole_gains = gather_weights(weights + (gains,), ndp)
        whole = [w.reshape(-1, w.shape[-1]) for w in whole]
        whole_gains = whole_gains[:, :3]
    else:
        whole = [lax.all_gather(w, "dp", axis=0, tiled=True) for w in weights]
        whole_gains = lax.all_gather(gains, "dp", axis=0)
    whole_gains = jnp.transpose(whole_gains, (1, 0, 2)).reshape(3, -1)
    full_gain_attn, full_gain_cross, full_gain_ffn = whole_gains
    (
        full_key,
        full_value,
        full_query,
        full_relative,
        full_attn_out,
        full_ckey,
        full_cvalue,
        full_cquery,
        full_cout,
        full_up,
        full_down,
    ) = whole
    streams, row_count, local_len, width = hidden.shape
    enc_local = encoder.shape[1]
    seq_len = local_len * lax.axis_size("seq")
    enc_len = enc_local * lax.axis_size("seq")
    head_shape = (streams, row_count, local_len, HEADS, HEAD_DIM)
    flat_shape = (streams, row_count, local_len, width)
    query_low = (project(hidden, full_query) * 0.125).astype(jnp.bfloat16)
    key_low = project(hidden, full_key).astype(jnp.bfloat16)
    value_low = project(hidden, full_value).astype(jnp.bfloat16)
    rel_low = project(hidden, full_relative).astype(jnp.bfloat16)
    enc_key_low = project(encoder, full_ckey).astype(jnp.bfloat16)
    enc_value_low = project(encoder, full_cvalue).astype(jnp.bfloat16)
    main_keys, main_values, enc_keys, enc_values = (
        lax.all_gather(key_low[0], "seq", axis=1, tiled=True),
        lax.all_gather(value_low[0], "seq", axis=1, tiled=True),
        lax.all_gather(enc_key_low, "seq", axis=1, tiled=True),
        lax.all_gather(enc_value_low, "seq", axis=1, tiled=True),
    )
    query_heads = query_low.reshape(head_shape)
    key_heads = key_low.reshape(head_shape)
    value_heads = value_low.reshape(head_shape)
    rel_heads = rel_low.reshape(streams, row_count, local_len, HEADS, BUCKETS)
    all_keys = main_keys.reshape(row_count, seq_len, HEADS, HEAD_DIM)
    all_values = main_values.reshape(row_count, seq_len, HEADS, HEAD_DIM)
    all_enc_keys = enc_keys.reshape(row_count, enc_len, HEADS, HEAD_DIM)
    all_enc_values = enc_values.reshape(row_count, enc_len, HEADS, HEAD_DIM)
    query_pos = lax.axis_index("seq") * local_len + jnp.arange(local_len, dtype=jnp.int32)
    key_pos = jnp.arange(seq_len, dtype=jnp.int32)
    hot = bucket_hot(query_pos, key_pos, jnp.bfloat16)
    allowed, own_ok = score_masks(query_pos, key_pos, lengths, streams)
    raw_scores = jnp.einsum(
        "jrthe,rshe->jrhts", query_heads, all_keys, preferred_element_type=jnp.float32
    )
    rel_bias = jnp.einsum("jrthb,tsb->jrhts", rel_heads, hot, preferred_element_type=jnp.float32)
    main_scores = jnp.where(allowed, raw_scores + rel_bias, -1000000000.0)
    own_raw = jnp.einsum(
        "jrthe,jrthe->jrth", query_heads, key_heads, preferred_element_type=jnp.float32
    ) + rel_heads[..., 0].astype(jnp.float32)
    own_scores = jnp.where(own_ok, turned(own_raw), -1000000000.0)
    (main_prob, own_prob), softmax_pull = jax.vjp(stream_softmax, main_scores, own_scores)
    main_low = main_prob.astype(jnp.bfloat16)
    context = jnp.einsum(
        "jrhts,rshe->jrthe", main_low, all_values, preferred_element_type=jnp.float32
    )
    context = context + turned(own_prob)[..., None] * value_heads.astype(jnp.float32)
    context_low = context.reshape(flat_shape).astype(jnp.bfloat16)
    attn_out = project(context_low, full_attn_out)
    normed, norm_attn_pull = jax.vjp(
        layer_norm, hidden.astype(jnp.float32) + attn_out, full_gain_attn.astype(jnp.float32)
    )
    normed_low = normed.astype(jnp.bfloat16)
    cross_query_low = (project(normed_low, full_cquery) * 0.125).astype(jnp.bfloat16)
    cross_heads = cross_query_low.reshape(head_shape)
    enc_live = (jnp.arange(enc_len, dtype=jnp.int32)[None, :] < enc_lengths[:, None])[
        None, :, None, None, :
    ]
    cross_raw = jnp.einsum(
        "jrthe,rshe->jrhts", cross_heads, all_enc_keys, preferred_element_type=jnp.float32
    )
    cross_scores = jnp.where(enc_live, cross_raw, -1000000000.0)
    cross_prob, cross_pull = jax.vjp(cross_softmax, cross_scores)
    cross_low = cross_prob.astype(jnp.bfloat16)
    cross_context = jnp.einsum(
        "jrhts,rshe->jrthe", cross_low, all_enc_values, preferred_element_type=jnp.float32
    )
    cross_context_low = cross_context.reshape(flat_shape).astype(jnp.bfloat16)
    cross_out = project(cross_context_low, full_cout)
    crossed, norm_cross_pull = jax.vjp(
        layer_norm, normed + cross_out, full_gain_cross.astype(jnp.float32)
    )
    crossed_low = crossed.astype(jnp.bfloat16)
    upward = project(crossed_low, full_up)
    activated, gelu_pull = jax.vjp(exact_gelu, upward)
    activated_low = activated.astype(jnp.bfloat16)
    down = project(activated_low, full_down)
    result, norm_ffn_pull = jax.vjp(layer_norm, crossed + down, full_gain_ffn.astype(jnp.float32))
    ffn_grad, gainffn_part = norm_ffn_pull(cotangent.astype(jnp.float32))
    down_low = ffn_grad.astype(jnp.bfloat16)
    (upward_grad,) = gelu_pull(project_back(down_low, full_down))
    upward_low = upward_grad.astype(jnp.bfloat16)
    crossed_grad = ffn_grad + project_back(upward_low, full_up)
    cross_res_grad, gaincross_part = norm_cross_pull(crossed_grad)
    cross_res_low = cross_res_grad.astype(jnp.bfloat16)
    cross_ctx_grad = project_back(cross_res_low, full_cout).astype(jnp.bfloat16).reshape(head_shape)
    cross_prob_grad = jnp.einsum(
        "jrthe,rshe->jrhts", cross_ctx_grad, all_enc_values, preferred_element_type=jnp.float32
    )
    enc_value_main = jnp.einsum(
        "jrhts,jrthe->rshe", cross_low, cross_ctx_grad, preferred_element_type=jnp.float32
    )
    (cross_score_grad,) = cross_pull(cross_prob_grad)
    cross_score_low = jnp.where(enc_live, cross_score_grad, 0.0).astype(jnp.bfloat16)
    cross_query_grad = jnp.einsum(
        "jrhts,rshe->jrthe", cross_score_low, all_enc_keys, preferred_element_type=jnp.float32
    )
    enc_key_main = jnp.einsum(
        "jrhts,jrthe->rshe", cross_score_low, cross_heads, preferred_element_type=jnp.float32
    )
    cross_query_back = (cross_query_grad.astype(jnp.bfloat16) * 0.125).reshape(flat_shape)
    normed_grad = cross_res_grad + project_back(cross_query_back, full_cquery)
    residual_grad, gainattn_part = norm_attn_pull(normed_grad)
    attn_low = residual_grad.astype(jnp.bfloat16)
    context_grad = project_back(attn_low, full_attn_out).astype(jnp.bfloat16).reshape(head_shape)
    main_prob_grad = jnp.einsum(
        "jrthe,rshe->jrhts", context_grad, all_values, preferred_element_type=jnp.float32
    )
    own_prob_grad = turned(
        jnp.einsum(
            "jrthe,jrthe->jrth", context_grad, value_heads, preferred_element_type=jnp.float32
        )
    )
    value_main = jnp.einsum(
        "jrhts,jrthe->rshe", main_low, context_grad, preferred_element_type=jnp.float32
    )
    value_own = turned(own_prob)[..., None] * context_grad.astype(jnp.float32)
    main_score_grad, own_score_grad = softmax_pull((main_prob_grad, own_prob_grad))
    score_low = jnp.where(allowed, main_score_grad, 0.0).astype(jnp.bfloat16)
    own_grad = turned(jnp.where(own_ok, own_score_grad, 0.0))
    query_grad = jnp.einsum(
        "jrhts,rshe->jrthe", score_low, all_keys, preferred_element_type=jnp.float32
    )
    query_grad = query_grad + own_grad[..., None] * key_heads.astype(jnp.float32)
    key_main = jnp.einsum(
        "jrhts,jrthe->rshe", score_low, query_heads, preferred_element_type=jnp.float32
    )
    key_own = own_grad[..., None] * query_heads.astype(jnp.float32)
    first_bucket = (jnp.arange(BUCKETS) == 0).astype(jnp.float32)
    rel_grad = (
        jnp.einsum("jrhts,tsb->jrthb", score_low, hot, preferred_element_type=jnp.float32)
        + own_grad[..., None] * first_bucket
    )
    key_sum, value_sum, enc_key_sum, enc_value_sum = (
        lax.psum_scatter(
            key_main.astype(jnp.bfloat16), "seq", scatter_dimension=1, tiled=True
        ).astype(jnp.float32),
        lax.psum_scatter(
            value_main.astype(jnp.bfloat16), "seq", scatter_dimension=1, tiled=True
        ).astype(jnp.float32),
        lax.psum_scatter(
            enc_key_main.astype(jnp.bfloat16), "seq", scatter_dimension=1, tiled=True
        ).astype(jnp.float32),
        lax.psum_scatter(
            enc_value_main.astype(jnp.bfloat16), "seq", scatter_dimension=1, tiled=True
        ).astype(jnp.float32),
    )
    key_grad = jnp.concatenate([key_sum[None], key_own[1:]], axis=0)
    value_grad = jnp.concatenate([value_sum[None], value_own[1:]], axis=0)
    query_back = (query_grad.astype(jnp.bfloat16) * 0.125).reshape(flat_shape)
    key_back = key_grad.reshape(flat_shape).astype(jnp.bfloat16)
    value_back = value_grad.reshape(flat_shape).astype(jnp.bfloat16)
    rel_back = rel_grad.reshape(streams, row_count, local_len, HEADS * BUCKETS).astype(jnp.bfloat16)
    enc_key_back = enc_key_sum.reshape(row_count, enc_local, width).astype(jnp.bfloat16)
    enc_value_back = enc_value_sum.reshape(row_count, enc_local, width).astype(jnp.bfloat16)
    encoder_grad = project_back(enc_key_back, full_ckey) + project_back(enc_value_back, full_cvalue)
    hidden_grad = (
        residual_grad + project_back(query_back, full_query) + project_back(key_back, full_key)
    )
    hidden_grad = (
        hidden_grad + project_back(value_back, full_value) + project_back(rel_back, full_relative)
    )
    xs = [
        flatten_rows(array)
        for array in (
            activated_low,
            crossed_low,
            cross_context_low,
            normed_low,
            context_low,
            hidden,
            encoder,
        )
    ]
    gs = [
        flatten_rows(array)
        for array in (
            down_low,
            upward_low,
            cross_res_low,
            cross_query_back,
            attn_low,
            query_back,
            key_back,
            value_back,
            rel_back,
            enc_key_back,
            enc_value_back,
        )
    ]
    pairs = [(0, 0), (1, 1), (2, 2), (3, 3), (4, 4), (5, 5), (5, 6), (5, 7), (5, 8), (6, 9), (6, 10)]
    gain_parts = jnp.stack([gainattn_part, gaincross_part, gainffn_part])
    if kernels:
        gain_parts = jnp.transpose(gain_parts.reshape(3, devices, -1), (1, 0, 2))
        gain_parts = jnp.pad(gain_parts, ((0, 0), (0, 5), (0, 128 - gain_parts.shape[2])))
        gain_parts = gain_parts.reshape(2, 2, ndp // 2, 2, 8, 128)
        *sums, gain_sums = reduce_grads(xs, gs, pairs, gain_parts, ndp // 2)
        gain_sums = gain_sums[:3, : width // devices]
    else:
        sums = [
            lax.psum_scatter(
                weight_grad(xs[i], gs[j]), ("seq", "dp"), scatter_dimension=0, tiled=True
            )
            for i, j in pairs
        ]
        gain_sums = lax.psum_scatter(gain_parts, ("seq", "dp"), scatter_dimension=1, tiled=True)
    gainattn_sum, gaincross_sum, gainffn_sum = gain_sums
    (
        down_sum,
        up_sum,
        cout_sum,
        cquery_sum,
        outproj_sum,
        query_sum,
        keyw_sum,
        valuew_sum,
        relative_sum,
        ckey_sum,
        cvalue_sum,
    ) = sums
    return (
        result.astype(jnp.bfloat16),
        hidden_grad,
        encoder_grad,
        query_sum,
        keyw_sum,
        valuew_sum,
        outproj_sum,
        relative_sum,
        cquery_sum,
        ckey_sum,
        cvalue_sum,
        cout_sum,
        up_sum,
        down_sum,
        gainattn_sum,
        gaincross_sum,
        gainffn_sum,
    )


def solution(mesh):
    in_specs = (
        P(None, "dp", "seq", None),
        P("dp", "seq", None),
        P("dp"),
        P("dp"),
        P("dp", None),
        P("dp", None),
        P("dp", None),
        P("dp", None),
        P("dp", None),
        P("dp", None),
        P("dp", None),
        P("dp", None),
        P("dp", None),
        P("dp", None),
        P("dp", None),
        P("dp"),
        P("dp"),
        P("dp"),
        P(None, "dp", "seq", None),
    )
    out_specs = (
        P(None, "dp", "seq", None),
        P(None, "dp", "seq", None),
        P("dp", "seq", None),
        P(("seq", "dp"), None),
        P(("seq", "dp"), None),
        P(("seq", "dp"), None),
        P(("seq", "dp"), None),
        P(("seq", "dp"), None),
        P(("seq", "dp"), None),
        P(("seq", "dp"), None),
        P(("seq", "dp"), None),
        P(("seq", "dp"), None),
        P(("seq", "dp"), None),
        P(("seq", "dp"), None),
        P(("seq", "dp")),
        P(("seq", "dp")),
        P(("seq", "dp")),
    )
    return jax.shard_map(local, mesh=mesh, in_specs=in_specs, out_specs=out_specs, check_vma=False)
```

```python
import math

import jax
import jax.numpy as jnp
from jax import lax
from jax.experimental import pallas as pl
from jax.experimental.pallas import tpu as pltpu
from jax.sharding import PartitionSpec as P

MESH = pl.DeviceIdType.MESH

HEADS = 16
HEAD_DIM = 64
BUCKETS = 32


eps_norm = 1e-05
bucket_edges = [step_index for step_index in range(1, 16)] + [
    int(math.ceil(16 * 8 ** ((step_index - 16) / 16))) for step_index in range(16, 32)
]


def flatten_rows(array):
    return array.reshape(-1, array.shape[-1])


def weight_grad(array, grad_rows):
    return jnp.einsum(
        "nd,ne->de",
        flatten_rows(array),
        flatten_rows(grad_rows),
        preferred_element_type=jnp.float32,
    )


def remote(src, dst, send, recv, to):
    return pltpu.make_async_remote_copy(
        src_ref=src, dst_ref=dst, send_sem=send, recv_sem=recv, device_id=to, device_id_type=MESH
    )


def place():
    s = lax.axis_index("seq")
    d = lax.axis_index("dp")
    z, c = d // 2, lax.rem(d, 2)
    sx = s + 1 - 2 * lax.rem(s, 2)
    sy = lax.rem(s + 2, 4)
    return s, z, c, sx, sy


def greet(nz):
    s, z, c, sx, sy = place()
    barrier = pltpu.get_barrier_semaphore()
    dests = [(s, 2 * z + 1 - c), (sx, 2 * z + c), (sy, 2 * z + c)]
    for dz in range(1, nz):
        dests.append((s, 2 * lax.rem(z + dz, nz) + c))
    for dest in dests:
        pl.semaphore_signal(barrier, inc=1, device_id=dest, device_id_type=MESH)
    pl.semaphore_wait(barrier, len(dests))


def gather_weights_kernel(count, nz, *refs):
    shards, planes = refs[:count], refs[count : count + 2]
    wholes, full_planes = refs[count + 2 : 2 * count + 2], refs[2 * count + 2 : 2 * count + 4]
    local_sem, send, recv, plane_send, plane_recv = refs[2 * count + 4 :]
    s, z, c, sx, sy = place()
    own = 2 * z + c
    core = (s, 2 * z + 1 - c)
    beside_x, beside_y = (sx, own), (sy, own)
    greet(nz)
    started = []

    def put(copy):
        copy.start()
        started.append(copy)

    items = []
    for w in range(count):
        if shards[w].shape[0] % 128:
            items.append((w, 0, 0, None))
            continue
        for row in range(0, shards[w].shape[0], 128):
            wide = min(shards[w].shape[1], 1024)
            for col in range(0, shards[w].shape[1], wide):
                items.append((w, row, 128, pl.ds(col, wide)))
    steps = len(items)
    split = [item[2] > 0 for item in items]

    def cut(ref, i, q=None, half=None):
        _, row, height, cols = items[i]
        if not height:
            return ref
        if q is not None:
            height = height // 4
            row = row + q * height
        if half is not None:
            height = height // 2
            row = row + half * height
        return ref.at[pl.ds(row, height), cols]

    def shard(i, q=None):
        return cut(shards[items[i][0]], i, q)

    def whole(i, block, q=None, half=None):
        return cut(wholes[items[i][0]].at[block], i, q, half)

    def along_z(i):
        here = pltpu.make_async_copy(shard(i), whole(i, own), local_sem.at[i])
        here.start()
        started.append(here)
        q = s if split[i] else None
        for dz in range(1, nz):
            to = (s, 2 * lax.rem(z + dz, nz) + c)
            put(remote(shard(i, q), whole(i, own, q), send.at[i, dz, 0], recv.at[i, dz, 0], to))
        put(remote(shard(i), whole(i, own), send.at[i, 0, 0], recv.at[i, 0, 0], core))

    def moved(i, dz, kind, q, half, to):
        part = whole(i, 2 * lax.rem(z + nz - dz, nz) + c, q if split[i] else None, half)
        return remote(part, part, send.at[i, dz, kind], recv.at[i, dz, kind], to)

    def to_core(i, dz, kind, q, half):
        put(moved(i, dz, kind, q, half, core))

    def first(i):
        for dz in range(1, nz):
            moved(i, dz, 0, s, None, core).wait_recv()
            if split[i]:
                put(moved(i, dz, 1, s, None, beside_x))
                put(moved(i, dz, 2, s, None, beside_y))
            to_core(i, dz, 5, s, None)

    def second(i):
        if not split[i]:
            return
        for dz in range(1, nz):
            moved(i, dz, 1, sx, None, core).wait_recv()
            put(moved(i, dz, 4, sx, 0, beside_y))
            to_core(i, dz, 6, sx, None)
            moved(i, dz, 2, sy, None, core).wait_recv()
            put(moved(i, dz, 3, sy, 1, beside_x))
            to_core(i, dz, 7, sy, None)

    def third(i):
        if not split[i]:
            return
        for dz in range(1, nz):
            moved(i, dz, 4, 3 - s, 0, core).wait_recv()
            to_core(i, dz, 8, 3 - s, 0)
            moved(i, dz, 3, 3 - s, 1, core).wait_recv()
            to_core(i, dz, 9, 3 - s, 1)

    def last(i):
        other = 1 - c
        block = whole(i, 2 * z + other)
        remote(block, block, send.at[i, 0, 0], recv.at[i, 0, 0], core).wait_recv()
        for dz in range(1, nz):
            kinds = [(5, s if split[i] else None, None)]
            if split[i]:
                kinds += [(6, sx, None), (7, sy, None), (8, 3 - s, 0), (9, 3 - s, 1)]
            for kind, q, half in kinds:
                part = whole(i, 2 * lax.rem(z + nz - dz, nz) + other, q, half)
                remote(part, part, send.at[i, dz, kind], recv.at[i, dz, kind], core).wait_recv()

    def plane(i, kind, q, half, to):
        rows = full_planes[i].shape[0]
        part = full_planes[i].at[pl.ds(half * (rows // 2), rows // 2), q]
        return remote(part, part, plane_send.at[i, kind], plane_recv.at[i, kind], to)

    def plane_part(i):
        return planes[i].at[0] if len(planes[i].shape) == 4 else planes[i]

    def plane_whole(i, kind, q, to):
        return remote(
            plane_part(i), full_planes[i].at[:, q], plane_send.at[i, kind], plane_recv.at[i, kind], to
        )

    def plane_first(i):
        here = pltpu.make_async_copy(plane_part(i), full_planes[i].at[:, s], local_sem.at[steps + i])
        here.start()
        started.append(here)
        put(plane_whole(i, 0, s, beside_x))
        put(plane_whole(i, 1, s, beside_y))

    def plane_second(i):
        plane_whole(i, 0, sx, core).wait_recv()
        put(plane(i, 2, sx, 0, beside_y))
        plane_whole(i, 1, sy, core).wait_recv()
        put(plane(i, 3, sy, 1, beside_x))

    def plane_last(i):
        plane(i, 2, 3 - s, 0, core).wait_recv()
        plane(i, 3, 3 - s, 1, core).wait_recv()

    ahead = 4
    for i in range(2):
        plane_first(i)
    for i in range(min(ahead, steps)):
        along_z(i)
    for i in range(steps + 2):
        if i < steps:
            first(i)
        if ahead + i < steps:
            along_z(ahead + i)
        if 1 <= i <= steps:
            second(i - 1)
        if i in (1, 2):
            plane_second(i - 1)
        if i >= 2:
            third(i - 2)
    for i in range(2):
        plane_last(i)
    for i in range(steps):
        last(i)
    for copy in started:
        if hasattr(copy, "wait_send") and copy.is_remote:
            copy.wait_send()
        else:
            copy.wait()


def gather_weights(shards, hidden, encoder, ndp):
    nz = ndp // 2
    count = len(shards)
    steps = sum(max(1, w.size // (128 * 1024)) for w in shards)
    planes = jax.ShapeDtypeStruct((encoder.shape[0], 4) + encoder.shape[1:], encoder.dtype)
    return pl.pallas_call(
        lambda *refs: gather_weights_kernel(count, nz, *refs),
        out_shape=[jax.ShapeDtypeStruct((ndp,) + w.shape, w.dtype) for w in shards] + [planes] * 2,
        in_specs=[pl.BlockSpec(memory_space=pltpu.VMEM)] * (count + 2),
        out_specs=[pl.BlockSpec(memory_space=pl.ANY)] * (count + 2),
        scratch_shapes=[
            pltpu.SemaphoreType.DMA((steps + 2,)),
            pltpu.SemaphoreType.DMA((steps, nz, 10)),
            pltpu.SemaphoreType.DMA((steps, nz, 10)),
            pltpu.SemaphoreType.DMA((2, 4)),
            pltpu.SemaphoreType.DMA((2, 4)),
        ],
        compiler_params=pltpu.CompilerParams(collective_id=0, has_side_effects=True),
        name="gather_weights",
    )(*shards, hidden, encoder)


RING = 8


def reduce_grads_kernel(plan, nz, n_x, n_g, n_out, *refs):
    at = 0
    xs, at = refs[at : at + n_x], at + n_x
    gs, at = refs[at : at + n_g], at + n_g
    gain_part, at = refs[at], at + 1
    shares, at = refs[at : at + 2], at + 2
    outs, at = refs[at : at + n_out], at + n_out
    gain_out, at = refs[at], at + 1
    share_outs, at = refs[at : at + 2], at + 2
    kinds = []
    for _ in range(3):
        kinds.append(refs[at : at + 5])
        at += 5
    share1, share2, send, recv, credit = refs[at:]
    s, z, c, sx, sy = place()
    own = 2 * z + c
    x, y = lax.rem(s, 2), s // 2
    core = (s, 2 * z + 1 - c)
    beside_x, beside_y = (sx, own), (sy, own)
    greet(nz)
    count = len(plan)

    def buffers(k):
        kind, slot = plan[k][0], plan[k][1]
        if kind == 3:
            return None, shares[slot // 2].at[:, :, slot % 2], share1.at[slot], share2.at[slot], None
        part, held0, held1, held2, held3 = kinds[kind]
        if kind == 2:
            return gain_part, held0.at[slot], held1.at[slot], held2.at[slot], held3.at[slot]
        return (part.at[slot % 2], held0.at[slot % RING], held1.at[slot], held2.at[slot], held3.at[slot])

    def core_copy(k):
        part, held0 = buffers(k)[:2]
        return remote(part.at[:, :, :, 1 - c], held0, send.at[k, 0], recv.at[k, 0], core)

    def first_copy(k):
        _, held0, held1 = buffers(k)[:3]
        if k % 2 == 0:
            return remote(held0.at[:, 1 - x], held1, send.at[k, 1], recv.at[k, 1], beside_x)
        return remote(held0.at[1 - y], held1, send.at[k, 1], recv.at[k, 1], beside_y)

    def second_copy(k):
        held1, held2 = buffers(k)[2:4]
        if k % 2 == 0:
            return remote(held1.at[1 - y], held2, send.at[k, 2], recv.at[k, 2], beside_y)
        return remote(held1.at[1 - x], held2, send.at[k, 2], recv.at[k, 2], beside_x)

    def z_copy(k, dz):
        held2, held3 = buffers(k)[3:5]
        zt = lax.rem(z + dz, nz)
        return remote(
            held2.at[zt], held3.at[dz - 1], send.at[k, 2 + dz], recv.at[k, 2 + dz], (s, 2 * zt + c)
        )

    def added(held, mine):
        held[...] = (held[...].astype(jnp.float32) + mine.astype(jnp.float32)).astype(held.dtype)

    def make(k):
        kind, slot, xi, gi, _, col, wide = plan[k]
        if kind == 3:
            return
        if kind < 2:
            part = buffers(k)[0]
            left, right = xs[xi], gs[gi]
            block = part.shape[4]
            if slot >= 2:
                core_copy(before[k]).wait_send()
            group = 256 // block
            for i in range(left.shape[1] // 256):
                product = lax.dot_general(
                    left[:, i * 256 : (i + 1) * 256],
                    right[:, col : col + wide],
                    (((0,), (0,)), ((), ())),
                    preferred_element_type=jnp.float32,
                )
                index = i * group
                i_s, rest = divmod(index, 2 * nz)
                zs = rest // 2
                part[i_s // 2, i_s % 2, zs : zs + group // 2] = product.reshape(group // 2, 2, block, wide).astype(
                    part.dtype
                )
        if kind < 2 and slot >= RING:
            pl.semaphore_wait(credit.at[kind], 1)
        core_copy(k).start()

    def after_core(k):
        part, held0 = buffers(k)[:2]
        if plan[k][0] == 3:
            first_copy(k).start()
            return
        core_copy(k).wait_recv()
        added(held0, part[:, :, :, c])
        first_copy(k).start()

    def after_first(k):
        _, held0, held1 = buffers(k)[:3]
        first_copy(k).wait_recv()
        added(held1, held0[:, x] if k % 2 == 0 else held0[y])
        second_copy(k).start()
        kind, slot = plan[k][:2]
        first_copy(k).wait_send()
        if kind < 2 and slot + RING < sum(p[0] == kind for p in plan):
            pl.semaphore_signal(credit.at[kind], inc=1, device_id=core, device_id_type=MESH)

    def after_second(k):
        held1, held2 = buffers(k)[2:4]
        second_copy(k).wait_recv()
        if plan[k][0] == 3:
            mine = (held1[y] if k % 2 == 0 else held1[x]).astype(jnp.float32)
            slot = plan[k][1]
            share_outs[slot // 2][slot % 2] = held2[...].astype(jnp.float32) + mine
            return
        added(held2, held1[y] if k % 2 == 0 else held1[x])
        for dz in range(1, nz):
            z_copy(k, dz).start()

    def finish(k):
        if plan[k][0] == 3:
            return
        held2, held3 = buffers(k)[3:5]
        total = held2[z].astype(jnp.float32)
        for dz in range(1, nz):
            z_copy(k, dz).wait_recv()
            total = total + held3[dz - 1].astype(jnp.float32)
        kind, _, _, _, oi, col, wide = plan[k]
        if kind == 2:
            gain_out[...] = total
        else:
            outs[oi][:, col : col + wide] = total

    before = {}
    recent = {}
    for k in range(count):
        kind, slot = plan[k][0], plan[k][1]
        before[k] = recent.get((kind, slot - 2))
        recent[(kind, slot)] = k
    followed = set(v for v in before.values() if v is not None)

    for t in range(count + 7):
        if t >= 7:
            finish(t - 7)
        if 5 <= t < count + 5:
            after_second(t - 5)
        if 3 <= t < count + 3:
            after_first(t - 3)
        if t < count:
            make(t)
        if 1 <= t < count + 1:
            after_core(t - 1)
    for k in range(count):
        if k not in followed and plan[k][0] < 3:
            core_copy(k).wait_send()
        second_copy(k).wait_send()
        for dz in range(1, nz if plan[k][0] < 3 else 1):
            z_copy(k, dz).wait_send()


def reduce_grads(xs, gs, pairs, gain_part, shares, nz):
    plan, slots = [(3, i, 0, 0, 0, 0, 0) for i in range(4)], [0, 0, 0]
    blocks, columns = [], []
    ndev = 8 * nz
    for oi, (xi, gi) in enumerate(pairs):
        rows, wide = xs[xi].shape[1], gs[gi].shape[1]
        columns.append((rows // ndev, wide))
        kind = 0 if rows // ndev <= 32 else 1
        step = (512, 256)[kind]
        for col in range(0, wide, step):
            plan.append((kind, slots[kind], xi, gi, oi, col, step))
            slots[kind] += 1
    plan.append((2, 0, 0, 0, 0, 0, 128))
    rb = min(rows for rows, _ in columns)
    shapes = [((rb, 512), jnp.bfloat16, slots[0]), ((max(rows for rows, _ in columns), 256), jnp.bfloat16, slots[1])]
    scratch = []
    for (tail, kind_type, n) in shapes + [((8, 128), jnp.float32, 1)]:
        scratch.append(
            pltpu.VMEM((2, 2, 2, nz, 2) + tail if kind_type == jnp.bfloat16 else (8, 128), kind_type)
        )
        scratch.append(pltpu.VMEM((min(n, RING), 2, 2, nz) + tail, kind_type))
        scratch.append(pltpu.VMEM((n, 2, nz) + tail, kind_type))
        scratch.append(pltpu.VMEM((n, nz) + tail, kind_type))
        scratch.append(pltpu.VMEM((n, nz - 1) + tail, kind_type))
    n = len(plan)
    vmem = pl.BlockSpec(memory_space=pltpu.VMEM)
    outs = [jax.ShapeDtypeStruct(shape, jnp.float32) for shape in columns]
    outs.append(jax.ShapeDtypeStruct((8, 128), jnp.float32))
    share = shares[0].shape[3:]
    outs += [jax.ShapeDtypeStruct(a.shape[2:], jnp.float32) for a in shares]
    return pl.pallas_call(
        lambda *refs: reduce_grads_kernel(plan, nz, len(xs), len(gs), len(columns), *refs),
        out_shape=outs,
        in_specs=[vmem] * (len(xs) + len(gs) + 3),
        out_specs=[vmem] * len(outs),
        scratch_shapes=scratch
        + [pltpu.VMEM((4, 2) + share, jnp.bfloat16), pltpu.VMEM((4,) + share, jnp.bfloat16)]
        + [pltpu.SemaphoreType.DMA((n, 2 + nz)), pltpu.SemaphoreType.DMA((n, 2 + nz))]
        + [pltpu.SemaphoreType.REGULAR((2,))],
        compiler_params=pltpu.CompilerParams(
            collective_id=1, has_side_effects=True, vmem_limit_bytes=62 * 2**20
        ),
        name="reduce_grads",
    )(*xs, *gs, gain_part, *shares)

NEG = -1000000000.0


def mm(left, right):
    return jnp.dot(left, right, preferred_element_type=jnp.float32)


def mm_back(left, right):
    return lax.dot_general(
        left, right, (((1,), (1,)), ((), ())), preferred_element_type=jnp.float32
    )


def mm_grad(left, right):
    return lax.dot_general(
        left, right, (((0,), (0,)), ((), ())), preferred_element_type=jnp.float32
    )


def tiles(width, body):
    def step(i, carry):
        body(pl.ds(pl.multiple_of(i * 256, 256), 256))
        return carry

    lax.fori_loop(0, width // 256, step, 0)


def row_tiles(rows, body, step_rows=64):
    def step(i, carry):
        body(pl.ds(pl.multiple_of(i * step_rows, step_rows), step_rows))
        return carry

    lax.fori_loop(0, rows // step_rows, step, 0)


def heads_in(tile):
    lane = lax.broadcasted_iota(jnp.int32, tile.shape, 1) // (tile.shape[1] // 4)
    return jnp.concatenate(
        [jnp.where(lane == h, tile, jnp.zeros_like(tile)) for h in range(4)], axis=0
    )


def heads_out(stacked):
    n, wide = stacked.shape[0] // 4, stacked.shape[1]
    lane = lax.broadcasted_iota(jnp.int32, (n, wide), 1) // (wide // 4)
    result = stacked[3 * n :]
    for h in (2, 1, 0):
        result = jnp.where(lane == h, stacked[h * n : (h + 1) * n], result)
    return result


def head_lanes(columns, wide):
    n = columns[0].shape[0]
    lane = lax.broadcasted_iota(jnp.int32, (n, wide), 1) // (wide // 4)
    result = jnp.broadcast_to(columns[3], (n, wide))
    for h in (2, 1, 0):
        result = jnp.where(lane == h, jnp.broadcast_to(columns[h], (n, wide)), result)
    return result


def head_sums(product):
    n, wide = product.shape
    lane = lax.broadcasted_iota(jnp.int32, (n, wide), 1) // (wide // 4)
    return [
        jnp.sum(jnp.where(lane == h, product, 0.0), axis=1, keepdims=True) for h in range(4)
    ]


def bucket_of(distance):
    total = jnp.zeros_like(distance)
    for edge in bucket_edges:
        total = total + (distance >= edge).astype(jnp.int32)
    return total


def hot_forward(start, span):
    lag = lax.broadcasted_iota(jnp.int32, (128, span), 1)
    row = lax.rem(lax.broadcasted_iota(jnp.int32, (128, span), 0), BUCKETS)
    distance = lax.rem(start - lag + span, span)
    return jnp.where(bucket_of(distance) == row, 1.0, 0.0).astype(jnp.bfloat16)


def hot_backward(start, span):
    lag = lax.broadcasted_iota(jnp.int32, (span, 128), 0)
    column = lax.rem(lax.broadcasted_iota(jnp.int32, (span, 128), 1), BUCKETS)
    distance = lax.rem(start + lag + 1, span)
    return jnp.where(bucket_of(distance) == column, 1.0, 0.0).astype(jnp.bfloat16)


def skewed(array, block):
    return jnp.concatenate(
        [
            pltpu.roll(array[i : i + block], 0, 1, stride=1, stride_axis=0)
            for i in range(0, array.shape[0], block)
        ],
        axis=0,
    )


def norm_rows(values):
    centred = values - jnp.mean(values, axis=1, keepdims=True)
    scale = lax.rsqrt(jnp.mean(centred * centred, axis=1, keepdims=True) + eps_norm)
    return centred * scale, scale


def norm_back(grad, normal, scale, gain):
    grad = grad * gain
    return scale * (
        grad
        - jnp.mean(grad, axis=1, keepdims=True)
        - normal * jnp.mean(grad * normal, axis=1, keepdims=True)
    )


def add_rows(total_ref, index, product):
    total_ref[index] += jnp.sum(product.reshape(-1, 8, product.shape[1]), axis=0)


class Fetch:
    def __init__(self, sources, targets, sems):
        self.copies = [
            pltpu.make_async_copy(src, dst, sems.at[i])
            for i, (src, dst) in enumerate(zip(sources, targets))
        ]
        self.targets = targets
        self.waited = set()
        for copy in self.copies:
            copy.start()

    def __getitem__(self, i):
        if i not in self.waited:
            self.waited.add(i)
            self.copies[i].wait()
        return self.targets[i]


def forward_kernel(rows, local_len, *refs):
    (
        hidden,
        mains,
        states,
        lengths,
        enc_lengths,
        gains,
        *weights,
    ) = refs[:14]
    (hid, x_all, query, keys, values, prob, prob_own, context, ckeys, cvalues) = refs[14:24]
    (normal, normal_scale, normed_low, cquery, cprob, ccontext) = refs[24:30]
    rel, residual = refs[30:32]
    fetch = Fetch(weights, refs[32:40], refs[40])
    w_key, w_value, w_query, w_relative, w_ckey, w_cvalue, w_out, w_cquery = range(8)
    width = hid.shape[1]
    mine = 3 * local_len
    span = mains.shape[0] // rows
    start = lax.axis_index("seq") * local_len
    x_all[: rows * span] = mains[...]
    for r in range(rows):
        for j in range(3):
            tile = hidden[j, r]
            hid[r * mine + j * local_len : r * mine + (j + 1) * local_len] = tile
            if j:
                at = rows * span + (2 * r + j - 1) * local_len
                x_all[at : at + local_len] = tile

    def project(left, w, target, scale=None):
        weight = fetch[w]

        def body(cols):
            product = mm(left[...], weight[:, cols])
            if scale is not None:
                product = product * scale
            target[:, cols] = product.astype(target.dtype)

        tiles(target.shape[1], body)

    project(x_all, w_key, keys)
    project(x_all, w_value, values)
    project(hid, w_query, query, 0.125)
    project(hid, w_relative, rel)
    hot = hot_forward(start, span)

    def attend(step, carry):
        r, g = step // 4, lax.rem(step, 4)
        cols = pl.ds(pl.multiple_of(g * 256, 256), 256)
        own_rows = pl.ds(pl.multiple_of(r * mine, local_len), mine)
        main_rows = pl.ds(pl.multiple_of(r * span, span), span)
        side_rows = pl.ds(pl.multiple_of(rows * span + r * 2 * local_len, local_len), 2 * local_len)
        q_tile = query[own_rows, cols]
        rel_tile = rel[own_rows, pl.ds(pl.multiple_of(g * 128, 128), 128)]
        side_key = keys[side_rows, cols].astype(jnp.float32)
        side_value = values[side_rows, cols].astype(jnp.float32)
        zero = jnp.zeros((local_len, 256), jnp.float32)
        scores = mm_back(heads_in(q_tile), keys[main_rows, cols])
        bias = skewed(mm(heads_in(rel_tile), hot), local_len)
        products = q_tile.astype(jnp.float32) * jnp.concatenate([zero, side_key], axis=0)
        own_dot = head_sums(products)
        rel_lane = lax.broadcasted_iota(jnp.int32, (mine, 128), 1)
        rel_wide = rel_tile.astype(jnp.float32)
        row = lax.broadcasted_iota(jnp.int32, (mine, span), 0)
        at = lax.broadcasted_iota(jnp.int32, (mine, span), 1)
        ahead = start + lax.rem(row, local_len) + jnp.where(row < local_len, 1, 0)
        kept = (at < ahead) & (at < lengths[r])
        first = lax.broadcasted_iota(jnp.int32, (mine, 1), 0) < local_len
        low, owns = [], []
        for h in range(4):
            part = slice(h * mine, (h + 1) * mine)
            score = jnp.where(kept, scores[part] + bias[part], NEG)
            near = jnp.sum(jnp.where(rel_lane == h * BUCKETS, rel_wide, 0.0), axis=1, keepdims=True)
            own = jnp.where(first, NEG, own_dot[h] + near)
            peak = jnp.maximum(jnp.max(score, axis=1, keepdims=True), own)
            power = jnp.exp(score - peak)
            own_power = jnp.exp(own - peak)
            share = 1.0 / (jnp.sum(power, axis=1, keepdims=True) + own_power)
            low.append((power * share).astype(jnp.bfloat16))
            owns.append(own_power * share)
        low = jnp.concatenate(low, axis=0)
        prob[step] = low
        spread = head_lanes(owns, 256)
        prob_own[own_rows, cols] = spread
        total = heads_out(mm(low, values[main_rows, cols]))
        total = total + spread * jnp.concatenate([zero, side_value], axis=0)
        context[own_rows, cols] = total.astype(context.dtype)
        return carry

    lax.fori_loop(0, 4 * rows, attend, 0)
    project(states, w_ckey, ckeys)
    project(states, w_cvalue, cvalues)
    weight_out = fetch[w_out]

    def out_body(cols):
        residual[:, cols] = hid[:, cols].astype(jnp.float32) + mm(context[...], weight_out[:, cols])

    tiles(width, out_body)

    def norm_body(part):
        normal[part], scale = norm_rows(residual[part])
        normal_scale[part] = jnp.broadcast_to(scale, (scale.shape[0], 128))
        normed_low[part] = (normal[part] * gains[0:1]).astype(jnp.bfloat16)

    row_tiles(hid.shape[0], norm_body)
    project(normed_low, w_cquery, cquery, 0.125)

    def cross(step, carry):
        r, g = step // 4, lax.rem(step, 4)
        cols = pl.ds(pl.multiple_of(g * 256, 256), 256)
        own_rows = pl.ds(pl.multiple_of(r * mine, local_len), mine)
        main_rows = pl.ds(pl.multiple_of(r * span, span), span)
        scores = mm_back(heads_in(cquery[own_rows, cols]), ckeys[main_rows, cols])
        at = lax.broadcasted_iota(jnp.int32, (mine, span), 1)
        kept = at < enc_lengths[r]
        low = []
        for h in range(4):
            score = jnp.where(kept, scores[h * mine : (h + 1) * mine], NEG)
            power = jnp.exp(score - jnp.max(score, axis=1, keepdims=True))
            share = 1.0 / jnp.sum(power, axis=1, keepdims=True)
            low.append((power * share).astype(jnp.bfloat16))
        low = jnp.concatenate(low, axis=0)
        cprob[step] = low
        ccontext[own_rows, cols] = heads_out(mm(low, cvalues[main_rows, cols])).astype(
            ccontext.dtype
        )
        return carry

    lax.fori_loop(0, 4 * rows, cross, 0)


def middle_kernel(
    rows,
    local_len,
    normal,
    ccontext,
    gains,
    cotangent,
    any_cout,
    any_up,
    any_down,
    output,
    crossed_low,
    activated,
    last_low,
    up_back,
    cross_grad,
    cross_low,
    ccontext_back,
    gain_total,
    normal2,
    scale2,
    slope,
    residual,
    v_cout,
    v_up,
    v_down,
    sems,
):
    fetch = Fetch((any_cout, any_up, any_down), (v_cout, v_up, v_down), sems)
    tokens, width = normal.shape
    mine = 3 * local_len
    gain_total[...] = jnp.zeros_like(gain_total)
    weight_cout = fetch[0]

    def cross_body(cols):
        residual[:, cols] = normal[:, cols] * gains[0:1, cols] + mm(
            ccontext[...], weight_cout[:, cols]
        )

    tiles(width, cross_body)

    def norm_body(part):
        normal2[part], scale = norm_rows(residual[part])
        scale2[part] = jnp.broadcast_to(scale, (scale.shape[0], 128))
        crossed_low[part] = (normal2[part] * gains[1:2]).astype(jnp.bfloat16)

    row_tiles(tokens, norm_body)
    weight_up = fetch[1]

    def up_body(cols):
        value = mm(crossed_low[...], weight_up[:, cols])
        below = 0.5 + 0.5 * lax.erf(value * (0.5**0.5))
        activated[:, cols] = (value * below).astype(jnp.bfloat16)
        density = jnp.exp(-0.5 * value * value) * (1.0 / math.sqrt(2.0 * math.pi))
        slope[:, cols] = (below + value * density).astype(jnp.bfloat16)

    tiles(activated.shape[1], up_body)
    weight_down = fetch[2]

    def down_body(cols):
        residual[:, cols] = normal2[:, cols] * gains[1:2, cols] + mm(
            activated[...], weight_down[:, cols]
        )

    tiles(width, down_body)
    for r in range(rows):
        for j in range(3):
            at = r * mine + j * local_len
            part = slice(at, at + local_len)
            normal3, scale = norm_rows(residual[part])
            output[j, r] = (normal3 * gains[2:3]).astype(output.dtype)
            above = cotangent[j, r].astype(jnp.float32)
            add_rows(gain_total, 2, above * normal3)
            grad = norm_back(above, normal3, scale, gains[2:3])
            residual[part] = grad
            last_low[part] = grad.astype(jnp.bfloat16)

    def down_back(cols):
        product = mm_back(last_low[...], weight_down[cols, :])
        up_back[:, cols] = (product * slope[:, cols].astype(jnp.float32)).astype(jnp.bfloat16)

    tiles(activated.shape[1], down_back)

    def up_back_body(cols):
        residual[:, cols] = residual[:, cols] + mm_back(up_back[...], weight_up[cols, :])

    tiles(width, up_back_body)

    def cross_norm_back(part):
        above = residual[part]
        add_rows(gain_total, 1, above * normal2[part])
        grad = norm_back(above, normal2[part], scale2[part][:, 0:1], gains[1:2])
        cross_grad[part] = grad
        cross_low[part] = grad.astype(jnp.bfloat16)

    row_tiles(tokens, cross_norm_back)

    def cout_back(cols):
        ccontext_back[:, cols] = mm_back(cross_low[...], weight_cout[cols, :]).astype(jnp.bfloat16)

    tiles(width, cout_back)


def backward_kernel(rows, local_len, *refs):
    (
        ccontext_back,
        cross_grad,
        cquery,
        ckeys,
        cvalues,
        cprob,
        normal,
        normal_scale,
        gains,
        query,
        keys,
        values,
        prob,
        prob_own,
        *weights,
    ) = refs[:22]
    (cquery_back, ckey_back, cvalue_back, attn_low, query_back, key_back) = refs[22:28]
    (value_back, rel_back, hidden_own, main_part, states_part, gain_total) = refs[28:34]
    residual, context_back = refs[34:36]
    fetch = Fetch(weights, refs[36:44], refs[44])
    w_cquery, w_out, w_ckey, w_cvalue, w_query, w_relative, w_key, w_value = range(8)
    tokens, width = query.shape
    mine = 3 * local_len
    span = ckeys.shape[0] // rows
    start = lax.axis_index("seq") * local_len
    gain_total[...] = jnp.zeros_like(gain_total)

    def cross(step, carry):
        r, g = step // 4, lax.rem(step, 4)
        cols = pl.ds(pl.multiple_of(g * 256, 256), 256)
        own_rows = pl.ds(pl.multiple_of(r * mine, local_len), mine)
        main_rows = pl.ds(pl.multiple_of(r * span, span), span)
        above = heads_in(ccontext_back[own_rows, cols])
        grads = mm_back(above, cvalues[main_rows, cols])
        low = []
        for h in range(4):
            part = slice(h * mine, (h + 1) * mine)
            share = cprob[step, part].astype(jnp.float32)
            weighted = share * grads[part]
            low.append(
                (weighted - share * jnp.sum(weighted, axis=1, keepdims=True)).astype(jnp.bfloat16)
            )
        low = jnp.concatenate(low, axis=0)
        back = heads_out(mm(low, ckeys[main_rows, cols])).astype(jnp.bfloat16)
        cquery_back[own_rows, cols] = back * jnp.bfloat16(0.125)
        ckey_back[main_rows, cols] = mm_grad(low, heads_in(cquery[own_rows, cols])).astype(
            jnp.bfloat16
        )
        cvalue_back[main_rows, cols] = mm_grad(cprob[step], above).astype(jnp.bfloat16)
        return carry

    lax.fori_loop(0, 4 * rows, cross, 0)
    weight_cquery = fetch[w_cquery]

    def cquery_body(cols):
        residual[:, cols] = cross_grad[:, cols] + mm_back(cquery_back[...], weight_cquery[cols, :])

    tiles(width, cquery_body)

    def attn_norm_back(part):
        above = residual[part]
        add_rows(gain_total, 0, above * normal[part])
        grad = norm_back(above, normal[part], normal_scale[part][:, 0:1], gains[0:1])
        residual[part] = grad
        attn_low[part] = grad.astype(jnp.bfloat16)

    row_tiles(tokens, attn_norm_back)
    weight_out = fetch[w_out]

    def out_back(cols):
        context_back[:, cols] = mm_back(attn_low[...], weight_out[cols, :]).astype(jnp.bfloat16)

    tiles(width, out_back)
    hot = hot_backward(start, span)
    turn = jnp.where(
        lax.broadcasted_iota(jnp.int32, (span, span), 0)
        + lax.broadcasted_iota(jnp.int32, (span, span), 1)
        == span - 1,
        1.0,
        0.0,
    ).astype(jnp.bfloat16)

    def attend(step, carry):
        r, g = step // 4, lax.rem(step, 4)
        cols = pl.ds(pl.multiple_of(g * 256, 256), 256)
        own_rows = pl.ds(pl.multiple_of(r * mine, local_len), mine)
        main_rows = pl.ds(pl.multiple_of(r * span, span), span)
        side_rows = pl.ds(pl.multiple_of(rows * span + r * 2 * local_len, local_len), 2 * local_len)
        above_tile = context_back[own_rows, cols]
        above = heads_in(above_tile)
        above_wide = above_tile.astype(jnp.float32)
        q_tile = query[own_rows, cols]
        zero = jnp.zeros((local_len, 256), jnp.float32)
        side_key = jnp.concatenate([zero, keys[side_rows, cols].astype(jnp.float32)], axis=0)
        side_value = jnp.concatenate([zero, values[side_rows, cols].astype(jnp.float32)], axis=0)
        spread = prob_own[own_rows, cols]
        grads = mm_back(above, values[main_rows, cols])
        own_grads = head_sums(above_wide * side_value)
        low, own_low = [], []
        for h in range(4):
            part = slice(h * mine, (h + 1) * mine)
            share = prob[step, part].astype(jnp.float32)
            own_share = spread[:, h * 64 : h * 64 + 1]
            weighted = share * grads[part]
            delta = jnp.sum(weighted, axis=1, keepdims=True) + own_share * own_grads[h]
            low.append((weighted - share * delta).astype(jnp.bfloat16))
            own_low.append(own_share * (own_grads[h] - delta))
        low = jnp.concatenate(low, axis=0)
        own_spread = head_lanes(own_low, 256)
        back = heads_out(mm(low, keys[main_rows, cols])) + own_spread * side_key
        query_back[own_rows, cols] = back.astype(jnp.bfloat16) * jnp.bfloat16(0.125)
        key_back[main_rows, cols] = mm_grad(low, heads_in(q_tile)).astype(jnp.bfloat16)
        value_back[main_rows, cols] = mm_grad(prob[step], above).astype(jnp.bfloat16)
        key_back[side_rows, cols] = (own_spread * q_tile.astype(jnp.float32))[local_len:].astype(
            jnp.bfloat16
        )
        value_back[side_rows, cols] = (spread * above_wide)[local_len:].astype(jnp.bfloat16)
        turned_low = skewed(mm(low, turn), local_len).astype(jnp.bfloat16)
        rel_total = heads_out(mm(turned_low, hot))
        near = lax.rem(lax.broadcasted_iota(jnp.int32, rel_total.shape, 1), BUCKETS) == 0
        rel_total = rel_total + jnp.where(near, head_lanes(own_low, 128), 0.0)
        rel_back[own_rows, pl.ds(pl.multiple_of(g * 128, 128), 128)] = rel_total.astype(
            jnp.bfloat16
        )
        return carry

    lax.fori_loop(0, 4 * rows, attend, 0)
    weight_ckey, weight_cvalue = fetch[w_ckey], fetch[w_cvalue]
    weight_query, weight_relative = fetch[w_query], fetch[w_relative]
    weight_key, weight_value = fetch[w_key], fetch[w_value]
    chips = rows * span // (rows * local_len)

    def states_body(cols):
        total = mm_back(ckey_back[...], weight_ckey[cols, :])
        total = total + mm_back(cvalue_back[...], weight_cvalue[cols, :])
        total = total.astype(jnp.bfloat16)
        for r in range(rows):
            for p in range(chips):
                at = r * span + p * local_len
                states_part[p, r, :, cols] = total[at : at + local_len]

    tiles(width, states_body)

    def hidden_body(cols):
        total = mm_back(key_back[...], weight_key[cols, :])
        total = total + mm_back(value_back[...], weight_value[cols, :])
        mains = total[: rows * span].astype(jnp.bfloat16)
        for r in range(rows):
            for p in range(chips):
                at = r * span + p * local_len
                main_part[p, r, :, cols] = mains[at : at + local_len]
        own = residual[:, cols] + mm_back(query_back[...], weight_query[cols, :])
        own = own + mm_back(rel_back[...], weight_relative[cols, :])
        for r in range(rows):
            for j in range(3):
                tile = own[r * mine + j * local_len : r * mine + (j + 1) * local_len]
                if j:
                    at = rows * span + (2 * r + j - 1) * local_len
                    tile = tile + total[at : at + local_len]
                hidden_own[j, r, :, cols] = tile

    tiles(width, hidden_body)


def finish_kernel(count, *refs):
    sums, (hidden_own, main_sum, states_sum) = refs[:count], refs[count : count + 3]
    outs, (hidden_grad, states_grad), sems = (
        refs[count + 3 : 2 * count + 3],
        refs[2 * count + 3 : 2 * count + 5],
        refs[2 * count + 5],
    )
    copies = [
        pltpu.make_async_copy(src, dst, sems.at[i])
        for i, (src, dst) in enumerate(zip(sums + (states_sum,), outs + (states_grad,)))
    ]
    for copy in copies:
        copy.start()
    hidden_grad[0] = hidden_own[0] + main_sum[...]
    hidden_grad[1:] = hidden_own[1:]
    for copy in copies:
        copy.wait()


def finish(sums, hidden_own, main_sum, states_sum):
    shapes = [jax.ShapeDtypeStruct(a.shape, a.dtype) for a in (*sums, hidden_own, states_sum)]
    place = [pl.BlockSpec(memory_space=pl.ANY)]
    vmem = [pl.BlockSpec(memory_space=pltpu.VMEM)]
    count = len(sums)
    return pl.pallas_call(
        lambda *refs: finish_kernel(count, *refs),
        out_shape=shapes,
        in_specs=vmem * (count + 3),
        out_specs=place * count + vmem + place,
        scratch_shapes=[pltpu.SemaphoreType.DMA((count + 1,))],
        compiler_params=pltpu.CompilerParams(vmem_limit_bytes=62 * 2**20),
        name="finish",
    )(*sums, hidden_own, main_sum, states_sum)


def plain_call(kernel, name, ins, spaces, outs, scratch, flops):
    space = {"v": pltpu.VMEM, "s": pltpu.SMEM, "a": pl.ANY}
    out_shape = [jax.ShapeDtypeStruct(shape, kind) for shape, kind in outs]
    moved = sum(a.size * a.dtype.itemsize for a in list(ins) + out_shape)
    return pl.pallas_call(
        kernel,
        out_shape=out_shape,
        in_specs=[pl.BlockSpec(memory_space=space[p]) for p in spaces],
        out_specs=[pl.BlockSpec(memory_space=pltpu.VMEM)] * len(outs),
        scratch_shapes=scratch,
        compiler_params=pltpu.CompilerParams(vmem_limit_bytes=62 * 2**20),
        cost_estimate=pl.CostEstimate(flops=flops, bytes_accessed=moved, transcendentals=0),
        name=name,
    )(*ins)


def copies_of(arrays):
    return [pltpu.VMEM(a.shape, a.dtype) for a in arrays] + [
        pltpu.SemaphoreType.DMA((len(arrays),))
    ]


def local(
    hidden,
    encoder,
    lengths,
    enc_lengths,
    w_query,
    w_key,
    w_value,
    w_attn_out,
    w_relative,
    w_cross_query,
    w_cross_key,
    w_cross_value,
    w_cross_out,
    w_up,
    w_down,
    gain_attn,
    gain_cross,
    gain_ffn,
    cotangent,
):
    ndp, chips = lax.axis_size("dp"), lax.axis_size("seq")
    devices = ndp * chips
    low, wide = jnp.bfloat16, jnp.float32
    _, rows, local_len, width = hidden.shape
    span, tokens = local_len * chips, 3 * rows * local_len
    weights = (
        w_key,
        w_value,
        w_query,
        w_relative,
        w_attn_out,
        w_cross_key,
        w_cross_value,
        w_cross_query,
        w_cross_out,
        w_up,
        w_down,
    )
    gains = jnp.stack([gain_attn, gain_cross, gain_ffn])
    kernels = chips == 4 and w_query.shape[0] % 128 == 0
    if kernels:
        gains = jnp.pad(gains, ((0, 13), (0, 0)))
        *whole, whole_gains, mains, states = gather_weights(
            weights + (gains,), hidden, encoder, ndp
        )
        whole = [w.reshape(-1, w.shape[-1]) for w in whole]
        whole_gains = whole_gains[:, :8]
    else:
        gains = jnp.pad(gains, ((0, 5), (0, 0)))
        whole = [lax.all_gather(w, "dp", axis=0, tiled=True) for w in weights]
        whole_gains = lax.all_gather(gains, "dp", axis=0)
        mains = lax.all_gather(hidden[0], "seq", axis=1)
        states = lax.all_gather(encoder, "seq", axis=1)
    mains, states = mains.reshape(-1, width), states.reshape(-1, width)
    gains = jnp.transpose(whole_gains.astype(wide), (1, 0, 2)).reshape(8, -1)
    (
        full_key,
        full_value,
        full_query,
        full_relative,
        full_attn_out,
        full_ckey,
        full_cvalue,
        full_cquery,
        full_cout,
        full_up,
        full_down,
    ) = whole
    ff = full_up.shape[1]
    every = rows * (span + 2 * local_len)
    fetched = (
        full_key,
        full_value,
        full_query,
        full_relative,
        full_ckey,
        full_cvalue,
        full_attn_out,
        full_cquery,
    )
    (
        hid,
        x_all,
        query,
        keys,
        values,
        prob,
        prob_own,
        context,
        ckeys,
        cvalues,
        normal,
        normal_scale,
        normed_low,
        cquery,
        cprob,
        ccontext,
    ) = plain_call(
        lambda *refs: forward_kernel(rows, local_len, *refs),
        "forward_attention",
        (hidden, mains, states, lengths, enc_lengths, gains) + fetched,
        "vvvssv" + "a" * len(fetched),
        [
            ((tokens, width), low),
            ((every, width), low),
            ((tokens, width), low),
            ((every, width), low),
            ((every, width), low),
            ((4 * rows, 12 * local_len, span), low),
            ((tokens, width), wide),
            ((tokens, width), low),
            ((rows * span, width), low),
            ((rows * span, width), low),
            ((tokens, width), wide),
            ((tokens, 128), wide),
            ((tokens, width), low),
            ((tokens, width), low),
            ((4 * rows, 12 * local_len, span), low),
            ((tokens, width), low),
        ],
        [
            pltpu.VMEM((tokens, full_relative.shape[1]), low),
            pltpu.VMEM((tokens, width), wide),
        ]
        + copies_of(fetched),
        12 * 10**9,
    )
    fetched = (full_cout, full_up, full_down)
    (
        output,
        crossed_low,
        activated,
        last_low,
        up_back,
        cross_grad,
        cross_low,
        ccontext_back,
        gain_middle,
    ) = plain_call(
        lambda *refs: middle_kernel(rows, local_len, *refs),
        "feed_forward",
        (normal, ccontext, gains, cotangent) + fetched,
        "vvvv" + "a" * len(fetched),
        [
            (hidden.shape, low),
            ((tokens, width), low),
            ((tokens, ff), low),
            ((tokens, width), low),
            ((tokens, ff), low),
            ((tokens, width), wide),
            ((tokens, width), low),
            ((tokens, width), low),
            ((3, 8, width), wide),
        ],
        [
            pltpu.VMEM((tokens, width), wide),
            pltpu.VMEM((tokens, 128), wide),
            pltpu.VMEM((tokens, ff), low),
            pltpu.VMEM((tokens, width), wide),
        ]
        + copies_of(fetched),
        14 * 10**9,
    )
    fetched = (
        full_cquery,
        full_attn_out,
        full_ckey,
        full_cvalue,
        full_query,
        full_relative,
        full_key,
        full_value,
    )
    (
        cquery_back,
        ckey_back,
        cvalue_back,
        attn_low,
        query_back,
        key_back,
        value_back,
        rel_back,
        hidden_own,
        main_part,
        states_part,
        gain_back,
    ) = plain_call(
        lambda *refs: backward_kernel(rows, local_len, *refs),
        "backward_attention",
        (
            ccontext_back,
            cross_grad,
            cquery,
            ckeys,
            cvalues,
            cprob,
            normal,
            normal_scale,
            gains,
            query,
            keys,
            values,
            prob,
            prob_own,
        )
        + fetched,
        "v" * 14 + "a" * len(fetched),
        [
            ((tokens, width), low),
            ((rows * span, width), low),
            ((rows * span, width), low),
            ((tokens, width), low),
            ((tokens, width), low),
            ((every, width), low),
            ((every, width), low),
            ((tokens, full_relative.shape[1]), low),
            (hidden.shape, wide),
            ((chips, rows, local_len, width), low),
            ((chips, rows, local_len, width), low),
            ((3, 8, width), wide),
        ],
        [pltpu.VMEM((tokens, width), wide), pltpu.VMEM((tokens, width), low)] + copies_of(fetched),
        14 * 10**9,
    )
    xs = [activated, crossed_low, ccontext, normed_low, context, hid, x_all, states]
    gs = [
        last_low,
        up_back,
        cross_low,
        cquery_back,
        attn_low,
        query_back,
        rel_back,
        key_back,
        value_back,
        ckey_back,
        cvalue_back,
    ]
    pairs = [(0, 0), (1, 1), (2, 2), (3, 3), (4, 4), (5, 5), (5, 6), (6, 7), (6, 8), (7, 9), (7, 10)]
    gain_parts = jnp.sum(gain_middle + gain_back, axis=1)
    if kernels:
        gain_parts = jnp.transpose(gain_parts.reshape(3, devices, -1), (1, 0, 2))
        gain_parts = jnp.pad(gain_parts, ((0, 0), (0, 5), (0, 128 - gain_parts.shape[2])))
        gain_parts = gain_parts.reshape(2, 2, ndp // 2, 2, 8, 128)
        shares = (main_part, states_part)
        shares = [a.reshape((2, 2) + a.shape[1:]) for a in shares]
        *sums, gain_sums, main_sum, states_sum = reduce_grads(
            xs, gs, pairs, gain_parts, shares, ndp // 2
        )
        gain_sums = gain_sums[:3, : width // devices]
        *sums, hidden_grad, states_sum = finish(sums, hidden_own, main_sum, states_sum)
    else:
        sums = [
            lax.psum_scatter(
                weight_grad(xs[i], gs[j]), ("seq", "dp"), scatter_dimension=0, tiled=True
            )
            for i, j in pairs
        ]
        gain_sums = lax.psum_scatter(gain_parts, ("seq", "dp"), scatter_dimension=1, tiled=True)
        main_sum, states_sum = (
            lax.psum_scatter(part, "seq", scatter_dimension=0).astype(wide)
            for part in (main_part, states_part)
        )
        hidden_grad = hidden_own.at[0].add(main_sum)
    gainattn_sum, gaincross_sum, gainffn_sum = gain_sums
    (
        down_sum,
        up_sum,
        cout_sum,
        cquery_sum,
        outproj_sum,
        query_sum,
        relative_sum,
        keyw_sum,
        valuew_sum,
        ckey_sum,
        cvalue_sum,
    ) = sums
    return (
        output,
        hidden_grad,
        states_sum,
        query_sum,
        keyw_sum,
        valuew_sum,
        outproj_sum,
        relative_sum,
        cquery_sum,
        ckey_sum,
        cvalue_sum,
        cout_sum,
        up_sum,
        down_sum,
        gainattn_sum,
        gaincross_sum,
        gainffn_sum,
    )


def solution(mesh):
    in_specs = (
        P(None, "dp", "seq", None),
        P("dp", "seq", None),
        P("dp"),
        P("dp"),
        P("dp", None),
        P("dp", None),
        P("dp", None),
        P("dp", None),
        P("dp", None),
        P("dp", None),
        P("dp", None),
        P("dp", None),
        P("dp", None),
        P("dp", None),
        P("dp", None),
        P("dp"),
        P("dp"),
        P("dp"),
        P(None, "dp", "seq", None),
    )
    out_specs = (
        P(None, "dp", "seq", None),
        P(None, "dp", "seq", None),
        P("dp", "seq", None),
        P(("seq", "dp"), None),
        P(("seq", "dp"), None),
        P(("seq", "dp"), None),
        P(("seq", "dp"), None),
        P(("seq", "dp"), None),
        P(("seq", "dp"), None),
        P(("seq", "dp"), None),
        P(("seq", "dp"), None),
        P(("seq", "dp"), None),
        P(("seq", "dp"), None),
        P(("seq", "dp"), None),
        P(("seq", "dp")),
        P(("seq", "dp")),
        P(("seq", "dp")),
    )
    return jax.shard_map(local, mesh=mesh, in_specs=in_specs, out_specs=out_specs, check_vma=False)
```

```python
import functools
import math

import jax
import jax.numpy as jnp
from jax import lax
from jax.experimental import pallas as pl
from jax.experimental.pallas import tpu as pltpu
from jax.sharding import PartitionSpec as P

MESH = pl.DeviceIdType.MESH

HEADS = 16
HEAD_DIM = 64
BUCKETS = 32


eps_norm = 1e-05
bucket_edges = [step_index for step_index in range(1, 16)] + [
    int(math.ceil(16 * 8 ** ((step_index - 16) / 16))) for step_index in range(16, 32)
]


def flatten_rows(array):
    return array.reshape(-1, array.shape[-1])


def weight_grad(array, grad_rows):
    return jnp.einsum(
        "nd,ne->de",
        flatten_rows(array),
        flatten_rows(grad_rows),
        preferred_element_type=jnp.float32,
    )


def remote(src, dst, send, recv, to):
    return pltpu.make_async_remote_copy(
        src_ref=src, dst_ref=dst, send_sem=send, recv_sem=recv, device_id=to, device_id_type=MESH
    )


def place():
    s = lax.axis_index("seq")
    d = lax.axis_index("dp")
    z, c = d // 2, lax.rem(d, 2)
    sx = s + 1 - 2 * lax.rem(s, 2)
    sy = lax.rem(s + 2, 4)
    return s, z, c, sx, sy


def greet(nz):
    s, z, c, sx, sy = place()
    barrier = pltpu.get_barrier_semaphore()
    dests = [(s, 2 * z + 1 - c), (sx, 2 * z + c), (sy, 2 * z + c)]
    for dz in range(1, nz):
        dests.append((s, 2 * lax.rem(z + dz, nz) + c))
    for dest in dests:
        pl.semaphore_signal(barrier, inc=1, device_id=dest, device_id_type=MESH)
    pl.semaphore_wait(barrier, len(dests))


RING = 8


def reduce_grads_kernel(plan, nz, n_x, n_g, n_out, *refs):
    at = 0
    xs, at = refs[at : at + n_x], at + n_x
    gs, at = refs[at : at + n_g], at + n_g
    gain_part, at = refs[at], at + 1
    shares, at = refs[at : at + 2], at + 2
    outs, at = refs[at : at + n_out], at + n_out
    gain_out, at = refs[at], at + 1
    share_outs, at = refs[at : at + 2], at + 2
    kinds = []
    for _ in range(3):
        kinds.append(refs[at : at + 5])
        at += 5
    share1, share2, send, recv, credit = refs[at:]
    s, z, c, sx, sy = place()
    own = 2 * z + c
    x, y = lax.rem(s, 2), s // 2
    core = (s, 2 * z + 1 - c)
    beside_x, beside_y = (sx, own), (sy, own)
    greet(nz)
    count = len(plan)

    def buffers(k):
        kind, slot = plan[k][0], plan[k][1]
        if kind == 3:
            return None, shares[slot // 2].at[:, :, slot % 2], share1.at[slot], share2.at[slot], None
        part, held0, held1, held2, held3 = kinds[kind]
        if kind == 2:
            return gain_part, held0.at[slot], held1.at[slot], held2.at[slot], held3.at[slot]
        return (part.at[slot % 2], held0.at[slot % RING], held1.at[slot], held2.at[slot], held3.at[slot])

    def core_copy(k):
        part, held0 = buffers(k)[:2]
        return remote(part.at[:, :, :, 1 - c], held0, send.at[k, 0], recv.at[k, 0], core)

    def first_copy(k):
        _, held0, held1 = buffers(k)[:3]
        if k % 2 == 0:
            return remote(held0.at[:, 1 - x], held1, send.at[k, 1], recv.at[k, 1], beside_x)
        return remote(held0.at[1 - y], held1, send.at[k, 1], recv.at[k, 1], beside_y)

    def second_copy(k):
        held1, held2 = buffers(k)[2:4]
        if k % 2 == 0:
            return remote(held1.at[1 - y], held2, send.at[k, 2], recv.at[k, 2], beside_y)
        return remote(held1.at[1 - x], held2, send.at[k, 2], recv.at[k, 2], beside_x)

    def z_copy(k, dz):
        held2, held3 = buffers(k)[3:5]
        zt = lax.rem(z + dz, nz)
        return remote(
            held2.at[zt], held3.at[dz - 1], send.at[k, 2 + dz], recv.at[k, 2 + dz], (s, 2 * zt + c)
        )

    def added(held, mine):
        held[...] = (held[...].astype(jnp.float32) + mine.astype(jnp.float32)).astype(held.dtype)

    def make(k):
        kind, slot, xi, gi, _, col, wide = plan[k]
        if kind == 3:
            return
        if kind < 2:
            part = buffers(k)[0]
            left, right = xs[xi], gs[gi]
            block = part.shape[4]
            if slot >= 2:
                core_copy(before[k]).wait_send()
            group = 256 // block
            for i in range(left.shape[1] // 256):
                product = lax.dot_general(
                    left[:, i * 256 : (i + 1) * 256],
                    right[:, col : col + wide],
                    (((0,), (0,)), ((), ())),
                    preferred_element_type=jnp.float32,
                )
                index = i * group
                i_s, rest = divmod(index, 2 * nz)
                zs = rest // 2
                part[i_s // 2, i_s % 2, zs : zs + group // 2] = product.reshape(group // 2, 2, block, wide).astype(
                    part.dtype
                )
        if kind < 2 and slot >= RING:
            pl.semaphore_wait(credit.at[kind], 1)
        core_copy(k).start()

    def after_core(k):
        part, held0 = buffers(k)[:2]
        if plan[k][0] == 3:
            first_copy(k).start()
            return
        core_copy(k).wait_recv()
        added(held0, part[:, :, :, c])
        first_copy(k).start()

    def after_first(k):
        _, held0, held1 = buffers(k)[:3]
        first_copy(k).wait_recv()
        added(held1, held0[:, x] if k % 2 == 0 else held0[y])
        second_copy(k).start()
        kind, slot = plan[k][:2]
        first_copy(k).wait_send()
        if kind < 2 and slot + RING < sum(p[0] == kind for p in plan):
            pl.semaphore_signal(credit.at[kind], inc=1, device_id=core, device_id_type=MESH)

    def after_second(k):
        held1, held2 = buffers(k)[2:4]
        second_copy(k).wait_recv()
        if plan[k][0] == 3:
            mine = (held1[y] if k % 2 == 0 else held1[x]).astype(jnp.float32)
            slot = plan[k][1]
            share_outs[slot // 2][slot % 2] = held2[...].astype(jnp.float32) + mine
            return
        added(held2, held1[y] if k % 2 == 0 else held1[x])
        for dz in range(1, nz):
            z_copy(k, dz).start()

    def finish(k):
        if plan[k][0] == 3:
            return
        held2, held3 = buffers(k)[3:5]
        total = held2[z].astype(jnp.float32)
        for dz in range(1, nz):
            z_copy(k, dz).wait_recv()
            total = total + held3[dz - 1].astype(jnp.float32)
        kind, _, _, _, oi, col, wide = plan[k]
        if kind == 2:
            gain_out[...] = total
        else:
            outs[oi][:, col : col + wide] = total

    before = {}
    recent = {}
    for k in range(count):
        kind, slot = plan[k][0], plan[k][1]
        before[k] = recent.get((kind, slot - 2))
        recent[(kind, slot)] = k
    followed = set(v for v in before.values() if v is not None)

    for t in range(count + 7):
        if t >= 7:
            finish(t - 7)
        if 5 <= t < count + 5:
            after_second(t - 5)
        if 3 <= t < count + 3:
            after_first(t - 3)
        if t < count:
            make(t)
        if 1 <= t < count + 1:
            after_core(t - 1)
    for k in range(count):
        if k not in followed and plan[k][0] < 3:
            core_copy(k).wait_send()
        second_copy(k).wait_send()
        for dz in range(1, nz if plan[k][0] < 3 else 1):
            z_copy(k, dz).wait_send()


def reduce_grads(xs, gs, pairs, gain_part, shares, nz):
    plan, slots = [(3, i, 0, 0, 0, 0, 0) for i in range(4)], [0, 0, 0]
    blocks, columns = [], []
    ndev = 8 * nz
    for oi, (xi, gi) in enumerate(pairs):
        rows, wide = xs[xi].shape[1], gs[gi].shape[1]
        columns.append((rows // ndev, wide))
        kind = 0 if rows // ndev <= 32 else 1
        step = (512, 256)[kind]
        for col in range(0, wide, step):
            plan.append((kind, slots[kind], xi, gi, oi, col, step))
            slots[kind] += 1
    plan.append((2, 0, 0, 0, 0, 0, 128))
    rb = min(rows for rows, _ in columns)
    shapes = [((rb, 512), jnp.bfloat16, slots[0]), ((max(rows for rows, _ in columns), 256), jnp.bfloat16, slots[1])]
    scratch = []
    for (tail, kind_type, n) in shapes + [((8, 128), jnp.float32, 1)]:
        scratch.append(
            pltpu.VMEM((2, 2, 2, nz, 2) + tail if kind_type == jnp.bfloat16 else (8, 128), kind_type)
        )
        scratch.append(pltpu.VMEM((min(n, RING), 2, 2, nz) + tail, kind_type))
        scratch.append(pltpu.VMEM((n, 2, nz) + tail, kind_type))
        scratch.append(pltpu.VMEM((n, nz) + tail, kind_type))
        scratch.append(pltpu.VMEM((n, nz - 1) + tail, kind_type))
    n = len(plan)
    vmem = pl.BlockSpec(memory_space=pltpu.VMEM)
    outs = [jax.ShapeDtypeStruct(shape, jnp.float32) for shape in columns]
    outs.append(jax.ShapeDtypeStruct((8, 128), jnp.float32))
    share = shares[0].shape[3:]
    outs += [jax.ShapeDtypeStruct(a.shape[2:], jnp.float32) for a in shares]
    return pl.pallas_call(
        lambda *refs: reduce_grads_kernel(plan, nz, len(xs), len(gs), len(columns), *refs),
        out_shape=outs,
        in_specs=[vmem] * (len(xs) + len(gs) + 3),
        out_specs=[vmem] * len(outs),
        scratch_shapes=scratch
        + [pltpu.VMEM((4, 2) + share, jnp.bfloat16), pltpu.VMEM((4,) + share, jnp.bfloat16)]
        + [pltpu.SemaphoreType.DMA((n, 2 + nz)), pltpu.SemaphoreType.DMA((n, 2 + nz))]
        + [pltpu.SemaphoreType.REGULAR((2,))],
        compiler_params=pltpu.CompilerParams(
            collective_id=1, has_side_effects=True, vmem_limit_bytes=62 * 2**20
        ),
        name="reduce_grads",
    )(*xs, *gs, gain_part, *shares)

NEG = -1000000000.0


def mm(left, right):
    return jnp.dot(left, right, preferred_element_type=jnp.float32)


def mm_back(left, right):
    return lax.dot_general(
        left, right, (((1,), (1,)), ((), ())), preferred_element_type=jnp.float32
    )


def mm_grad(left, right):
    return lax.dot_general(
        left, right, (((0,), (0,)), ((), ())), preferred_element_type=jnp.float32
    )


def tiles(width, body):
    def step(i, carry):
        body(pl.ds(pl.multiple_of(i * 256, 256), 256))
        return carry

    lax.fori_loop(0, width // 256, step, 0)


def row_tiles(rows, body, step_rows=64):
    def step(i, carry):
        body(pl.ds(pl.multiple_of(i * step_rows, step_rows), step_rows))
        return carry

    lax.fori_loop(0, rows // step_rows, step, 0)


def heads_in(tile):
    lane = lax.broadcasted_iota(jnp.int32, tile.shape, 1) // (tile.shape[1] // 4)
    return jnp.concatenate(
        [jnp.where(lane == h, tile, jnp.zeros_like(tile)) for h in range(4)], axis=0
    )


def heads_out(stacked):
    n, wide = stacked.shape[0] // 4, stacked.shape[1]
    lane = lax.broadcasted_iota(jnp.int32, (n, wide), 1) // (wide // 4)
    result = stacked[3 * n :]
    for h in (2, 1, 0):
        result = jnp.where(lane == h, stacked[h * n : (h + 1) * n], result)
    return result


def head_lanes(columns, wide):
    n = columns[0].shape[0]
    lane = lax.broadcasted_iota(jnp.int32, (n, wide), 1) // (wide // 4)
    result = jnp.broadcast_to(columns[3], (n, wide))
    for h in (2, 1, 0):
        result = jnp.where(lane == h, jnp.broadcast_to(columns[h], (n, wide)), result)
    return result


def head_sums(product):
    n, wide = product.shape
    lane = lax.broadcasted_iota(jnp.int32, (n, wide), 1) // (wide // 4)
    return [
        jnp.sum(jnp.where(lane == h, product, 0.0), axis=1, keepdims=True) for h in range(4)
    ]


def bucket_of(distance):
    total = jnp.zeros_like(distance)
    for edge in bucket_edges:
        total = total + (distance >= edge).astype(jnp.int32)
    return total


def hot_forward(start, span):
    lag = lax.broadcasted_iota(jnp.int32, (128, span), 1)
    row = lax.rem(lax.broadcasted_iota(jnp.int32, (128, span), 0), BUCKETS)
    distance = lax.rem(start - lag + span, span)
    return jnp.where(bucket_of(distance) == row, 1.0, 0.0).astype(jnp.bfloat16)


def hot_backward(start, span):
    lag = lax.broadcasted_iota(jnp.int32, (span, 128), 0)
    column = lax.rem(lax.broadcasted_iota(jnp.int32, (span, 128), 1), BUCKETS)
    distance = lax.rem(start + lag + 1, span)
    return jnp.where(bucket_of(distance) == column, 1.0, 0.0).astype(jnp.bfloat16)


def skewed(array, block):
    return jnp.concatenate(
        [
            pltpu.roll(array[i : i + block], 0, 1, stride=1, stride_axis=0)
            for i in range(0, array.shape[0], block)
        ],
        axis=0,
    )


def norm_rows(values):
    centred = values - jnp.mean(values, axis=1, keepdims=True)
    scale = lax.rsqrt(jnp.mean(centred * centred, axis=1, keepdims=True) + eps_norm)
    return centred * scale, scale


def norm_back(grad, normal, scale, gain):
    grad = grad * gain
    return scale * (
        grad
        - jnp.mean(grad, axis=1, keepdims=True)
        - normal * jnp.mean(grad * normal, axis=1, keepdims=True)
    )


def add_rows(total_ref, index, product):
    total_ref[index] += jnp.sum(product.reshape(-1, 8, product.shape[1]), axis=0)


class Fetch:
    def __init__(self, sources, targets, sems):
        self.copies = [
            pltpu.make_async_copy(src, dst, sems.at[i])
            for i, (src, dst) in enumerate(zip(sources, targets))
        ]
        self.targets = targets
        self.waited = set()
        for copy in self.copies:
            copy.start()

    def __getitem__(self, i):
        if i not in self.waited:
            self.waited.add(i)
            self.copies[i].wait()
        return self.targets[i]


def attend_step(
    r, g, step, start, mine, span, local_len, rows, lengths, query, rel, keys, values, prob, prob_own, context, hot
):
    cols = pl.ds(pl.multiple_of(g * 256, 256), 256)
    own_rows = pl.ds(pl.multiple_of(r * mine, local_len), mine)
    main_rows = pl.ds(pl.multiple_of(r * span, span), span)
    side_rows = pl.ds(pl.multiple_of(rows * span + r * 2 * local_len, local_len), 2 * local_len)
    q_tile = query[own_rows, cols]
    rel_tile = rel[own_rows, pl.ds(pl.multiple_of(g * 128, 128), 128)]
    side_key = keys[side_rows, cols].astype(jnp.float32)
    side_value = values[side_rows, cols].astype(jnp.float32)
    zero = jnp.zeros((local_len, 256), jnp.float32)
    scores = mm_back(heads_in(q_tile), keys[main_rows, cols])
    bias = skewed(mm(heads_in(rel_tile), hot), local_len)
    products = q_tile.astype(jnp.float32) * jnp.concatenate([zero, side_key], axis=0)
    own_dot = head_sums(products)
    rel_lane = lax.broadcasted_iota(jnp.int32, (mine, 128), 1)
    rel_wide = rel_tile.astype(jnp.float32)
    row = lax.broadcasted_iota(jnp.int32, (mine, span), 0)
    at = lax.broadcasted_iota(jnp.int32, (mine, span), 1)
    ahead = start + lax.rem(row, local_len) + jnp.where(row < local_len, 1, 0)
    kept = (at < ahead) & (at < lengths[r])
    first = lax.broadcasted_iota(jnp.int32, (mine, 1), 0) < local_len
    low, owns = [], []
    for h in range(4):
        part = slice(h * mine, (h + 1) * mine)
        score = jnp.where(kept, scores[part] + bias[part], NEG)
        near = jnp.sum(jnp.where(rel_lane == h * BUCKETS, rel_wide, 0.0), axis=1, keepdims=True)
        own = jnp.where(first, NEG, own_dot[h] + near)
        peak = jnp.maximum(jnp.max(score, axis=1, keepdims=True), own)
        power = jnp.exp(score - peak)
        own_power = jnp.exp(own - peak)
        share = 1.0 / (jnp.sum(power, axis=1, keepdims=True) + own_power)
        low.append((power * share).astype(jnp.bfloat16))
        owns.append(own_power * share)
    low = jnp.concatenate(low, axis=0)
    prob[step] = low
    spread = head_lanes(owns, 256)
    prob_own[own_rows, cols] = spread.astype(prob_own.dtype)
    total = heads_out(mm(low, values[main_rows, cols]))
    total = total + spread * jnp.concatenate([zero, side_value], axis=0)
    context[own_rows, cols] = total.astype(context.dtype)


def cross_step(
    r, g, step, mine, span, local_len, enc_lengths, cquery, ckeys, cvalues, cprob, ccontext
):
    cols = pl.ds(pl.multiple_of(g * 256, 256), 256)
    own_rows = pl.ds(pl.multiple_of(r * mine, local_len), mine)
    main_rows = pl.ds(pl.multiple_of(r * span, span), span)
    scores = mm_back(heads_in(cquery[own_rows, cols]), ckeys[main_rows, cols])
    at = lax.broadcasted_iota(jnp.int32, (mine, span), 1)
    kept = at < enc_lengths[r]
    low = []
    for h in range(4):
        score = jnp.where(kept, scores[h * mine : (h + 1) * mine], NEG)
        power = jnp.exp(score - jnp.max(score, axis=1, keepdims=True))
        share = 1.0 / jnp.sum(power, axis=1, keepdims=True)
        low.append((power * share).astype(jnp.bfloat16))
    low = jnp.concatenate(low, axis=0)
    cprob[step] = low
    ccontext[own_rows, cols] = heads_out(mm(low, cvalues[main_rows, cols])).astype(
        ccontext.dtype
    )


def forward_kernel(rows, local_len, *refs):
    (
        hidden,
        mains,
        states,
        lengths,
        enc_lengths,
        gains,
        *weights,
    ) = refs[:14]
    (hid, x_all, query, keys, values, prob, prob_own, context, ckeys, cvalues) = refs[14:24]
    (normal, normal_scale, normed_low, cquery, cprob, ccontext) = refs[24:30]
    rel, residual = refs[30:32]
    fetch = Fetch(weights, refs[32:40], refs[40])
    w_key, w_value, w_query, w_relative, w_ckey, w_cvalue, w_out, w_cquery = range(8)
    width = hid.shape[1]
    mine = 3 * local_len
    span = mains.shape[0] // rows
    start = lax.axis_index("seq") * local_len
    x_all[: rows * span] = mains[...]
    for r in range(rows):
        for j in range(3):
            tile = hidden[j, r]
            hid[r * mine + j * local_len : r * mine + (j + 1) * local_len] = tile
            if j:
                at = rows * span + (2 * r + j - 1) * local_len
                x_all[at : at + local_len] = tile

    def project(left, w, target, scale=None):
        weight = fetch[w]

        def body(cols):
            product = mm(left[...], weight[:, cols])
            if scale is not None:
                product = product * scale
            target[:, cols] = product.astype(target.dtype)

        tiles(target.shape[1], body)

    project(x_all, w_key, keys)
    project(x_all, w_value, values)
    project(hid, w_query, query, 0.125)
    project(hid, w_relative, rel)
    hot = hot_forward(start, span)

    def attend(step, carry):
        attend_step(
            step // 4, lax.rem(step, 4), step, start, mine, span, local_len, rows, lengths,
            query, rel, keys, values, prob, prob_own, context, hot,
        )
        return carry

    lax.fori_loop(0, 4 * rows, attend, 0)
    project(states, w_ckey, ckeys)
    project(states, w_cvalue, cvalues)
    weight_out = fetch[w_out]

    def out_body(cols):
        residual[:, cols] = hid[:, cols].astype(jnp.float32) + mm(context[...], weight_out[:, cols])

    tiles(width, out_body)

    def norm_body(part):
        normal[part], scale = norm_rows(residual[part])
        normal_scale[part] = jnp.broadcast_to(scale, (scale.shape[0], 128))
        normed_low[part] = (normal[part] * gains[0:1]).astype(jnp.bfloat16)

    row_tiles(hid.shape[0], norm_body)
    project(normed_low, w_cquery, cquery, 0.125)

    def cross(step, carry):
        cross_step(
            step // 4, lax.rem(step, 4), step, mine, span, local_len, enc_lengths,
            cquery, ckeys, cvalues, cprob, ccontext,
        )
        return carry

    lax.fori_loop(0, 4 * rows, cross, 0)


def middle_kernel(
    rows,
    local_len,
    normal,
    ccontext,
    gains,
    cotangent,
    any_cout,
    any_up,
    any_down,
    output,
    crossed_low,
    activated,
    last_low,
    up_back,
    cross_grad,
    cross_low,
    ccontext_back,
    gain_total,
    normal2,
    scale2,
    slope,
    residual,
    v_cout,
    v_up,
    v_down,
    sems,
):
    fetch = Fetch((any_cout, any_up, any_down), (v_cout, v_up, v_down), sems)
    tokens, width = normal.shape
    mine = 3 * local_len
    gain_total[...] = jnp.zeros_like(gain_total)
    weight_cout = fetch[0]

    def cross_body(cols):
        residual[:, cols] = normal[:, cols] * gains[0:1, cols] + mm(
            ccontext[...], weight_cout[:, cols]
        )

    tiles(width, cross_body)

    def norm_body(part):
        normal2[part], scale = norm_rows(residual[part])
        scale2[part] = jnp.broadcast_to(scale, (scale.shape[0], 128))
        crossed_low[part] = (normal2[part] * gains[1:2]).astype(jnp.bfloat16)

    row_tiles(tokens, norm_body)
    weight_up = fetch[1]

    def up_body(cols):
        value = mm(crossed_low[...], weight_up[:, cols])
        below = 0.5 + 0.5 * lax.erf(value * (0.5**0.5))
        activated[:, cols] = (value * below).astype(jnp.bfloat16)
        density = jnp.exp(-0.5 * value * value) * (1.0 / math.sqrt(2.0 * math.pi))
        slope[:, cols] = (below + value * density).astype(jnp.bfloat16)

    tiles(activated.shape[1], up_body)
    weight_down = fetch[2]

    def down_body(cols):
        residual[:, cols] = normal2[:, cols] * gains[1:2, cols] + mm(
            activated[...], weight_down[:, cols]
        )

    tiles(width, down_body)
    for r in range(rows):
        for j in range(3):
            at = r * mine + j * local_len
            part = slice(at, at + local_len)
            normal3, scale = norm_rows(residual[part])
            output[j, r] = (normal3 * gains[2:3]).astype(output.dtype)
            above = cotangent[j, r].astype(jnp.float32)
            add_rows(gain_total, 2, above * normal3)
            grad = norm_back(above, normal3, scale, gains[2:3])
            residual[part] = grad
            last_low[part] = grad.astype(jnp.bfloat16)

    def down_back(cols):
        product = mm_back(last_low[...], weight_down[cols, :])
        up_back[:, cols] = (product * slope[:, cols].astype(jnp.float32)).astype(jnp.bfloat16)

    tiles(activated.shape[1], down_back)

    def up_back_body(cols):
        residual[:, cols] = residual[:, cols] + mm_back(up_back[...], weight_up[cols, :])

    tiles(width, up_back_body)

    def cross_norm_back(part):
        above = residual[part]
        add_rows(gain_total, 1, above * normal2[part])
        grad = norm_back(above, normal2[part], scale2[part][:, 0:1], gains[1:2])
        cross_grad[part] = grad
        cross_low[part] = grad.astype(jnp.bfloat16)

    row_tiles(tokens, cross_norm_back)

    def cout_back(cols):
        ccontext_back[:, cols] = mm_back(cross_low[...], weight_cout[cols, :]).astype(jnp.bfloat16)

    tiles(width, cout_back)


def backward_kernel(rows, local_len, *refs):
    (
        ccontext_back,
        cross_grad,
        cquery,
        ckeys,
        cvalues,
        cprob,
        normal,
        normal_scale,
        gains,
        query,
        keys,
        values,
        prob,
        prob_own,
        *weights,
    ) = refs[:22]
    (cquery_back, ckey_back, cvalue_back, attn_low, query_back, key_back) = refs[22:28]
    (value_back, rel_back, hidden_own, main_part, states_part, gain_total) = refs[28:34]
    residual, context_back = refs[34:36]
    fetch = Fetch(weights, refs[36:44], refs[44])
    w_cquery, w_out, w_ckey, w_cvalue, w_query, w_relative, w_key, w_value = range(8)
    tokens, width = query.shape
    mine = 3 * local_len
    span = ckeys.shape[0] // rows
    start = lax.axis_index("seq") * local_len
    gain_total[...] = jnp.zeros_like(gain_total)

    def cross(step, carry):
        r, g = step // 4, lax.rem(step, 4)
        cols = pl.ds(pl.multiple_of(g * 256, 256), 256)
        own_rows = pl.ds(pl.multiple_of(r * mine, local_len), mine)
        main_rows = pl.ds(pl.multiple_of(r * span, span), span)
        above = heads_in(ccontext_back[own_rows, cols])
        grads = mm_back(above, cvalues[main_rows, cols])
        low = []
        for h in range(4):
            part = slice(h * mine, (h + 1) * mine)
            share = cprob[step, part].astype(jnp.float32)
            weighted = share * grads[part]
            low.append(
                (weighted - share * jnp.sum(weighted, axis=1, keepdims=True)).astype(jnp.bfloat16)
            )
        low = jnp.concatenate(low, axis=0)
        back = heads_out(mm(low, ckeys[main_rows, cols])).astype(jnp.bfloat16)
        cquery_back[own_rows, cols] = back * jnp.bfloat16(0.125)
        ckey_back[main_rows, cols] = mm_grad(low, heads_in(cquery[own_rows, cols])).astype(
            jnp.bfloat16
        )
        cvalue_back[main_rows, cols] = mm_grad(cprob[step], above).astype(jnp.bfloat16)
        return carry

    lax.fori_loop(0, 4 * rows, cross, 0)
    weight_cquery = fetch[w_cquery]

    def cquery_body(cols):
        residual[:, cols] = cross_grad[:, cols] + mm_back(cquery_back[...], weight_cquery[cols, :])

    tiles(width, cquery_body)

    def attn_norm_back(part):
        above = residual[part]
        add_rows(gain_total, 0, above * normal[part])
        grad = norm_back(above, normal[part], normal_scale[part][:, 0:1], gains[0:1])
        residual[part] = grad
        attn_low[part] = grad.astype(jnp.bfloat16)

    row_tiles(tokens, attn_norm_back)
    weight_out = fetch[w_out]

    def out_back(cols):
        context_back[:, cols] = mm_back(attn_low[...], weight_out[cols, :]).astype(jnp.bfloat16)

    tiles(width, out_back)
    hot = hot_backward(start, span)
    turn = jnp.where(
        lax.broadcasted_iota(jnp.int32, (span, span), 0)
        + lax.broadcasted_iota(jnp.int32, (span, span), 1)
        == span - 1,
        1.0,
        0.0,
    ).astype(jnp.bfloat16)

    def attend(step, carry):
        r, g = step // 4, lax.rem(step, 4)
        cols = pl.ds(pl.multiple_of(g * 256, 256), 256)
        own_rows = pl.ds(pl.multiple_of(r * mine, local_len), mine)
        main_rows = pl.ds(pl.multiple_of(r * span, span), span)
        side_rows = pl.ds(pl.multiple_of(rows * span + r * 2 * local_len, local_len), 2 * local_len)
        above_tile = context_back[own_rows, cols]
        above = heads_in(above_tile)
        above_wide = above_tile.astype(jnp.float32)
        q_tile = query[own_rows, cols]
        zero = jnp.zeros((local_len, 256), jnp.float32)
        side_key = jnp.concatenate([zero, keys[side_rows, cols].astype(jnp.float32)], axis=0)
        side_value = jnp.concatenate([zero, values[side_rows, cols].astype(jnp.float32)], axis=0)
        spread = prob_own[own_rows, cols].astype(jnp.float32)
        grads = mm_back(above, values[main_rows, cols])
        own_grads = head_sums(above_wide * side_value)
        low, own_low = [], []
        for h in range(4):
            part = slice(h * mine, (h + 1) * mine)
            share = prob[step, part].astype(jnp.float32)
            own_share = spread[:, h * 64 : h * 64 + 1]
            weighted = share * grads[part]
            delta = jnp.sum(weighted, axis=1, keepdims=True) + own_share * own_grads[h]
            low.append((weighted - share * delta).astype(jnp.bfloat16))
            own_low.append(own_share * (own_grads[h] - delta))
        low = jnp.concatenate(low, axis=0)
        own_spread = head_lanes(own_low, 256)
        back = heads_out(mm(low, keys[main_rows, cols])) + own_spread * side_key
        query_back[own_rows, cols] = back.astype(jnp.bfloat16) * jnp.bfloat16(0.125)
        key_back[main_rows, cols] = mm_grad(low, heads_in(q_tile)).astype(jnp.bfloat16)
        value_back[main_rows, cols] = mm_grad(prob[step], above).astype(jnp.bfloat16)
        key_back[side_rows, cols] = (own_spread * q_tile.astype(jnp.float32))[local_len:].astype(
            jnp.bfloat16
        )
        value_back[side_rows, cols] = (spread * above_wide)[local_len:].astype(jnp.bfloat16)
        turned_low = skewed(mm(low, turn), local_len).astype(jnp.bfloat16)
        rel_total = heads_out(mm(turned_low, hot))
        near = lax.rem(lax.broadcasted_iota(jnp.int32, rel_total.shape, 1), BUCKETS) == 0
        rel_total = rel_total + jnp.where(near, head_lanes(own_low, 128), 0.0)
        rel_back[own_rows, pl.ds(pl.multiple_of(g * 128, 128), 128)] = rel_total.astype(
            jnp.bfloat16
        )
        return carry

    lax.fori_loop(0, 4 * rows, attend, 0)
    weight_ckey, weight_cvalue = fetch[w_ckey], fetch[w_cvalue]
    weight_query, weight_relative = fetch[w_query], fetch[w_relative]
    weight_key, weight_value = fetch[w_key], fetch[w_value]
    chips = rows * span // (rows * local_len)

    def states_body(cols):
        total = mm_back(ckey_back[...], weight_ckey[cols, :])
        total = total + mm_back(cvalue_back[...], weight_cvalue[cols, :])
        total = total.astype(jnp.bfloat16)
        for r in range(rows):
            for p in range(chips):
                at = r * span + p * local_len
                states_part[p, r, :, cols] = total[at : at + local_len]

    tiles(width, states_body)

    def hidden_body(cols):
        total = mm_back(key_back[...], weight_key[cols, :])
        total = total + mm_back(value_back[...], weight_value[cols, :])
        mains = total[: rows * span].astype(jnp.bfloat16)
        for r in range(rows):
            for p in range(chips):
                at = r * span + p * local_len
                main_part[p, r, :, cols] = mains[at : at + local_len]
        own = residual[:, cols] + mm_back(query_back[...], weight_query[cols, :])
        own = own + mm_back(rel_back[...], weight_relative[cols, :])
        for r in range(rows):
            for j in range(3):
                tile = own[r * mine + j * local_len : r * mine + (j + 1) * local_len]
                if j:
                    at = rows * span + (2 * r + j - 1) * local_len
                    tile = tile + total[at : at + local_len]
                hidden_own[j, r, :, cols] = tile

    tiles(width, hidden_body)


def gather_steps(shards, planes, wholes, full_planes, nz, sems):
    local_sem, send, recv, plane_send, plane_recv = sems
    s, z, c, sx, sy = place()
    own = 2 * z + c
    core = (s, 2 * z + 1 - c)
    beside_x, beside_y = (sx, own), (sy, own)
    greet(nz)
    started = []

    def put(copy):
        copy.start()
        started.append(copy)

    items = []
    for w, shard_ref in enumerate(shards):
        if shard_ref.shape[0] % 128:
            items.append((w, 0, 0, None))
            continue
        for row in range(0, shard_ref.shape[0], 128):
            wide = min(shard_ref.shape[1], 1024)
            for col in range(0, shard_ref.shape[1], wide):
                items.append((w, row, 128, pl.ds(col, wide)))
    count = len(items)
    split = [item[2] > 0 for item in items]

    def cut(ref, i, q=None, half=None):
        _, row, height, cols = items[i]
        if not height:
            return ref
        if q is not None:
            height = height // 4
            row = row + q * height
        if half is not None:
            height = height // 2
            row = row + half * height
        return ref.at[pl.ds(row, height), cols]

    def shard(i, q=None):
        return cut(shards[items[i][0]], i, q)

    def whole(i, block, q=None, half=None):
        return cut(wholes[items[i][0]].at[block], i, q, half)

    def every_block(i):
        w, row, height, cols = items[i]
        return wholes[w].at[:, pl.ds(row, height), cols] if height else wholes[w]

    def along_z(i):
        pltpu.make_async_copy(shard(i), whole(i, own), local_sem.at[i]).start()
        q = s if split[i] else None
        for dz in range(1, nz):
            to = (s, 2 * lax.rem(z + dz, nz) + c)
            put(remote(shard(i, q), whole(i, own, q), send.at[i, dz, 0], recv.at[i, dz, 0], to))
        put(remote(shard(i), whole(i, own), send.at[i, 0, 0], recv.at[i, 0, 0], core))

    def moved(i, dz, kind, q, half, to):
        part = whole(i, 2 * lax.rem(z + nz - dz, nz) + c, q if split[i] else None, half)
        return remote(part, part, send.at[i, dz, kind], recv.at[i, dz, kind], to)

    def to_core(i, dz, kind, q, half):
        put(moved(i, dz, kind, q, half, core))

    def first(i, dz):
        moved(i, dz, 0, s, None, core).wait_recv()
        if split[i]:
            put(moved(i, dz, 1, s, None, beside_x))
            put(moved(i, dz, 2, s, None, beside_y))
        to_core(i, dz, 5, s, None)

    def second(i, dz):
        moved(i, dz, 1, sx, None, core).wait_recv()
        put(moved(i, dz, 4, sx, 0, beside_y))
        to_core(i, dz, 6, sx, None)
        moved(i, dz, 2, sy, None, core).wait_recv()
        put(moved(i, dz, 3, sy, 1, beside_x))
        to_core(i, dz, 7, sy, None)

    def third(i, dz):
        moved(i, dz, 4, 3 - s, 0, core).wait_recv()
        to_core(i, dz, 8, 3 - s, 0)
        moved(i, dz, 3, 3 - s, 1, core).wait_recv()
        to_core(i, dz, 9, 3 - s, 1)

    def arrive(i):
        other = 1 - c
        pltpu.make_async_copy(shard(i), whole(i, own), local_sem.at[i]).wait()
        block = whole(i, 2 * z + other)
        remote(block, block, send.at[i, 0, 0], recv.at[i, 0, 0], core).wait_recv()
        for dz in range(1, nz):
            kinds = [(5, s if split[i] else None, None)]
            if split[i]:
                kinds += [(6, sx, None), (7, sy, None), (8, 3 - s, 0), (9, 3 - s, 1)]
            for kind, q, half in kinds:
                part = whole(i, 2 * lax.rem(z + nz - dz, nz) + other, q, half)
                remote(part, part, send.at[i, dz, kind], recv.at[i, dz, kind], core).wait_recv()

    def plane(i, kind, q, half, to):
        rows = full_planes[i].shape[0]
        part = full_planes[i].at[pl.ds(half * (rows // 2), rows // 2), q]
        return remote(part, part, plane_send.at[i, kind], plane_recv.at[i, kind], to)

    def plane_part(i):
        return planes[i].at[0] if len(planes[i].shape) == 4 else planes[i]

    def plane_whole(i, kind, q, to):
        return remote(
            plane_part(i), full_planes[i].at[:, q], plane_send.at[i, kind], plane_recv.at[i, kind], to
        )

    def plane_here(i):
        return pltpu.make_async_copy(
            plane_part(i), full_planes[i].at[:, s], local_sem.at[count + i]
        )

    def plane_first(i):
        plane_here(i).start()
        put(plane_whole(i, 0, s, beside_x))
        put(plane_whole(i, 1, s, beside_y))

    def plane_second(i):
        plane_whole(i, 0, sx, core).wait_recv()
        put(plane(i, 2, sx, 0, beside_y))
        plane_whole(i, 1, sy, core).wait_recv()
        put(plane(i, 3, sy, 1, beside_x))

    def plane_arrive(i):
        plane_here(i).wait()
        plane(i, 2, 3 - s, 0, core).wait_recv()
        plane(i, 3, 3 - s, 1, core).wait_recv()

    def settle():
        for copy in started:
            copy.wait_send()

    steps, ready = [], {}

    def step(call, *args):
        steps.append(lambda: call(*args))

    ahead = 4
    for i in range(2):
        plane_first(i)
    for i in range(min(ahead, count)):
        along_z(i)
    for i in range(count + 3):
        for dz in range(1, nz):
            if i < count:
                step(first, i, dz)
            if 1 <= i <= count and split[i - 1]:
                step(second, i - 1, dz)
            if 2 <= i < count + 2 and split[i - 2]:
                step(third, i - 2, dz)
        if ahead + i < count:
            step(along_z, ahead + i)
        if i in (1, 2):
            step(plane_second, i - 1)
        if i == 3:
            ready["planes"] = len(steps)
        if i >= 3:
            ready[i - 3] = len(steps)
    return steps, ready, arrive, plane_arrive, every_block, settle


SLOTS = 8
LAYER_OUTS = 25


def layer_kernel(count, nz, rows, local_len, *refs):
    at = 0

    def take(n):
        nonlocal at
        at += n
        return refs[at - n : at]

    shards = take(count)
    hidden, encoder, cotangent, lengths, enc_lengths = take(5)
    wholes, outs = take(count), take(LAYER_OUTS)
    gains, residual = take(2)
    held = list(take(LAYER_OUTS - 1))
    held.insert(14, held[5])
    (hid, x_all, query, keys, values, prob, prob_own, context, ckeys, cvalues) = held[:10]
    (normal, normal_scale, normed_low, cquery, cprob, ccontext, output) = held[10:17]
    (crossed_low, activated, last_low, up_back, cross_low, ccontext_back, gain_total) = held[17:24]
    states = held[24]
    land_gains, rel, normal2, scale2, pool, mains, hot_ref = take(7)
    load_sems, out_sems = take(2)
    steps, ready, arrive, plane_arrive, every_block, settle = gather_steps(
        shards, (hidden, encoder), wholes, (mains, states), nz, take(5)
    )
    tokens, width = hid.shape
    mine = 3 * local_len
    span = mains.shape[1] * local_len
    start = lax.axis_index("seq") * local_len
    emitted = []

    def leave(i):
        return pltpu.make_async_copy(held[i], outs[i], out_sems.at[i])

    def emit(*targets):
        for target in targets:
            i = next(i for i, ref in enumerate(held) if ref is target)
            leave(i).start()
            if target is not prob:
                emitted.append(leave(i))

    def emit_cross():
        leave(14).start()
        emitted.append(leave(14))

    order = list(range(1, 18)) + [10, 11, 12, 13, 9]
    KEY, VALUE, QUERY, REL, CKEY, CVALUE, OUT, CQUERY, COUT, UP, DOWN = (*range(9), 9, 13)
    UP_AGAIN, COUT_AGAIN = 17, 21

    def slot_of(load):
        return 4 + load - DOWN if DOWN <= load < UP_AGAIN else load % 4 if load >= 9 else load % SLOTS

    def load_copy(load):
        source = every_block(order[load])
        target = pool.at[slot_of(load)]
        if source.shape[2] < target.shape[2]:
            target = target.at[:, :, : source.shape[2]]
        return pltpu.make_async_copy(source, target, load_sems.at[load])

    def weight(load):
        return pool.at[slot_of(load)]

    def columns(load, cols):
        return pool[slot_of(load), :, :, cols].reshape(width, 256)

    def pair_rows(load, i):
        return pool[slot_of(load), pl.ds(2 * i, 2)].reshape(256, width)

    def project(left, load, target, scale=None):
        def body(cols):
            product = mm(left[...], columns(load, cols))
            if scale is not None:
                product = product * scale
            target[:, cols] = product.astype(target.dtype)

        tiles(target.shape[1], body)

    def prepare():
        plane_arrive(0)
        plane_arrive(1)
        for r in range(rows):
            for j in range(3):
                tile = hidden[j, r]
                hid[r * mine + j * local_len : r * mine + (j + 1) * local_len] = tile
                if j:
                    to = rows * span + (2 * r + j - 1) * local_len
                    x_all[to : to + local_len] = tile
        x_all[: rows * span] = mains[...].reshape(rows * span, width)
        gain_total[...] = jnp.zeros_like(gain_total)
        hot_ref[...] = hot_forward(start, span)
        emit(hid, x_all, states)

    def take_gains():
        arrive(0)
        copy = pltpu.make_async_copy(wholes[0], land_gains, load_sems.at[len(order)])
        copy.start()
        copy.wait()
        for d in range(land_gains.shape[0]):
            gains[:, d * 128 : (d + 1) * 128] = land_gains[d].astype(jnp.float32)

    def attend(step, carry):
        r, g = step // 4, lax.rem(step, 4)
        attend_step(
            r, g, step, start, mine, span, local_len, rows, lengths, query, rel, keys, values,
            prob, prob_own, context, hot_ref[...],
        )
        return carry

    def cross(step, carry):
        r, g = step // 4, lax.rem(step, 4)
        cross_step(r, g, step, mine, span, local_len, enc_lengths, cquery, ckeys, cvalues, cprob, ccontext)
        return carry

    def out_body(cols):
        residual[:, cols] = hid[:, cols].astype(jnp.float32) + mm(context[...], columns(OUT, cols))

    def norm_body(part):
        normal[part], scale = norm_rows(residual[part])
        normal_scale[part] = jnp.broadcast_to(scale, (scale.shape[0], 128))
        normed_low[part] = (normal[part] * gains[0:1]).astype(jnp.bfloat16)

    def after_attention():
        tiles(width, out_body)
        row_tiles(tokens, norm_body)
        emit(context, normal, normal_scale, normed_low)

    def after_cross_query():
        project(normed_low, CQUERY, cquery, 0.125)
        emit(cquery)
        leave(5).wait()

    def cross_body(cols):
        residual[:, cols] = normal[:, cols] * gains[0:1, cols] + mm(ccontext[...], columns(COUT, cols))

    def cross_norm_body(part):
        normal2[part], scale = norm_rows(residual[part])
        scale2[part] = jnp.broadcast_to(scale, (scale.shape[0], 128))
        after = normal2[part] * gains[1:2]
        crossed_low[part] = after.astype(jnp.bfloat16)
        residual[part] = after

    def after_cross():
        tiles(width, cross_body)
        row_tiles(tokens, cross_norm_body)
        emit(ccontext, crossed_low)

    slope = up_back

    def up(k):
        def body(i, carry):
            cols = pl.ds(pl.multiple_of(i * 256, 256), 256)
            to = pl.ds(pl.multiple_of(k * width + i * 256, 256), 256)
            value = mm(crossed_low[...], columns(UP + k, cols))
            below = 0.5 + 0.5 * lax.erf(value * (0.5**0.5))
            activated[:, to] = (value * below).astype(jnp.bfloat16)
            density = jnp.exp(-0.5 * value * value) * (1.0 / math.sqrt(2.0 * math.pi))
            slope[:, to] = (below + value * density).astype(jnp.bfloat16)
            return carry

        lax.fori_loop(0, width // 256, body, 0)
        if k == 3:
            emit(activated)

    blocks = pool.shape[1]

    def of_down(k, d):
        return d * 4 * 128 + k * 128

    def down(k):
        def body(cols):
            left = jnp.concatenate(
                [activated[:, of_down(k, d) : of_down(k, d) + 128] for d in range(blocks)], axis=1
            )
            residual[:, cols] += mm(left, columns(DOWN + k, cols))

        tiles(width, body)

    def last_norm():
        for r in range(rows):
            for j in range(3):
                part = slice(r * mine + j * local_len, r * mine + (j + 1) * local_len)
                normal3, scale = norm_rows(residual[part])
                output[j, r] = (normal3 * gains[2:3]).astype(output.dtype)
                above = cotangent[j, r].astype(jnp.float32)
                add_rows(gain_total, 2, above * normal3)
                grad = norm_back(above, normal3, scale, gains[2:3])
                residual[part] = grad
                last_low[part] = grad.astype(jnp.bfloat16)
        emit(output, last_low)

    def down_back(k):
        for i in range(blocks // 2):
            product = mm_back(last_low[...], pair_rows(DOWN + k, i))
            for d in range(2):
                cols = slice(of_down(k, 2 * i + d), of_down(k, 2 * i + d) + 128)
                slopes = slope[:, cols].astype(jnp.float32)
                up_back[:, cols] = (product[:, d * 128 : (d + 1) * 128] * slopes).astype(jnp.bfloat16)
        if k == 3:
            emit(up_back)

    def up_again(k):
        def body(i, carry):
            cols = pl.ds(pl.multiple_of(i * 256, 256), 256)
            left = up_back[:, k * width : (k + 1) * width]
            residual[:, cols] += mm_back(left, pair_rows(UP_AGAIN + k, i))
            return carry

        lax.fori_loop(0, width // 256, body, 0)

    def cross_norm_back(part):
        above = residual[part]
        add_rows(gain_total, 1, above * normal2[part])
        grad = norm_back(above, normal2[part], scale2[part][:, 0:1], gains[1:2])
        residual[part] = grad
        cross_low[part] = grad.astype(jnp.bfloat16)

    def cout_again():
        row_tiles(tokens, cross_norm_back)

        def body(i, carry):
            cols = pl.ds(pl.multiple_of(i * 256, 256), 256)
            ccontext_back[:, cols] = mm_back(
                cross_low[...], pair_rows(COUT_AGAIN, i)
            ).astype(jnp.bfloat16)
            return carry

        lax.fori_loop(0, width // 256, body, 0)
        emit(cross_low, ccontext_back, gain_total)

    pieces = [("planes", 2, prepare)]
    pieces += [
        (KEY, 3, lambda: project(x_all, KEY, keys)),
        (VALUE, 3, lambda: project(x_all, VALUE, values)),
        (QUERY, 2, lambda: project(hid, QUERY, query, 0.125)),
        (REL, 1, lambda: project(hid, REL, rel)),
    ]
    half = 2
    for i in range(0, 4 * rows, half):
        pieces.append((REL, 5, lambda i=i: lax.fori_loop(i, i + half, attend, 0)))
    pieces += [
        (REL, 0, lambda: emit(query, keys, values, prob, prob_own)),
        (CKEY, 2, lambda: project_states(CKEY, ckeys)),
        (CVALUE, 2, lambda: project_states(CVALUE, cvalues)),
        (OUT, 0, take_gains),
        (OUT, 3, after_attention),
        (CQUERY, 2, after_cross_query),
    ]

    def project_states(load, target):
        def body(cols):
            left = states[...].reshape(rows * span, width)
            target[:, cols] = mm(left, columns(load, cols)).astype(target.dtype)

        tiles(width, body)
        emit(target)

    for i in range(0, 4 * rows, half):
        pieces.append((CQUERY, 3, lambda i=i: lax.fori_loop(i, i + half, cross, 0)))
    pieces += [(CQUERY, 0, emit_cross), (COUT, 3, after_cross)]
    pieces += [(UP + k, 3, functools.partial(up, k)) for k in range(4)]
    pieces += [(DOWN + k, 1, functools.partial(down, k)) for k in range(4)]
    pieces.append((DOWN + 3, 3, last_norm))
    pieces += [(DOWN + k, 1, functools.partial(down_back, k)) for k in range(4)]
    pieces += [(UP_AGAIN + k, 1, functools.partial(up_again, k)) for k in range(4)]
    pieces.append((COUT_AGAIN, 3, cout_again))

    last_use = {}
    for index, (need, _, _) in enumerate(pieces):
        last_use[need] = index
    state = {"step": 0, "load": 0}
    arrived, waited = set(), set()

    def run_to(n):
        while state["step"] < min(n, len(steps)):
            steps[state["step"]]()
            state["step"] += 1

    def free(load, done):
        return all(
            last_use[other] < done for other in range(load) if slot_of(other) == slot_of(load)
        )

    def begin_load():
        load = state["load"]
        if order[load] not in arrived:
            arrive(order[load])
            arrived.add(order[load])
        load_copy(load).start()
        state["load"] += 1

    rate = len(steps) / 130.0
    for index, (need, cost, call) in enumerate(pieces):
        if need == "planes":
            run_to(ready["planes"])
        else:
            while state["load"] <= need:
                run_to(ready[order[state["load"]]])
                begin_load()
            if need not in waited:
                waited.add(need)
                load_copy(need).wait()
        call()
        run_to(state["step"] + int(cost * rate + 0.5))
        while (
            state["load"] < len(order)
            and free(state["load"], index + 1)
            and ready[order[state["load"]]] <= state["step"]
        ):
            begin_load()
    run_to(len(steps))
    for copy in emitted:
        copy.wait()
    settle()


def layer(shards, hidden, encoder, cotangent, lengths, enc_lengths, ndp):
    nz = ndp // 2
    count = len(shards)
    low, wide = jnp.bfloat16, jnp.float32
    _, rows, local_len, width = hidden.shape
    tokens, span = 3 * rows * local_len, 4 * local_len
    every = rows * (span + 2 * local_len)
    ff = shards[-2].shape[1]
    steps = sum(max(1, w.size // (128 * 1024)) for w in shards)
    results = [
        ((tokens, width), low),
        ((every, width), low),
        ((tokens, width), low),
        ((every, width), low),
        ((every, width), low),
        ((4 * rows, 12 * local_len, span), low),
        ((tokens, width), low),
        ((tokens, width), low),
        ((rows * span, width), low),
        ((rows * span, width), low),
        ((tokens, width), wide),
        ((tokens, 128), wide),
        ((tokens, width), low),
        ((tokens, width), low),
        ((4 * rows, 12 * local_len, span), low),
        ((tokens, width), low),
        (hidden.shape, low),
        ((tokens, width), low),
        ((tokens, ff), low),
        ((tokens, width), low),
        ((tokens, ff), low),
        ((tokens, width), low),
        ((tokens, width), low),
        ((3, 8, width), wide),
        ((rows, 4, local_len, width), low),
    ]
    more = [((16, width), wide), ((tokens, width), wide)]
    vmem = pl.BlockSpec(memory_space=pltpu.VMEM)
    smem = pl.BlockSpec(memory_space=pltpu.SMEM)
    anywhere = pl.BlockSpec(memory_space=pl.ANY)
    return pl.pallas_call(
        lambda *refs: layer_kernel(count, nz, rows, local_len, *refs),
        out_shape=[jax.ShapeDtypeStruct((ndp,) + w.shape, w.dtype) for w in shards]
        + [jax.ShapeDtypeStruct(*result) for result in results]
        + [jax.ShapeDtypeStruct(*result) for result in more],
        in_specs=[vmem] * (count + 3) + [smem] * 2,
        out_specs=[anywhere] * (count + len(results)) + [vmem] * 2,
        scratch_shapes=[pltpu.VMEM(*result) for i, result in enumerate(results) if i != 14]
        + [
            pltpu.VMEM((ndp,) + shards[0].shape, low),
            pltpu.VMEM((tokens, width // 2), low),
            pltpu.VMEM((tokens, width), wide),
            pltpu.VMEM((tokens, 128), wide),
            pltpu.VMEM((SLOTS, ndp, 128, width), low),
            pltpu.VMEM((rows, 4, local_len, width), low),
            pltpu.VMEM((128, span), low),
            pltpu.SemaphoreType.DMA((23,)),
            pltpu.SemaphoreType.DMA((len(results),)),
            pltpu.SemaphoreType.DMA((steps + 2,)),
            pltpu.SemaphoreType.DMA((steps, nz, 10)),
            pltpu.SemaphoreType.DMA((steps, nz, 10)),
            pltpu.SemaphoreType.DMA((2, 4)),
            pltpu.SemaphoreType.DMA((2, 4)),
        ],
        compiler_params=pltpu.CompilerParams(
            collective_id=0, has_side_effects=True, vmem_limit_bytes=62 * 2**20
        ),
        name="layer",
    )(*shards, hidden, encoder, cotangent, lengths, enc_lengths)


def finish_kernel(count, *refs):
    sums, (hidden_own, main_sum, states_sum) = refs[:count], refs[count : count + 3]
    outs, (hidden_grad, states_grad), sems = (
        refs[count + 3 : 2 * count + 3],
        refs[2 * count + 3 : 2 * count + 5],
        refs[2 * count + 5],
    )
    copies = [
        pltpu.make_async_copy(src, dst, sems.at[i])
        for i, (src, dst) in enumerate(zip(sums + (states_sum,), outs + (states_grad,)))
    ]
    for copy in copies:
        copy.start()
    hidden_grad[0] = hidden_own[0] + main_sum[...]
    hidden_grad[1:] = hidden_own[1:]
    for copy in copies:
        copy.wait()


def finish(sums, hidden_own, main_sum, states_sum):
    shapes = [jax.ShapeDtypeStruct(a.shape, a.dtype) for a in (*sums, hidden_own, states_sum)]
    place = [pl.BlockSpec(memory_space=pl.ANY)]
    vmem = [pl.BlockSpec(memory_space=pltpu.VMEM)]
    count = len(sums)
    return pl.pallas_call(
        lambda *refs: finish_kernel(count, *refs),
        out_shape=shapes,
        in_specs=vmem * (count + 3),
        out_specs=place * count + vmem + place,
        scratch_shapes=[pltpu.SemaphoreType.DMA((count + 1,))],
        compiler_params=pltpu.CompilerParams(vmem_limit_bytes=62 * 2**20),
        name="finish",
    )(*sums, hidden_own, main_sum, states_sum)


def plain_call(kernel, name, ins, spaces, outs, scratch, flops):
    space = {"v": pltpu.VMEM, "s": pltpu.SMEM, "a": pl.ANY}
    out_shape = [jax.ShapeDtypeStruct(shape, kind) for shape, kind in outs]
    moved = sum(a.size * a.dtype.itemsize for a in list(ins) + out_shape)
    return pl.pallas_call(
        kernel,
        out_shape=out_shape,
        in_specs=[pl.BlockSpec(memory_space=space[p]) for p in spaces],
        out_specs=[pl.BlockSpec(memory_space=pltpu.VMEM)] * len(outs),
        scratch_shapes=scratch,
        compiler_params=pltpu.CompilerParams(vmem_limit_bytes=62 * 2**20),
        cost_estimate=pl.CostEstimate(flops=flops, bytes_accessed=moved, transcendentals=0),
        name=name,
    )(*ins)


def copies_of(arrays):
    return [pltpu.VMEM(a.shape, a.dtype) for a in arrays] + [
        pltpu.SemaphoreType.DMA((len(arrays),))
    ]


def local(
    hidden,
    encoder,
    lengths,
    enc_lengths,
    w_query,
    w_key,
    w_value,
    w_attn_out,
    w_relative,
    w_cross_query,
    w_cross_key,
    w_cross_value,
    w_cross_out,
    w_up,
    w_down,
    gain_attn,
    gain_cross,
    gain_ffn,
    cotangent,
):
    ndp, chips = lax.axis_size("dp"), lax.axis_size("seq")
    devices = ndp * chips
    low, wide = jnp.bfloat16, jnp.float32
    _, rows, local_len, width = hidden.shape
    span, tokens = local_len * chips, 3 * rows * local_len
    weights = (
        w_key,
        w_value,
        w_query,
        w_relative,
        w_cross_key,
        w_cross_value,
        w_attn_out,
        w_cross_query,
        w_cross_out,
        w_up,
        w_down,
    )
    gains = jnp.stack([gain_attn, gain_cross, gain_ffn])
    every = rows * (span + 2 * local_len)
    kernels = chips == 4 and w_query.shape[0] == 128 and w_down.shape[0] == 512
    if kernels:
        gains = jnp.pad(gains, ((0, 13), (0, 0)))
        results = layer(
            (gains,) + weights, hidden, encoder, cotangent, lengths, enc_lengths, ndp
        )
        whole, results = results[1 : len(weights) + 1], results[len(weights) + 1 :]
        whole = [w.reshape(-1, w.shape[-1]) for w in whole]
        (hid, x_all, query, keys, values, prob, prob_own, context, ckeys, cvalues) = results[:10]
        (normal, normal_scale, normed_low, cquery, cprob, ccontext, output) = results[10:17]
        (crossed_low, activated, last_low, up_back, cross_low) = results[17:22]
        (ccontext_back, gain_middle, states, gains, cross_grad) = results[22:]
        states = states.reshape(-1, width)
    else:
        gains = jnp.pad(gains, ((0, 5), (0, 0)))
        whole = [lax.all_gather(w, "dp", axis=0, tiled=True) for w in weights]
        gains = lax.all_gather(gains, "dp", axis=1, tiled=True).astype(wide)
        mains = lax.all_gather(hidden[0], "seq", axis=1).reshape(-1, width)
        states = lax.all_gather(encoder, "seq", axis=1).reshape(-1, width)
    (
        full_key,
        full_value,
        full_query,
        full_relative,
        full_ckey,
        full_cvalue,
        full_attn_out,
        full_cquery,
        full_cout,
        full_up,
        full_down,
    ) = whole
    if not kernels:
        ff = full_up.shape[1]
        fetched = (
            full_key,
            full_value,
            full_query,
            full_relative,
            full_ckey,
            full_cvalue,
            full_attn_out,
            full_cquery,
        )
        (
            hid,
            x_all,
            query,
            keys,
            values,
            prob,
            prob_own,
            context,
            ckeys,
            cvalues,
            normal,
            normal_scale,
            normed_low,
            cquery,
            cprob,
            ccontext,
        ) = plain_call(
            lambda *refs: forward_kernel(rows, local_len, *refs),
            "forward_attention",
            (hidden, mains, states, lengths, enc_lengths, gains) + fetched,
            "vvvssv" + "a" * len(fetched),
            [
                ((tokens, width), low),
                ((every, width), low),
                ((tokens, width), low),
                ((every, width), low),
                ((every, width), low),
                ((4 * rows, 12 * local_len, span), low),
                ((tokens, width), low),
                ((tokens, width), low),
                ((rows * span, width), low),
                ((rows * span, width), low),
                ((tokens, width), wide),
                ((tokens, 128), wide),
                ((tokens, width), low),
                ((tokens, width), low),
                ((4 * rows, 12 * local_len, span), low),
                ((tokens, width), low),
            ],
            [
                pltpu.VMEM((tokens, full_relative.shape[1]), low),
                pltpu.VMEM((tokens, width), wide),
            ]
            + copies_of(fetched),
            12 * 10**9,
        )
        fetched = (full_cout, full_up, full_down)
        (
            output,
            crossed_low,
            activated,
            last_low,
            up_back,
            cross_grad,
            cross_low,
            ccontext_back,
            gain_middle,
        ) = plain_call(
            lambda *refs: middle_kernel(rows, local_len, *refs),
            "feed_forward",
            (normal, ccontext, gains, cotangent) + fetched,
            "vvvv" + "a" * len(fetched),
            [
                (hidden.shape, low),
                ((tokens, width), low),
                ((tokens, ff), low),
                ((tokens, width), low),
                ((tokens, ff), low),
                ((tokens, width), wide),
                ((tokens, width), low),
                ((tokens, width), low),
                ((3, 8, width), wide),
            ],
            [
                pltpu.VMEM((tokens, width), wide),
                pltpu.VMEM((tokens, 128), wide),
                pltpu.VMEM((tokens, ff), low),
                pltpu.VMEM((tokens, width), wide),
            ]
            + copies_of(fetched),
            14 * 10**9,
        )
    fetched = (
        full_cquery,
        full_attn_out,
        full_ckey,
        full_cvalue,
        full_query,
        full_relative,
        full_key,
        full_value,
    )
    (
        cquery_back,
        ckey_back,
        cvalue_back,
        attn_low,
        query_back,
        key_back,
        value_back,
        rel_back,
        hidden_own,
        main_part,
        states_part,
        gain_back,
    ) = plain_call(
        lambda *refs: backward_kernel(rows, local_len, *refs),
        "backward_attention",
        (
            ccontext_back,
            cross_grad,
            cquery,
            ckeys,
            cvalues,
            cprob,
            normal,
            normal_scale,
            gains,
            query,
            keys,
            values,
            prob,
            prob_own,
        )
        + fetched,
        "v" * 14 + "a" * len(fetched),
        [
            ((tokens, width), low),
            ((rows * span, width), low),
            ((rows * span, width), low),
            ((tokens, width), low),
            ((tokens, width), low),
            ((every, width), low),
            ((every, width), low),
            ((tokens, full_relative.shape[1]), low),
            (hidden.shape, wide),
            ((chips, rows, local_len, width), low),
            ((chips, rows, local_len, width), low),
            ((3, 8, width), wide),
        ],
        [pltpu.VMEM((tokens, width), wide), pltpu.VMEM((tokens, width), low)] + copies_of(fetched),
        14 * 10**9,
    )
    xs = [activated, crossed_low, ccontext, normed_low, context, hid, x_all, states]
    gs = [
        last_low,
        up_back,
        cross_low,
        cquery_back,
        attn_low,
        query_back,
        rel_back,
        key_back,
        value_back,
        ckey_back,
        cvalue_back,
    ]
    pairs = [(0, 0), (1, 1), (2, 2), (3, 3), (4, 4), (5, 5), (5, 6), (6, 7), (6, 8), (7, 9), (7, 10)]
    gain_parts = jnp.sum(gain_middle + gain_back, axis=1)
    if kernels:
        gain_parts = jnp.transpose(gain_parts.reshape(3, devices, -1), (1, 0, 2))
        gain_parts = jnp.pad(gain_parts, ((0, 0), (0, 5), (0, 128 - gain_parts.shape[2])))
        gain_parts = gain_parts.reshape(2, 2, ndp // 2, 2, 8, 128)
        shares = (main_part, states_part)
        shares = [a.reshape((2, 2) + a.shape[1:]) for a in shares]
        *sums, gain_sums, main_sum, states_sum = reduce_grads(
            xs, gs, pairs, gain_parts, shares, ndp // 2
        )
        gain_sums = gain_sums[:3, : width // devices]
        *sums, output, hidden_grad, states_sum = finish(
            sums + [output], hidden_own, main_sum, states_sum
        )
    else:
        sums = [
            lax.psum_scatter(
                weight_grad(xs[i], gs[j]), ("seq", "dp"), scatter_dimension=0, tiled=True
            )
            for i, j in pairs
        ]
        gain_sums = lax.psum_scatter(gain_parts, ("seq", "dp"), scatter_dimension=1, tiled=True)
        main_sum, states_sum = (
            lax.psum_scatter(part, "seq", scatter_dimension=0).astype(wide)
            for part in (main_part, states_part)
        )
        hidden_grad = hidden_own.at[0].add(main_sum)
    gainattn_sum, gaincross_sum, gainffn_sum = gain_sums
    (
        down_sum,
        up_sum,
        cout_sum,
        cquery_sum,
        outproj_sum,
        query_sum,
        relative_sum,
        keyw_sum,
        valuew_sum,
        ckey_sum,
        cvalue_sum,
    ) = sums
    return (
        output,
        hidden_grad,
        states_sum,
        query_sum,
        keyw_sum,
        valuew_sum,
        outproj_sum,
        relative_sum,
        cquery_sum,
        ckey_sum,
        cvalue_sum,
        cout_sum,
        up_sum,
        down_sum,
        gainattn_sum,
        gaincross_sum,
        gainffn_sum,
    )


def solution(mesh):
    in_specs = (
        P(None, "dp", "seq", None),
        P("dp", "seq", None),
        P("dp"),
        P("dp"),
        P("dp", None),
        P("dp", None),
        P("dp", None),
        P("dp", None),
        P("dp", None),
        P("dp", None),
        P("dp", None),
        P("dp", None),
        P("dp", None),
        P("dp", None),
        P("dp", None),
        P("dp"),
        P("dp"),
        P("dp"),
        P(None, "dp", "seq", None),
    )
    out_specs = (
        P(None, "dp", "seq", None),
        P(None, "dp", "seq", None),
        P("dp", "seq", None),
        P(("seq", "dp"), None),
        P(("seq", "dp"), None),
        P(("seq", "dp"), None),
        P(("seq", "dp"), None),
        P(("seq", "dp"), None),
        P(("seq", "dp"), None),
        P(("seq", "dp"), None),
        P(("seq", "dp"), None),
        P(("seq", "dp"), None),
        P(("seq", "dp"), None),
        P(("seq", "dp"), None),
        P(("seq", "dp")),
        P(("seq", "dp")),
        P(("seq", "dp")),
    )
    return jax.shard_map(local, mesh=mesh, in_specs=in_specs, out_specs=out_specs, check_vma=False)
```

```python
import functools
import math

import jax
import jax.numpy as jnp
from jax import lax
from jax.experimental import pallas as pl
from jax.experimental.pallas import tpu as pltpu
from jax.sharding import PartitionSpec as P

MESH = pl.DeviceIdType.MESH

HEADS = 16
HEAD_DIM = 64
BUCKETS = 32


eps_norm = 1e-05
bucket_edges = [step_index for step_index in range(1, 16)] + [
    int(math.ceil(16 * 8 ** ((step_index - 16) / 16))) for step_index in range(16, 32)
]


def flatten_rows(array):
    return array.reshape(-1, array.shape[-1])


def weight_grad(array, grad_rows):
    return jnp.einsum(
        "nd,ne->de",
        flatten_rows(array),
        flatten_rows(grad_rows),
        preferred_element_type=jnp.float32,
    )


def remote(src, dst, send, recv, to):
    return pltpu.make_async_remote_copy(
        src_ref=src, dst_ref=dst, send_sem=send, recv_sem=recv, device_id=to, device_id_type=MESH
    )


def place():
    s = lax.axis_index("seq")
    d = lax.axis_index("dp")
    z, c = d // 2, lax.rem(d, 2)
    sx = s + 1 - 2 * lax.rem(s, 2)
    sy = lax.rem(s + 2, 4)
    return s, z, c, sx, sy


def greet(nz):
    s, z, c, sx, sy = place()
    barrier = pltpu.get_barrier_semaphore()
    dests = [(s, 2 * z + 1 - c), (sx, 2 * z + c), (sy, 2 * z + c)]
    for dz in range(1, nz):
        dests.append((s, 2 * lax.rem(z + dz, nz) + c))
    for dest in dests:
        pl.semaphore_signal(barrier, inc=1, device_id=dest, device_id_type=MESH)
    pl.semaphore_wait(barrier, len(dests))


NEG = -1000000000.0


def mm(left, right):
    return jnp.dot(left, right, preferred_element_type=jnp.float32)


def mm_back(left, right):
    return lax.dot_general(
        left, right, (((1,), (1,)), ((), ())), preferred_element_type=jnp.float32
    )


def mm_grad(left, right):
    return lax.dot_general(
        left, right, (((0,), (0,)), ((), ())), preferred_element_type=jnp.float32
    )


def tiles(width, body):
    def step(i, carry):
        body(pl.ds(pl.multiple_of(i * 256, 256), 256))
        return carry

    lax.fori_loop(0, width // 256, step, 0)


def row_tiles(rows, body, step_rows=64):
    def step(i, carry):
        body(pl.ds(pl.multiple_of(i * step_rows, step_rows), step_rows))
        return carry

    lax.fori_loop(0, rows // step_rows, step, 0)


def heads_in(tile):
    lane = lax.broadcasted_iota(jnp.int32, tile.shape, 1) // (tile.shape[1] // 4)
    return jnp.concatenate(
        [jnp.where(lane == h, tile, jnp.zeros_like(tile)) for h in range(4)], axis=0
    )


def heads_out(stacked):
    n, wide = stacked.shape[0] // 4, stacked.shape[1]
    lane = lax.broadcasted_iota(jnp.int32, (n, wide), 1) // (wide // 4)
    result = stacked[3 * n :]
    for h in (2, 1, 0):
        result = jnp.where(lane == h, stacked[h * n : (h + 1) * n], result)
    return result


def head_lanes(columns, wide):
    n = columns[0].shape[0]
    lane = lax.broadcasted_iota(jnp.int32, (n, wide), 1) // (wide // 4)
    result = jnp.broadcast_to(columns[3], (n, wide))
    for h in (2, 1, 0):
        result = jnp.where(lane == h, jnp.broadcast_to(columns[h], (n, wide)), result)
    return result


def head_sums(product):
    n, wide = product.shape
    lane = lax.broadcasted_iota(jnp.int32, (n, wide), 1) // (wide // 4)
    return [
        jnp.sum(jnp.where(lane == h, product, 0.0), axis=1, keepdims=True) for h in range(4)
    ]


def bucket_of(distance):
    total = jnp.zeros_like(distance)
    for edge in bucket_edges:
        total = total + (distance >= edge).astype(jnp.int32)
    return total


def hot_forward(start, span):
    lag = lax.broadcasted_iota(jnp.int32, (128, span), 1)
    row = lax.rem(lax.broadcasted_iota(jnp.int32, (128, span), 0), BUCKETS)
    distance = lax.rem(start - lag + span, span)
    return jnp.where(bucket_of(distance) == row, 1.0, 0.0).astype(jnp.bfloat16)


def hot_backward(start, span):
    lag = lax.broadcasted_iota(jnp.int32, (span, 128), 0)
    column = lax.rem(lax.broadcasted_iota(jnp.int32, (span, 128), 1), BUCKETS)
    distance = lax.rem(start + lag + 1, span)
    return jnp.where(bucket_of(distance) == column, 1.0, 0.0).astype(jnp.bfloat16)


def skewed(array, block):
    return jnp.concatenate(
        [
            pltpu.roll(array[i : i + block], 0, 1, stride=1, stride_axis=0)
            for i in range(0, array.shape[0], block)
        ],
        axis=0,
    )


def norm_rows(values):
    centred = values - jnp.mean(values, axis=1, keepdims=True)
    scale = lax.rsqrt(jnp.mean(centred * centred, axis=1, keepdims=True) + eps_norm)
    return centred * scale, scale


def norm_back(grad, normal, scale, gain):
    grad = grad * gain
    return scale * (
        grad
        - jnp.mean(grad, axis=1, keepdims=True)
        - normal * jnp.mean(grad * normal, axis=1, keepdims=True)
    )


def add_rows(total_ref, index, product):
    total_ref[index] += jnp.sum(product.reshape(-1, 8, product.shape[1]), axis=0)


class Fetch:
    def __init__(self, sources, targets, sems):
        self.copies = [
            pltpu.make_async_copy(src, dst, sems.at[i])
            for i, (src, dst) in enumerate(zip(sources, targets))
        ]
        self.targets = targets
        self.waited = set()
        for copy in self.copies:
            copy.start()

    def __getitem__(self, i):
        if i not in self.waited:
            self.waited.add(i)
            self.copies[i].wait()
        return self.targets[i]


def attend_step(
    r, g, step, start, mine, span, local_len, rows, lengths, query, rel, keys, values, prob, prob_own, context, hot
):
    cols = pl.ds(pl.multiple_of(g * 256, 256), 256)
    own_rows = pl.ds(pl.multiple_of(r * mine, local_len), mine)
    main_rows = pl.ds(pl.multiple_of(r * span, span), span)
    side_rows = pl.ds(pl.multiple_of(rows * span + r * 2 * local_len, local_len), 2 * local_len)
    q_tile = query[own_rows, cols]
    rel_tile = rel[own_rows, pl.ds(pl.multiple_of(g * 128, 128), 128)]
    side_key = keys[side_rows, cols].astype(jnp.float32)
    side_value = values[side_rows, cols].astype(jnp.float32)
    zero = jnp.zeros((local_len, 256), jnp.float32)
    scores = mm_back(heads_in(q_tile), keys[main_rows, cols])
    bias = skewed(mm(heads_in(rel_tile), hot), local_len)
    products = q_tile.astype(jnp.float32) * jnp.concatenate([zero, side_key], axis=0)
    own_dot = head_sums(products)
    rel_lane = lax.broadcasted_iota(jnp.int32, (mine, 128), 1)
    rel_wide = rel_tile.astype(jnp.float32)
    row = lax.broadcasted_iota(jnp.int32, (mine, span), 0)
    at = lax.broadcasted_iota(jnp.int32, (mine, span), 1)
    ahead = start + lax.rem(row, local_len) + jnp.where(row < local_len, 1, 0)
    kept = (at < ahead) & (at < lengths[r])
    first = lax.broadcasted_iota(jnp.int32, (mine, 1), 0) < local_len
    low, owns = [], []
    for h in range(4):
        part = slice(h * mine, (h + 1) * mine)
        score = jnp.where(kept, scores[part] + bias[part], NEG)
        near = jnp.sum(jnp.where(rel_lane == h * BUCKETS, rel_wide, 0.0), axis=1, keepdims=True)
        own = jnp.where(first, NEG, own_dot[h] + near)
        peak = jnp.maximum(jnp.max(score, axis=1, keepdims=True), own)
        power = jnp.exp(score - peak)
        own_power = jnp.exp(own - peak)
        share = 1.0 / (jnp.sum(power, axis=1, keepdims=True) + own_power)
        low.append((power * share).astype(jnp.bfloat16))
        owns.append(own_power * share)
    low = jnp.concatenate(low, axis=0)
    prob[step] = low
    spread = head_lanes(owns, 256)
    prob_own[own_rows, cols] = spread.astype(prob_own.dtype)
    total = heads_out(mm(low, values[main_rows, cols]))
    total = total + spread * jnp.concatenate([zero, side_value], axis=0)
    context[own_rows, cols] = total.astype(context.dtype)


def cross_step(
    r, g, step, mine, span, local_len, enc_lengths, cquery, ckeys, cvalues, cprob, ccontext
):
    cols = pl.ds(pl.multiple_of(g * 256, 256), 256)
    own_rows = pl.ds(pl.multiple_of(r * mine, local_len), mine)
    main_rows = pl.ds(pl.multiple_of(r * span, span), span)
    scores = mm_back(heads_in(cquery[own_rows, cols]), ckeys[main_rows, cols])
    at = lax.broadcasted_iota(jnp.int32, (mine, span), 1)
    kept = at < enc_lengths[r]
    low = []
    for h in range(4):
        score = jnp.where(kept, scores[h * mine : (h + 1) * mine], NEG)
        power = jnp.exp(score - jnp.max(score, axis=1, keepdims=True))
        share = 1.0 / jnp.sum(power, axis=1, keepdims=True)
        low.append((power * share).astype(jnp.bfloat16))
    low = jnp.concatenate(low, axis=0)
    cprob[step] = low
    ccontext[own_rows, cols] = heads_out(mm(low, cvalues[main_rows, cols])).astype(
        ccontext.dtype
    )


def forward_kernel(rows, local_len, *refs):
    (
        hidden,
        mains,
        states,
        lengths,
        enc_lengths,
        gains,
        *weights,
    ) = refs[:14]
    (hid, x_all, query, keys, values, prob, prob_own, context, ckeys, cvalues) = refs[14:24]
    (normal, normal_scale, normed_low, cquery, cprob, ccontext) = refs[24:30]
    rel, residual = refs[30:32]
    fetch = Fetch(weights, refs[32:40], refs[40])
    w_key, w_value, w_query, w_relative, w_ckey, w_cvalue, w_out, w_cquery = range(8)
    width = hid.shape[1]
    mine = 3 * local_len
    span = mains.shape[0] // rows
    start = lax.axis_index("seq") * local_len
    x_all[: rows * span] = mains[...]
    for r in range(rows):
        for j in range(3):
            tile = hidden[j, r]
            hid[r * mine + j * local_len : r * mine + (j + 1) * local_len] = tile
            if j:
                at = rows * span + (2 * r + j - 1) * local_len
                x_all[at : at + local_len] = tile

    def project(left, w, target, scale=None):
        weight = fetch[w]

        def body(cols):
            product = mm(left[...], weight[:, cols])
            if scale is not None:
                product = product * scale
            target[:, cols] = product.astype(target.dtype)

        tiles(target.shape[1], body)

    project(x_all, w_key, keys)
    project(x_all, w_value, values)
    project(hid, w_query, query, 0.125)
    project(hid, w_relative, rel)
    hot = hot_forward(start, span)

    def attend(step, carry):
        attend_step(
            step // 4, lax.rem(step, 4), step, start, mine, span, local_len, rows, lengths,
            query, rel, keys, values, prob, prob_own, context, hot,
        )
        return carry

    lax.fori_loop(0, 4 * rows, attend, 0)
    project(states, w_ckey, ckeys)
    project(states, w_cvalue, cvalues)
    weight_out = fetch[w_out]

    def out_body(cols):
        residual[:, cols] = hid[:, cols].astype(jnp.float32) + mm(context[...], weight_out[:, cols])

    tiles(width, out_body)

    def norm_body(part):
        normal[part], scale = norm_rows(residual[part])
        normal_scale[part] = jnp.broadcast_to(scale, (scale.shape[0], 128))
        normed_low[part] = (normal[part] * gains[0:1]).astype(jnp.bfloat16)

    row_tiles(hid.shape[0], norm_body)
    project(normed_low, w_cquery, cquery, 0.125)

    def cross(step, carry):
        cross_step(
            step // 4, lax.rem(step, 4), step, mine, span, local_len, enc_lengths,
            cquery, ckeys, cvalues, cprob, ccontext,
        )
        return carry

    lax.fori_loop(0, 4 * rows, cross, 0)


def middle_kernel(
    rows,
    local_len,
    normal,
    ccontext,
    gains,
    cotangent,
    any_cout,
    any_up,
    any_down,
    output,
    crossed_low,
    activated,
    last_low,
    up_back,
    cross_grad,
    cross_low,
    ccontext_back,
    gain_total,
    normal2,
    scale2,
    slope,
    residual,
    v_cout,
    v_up,
    v_down,
    sems,
):
    fetch = Fetch((any_cout, any_up, any_down), (v_cout, v_up, v_down), sems)
    tokens, width = normal.shape
    mine = 3 * local_len
    gain_total[...] = jnp.zeros_like(gain_total)
    weight_cout = fetch[0]

    def cross_body(cols):
        residual[:, cols] = normal[:, cols] * gains[0:1, cols] + mm(
            ccontext[...], weight_cout[:, cols]
        )

    tiles(width, cross_body)

    def norm_body(part):
        normal2[part], scale = norm_rows(residual[part])
        scale2[part] = jnp.broadcast_to(scale, (scale.shape[0], 128))
        crossed_low[part] = (normal2[part] * gains[1:2]).astype(jnp.bfloat16)

    row_tiles(tokens, norm_body)
    weight_up = fetch[1]

    def up_body(cols):
        value = mm(crossed_low[...], weight_up[:, cols])
        below = 0.5 + 0.5 * lax.erf(value * (0.5**0.5))
        activated[:, cols] = (value * below).astype(jnp.bfloat16)
        density = jnp.exp(-0.5 * value * value) * (1.0 / math.sqrt(2.0 * math.pi))
        slope[:, cols] = (below + value * density).astype(jnp.bfloat16)

    tiles(activated.shape[1], up_body)
    weight_down = fetch[2]

    def down_body(cols):
        residual[:, cols] = normal2[:, cols] * gains[1:2, cols] + mm(
            activated[...], weight_down[:, cols]
        )

    tiles(width, down_body)
    for r in range(rows):
        for j in range(3):
            at = r * mine + j * local_len
            part = slice(at, at + local_len)
            normal3, scale = norm_rows(residual[part])
            output[j, r] = (normal3 * gains[2:3]).astype(output.dtype)
            above = cotangent[j, r].astype(jnp.float32)
            add_rows(gain_total, 2, above * normal3)
            grad = norm_back(above, normal3, scale, gains[2:3])
            residual[part] = grad
            last_low[part] = grad.astype(jnp.bfloat16)

    def down_back(cols):
        product = mm_back(last_low[...], weight_down[cols, :])
        up_back[:, cols] = (product * slope[:, cols].astype(jnp.float32)).astype(jnp.bfloat16)

    tiles(activated.shape[1], down_back)

    def up_back_body(cols):
        residual[:, cols] = residual[:, cols] + mm_back(up_back[...], weight_up[cols, :])

    tiles(width, up_back_body)

    def cross_norm_back(part):
        above = residual[part]
        add_rows(gain_total, 1, above * normal2[part])
        grad = norm_back(above, normal2[part], scale2[part][:, 0:1], gains[1:2])
        cross_grad[part] = grad
        cross_low[part] = grad.astype(jnp.bfloat16)

    row_tiles(tokens, cross_norm_back)

    def cout_back(cols):
        ccontext_back[:, cols] = mm_back(cross_low[...], weight_cout[cols, :]).astype(jnp.bfloat16)

    tiles(width, cout_back)


def turning(span):
    return jnp.where(
        lax.broadcasted_iota(jnp.int32, (span, span), 0)
        + lax.broadcasted_iota(jnp.int32, (span, span), 1)
        == span - 1,
        1.0,
        0.0,
    ).astype(jnp.bfloat16)


def cross_back_step(
    r, g, step, mine, span, local_len, ccontext_back, cvalues, cprob, ckeys, cquery, cquery_back, ckey_back, cvalue_back
):
    cols = pl.ds(pl.multiple_of(g * 256, 256), 256)
    own_rows = pl.ds(pl.multiple_of(r * mine, local_len), mine)
    main_rows = pl.ds(pl.multiple_of(r * span, span), span)
    above = heads_in(ccontext_back[own_rows, cols])
    grads = mm_back(above, cvalues[main_rows, cols])
    low = []
    for h in range(4):
        part = slice(h * mine, (h + 1) * mine)
        share = cprob[step, part].astype(jnp.float32)
        weighted = share * grads[part]
        low.append(
            (weighted - share * jnp.sum(weighted, axis=1, keepdims=True)).astype(jnp.bfloat16)
        )
    low = jnp.concatenate(low, axis=0)
    back = heads_out(mm(low, ckeys[main_rows, cols])).astype(jnp.bfloat16)
    cquery_back[own_rows, cols] = back * jnp.bfloat16(0.125)
    ckey_back[main_rows, cols] = mm_grad(low, heads_in(cquery[own_rows, cols])).astype(
        jnp.bfloat16
    )
    cvalue_back[main_rows, cols] = mm_grad(cprob[step], above).astype(jnp.bfloat16)


def attend_back_step(
    r, g, step, mine, span, local_len, rows, context_back, query, keys, values, prob, prob_own,
    query_back, key_back, value_back, rel_back, hot, turn
):
    cols = pl.ds(pl.multiple_of(g * 256, 256), 256)
    own_rows = pl.ds(pl.multiple_of(r * mine, local_len), mine)
    main_rows = pl.ds(pl.multiple_of(r * span, span), span)
    side_rows = pl.ds(pl.multiple_of(rows * span + r * 2 * local_len, local_len), 2 * local_len)
    above_tile = context_back[own_rows, cols]
    above = heads_in(above_tile)
    above_wide = above_tile.astype(jnp.float32)
    q_tile = query[own_rows, cols]
    zero = jnp.zeros((local_len, 256), jnp.float32)
    side_key = jnp.concatenate([zero, keys[side_rows, cols].astype(jnp.float32)], axis=0)
    side_value = jnp.concatenate([zero, values[side_rows, cols].astype(jnp.float32)], axis=0)
    spread = prob_own[own_rows, cols].astype(jnp.float32)
    grads = mm_back(above, values[main_rows, cols])
    own_grads = head_sums(above_wide * side_value)
    low, own_low = [], []
    for h in range(4):
        part = slice(h * mine, (h + 1) * mine)
        share = prob[step, part].astype(jnp.float32)
        own_share = spread[:, h * 64 : h * 64 + 1]
        weighted = share * grads[part]
        delta = jnp.sum(weighted, axis=1, keepdims=True) + own_share * own_grads[h]
        low.append((weighted - share * delta).astype(jnp.bfloat16))
        own_low.append(own_share * (own_grads[h] - delta))
    low = jnp.concatenate(low, axis=0)
    own_spread = head_lanes(own_low, 256)
    back = heads_out(mm(low, keys[main_rows, cols])) + own_spread * side_key
    query_back[own_rows, cols] = back.astype(jnp.bfloat16) * jnp.bfloat16(0.125)
    key_back[main_rows, cols] = mm_grad(low, heads_in(q_tile)).astype(jnp.bfloat16)
    value_back[main_rows, cols] = mm_grad(prob[step], above).astype(jnp.bfloat16)
    key_back[side_rows, cols] = (own_spread * q_tile.astype(jnp.float32))[local_len:].astype(
        jnp.bfloat16
    )
    value_back[side_rows, cols] = (spread * above_wide)[local_len:].astype(jnp.bfloat16)
    turned_low = skewed(mm(low, turn), local_len).astype(jnp.bfloat16)
    rel_total = heads_out(mm(turned_low, hot))
    near = lax.rem(lax.broadcasted_iota(jnp.int32, rel_total.shape, 1), BUCKETS) == 0
    rel_total = rel_total + jnp.where(near, head_lanes(own_low, 128), 0.0)
    rel_back[own_rows, pl.ds(pl.multiple_of(g * 128, 128), 128)] = rel_total.astype(
        jnp.bfloat16
    )


def backward_kernel(rows, local_len, *refs):
    (
        ccontext_back,
        cross_grad,
        cquery,
        ckeys,
        cvalues,
        cprob,
        normal,
        normal_scale,
        gains,
        query,
        keys,
        values,
        prob,
        prob_own,
        *weights,
    ) = refs[:22]
    (cquery_back, ckey_back, cvalue_back, attn_low, query_back, key_back) = refs[22:28]
    (value_back, rel_back, hidden_own, main_part, states_part, gain_total) = refs[28:34]
    residual, context_back = refs[34:36]
    fetch = Fetch(weights, refs[36:44], refs[44])
    w_cquery, w_out, w_ckey, w_cvalue, w_query, w_relative, w_key, w_value = range(8)
    tokens, width = query.shape
    mine = 3 * local_len
    span = ckeys.shape[0] // rows
    start = lax.axis_index("seq") * local_len
    gain_total[...] = jnp.zeros_like(gain_total)

    def cross(step, carry):
        cross_back_step(
            step // 4, lax.rem(step, 4), step, mine, span, local_len, ccontext_back, cvalues,
            cprob, ckeys, cquery, cquery_back, ckey_back, cvalue_back,
        )
        return carry

    lax.fori_loop(0, 4 * rows, cross, 0)
    weight_cquery = fetch[w_cquery]

    def cquery_body(cols):
        residual[:, cols] = cross_grad[:, cols] + mm_back(cquery_back[...], weight_cquery[cols, :])

    tiles(width, cquery_body)

    def attn_norm_back(part):
        above = residual[part]
        add_rows(gain_total, 0, above * normal[part])
        grad = norm_back(above, normal[part], normal_scale[part][:, 0:1], gains[0:1])
        residual[part] = grad
        attn_low[part] = grad.astype(jnp.bfloat16)

    row_tiles(tokens, attn_norm_back)
    weight_out = fetch[w_out]

    def out_back(cols):
        context_back[:, cols] = mm_back(attn_low[...], weight_out[cols, :]).astype(jnp.bfloat16)

    tiles(width, out_back)
    hot = hot_backward(start, span)
    turn = turning(span)

    def attend(step, carry):
        attend_back_step(
            step // 4, lax.rem(step, 4), step, mine, span, local_len, rows, context_back, query,
            keys, values, prob, prob_own, query_back, key_back, value_back, rel_back, hot, turn,
        )
        return carry

    lax.fori_loop(0, 4 * rows, attend, 0)
    weight_ckey, weight_cvalue = fetch[w_ckey], fetch[w_cvalue]
    weight_query, weight_relative = fetch[w_query], fetch[w_relative]
    weight_key, weight_value = fetch[w_key], fetch[w_value]
    chips = rows * span // (rows * local_len)

    def states_body(cols):
        total = mm_back(ckey_back[...], weight_ckey[cols, :])
        total = total + mm_back(cvalue_back[...], weight_cvalue[cols, :])
        total = total.astype(jnp.bfloat16)
        for r in range(rows):
            for p in range(chips):
                at = r * span + p * local_len
                states_part[p, r, :, cols] = total[at : at + local_len]

    tiles(width, states_body)

    def hidden_body(cols):
        total = mm_back(key_back[...], weight_key[cols, :])
        total = total + mm_back(value_back[...], weight_value[cols, :])
        mains = total[: rows * span].astype(jnp.bfloat16)
        for r in range(rows):
            for p in range(chips):
                at = r * span + p * local_len
                main_part[p, r, :, cols] = mains[at : at + local_len]
        own = residual[:, cols] + mm_back(query_back[...], weight_query[cols, :])
        own = own + mm_back(rel_back[...], weight_relative[cols, :])
        for r in range(rows):
            for j in range(3):
                tile = own[r * mine + j * local_len : r * mine + (j + 1) * local_len]
                if j:
                    at = rows * span + (2 * r + j - 1) * local_len
                    tile = tile + total[at : at + local_len]
                hidden_own[j, r, :, cols] = tile

    tiles(width, hidden_body)


def gather_steps(shards, planes, wholes, full_planes, nz, sems):
    local_sem, send, recv, plane_send, plane_recv = sems
    s, z, c, sx, sy = place()
    own = 2 * z + c
    core = (s, 2 * z + 1 - c)
    beside_x, beside_y = (sx, own), (sy, own)
    greet(nz)
    started = []

    def put(copy):
        copy.start()
        started.append(copy)

    items = []
    for w, shard_ref in enumerate(shards):
        if shard_ref.shape[0] % 128:
            items.append((w, 0, 0, None))
            continue
        for row in range(0, shard_ref.shape[0], 128):
            wide = min(shard_ref.shape[1], 1024)
            for col in range(0, shard_ref.shape[1], wide):
                items.append((w, row, 128, pl.ds(col, wide)))
    count = len(items)
    split = [item[2] > 0 for item in items]

    def cut(ref, i, q=None, half=None):
        _, row, height, cols = items[i]
        if not height:
            return ref
        if q is not None:
            height = height // 4
            row = row + q * height
        if half is not None:
            height = height // 2
            row = row + half * height
        return ref.at[pl.ds(row, height), cols]

    def shard(i, q=None):
        return cut(shards[items[i][0]], i, q)

    def whole(i, block, q=None, half=None):
        return cut(wholes[items[i][0]].at[block], i, q, half)

    def every_block(i):
        w, row, height, cols = items[i]
        return wholes[w].at[:, pl.ds(row, height), cols] if height else wholes[w]

    def along_z(i):
        pltpu.make_async_copy(shard(i), whole(i, own), local_sem.at[i]).start()
        q = s if split[i] else None
        for dz in range(1, nz):
            to = (s, 2 * lax.rem(z + dz, nz) + c)
            put(remote(shard(i, q), whole(i, own, q), send.at[i, dz, 0], recv.at[i, dz, 0], to))
        put(remote(shard(i), whole(i, own), send.at[i, 0, 0], recv.at[i, 0, 0], core))

    def moved(i, dz, kind, q, half, to):
        part = whole(i, 2 * lax.rem(z + nz - dz, nz) + c, q if split[i] else None, half)
        return remote(part, part, send.at[i, dz, kind], recv.at[i, dz, kind], to)

    def to_core(i, dz, kind, q, half):
        put(moved(i, dz, kind, q, half, core))

    def first(i, dz):
        moved(i, dz, 0, s, None, core).wait_recv()
        if split[i]:
            put(moved(i, dz, 1, s, None, beside_x))
            put(moved(i, dz, 2, s, None, beside_y))
        to_core(i, dz, 5, s, None)

    def second(i, dz):
        moved(i, dz, 1, sx, None, core).wait_recv()
        put(moved(i, dz, 4, sx, 0, beside_y))
        to_core(i, dz, 6, sx, None)
        moved(i, dz, 2, sy, None, core).wait_recv()
        put(moved(i, dz, 3, sy, 1, beside_x))
        to_core(i, dz, 7, sy, None)

    def third(i, dz):
        moved(i, dz, 4, 3 - s, 0, core).wait_recv()
        to_core(i, dz, 8, 3 - s, 0)
        moved(i, dz, 3, 3 - s, 1, core).wait_recv()
        to_core(i, dz, 9, 3 - s, 1)

    def arrive(i):
        other = 1 - c
        pltpu.make_async_copy(shard(i), whole(i, own), local_sem.at[i]).wait()
        block = whole(i, 2 * z + other)
        remote(block, block, send.at[i, 0, 0], recv.at[i, 0, 0], core).wait_recv()
        for dz in range(1, nz):
            kinds = [(5, s if split[i] else None, None)]
            if split[i]:
                kinds += [(6, sx, None), (7, sy, None), (8, 3 - s, 0), (9, 3 - s, 1)]
            for kind, q, half in kinds:
                part = whole(i, 2 * lax.rem(z + nz - dz, nz) + other, q, half)
                remote(part, part, send.at[i, dz, kind], recv.at[i, dz, kind], core).wait_recv()

    def plane(i, kind, q, half, to):
        rows = full_planes[i].shape[0]
        part = full_planes[i].at[pl.ds(half * (rows // 2), rows // 2), q]
        return remote(part, part, plane_send.at[i, kind], plane_recv.at[i, kind], to)

    def plane_part(i):
        return planes[i].at[0] if len(planes[i].shape) == 4 else planes[i]

    def plane_whole(i, kind, q, to):
        return remote(
            plane_part(i), full_planes[i].at[:, q], plane_send.at[i, kind], plane_recv.at[i, kind], to
        )

    def plane_here(i):
        return pltpu.make_async_copy(
            plane_part(i), full_planes[i].at[:, s], local_sem.at[count + i]
        )

    def plane_first(i):
        plane_here(i).start()
        put(plane_whole(i, 0, s, beside_x))
        put(plane_whole(i, 1, s, beside_y))

    def plane_second(i):
        plane_whole(i, 0, sx, core).wait_recv()
        put(plane(i, 2, sx, 0, beside_y))
        plane_whole(i, 1, sy, core).wait_recv()
        put(plane(i, 3, sy, 1, beside_x))

    def plane_arrive(i):
        plane_here(i).wait()
        plane(i, 2, 3 - s, 0, core).wait_recv()
        plane(i, 3, 3 - s, 1, core).wait_recv()

    def settle():
        for copy in started:
            copy.wait_send()

    steps, ready = [], {}

    def step(call, *args):
        steps.append(lambda: call(*args))

    ahead = 4
    for i in range(2):
        plane_first(i)
    for i in range(min(ahead, count)):
        along_z(i)
    for i in range(count + 3):
        for dz in range(1, nz):
            if i < count:
                step(first, i, dz)
            if 1 <= i <= count and split[i - 1]:
                step(second, i - 1, dz)
            if 2 <= i < count + 2 and split[i - 2]:
                step(third, i - 2, dz)
        if ahead + i < count:
            step(along_z, ahead + i)
        if i in (1, 2):
            step(plane_second, i - 1)
        if i == 3:
            ready["planes"] = len(steps)
        if i >= 3:
            ready[i - 3] = len(steps)
    return steps, ready, arrive, plane_arrive, every_block, settle


SLOTS = 8
LAYER_OUTS = 25


def layer_kernel(count, nz, rows, local_len, *refs):
    at = 0

    def take(n):
        nonlocal at
        at += n
        return refs[at - n : at]

    shards = take(count)
    hidden, encoder, cotangent, lengths, enc_lengths = take(5)
    wholes, outs = take(count), take(LAYER_OUTS)
    gains, residual = take(2)
    held = list(take(LAYER_OUTS - 1))
    held.insert(14, held[5])
    (hid, x_all, query, keys, values, prob, prob_own, context, ckeys, cvalues) = held[:10]
    (normal, normal_scale, normed_low, cquery, cprob, ccontext, output) = held[10:17]
    (crossed_low, activated, last_low, slope, gain_total, normal2, scale2) = held[17:24]
    states = held[24]
    land_gains, rel, pool, mains, hot_ref = take(5)
    load_sems, out_sems = take(2)
    steps, ready, arrive, plane_arrive, every_block, settle = gather_steps(
        shards, (hidden, encoder), wholes, (mains, states), nz, take(5)
    )
    tokens, width = hid.shape
    mine = 3 * local_len
    span = mains.shape[1] * local_len
    start = lax.axis_index("seq") * local_len
    emitted = []

    def leave(i):
        return pltpu.make_async_copy(held[i], outs[i], out_sems.at[i])

    def emit(*targets):
        for target in targets:
            i = next(i for i, ref in enumerate(held) if ref is target)
            leave(i).start()
            if target is not prob:
                emitted.append(leave(i))

    def emit_cross():
        leave(14).start()
        emitted.append(leave(14))

    order = list(range(1, 18))
    KEY, VALUE, QUERY, REL, CKEY, CVALUE, OUT, CQUERY, COUT, UP, DOWN = (*range(9), 9, 13)

    def slot_of(load):
        return load % SLOTS

    def load_copy(load):
        source = every_block(order[load])
        target = pool.at[slot_of(load)]
        if source.shape[2] < target.shape[2]:
            target = target.at[:, :, : source.shape[2]]
        return pltpu.make_async_copy(source, target, load_sems.at[load])

    def weight(load):
        return pool.at[slot_of(load)]

    def columns(load, cols):
        return pool[slot_of(load), :, :, cols].reshape(width, 256)

    def project(left, load, target, scale=None):
        def body(cols):
            product = mm(left[...], columns(load, cols))
            if scale is not None:
                product = product * scale
            target[:, cols] = product.astype(target.dtype)

        tiles(target.shape[1], body)

    def prepare():
        plane_arrive(0)
        plane_arrive(1)
        for r in range(rows):
            for j in range(3):
                tile = hidden[j, r]
                hid[r * mine + j * local_len : r * mine + (j + 1) * local_len] = tile
                if j:
                    to = rows * span + (2 * r + j - 1) * local_len
                    x_all[to : to + local_len] = tile
        x_all[: rows * span] = mains[...].reshape(rows * span, width)
        gain_total[...] = jnp.zeros_like(gain_total)
        hot_ref[...] = hot_forward(start, span)
        emit(hid, x_all, states)

    def take_gains():
        arrive(0)
        copy = pltpu.make_async_copy(wholes[0], land_gains, load_sems.at[len(order)])
        copy.start()
        copy.wait()
        for d in range(land_gains.shape[0]):
            gains[:, d * 128 : (d + 1) * 128] = land_gains[d].astype(jnp.float32)

    def attend(step, carry):
        r, g = step // 4, lax.rem(step, 4)
        attend_step(
            r, g, step, start, mine, span, local_len, rows, lengths, query, rel, keys, values,
            prob, prob_own, context, hot_ref[...],
        )
        return carry

    def cross(step, carry):
        r, g = step // 4, lax.rem(step, 4)
        cross_step(r, g, step, mine, span, local_len, enc_lengths, cquery, ckeys, cvalues, cprob, ccontext)
        return carry

    def out_body(cols):
        residual[:, cols] = hid[:, cols].astype(jnp.float32) + mm(context[...], columns(OUT, cols))

    def norm_body(part):
        normal[part], scale = norm_rows(residual[part])
        normal_scale[part] = jnp.broadcast_to(scale, (scale.shape[0], 128))
        normed_low[part] = (normal[part] * gains[0:1]).astype(jnp.bfloat16)

    def after_attention():
        tiles(width, out_body)
        row_tiles(tokens, norm_body)
        emit(context, normal, normal_scale, normed_low)

    def after_cross_query():
        project(normed_low, CQUERY, cquery, 0.125)
        emit(cquery)
        leave(5).wait()

    def cross_body(cols):
        residual[:, cols] = normal[:, cols] * gains[0:1, cols] + mm(ccontext[...], columns(COUT, cols))

    def cross_norm_body(part):
        normal2[part], scale = norm_rows(residual[part])
        scale2[part] = jnp.broadcast_to(scale, (scale.shape[0], 128))
        after = normal2[part] * gains[1:2]
        crossed_low[part] = after.astype(jnp.bfloat16)
        residual[part] = after

    def after_cross():
        tiles(width, cross_body)
        row_tiles(tokens, cross_norm_body)
        emit(ccontext, crossed_low, normal2, scale2)

    def up(k):
        def body(i, carry):
            cols = pl.ds(pl.multiple_of(i * 256, 256), 256)
            to = pl.ds(pl.multiple_of(k * width + i * 256, 256), 256)
            value = mm(crossed_low[...], columns(UP + k, cols))
            below = 0.5 + 0.5 * lax.erf(value * (0.5**0.5))
            activated[:, to] = (value * below).astype(jnp.bfloat16)
            density = jnp.exp(-0.5 * value * value) * (1.0 / math.sqrt(2.0 * math.pi))
            slope[:, to] = (below + value * density).astype(jnp.bfloat16)
            return carry

        lax.fori_loop(0, width // 256, body, 0)
        if k == 3:
            emit(activated, slope)

    blocks = pool.shape[1]

    def of_down(k, d):
        return d * 4 * 128 + k * 128

    def down(k):
        def body(cols):
            left = jnp.concatenate(
                [activated[:, of_down(k, d) : of_down(k, d) + 128] for d in range(blocks)], axis=1
            )
            residual[:, cols] += mm(left, columns(DOWN + k, cols))

        tiles(width, body)

    def last_norm():
        for r in range(rows):
            for j in range(3):
                part = slice(r * mine + j * local_len, r * mine + (j + 1) * local_len)
                normal3, scale = norm_rows(residual[part])
                output[j, r] = (normal3 * gains[2:3]).astype(output.dtype)
                above = cotangent[j, r].astype(jnp.float32)
                add_rows(gain_total, 2, above * normal3)
                grad = norm_back(above, normal3, scale, gains[2:3])
                residual[part] = grad
                last_low[part] = grad.astype(jnp.bfloat16)
        emit(output, last_low, gain_total)

    pieces = [("planes", 2, prepare)]
    pieces += [
        (KEY, 3, lambda: project(x_all, KEY, keys)),
        (VALUE, 3, lambda: project(x_all, VALUE, values)),
        (QUERY, 2, lambda: project(hid, QUERY, query, 0.125)),
        (REL, 1, lambda: project(hid, REL, rel)),
    ]
    half = 2
    for i in range(0, 4 * rows, half):
        pieces.append((REL, 5, lambda i=i: lax.fori_loop(i, i + half, attend, 0)))
    pieces += [
        (REL, 0, lambda: emit(query, keys, values, prob, prob_own)),
        (CKEY, 2, lambda: project_states(CKEY, ckeys)),
        (CVALUE, 2, lambda: project_states(CVALUE, cvalues)),
        (OUT, 0, take_gains),
        (OUT, 3, after_attention),
        (CQUERY, 2, after_cross_query),
    ]

    def project_states(load, target):
        def body(cols):
            left = states[...].reshape(rows * span, width)
            target[:, cols] = mm(left, columns(load, cols)).astype(target.dtype)

        tiles(width, body)
        emit(target)

    for i in range(0, 4 * rows, half):
        pieces.append((CQUERY, 3, lambda i=i: lax.fori_loop(i, i + half, cross, 0)))
    pieces += [(CQUERY, 0, emit_cross), (COUT, 3, after_cross)]
    pieces += [(UP + k, 3, functools.partial(up, k)) for k in range(4)]
    pieces += [(DOWN + k, 1, functools.partial(down, k)) for k in range(4)]
    pieces.append((DOWN + 3, 3, last_norm))

    last_use = {}
    for index, (need, _, _) in enumerate(pieces):
        last_use[need] = index
    state = {"step": 0, "load": 0}
    arrived, waited = set(), set()

    def run_to(n):
        while state["step"] < min(n, len(steps)):
            steps[state["step"]]()
            state["step"] += 1

    def free(load, done):
        return all(
            last_use[other] < done for other in range(load) if slot_of(other) == slot_of(load)
        )

    def begin_load():
        load = state["load"]
        if order[load] not in arrived:
            arrive(order[load])
            arrived.add(order[load])
        load_copy(load).start()
        state["load"] += 1

    rate = len(steps) / 130.0
    for index, (need, cost, call) in enumerate(pieces):
        if need == "planes":
            run_to(ready["planes"])
        else:
            while state["load"] <= need:
                run_to(ready[order[state["load"]]])
                begin_load()
            if need not in waited:
                waited.add(need)
                load_copy(need).wait()
        call()
        run_to(state["step"] + int(cost * rate + 0.5))
        while (
            state["load"] < len(order)
            and free(state["load"], index + 1)
            and ready[order[state["load"]]] <= state["step"]
        ):
            begin_load()
    run_to(len(steps))
    for copy in emitted:
        copy.wait()
    settle()


def layer(shards, hidden, encoder, cotangent, lengths, enc_lengths, ndp):
    nz = ndp // 2
    count = len(shards)
    low, wide = jnp.bfloat16, jnp.float32
    _, rows, local_len, width = hidden.shape
    tokens, span = 3 * rows * local_len, 4 * local_len
    every = rows * (span + 2 * local_len)
    ff = shards[-2].shape[1]
    steps = sum(max(1, w.size // (128 * 1024)) for w in shards)
    results = [
        ((tokens, width), low),
        ((every, width), low),
        ((tokens, width), low),
        ((every, width), low),
        ((every, width), low),
        ((4 * rows, 12 * local_len, span), low),
        ((tokens, width), low),
        ((tokens, width), low),
        ((rows * span, width), low),
        ((rows * span, width), low),
        ((tokens, width), wide),
        ((tokens, 128), wide),
        ((tokens, width), low),
        ((tokens, width), low),
        ((4 * rows, 12 * local_len, span), low),
        ((tokens, width), low),
        (hidden.shape, low),
        ((tokens, width), low),
        ((tokens, ff), low),
        ((tokens, width), low),
        ((tokens, ff), low),
        ((3, 8, width), wide),
        ((tokens, width), wide),
        ((tokens, 128), wide),
        ((rows, 4, local_len, width), low),
    ]
    more = [((16, width), wide), ((tokens, width), wide)]
    vmem = pl.BlockSpec(memory_space=pltpu.VMEM)
    smem = pl.BlockSpec(memory_space=pltpu.SMEM)
    anywhere = pl.BlockSpec(memory_space=pl.ANY)
    return pl.pallas_call(
        lambda *refs: layer_kernel(count, nz, rows, local_len, *refs),
        out_shape=[jax.ShapeDtypeStruct((ndp,) + w.shape, w.dtype) for w in shards]
        + [jax.ShapeDtypeStruct(*result) for result in results]
        + [jax.ShapeDtypeStruct(*result) for result in more],
        in_specs=[vmem] * (count + 3) + [smem] * 2,
        out_specs=[anywhere] * (count + len(results)) + [vmem] * 2,
        scratch_shapes=[pltpu.VMEM(*result) for i, result in enumerate(results) if i != 14]
        + [
            pltpu.VMEM((ndp,) + shards[0].shape, low),
            pltpu.VMEM((tokens, width // 2), low),
            pltpu.VMEM((SLOTS, ndp, 128, width), low),
            pltpu.VMEM((rows, 4, local_len, width), low),
            pltpu.VMEM((128, span), low),
            pltpu.SemaphoreType.DMA((18,)),
            pltpu.SemaphoreType.DMA((len(results),)),
            pltpu.SemaphoreType.DMA((steps + 2,)),
            pltpu.SemaphoreType.DMA((steps, nz, 10)),
            pltpu.SemaphoreType.DMA((steps, nz, 10)),
            pltpu.SemaphoreType.DMA((2, 4)),
            pltpu.SemaphoreType.DMA((2, 4)),
        ],
        compiler_params=pltpu.CompilerParams(
            collective_id=0, has_side_effects=True, vmem_limit_bytes=62 * 2**20
        ),
        name="layer",
    )(*shards, hidden, encoder, cotangent, lengths, enc_lengths)


RING = 5
WIDE_RING = 8


def back_kernel(plan, nz, rows, local_len, n_out, *refs):
    at = 0

    def take(n):
        nonlocal at
        at += n
        return refs[at - n : at]

    (any_activated, any_last, any_grad, any_slope, any_crossed, any_normal2, any_scale2) = take(7)
    (any_normal, any_scale, any_ccontext, any_normed, any_context, any_hid, any_x_all) = take(7)
    (any_states, any_cquery, any_ckeys, any_cvalues, any_cprob, any_query, any_keys) = take(7)
    (any_values, any_prob, any_prob_own, any_gains, any_gain_total) = take(5)
    w_down, w_up, w_cout, w_cquery, w_out, w_ckey, w_cvalue, w_key, w_value, w_query, w_rel = take(11)
    outs = take(n_out)
    gain_out, states_sum, hidden_grad = take(3)
    (activated, last_low, residual, up_back, crossed_low, normal, scale, cross_low) = take(8)
    (ccontext_back, cquery, ckeys, cvalues, prob, query, keys, values, prob_own) = take(9)
    (gains, gain_total, cquery_back, ckey_back, cvalue_back, attn_low, query_back) = take(7)
    (key_back, value_back, rel_back, main_part, states_part, pool, hot_ref, turn_ref) = take(8)
    parts, held0s, held1s, held2s, held3s = take(2), take(3), take(3), take(3), take(3)
    gain_part, share1, share2 = take(3)
    load_sems, weight_sems, out_sems, send, recv, credit0, credit1, credit2 = take(8)
    shares = (main_part, states_part)
    context_back, slope = ccontext_back, up_back
    tokens, width = residual.shape
    mine = 3 * local_len
    span = ckeys.shape[0] // rows
    start = lax.axis_index("seq") * local_len
    s, z, c, sx, sy = place()
    own = 2 * z + c
    x, y = lax.rem(s, 2), s // 2
    core = (s, 2 * z + 1 - c)
    beside_x, beside_y = (sx, own), (sy, own)

    loads = []

    def load(source, target):
        copy = pltpu.make_async_copy(source, target, load_sems.at[len(loads)])
        loads.append(copy)
        copy.start()
        return copy

    begun = [
        load(any_activated, activated),
        load(any_last, last_low),
    ]
    first_loads = list(begun)
    ffn_loads = [
        load(any_slope, slope),
        load(any_grad, residual),
        load(any_crossed, crossed_low),
        load(any_normal2, normal),
        load(any_scale2, scale),
        load(any_gains, gains),
        load(any_gain_total, gain_total),
    ]
    cross_loads = [
        load(any_cquery, cquery),
        load(any_ckeys, ckeys),
        load(any_cvalues, cvalues),
        load(any_cprob, prob),
    ]
    attend_loads = [
        load(any_query, query),
        load(any_keys, keys),
        load(any_values, values),
        load(any_prob_own, prob_own),
    ]

    def await_all(copies):
        for copy in copies:
            copy.wait()
        copies.clear()

    blocks = [w_down.at[pl.ds(width * k, width)] for k in range(4)]
    blocks += [w_up.at[:, pl.ds(width * k, width)] for k in range(4)]
    blocks += [w_cout, w_cquery, w_out, w_ckey, w_cvalue, w_key, w_value, w_query, w_rel]
    DOWN, UP, COUT, CQUERY, OUT, CKEY, CVALUE, KEY, VALUE, QUERY, REL = (0, 4, *range(8, 17))

    def block_copy(i):
        target = pool.at[i % 2]
        if blocks[i].shape[1] < width:
            target = target.at[:, pl.ds(0, blocks[i].shape[1])]
        return pltpu.make_async_copy(blocks[i], target, weight_sems.at[i])

    started = []

    def need(i):
        while len(started) <= i:
            block_copy(len(started)).start()
            started.append(True)
        block_copy(i).wait()

    def release(i):
        if i + 2 < len(blocks) and len(started) <= i + 2:
            while len(started) <= i + 2:
                block_copy(len(started)).start()
                started.append(True)

    block_copy(0).start()
    block_copy(1).start()
    started += [True, True]
    greet(nz)
    gain_part[...] = jnp.zeros_like(gain_part)

    held = {}

    def buffers(k):
        kind, slot = plan[k][:2]
        if kind == 3:
            share = shares[slot // 2].at[:, :, slot % 2]
            return None, share, share1.at[slot], share2.at[slot], None
        if kind == 2:
            return (gain_part,) + tuple(h[2].at[0] for h in (held0s, held1s, held2s, held3s))
        ring = WIDE_RING if kind == 0 else held1s[1].shape[0]
        return (
            parts[kind].at[slot % 2],
            held0s[kind].at[slot % RING],
            held1s[kind].at[slot % ring],
            held2s[kind].at[slot % ring],
            held3s[kind].at[slot],
        )

    slots_of = [sum(p[0] == kind for p in plan) for kind in range(4)]

    def core_copy(k):
        part, held0 = buffers(k)[:2]
        return remote(part.at[:, :, :, 1 - c], held0, send.at[k, 0], recv.at[k, 0], core)

    def first_copy(k):
        _, held0, held1 = buffers(k)[:3]
        if k % 2 == 0:
            return remote(held0.at[:, 1 - x], held1, send.at[k, 1], recv.at[k, 1], beside_x)
        return remote(held0.at[1 - y], held1, send.at[k, 1], recv.at[k, 1], beside_y)

    def second_copy(k):
        held1, held2 = buffers(k)[2:4]
        if k % 2 == 0:
            return remote(held1.at[1 - y], held2, send.at[k, 2], recv.at[k, 2], beside_y)
        return remote(held1.at[1 - x], held2, send.at[k, 2], recv.at[k, 2], beside_x)

    def z_copy(k, dz):
        held2, held3 = buffers(k)[3:5]
        zt = lax.rem(z + dz, nz)
        return remote(
            held2.at[zt], held3.at[dz - 1], send.at[k, 2 + dz], recv.at[k, 2 + dz], (s, 2 * zt + c)
        )

    def grant(semaphore, to):
        pl.semaphore_signal(semaphore, inc=1, device_id=to, device_id_type=MESH)

    def added(held, mine):
        held[...] = (held[...].astype(jnp.float32) + mine.astype(jnp.float32)).astype(held.dtype)

    half = rows * span // 2
    whole_rows = (0, tokens)

    def segments(pair, i):
        cols = pl.ds(256 * i, 256)
        if pair == 0:
            return [(activated[:, cols], whole_rows)]
        if pair == 1:
            return [(crossed_low[:, cols], whole_rows)]
        if pair <= 6:
            column = width * min(pair - 2, 3) + 256 * i
            return [(activated[:, pl.ds(column, 256)], whole_rows)]
        if pair <= 8:
            return [
                (up_back[:, pl.ds(width * n + 256 * i, 256)], (tokens * n, tokens)) for n in range(2)
            ]
        return [
            (up_back[:half, pl.ds(width * (2 + n) + 256 * i, 256)], (half * n, half))
            for n in range(2)
        ]

    rights = (
        last_low, up_back, cross_low, cquery_back, attn_low, query_back, rel_back,
        key_back, value_back, ckey_back, cvalue_back,
    )
    late_loads = []

    def reload():
        for n, source in enumerate((any_ccontext, any_normed, any_context, any_hid)):
            late_loads.append(load(source, activated.at[:, pl.ds(width * n, width)]))
        for n in range(2):
            late_loads.append(
                load(any_x_all.at[pl.ds(tokens * n, tokens)], up_back.at[:, pl.ds(width * n, width)])
            )
            late_loads.append(
                load(
                    any_states.at[pl.ds(half * n, half)],
                    up_back.at[pl.ds(0, half), pl.ds(width * (2 + n), width)],
                )
            )

    before, recent = {}, {}
    for k, entry in enumerate(plan):
        before[k] = recent.get((entry[0], entry[1] - 2))
        recent[entry[:2]] = k
    followed = set(v for v in before.values() if v is not None)
    pairs_before = max(k for k, entry in enumerate(plan) if entry[0] < 2 and entry[2] < 2)

    def make(k):
        kind, slot, pair, col, wide = plan[k]
        if kind == 3:
            return
        if kind < 2:
            part = buffers(k)[0]
            block = part.shape[4]
            if pair == 0:
                await_all(first_loads)
            if pair >= 2:
                await_all(late_loads)
            if slot >= 2:
                core_copy(before[k]).wait_send()
            group = 256 // block
            for i in range(part.shape[0] * part.shape[1] * nz * 2 * block // 256):
                product = 0.0
                for left, (row, height) in segments(pair, i):
                    right = rights[pair][row : row + height, col : col + wide]
                    product = product + mm_grad(left, right)
                i_s, rest = divmod(i * group, 2 * nz)
                zs = rest // 2
                part[i_s // 2, i_s % 2, zs : zs + group // 2] = product.reshape(
                    group // 2, 2, block, wide
                ).astype(part.dtype)
            if k == pairs_before:
                reload()
            if slot >= RING:
                pl.semaphore_wait(credit0.at[kind], 1)
        else:
            lanes = width // (8 * nz)
            totals = jnp.concatenate(
                [jnp.sum(gain_total[g], axis=0, keepdims=True) for g in range(3)], axis=0
            )
            for b in range(8 * nz):
                i_s, rest = divmod(b, 2 * nz)
                gain_part[i_s // 2, i_s % 2, rest // 2, rest % 2, 0:3, 0:lanes] = totals[
                    :, b * lanes : (b + 1) * lanes
                ]
        core_copy(k).start()

    def after_core(k):
        part, held0 = buffers(k)[:2]
        kind, slot = plan[k][:2]
        if kind < 3:
            core_copy(k).wait_recv()
            added(held0, part[:, :, :, c])
        if kind == 0 and slot >= WIDE_RING:
            pl.semaphore_wait(credit1.at[k % 2], 1)
        first_copy(k).start()

    def after_first(k):
        _, held0, held1 = buffers(k)[:3]
        kind, slot = plan[k][:2]
        first_copy(k).wait_recv()
        added(held1, held0[:, x] if k % 2 == 0 else held0[y])
        if kind == 0 and slot >= WIDE_RING:
            pl.semaphore_wait(credit2.at[k % 2], 1)
        second_copy(k).start()
        first_copy(k).wait_send()
        if kind < 2 and slot + RING < slots_of[kind]:
            grant(credit0.at[kind], core)

    def after_second(k):
        held1, held2 = buffers(k)[2:4]
        kind, slot = plan[k][:2]
        second_copy(k).wait_recv()
        mine_part = held1[y] if k % 2 == 0 else held1[x]
        if kind == 3:
            total = held2[...].astype(jnp.float32) + mine_part.astype(jnp.float32)
            r = slot % 2
            if slot < 2:
                residual[r * mine : r * mine + local_len] += total
                hidden_copy(0, r).start()
            else:
                states_sum[r] = total
            return
        added(held2, mine_part)
        for dz in range(1, nz):
            z_copy(k, dz).start()
        second_copy(k).wait_send()
        if kind == 0 and slot + WIDE_RING < slots_of[kind]:
            grant(credit1.at[k % 2], beside_x if k % 2 == 0 else beside_y)

    def finish_chunk(k):
        kind, slot, pair, col, wide = plan[k]
        if kind == 3:
            return
        held2, held3 = buffers(k)[3:5]
        total = held2[z].astype(jnp.float32)
        for dz in range(1, nz):
            z_copy(k, dz).wait_recv()
            total = total + held3[dz - 1].astype(jnp.float32)
        if kind == 2:
            gain_out[...] = total
        else:
            outs[pair][:, col : col + wide] = total
        for dz in range(1, nz):
            z_copy(k, dz).wait_send()
        if kind == 0 and slot + WIDE_RING < slots_of[kind]:
            grant(credit2.at[k % 2], beside_y if k % 2 == 0 else beside_x)

    count = len(plan)
    total_ticks = count + 7

    def tick(t):
        if t >= 7:
            finish_chunk(t - 7)
        if 5 <= t < count + 5:
            after_second(t - 5)
        if 3 <= t < count + 3:
            after_first(t - 3)
        if t < count:
            make(t)
        if 1 <= t < count + 1:
            after_core(t - 1)

    def fours(body):
        def step(i, carry):
            body(pl.ds(pl.multiple_of(i * 256, 256), 256))
            return carry

        lax.fori_loop(0, width // 256, step, 0)

    def down_back(k):
        need(DOWN + k)
        if k == 0:
            await_all(ffn_loads)
        place_of = (DOWN + k) % 2

        def body(i, carry):
            to = pl.ds(pl.multiple_of(k * width + i * 256, 256), 256)
            product = mm_back(last_low[...], pool[place_of, pl.ds(pl.multiple_of(i * 256, 256), 256)])
            up_back[:, to] = (product * slope[:, to].astype(jnp.float32)).astype(jnp.bfloat16)
            return carry

        lax.fori_loop(0, width // 256, body, 0)
        release(DOWN + k)

    def up_again(k):
        need(UP + k)

        def body(cols):
            residual[:, cols] += mm_back(
                up_back[:, k * width : (k + 1) * width], pool[(UP + k) % 2, cols]
            )

        fours(body)
        release(UP + k)

    def cross_norm_back(part):
        above = residual[part]
        add_rows(gain_total, 1, above * normal[part])
        grad = norm_back(above, normal[part], scale[part][:, 0:1], gains[1:2])
        residual[part] = grad
        cross_low[part] = grad.astype(jnp.bfloat16)

    norm_loads = []

    def cout_back():
        row_tiles(tokens, cross_norm_back)
        norm_loads.append(load(any_normal, normal))
        norm_loads.append(load(any_scale, scale))
        need(COUT)

        def body(cols):
            ccontext_back[:, cols] = mm_back(cross_low[...], pool[COUT % 2, cols]).astype(
                jnp.bfloat16
            )

        fours(body)
        release(COUT)

    def cross(first, last):
        await_all(cross_loads)

        def step(i, carry):
            cross_back_step(
                i // 4, lax.rem(i, 4), i, mine, span, local_len, ccontext_back, cvalues, prob,
                ckeys, cquery, cquery_back, ckey_back, cvalue_back,
            )
            return carry

        lax.fori_loop(first, last, step, 0)
        if last == 4 * rows:
            attend_loads.append(load(any_prob, prob))

    def attn_norm_back(part):
        above = residual[part]
        add_rows(gain_total, 0, above * normal[part])
        grad = norm_back(above, normal[part], scale[part][:, 0:1], gains[0:1])
        residual[part] = grad
        attn_low[part] = grad.astype(jnp.bfloat16)

    def cquery_again():
        need(CQUERY)

        def body(cols):
            residual[:, cols] += mm_back(cquery_back[...], pool[CQUERY % 2, cols])

        fours(body)
        release(CQUERY)
        await_all(norm_loads)
        row_tiles(tokens, attn_norm_back)

    def out_back():
        need(OUT)

        def body(cols):
            context_back[:, cols] = mm_back(attn_low[...], pool[OUT % 2, cols]).astype(jnp.bfloat16)

        fours(body)
        release(OUT)
        hot_ref[...] = hot_backward(start, span)
        turn_ref[...] = turning(span)

    def attend(first, last):
        await_all(attend_loads)

        def step(i, carry):
            attend_back_step(
                i // 4, lax.rem(i, 4), i, mine, span, local_len, rows, context_back, query, keys,
                values, prob, prob_own, query_back, key_back, value_back, rel_back,
                hot_ref[...], turn_ref[...],
            )
            return carry

        lax.fori_loop(first, last, step, 0)

    def into(share, total, cols):
        total = total.astype(jnp.bfloat16)
        for r in range(rows):
            for p in range(4):
                row = r * span + p * local_len
                share[p // 2, p % 2, r, :, cols] = total[row : row + local_len]

    def states_back():
        need(CKEY)
        need(CVALUE)

        def body(cols):
            total = mm_back(ckey_back[...], pool[CKEY % 2, cols])
            into(states_part, total + mm_back(cvalue_back[...], pool[CVALUE % 2, cols]), cols)

        fours(body)
        release(CKEY)
        release(CVALUE)

    def keys_again():
        need(KEY)
        need(VALUE)

        def body(cols):
            total = mm_back(key_back[...], pool[KEY % 2, cols])
            total = total + mm_back(value_back[...], pool[VALUE % 2, cols])
            into(main_part, total[: rows * span], cols)
            for r in range(rows):
                to = r * mine + local_len
                row = rows * span + 2 * r * local_len
                residual[to : to + 2 * local_len, cols] += total[row : row + 2 * local_len]

        fours(body)
        release(KEY)
        release(VALUE)

    def hidden_copy(j, r):
        row = r * mine + j * local_len
        return pltpu.make_async_copy(
            residual.at[pl.ds(row, local_len)], hidden_grad.at[j, r], out_sems.at[j, r]
        )

    def query_again():
        need(QUERY)
        need(REL)
        deep = rel_back.shape[1]

        def body(cols):
            total = mm_back(query_back[...], pool[QUERY % 2, cols])
            residual[:, cols] += total + mm_back(rel_back[...], pool[REL % 2, cols, :deep])

        fours(body)
        for r in range(rows):
            for j in (1, 2):
                hidden_copy(j, r).start()

    ends = {}
    for k, entry in enumerate(plan):
        ends[entry[2] if entry[0] < 2 else 10 + entry[0]] = k + 1
    steps_of = range(0, 4 * rows, 2)
    pieces = [(1, functools.partial(down_back, k), ends[0]) for k in range(4)]
    pieces += [(1, functools.partial(up_again, k), ends[1] - 1) for k in range(4)]
    pieces.append((3, cout_back, ends[2]))
    pieces += [(4, functools.partial(cross, i, i + 2), ends[2]) for i in steps_of]
    pieces[-1] = pieces[-1][:2] + (ends[10],)
    pieces.append((2, cquery_again, ends[4]))
    pieces.append((1, out_back, ends[4]))
    pieces += [(5, functools.partial(attend, i, i + 2), ends[4]) for i in steps_of]
    pieces.append((3, states_back, ends[8]))
    pieces.append((5, keys_again, ends[8]))
    pieces.append((2, query_again, count))
    done = {"tick": 0, "spent": 0.0}

    def ticks_to(limit, wanted):
        while done["tick"] < min(limit, wanted):
            tick(done["tick"])
            done["tick"] += 1

    tick(0)
    done["tick"] = 1
    for cost, call, limit in pieces:
        call()
        done["spent"] += cost
        ticks_to(limit, 1 + int(done["spent"] / 3.5))
    ticks_to(total_ticks, total_ticks)
    for k in range(count):
        if plan[k][0] < 3 and k not in followed:
            core_copy(k).wait_send()
        if plan[k][0] == 3:
            second_copy(k).wait_send()
    for j in range(3):
        for r in range(rows):
            hidden_copy(j, r).wait()


def back(values, weights, shape, ndp):
    nz = ndp // 2
    low, wide = jnp.bfloat16, jnp.float32
    rows, local_len, width = shape[1:]
    tokens, span = 3 * rows * local_len, 4 * local_len
    every = rows * (span + 2 * local_len)
    ff = weights[0].shape[0]
    ndev = 8 * nz
    heights = [ff, width, width, width, width, width, width, width, width, width, width]
    wides = [width, ff, width, width, width, width, width // 2, width, width, width, width]
    plan, slots = [], [0, 0]
    for pair in (0, 1, 2, 3, 9, 10, 4, 5, 6, 7, 8):
        kind = int(heights[pair] > width)
        step = (512, 128)[kind]
        for col in range(0, wides[pair], step):
            plan.append((kind, slots[kind], pair, col, step))
            slots[kind] += 1
    plan += [(3, i, 0, 0, 0) for i in range(4)] + [(2, 0, 0, 0, 128)]
    n = len(plan)
    tails = [((width // ndev, 512), low), ((ff // ndev, 128), low), ((8, 128), wide)]
    counts = [
        (RING, WIDE_RING, WIDE_RING, slots[0]),
        (RING, slots[1], slots[1], slots[1]),
        (1, 1, 1, 1),
    ]
    leads = [(2, 2, nz), (2, nz), (nz,), (nz - 1,)]
    held = [
        pltpu.VMEM((counts[kind][stage],) + leads[stage] + tails[kind][0], tails[kind][1])
        for stage in range(4)
        for kind in range(3)
    ]
    parts = [pltpu.VMEM((2, 2, 2, nz, 2) + tails[kind][0], low) for kind in range(2)]
    share = (local_len, width)
    main = pltpu.VMEM((rows * span, width), low)
    token = pltpu.VMEM((tokens, width), low)
    fat = pltpu.VMEM((tokens, ff), low)
    all_rows = pltpu.VMEM((every, width), low)
    token_wide = pltpu.VMEM((tokens, width), wide)
    scratch = [fat, token, token_wide, fat, token, token_wide]
    scratch += [pltpu.VMEM((tokens, 128), wide), token, token, token, main, main]
    scratch += [pltpu.VMEM((4 * rows, 12 * local_len, span), low), token, all_rows, all_rows, token]
    scratch += [pltpu.VMEM((16, width), wide), pltpu.VMEM((3, 8, width), wide), token, main, main]
    scratch += [token, token, all_rows, all_rows, pltpu.VMEM((tokens, width // 2), low)]
    scratch += [pltpu.VMEM((2, 2, rows) + share, low)] * 2
    scratch += [pltpu.VMEM((2, width, width), low)]
    scratch += [pltpu.VMEM((span, 128), low), pltpu.VMEM((span, span), low)]
    scratch += parts + held
    scratch += [pltpu.VMEM((2, 2, nz, 2, 8, 128), wide)]
    scratch += [pltpu.VMEM((4, 2) + share, low), pltpu.VMEM((4,) + share, low)]
    scratch += [
        pltpu.SemaphoreType.DMA((32,)),
        pltpu.SemaphoreType.DMA((17,)),
        pltpu.SemaphoreType.DMA((3, rows)),
        pltpu.SemaphoreType.DMA((n, 2 + nz)),
        pltpu.SemaphoreType.DMA((n, 2 + nz)),
        pltpu.SemaphoreType.REGULAR((2,)),
        pltpu.SemaphoreType.REGULAR((2,)),
        pltpu.SemaphoreType.REGULAR((2,)),
    ]
    anywhere = pl.BlockSpec(memory_space=pl.ANY)
    vmem = pl.BlockSpec(memory_space=pltpu.VMEM)
    outs = [jax.ShapeDtypeStruct((h // ndev, w), wide) for h, w in zip(heights, wides)]
    outs.append(jax.ShapeDtypeStruct((8, 128), wide))
    outs.append(jax.ShapeDtypeStruct((rows,) + share, wide))
    outs.append(jax.ShapeDtypeStruct(shape, wide))
    return pl.pallas_call(
        lambda *refs: back_kernel(plan, nz, rows, local_len, len(heights), *refs),
        out_shape=outs,
        in_specs=[anywhere] * (len(values) + len(weights)),
        out_specs=[vmem] * (len(outs) - 1) + [anywhere],
        scratch_shapes=scratch,
        compiler_params=pltpu.CompilerParams(
            collective_id=1, has_side_effects=True, vmem_limit_bytes=62 * 2**20
        ),
        name="back",
    )(*values, *weights)


def finish_kernel(count, *refs):
    sems = refs[2 * count]
    copies = [
        pltpu.make_async_copy(refs[i], refs[count + i], sems.at[i]) for i in range(count)
    ]
    for copy in copies:
        copy.start()
    for copy in copies:
        copy.wait()


def finish(sums, hidden_grad, states_sum):
    arrays = (*sums, hidden_grad, states_sum)
    count = len(arrays)
    return pl.pallas_call(
        lambda *refs: finish_kernel(count, *refs),
        out_shape=[jax.ShapeDtypeStruct(a.shape, a.dtype) for a in arrays],
        in_specs=[pl.BlockSpec(memory_space=pltpu.VMEM)] * count,
        out_specs=[pl.BlockSpec(memory_space=pl.ANY)] * count,
        scratch_shapes=[pltpu.SemaphoreType.DMA((count,))],
        compiler_params=pltpu.CompilerParams(vmem_limit_bytes=62 * 2**20),
        name="finish",
    )(*arrays)


def plain_call(kernel, name, ins, spaces, outs, scratch, flops):
    space = {"v": pltpu.VMEM, "s": pltpu.SMEM, "a": pl.ANY}
    out_shape = [jax.ShapeDtypeStruct(shape, kind) for shape, kind in outs]
    moved = sum(a.size * a.dtype.itemsize for a in list(ins) + out_shape)
    return pl.pallas_call(
        kernel,
        out_shape=out_shape,
        in_specs=[pl.BlockSpec(memory_space=space[p]) for p in spaces],
        out_specs=[pl.BlockSpec(memory_space=pltpu.VMEM)] * len(outs),
        scratch_shapes=scratch,
        compiler_params=pltpu.CompilerParams(vmem_limit_bytes=62 * 2**20),
        cost_estimate=pl.CostEstimate(flops=flops, bytes_accessed=moved, transcendentals=0),
        name=name,
    )(*ins)


def copies_of(arrays):
    return [pltpu.VMEM(a.shape, a.dtype) for a in arrays] + [
        pltpu.SemaphoreType.DMA((len(arrays),))
    ]


def local(
    hidden,
    encoder,
    lengths,
    enc_lengths,
    w_query,
    w_key,
    w_value,
    w_attn_out,
    w_relative,
    w_cross_query,
    w_cross_key,
    w_cross_value,
    w_cross_out,
    w_up,
    w_down,
    gain_attn,
    gain_cross,
    gain_ffn,
    cotangent,
):
    ndp, chips = lax.axis_size("dp"), lax.axis_size("seq")
    devices = ndp * chips
    low, wide = jnp.bfloat16, jnp.float32
    _, rows, local_len, width = hidden.shape
    span, tokens = local_len * chips, 3 * rows * local_len
    weights = (
        w_key,
        w_value,
        w_query,
        w_relative,
        w_cross_key,
        w_cross_value,
        w_attn_out,
        w_cross_query,
        w_cross_out,
        w_up,
        w_down,
    )
    gains = jnp.stack([gain_attn, gain_cross, gain_ffn])
    every = rows * (span + 2 * local_len)
    kernels = chips == 4 and w_query.shape[0] == 128 and w_down.shape[0] == 512
    if kernels:
        gains = jnp.pad(gains, ((0, 13), (0, 0)))
        results = layer(
            (gains,) + weights, hidden, encoder, cotangent, lengths, enc_lengths, ndp
        )
        whole, results = results[1 : len(weights) + 1], results[len(weights) + 1 :]
        whole = [w.reshape(-1, w.shape[-1]) for w in whole]
        (hid, x_all, query, keys, values, prob, prob_own, context, ckeys, cvalues) = results[:10]
        (normal, normal_scale, normed_low, cquery, cprob, ccontext, output) = results[10:17]
        (crossed_low, activated, last_low, slope, gain_total, normal2, scale2) = results[17:24]
        (states, gains, grad) = results[24:]
        states = states.reshape(-1, width)
    else:
        gains = jnp.pad(gains, ((0, 5), (0, 0)))
        whole = [lax.all_gather(w, "dp", axis=0, tiled=True) for w in weights]
        gains = lax.all_gather(gains, "dp", axis=1, tiled=True).astype(wide)
        mains = lax.all_gather(hidden[0], "seq", axis=1).reshape(-1, width)
        states = lax.all_gather(encoder, "seq", axis=1).reshape(-1, width)
    (
        full_key,
        full_value,
        full_query,
        full_relative,
        full_ckey,
        full_cvalue,
        full_attn_out,
        full_cquery,
        full_cout,
        full_up,
        full_down,
    ) = whole
    if not kernels:
        ff = full_up.shape[1]
        fetched = (
            full_key,
            full_value,
            full_query,
            full_relative,
            full_ckey,
            full_cvalue,
            full_attn_out,
            full_cquery,
        )
        (
            hid,
            x_all,
            query,
            keys,
            values,
            prob,
            prob_own,
            context,
            ckeys,
            cvalues,
            normal,
            normal_scale,
            normed_low,
            cquery,
            cprob,
            ccontext,
        ) = plain_call(
            lambda *refs: forward_kernel(rows, local_len, *refs),
            "forward_attention",
            (hidden, mains, states, lengths, enc_lengths, gains) + fetched,
            "vvvssv" + "a" * len(fetched),
            [
                ((tokens, width), low),
                ((every, width), low),
                ((tokens, width), low),
                ((every, width), low),
                ((every, width), low),
                ((4 * rows, 12 * local_len, span), low),
                ((tokens, width), low),
                ((tokens, width), low),
                ((rows * span, width), low),
                ((rows * span, width), low),
                ((tokens, width), wide),
                ((tokens, 128), wide),
                ((tokens, width), low),
                ((tokens, width), low),
                ((4 * rows, 12 * local_len, span), low),
                ((tokens, width), low),
            ],
            [
                pltpu.VMEM((tokens, full_relative.shape[1]), low),
                pltpu.VMEM((tokens, width), wide),
            ]
            + copies_of(fetched),
            12 * 10**9,
        )
        fetched = (full_cout, full_up, full_down)
        (
            output,
            crossed_low,
            activated,
            last_low,
            up_back,
            cross_grad,
            cross_low,
            ccontext_back,
            gain_middle,
        ) = plain_call(
            lambda *refs: middle_kernel(rows, local_len, *refs),
            "feed_forward",
            (normal, ccontext, gains, cotangent) + fetched,
            "vvvv" + "a" * len(fetched),
            [
                (hidden.shape, low),
                ((tokens, width), low),
                ((tokens, ff), low),
                ((tokens, width), low),
                ((tokens, ff), low),
                ((tokens, width), wide),
                ((tokens, width), low),
                ((tokens, width), low),
                ((3, 8, width), wide),
            ],
            [
                pltpu.VMEM((tokens, width), wide),
                pltpu.VMEM((tokens, 128), wide),
                pltpu.VMEM((tokens, ff), low),
                pltpu.VMEM((tokens, width), wide),
            ]
            + copies_of(fetched),
            14 * 10**9,
        )
    if kernels:
        values_in = (
            activated, last_low, grad, slope, crossed_low, normal2, scale2, normal, normal_scale,
            ccontext, normed_low, context, hid, x_all, states, cquery, ckeys, cvalues, cprob,
            query, keys, values, prob, prob_own, gains, gain_total,
        )
        weights_in = (
            full_down, full_up, full_cout, full_cquery, full_attn_out, full_ckey, full_cvalue,
            full_key, full_value, full_query, full_relative,
        )
        *sums, gain_sums, states_sum, hidden_grad = back(values_in, weights_in, hidden.shape, ndp)
        gain_sums = gain_sums[:3, : width // devices]
        *sums, output, hidden_grad, states_sum = finish(sums + [output], hidden_grad, states_sum)
    else:
        fetched = (
            full_cquery,
            full_attn_out,
            full_ckey,
            full_cvalue,
            full_query,
            full_relative,
            full_key,
            full_value,
        )
        (
            cquery_back,
            ckey_back,
            cvalue_back,
            attn_low,
            query_back,
            key_back,
            value_back,
            rel_back,
            hidden_own,
            main_part,
            states_part,
            gain_back,
        ) = plain_call(
            lambda *refs: backward_kernel(rows, local_len, *refs),
            "backward_attention",
            (
                ccontext_back,
                cross_grad,
                cquery,
                ckeys,
                cvalues,
                cprob,
                normal,
                normal_scale,
                gains,
                query,
                keys,
                values,
                prob,
                prob_own,
            )
            + fetched,
            "v" * 14 + "a" * len(fetched),
            [
                ((tokens, width), low),
                ((rows * span, width), low),
                ((rows * span, width), low),
                ((tokens, width), low),
                ((tokens, width), low),
                ((every, width), low),
                ((every, width), low),
                ((tokens, full_relative.shape[1]), low),
                (hidden.shape, wide),
                ((chips, rows, local_len, width), low),
                ((chips, rows, local_len, width), low),
                ((3, 8, width), wide),
            ],
            [pltpu.VMEM((tokens, width), wide), pltpu.VMEM((tokens, width), low)] + copies_of(fetched),
            14 * 10**9,
        )
        xs = [activated, crossed_low, ccontext, normed_low, context, hid, x_all, states]
        gs = [
            last_low,
            up_back,
            cross_low,
            cquery_back,
            attn_low,
            query_back,
            rel_back,
            key_back,
            value_back,
            ckey_back,
            cvalue_back,
        ]
        pairs = [(0, 0), (1, 1), (2, 2), (3, 3), (4, 4), (5, 5), (5, 6), (6, 7), (6, 8), (7, 9), (7, 10)]
        gain_parts = jnp.sum(gain_middle + gain_back, axis=1)
        sums = [
            lax.psum_scatter(
                weight_grad(xs[i], gs[j]), ("seq", "dp"), scatter_dimension=0, tiled=True
            )
            for i, j in pairs
        ]
        gain_sums = lax.psum_scatter(gain_parts, ("seq", "dp"), scatter_dimension=1, tiled=True)
        main_sum, states_sum = (
            lax.psum_scatter(part, "seq", scatter_dimension=0).astype(wide)
            for part in (main_part, states_part)
        )
        hidden_grad = hidden_own.at[0].add(main_sum)
    gainattn_sum, gaincross_sum, gainffn_sum = gain_sums
    (
        down_sum,
        up_sum,
        cout_sum,
        cquery_sum,
        outproj_sum,
        query_sum,
        relative_sum,
        keyw_sum,
        valuew_sum,
        ckey_sum,
        cvalue_sum,
    ) = sums
    return (
        output,
        hidden_grad,
        states_sum,
        query_sum,
        keyw_sum,
        valuew_sum,
        outproj_sum,
        relative_sum,
        cquery_sum,
        ckey_sum,
        cvalue_sum,
        cout_sum,
        up_sum,
        down_sum,
        gainattn_sum,
        gaincross_sum,
        gainffn_sum,
    )


def solution(mesh):
    in_specs = (
        P(None, "dp", "seq", None),
        P("dp", "seq", None),
        P("dp"),
        P("dp"),
        P("dp", None),
        P("dp", None),
        P("dp", None),
        P("dp", None),
        P("dp", None),
        P("dp", None),
        P("dp", None),
        P("dp", None),
        P("dp", None),
        P("dp", None),
        P("dp", None),
        P("dp"),
        P("dp"),
        P("dp"),
        P(None, "dp", "seq", None),
    )
    out_specs = (
        P(None, "dp", "seq", None),
        P(None, "dp", "seq", None),
        P("dp", "seq", None),
        P(("seq", "dp"), None),
        P(("seq", "dp"), None),
        P(("seq", "dp"), None),
        P(("seq", "dp"), None),
        P(("seq", "dp"), None),
        P(("seq", "dp"), None),
        P(("seq", "dp"), None),
        P(("seq", "dp"), None),
        P(("seq", "dp"), None),
        P(("seq", "dp"), None),
        P(("seq", "dp"), None),
        P(("seq", "dp")),
        P(("seq", "dp")),
        P(("seq", "dp")),
    )
    return jax.shard_map(local, mesh=mesh, in_specs=in_specs, out_specs=out_specs, check_vma=False)
```

```python
import functools
import math

import jax
import jax.numpy as jnp
from jax import lax
from jax.experimental import pallas as pl
from jax.experimental.pallas import tpu as pltpu
from jax.sharding import PartitionSpec as P

MESH = pl.DeviceIdType.MESH

HEADS = 16
HEAD_DIM = 64
BUCKETS = 32


eps_norm = 1e-05
bucket_edges = [step_index for step_index in range(1, 16)] + [
    int(math.ceil(16 * 8 ** ((step_index - 16) / 16))) for step_index in range(16, 32)
]


def flatten_rows(array):
    return array.reshape(-1, array.shape[-1])


def weight_grad(array, grad_rows):
    return jnp.einsum(
        "nd,ne->de",
        flatten_rows(array),
        flatten_rows(grad_rows),
        preferred_element_type=jnp.float32,
    )


def remote(src, dst, send, recv, to):
    return pltpu.make_async_remote_copy(
        src_ref=src, dst_ref=dst, send_sem=send, recv_sem=recv, device_id=to, device_id_type=MESH
    )


def place():
    s = lax.axis_index("seq")
    d = lax.axis_index("dp")
    z, c = d // 2, lax.rem(d, 2)
    sx = s + 1 - 2 * lax.rem(s, 2)
    sy = lax.rem(s + 2, 4)
    return s, z, c, sx, sy


def greet(nz):
    s, z, c, sx, sy = place()
    barrier = pltpu.get_barrier_semaphore()
    dests = [(s, 2 * z + 1 - c), (sx, 2 * z + c), (sy, 2 * z + c)]
    for dz in range(1, nz):
        dests.append((s, 2 * lax.rem(z + dz, nz) + c))
    for dest in dests:
        pl.semaphore_signal(barrier, inc=1, device_id=dest, device_id_type=MESH)
    pl.semaphore_wait(barrier, len(dests))


NEG = -1000000000.0


def mm(left, right):
    return jnp.dot(left, right, preferred_element_type=jnp.float32)


def mm_back(left, right):
    return lax.dot_general(
        left, right, (((1,), (1,)), ((), ())), preferred_element_type=jnp.float32
    )


def mm_grad(left, right):
    return lax.dot_general(
        left, right, (((0,), (0,)), ((), ())), preferred_element_type=jnp.float32
    )


def tiles(width, body):
    def step(i, carry):
        body(pl.ds(pl.multiple_of(i * 256, 256), 256))
        return carry

    lax.fori_loop(0, width // 256, step, 0)


def row_tiles(rows, body, step_rows=64):
    def step(i, carry):
        body(pl.ds(pl.multiple_of(i * step_rows, step_rows), step_rows))
        return carry

    lax.fori_loop(0, rows // step_rows, step, 0)


def heads_in(tile):
    lane = lax.broadcasted_iota(jnp.int32, tile.shape, 1) // (tile.shape[1] // 4)
    return jnp.concatenate(
        [jnp.where(lane == h, tile, jnp.zeros_like(tile)) for h in range(4)], axis=0
    )


def heads_out(stacked):
    n, wide = stacked.shape[0] // 4, stacked.shape[1]
    lane = lax.broadcasted_iota(jnp.int32, (n, wide), 1) // (wide // 4)
    result = stacked[3 * n :]
    for h in (2, 1, 0):
        result = jnp.where(lane == h, stacked[h * n : (h + 1) * n], result)
    return result


def head_lanes(columns, wide):
    n = columns[0].shape[0]
    lane = lax.broadcasted_iota(jnp.int32, (n, wide), 1) // (wide // 4)
    result = jnp.broadcast_to(columns[3], (n, wide))
    for h in (2, 1, 0):
        result = jnp.where(lane == h, jnp.broadcast_to(columns[h], (n, wide)), result)
    return result


def head_sums(product):
    n, wide = product.shape
    lane = lax.broadcasted_iota(jnp.int32, (n, wide), 1) // (wide // 4)
    return [
        jnp.sum(jnp.where(lane == h, product, 0.0), axis=1, keepdims=True) for h in range(4)
    ]


def bucket_of(distance):
    total = jnp.zeros_like(distance)
    for edge in bucket_edges:
        total = total + (distance >= edge).astype(jnp.int32)
    return total


def hot_forward(start, span):
    lag = lax.broadcasted_iota(jnp.int32, (128, span), 1)
    row = lax.rem(lax.broadcasted_iota(jnp.int32, (128, span), 0), BUCKETS)
    distance = lax.rem(start - lag + span, span)
    return jnp.where(bucket_of(distance) == row, 1.0, 0.0).astype(jnp.bfloat16)


def hot_backward(start, span):
    lag = lax.broadcasted_iota(jnp.int32, (span, 128), 0)
    column = lax.rem(lax.broadcasted_iota(jnp.int32, (span, 128), 1), BUCKETS)
    distance = lax.rem(start + lag + 1, span)
    return jnp.where(bucket_of(distance) == column, 1.0, 0.0).astype(jnp.bfloat16)


def skewed(array, block):
    return jnp.concatenate(
        [
            pltpu.roll(array[i : i + block], 0, 1, stride=1, stride_axis=0)
            for i in range(0, array.shape[0], block)
        ],
        axis=0,
    )


def norm_rows(values):
    centred = values - jnp.mean(values, axis=1, keepdims=True)
    scale = lax.rsqrt(jnp.mean(centred * centred, axis=1, keepdims=True) + eps_norm)
    return centred * scale, scale


def norm_back(grad, normal, scale, gain):
    grad = grad * gain
    return scale * (
        grad
        - jnp.mean(grad, axis=1, keepdims=True)
        - normal * jnp.mean(grad * normal, axis=1, keepdims=True)
    )


def add_rows(total_ref, index, product):
    total_ref[index] += jnp.sum(product.reshape(-1, 8, product.shape[1]), axis=0)


class Fetch:
    def __init__(self, sources, targets, sems):
        self.copies = [
            pltpu.make_async_copy(src, dst, sems.at[i])
            for i, (src, dst) in enumerate(zip(sources, targets))
        ]
        self.targets = targets
        self.waited = set()
        for copy in self.copies:
            copy.start()

    def __getitem__(self, i):
        if i not in self.waited:
            self.waited.add(i)
            self.copies[i].wait()
        return self.targets[i]


def attend_step(
    r, g, step, start, mine, span, local_len, rows, lengths, query, rel, keys, values, prob, prob_own, context, hot
):
    cols = pl.ds(pl.multiple_of(g * 256, 256), 256)
    own_rows = pl.ds(pl.multiple_of(r * mine, local_len), mine)
    main_rows = pl.ds(pl.multiple_of(r * span, span), span)
    side_rows = pl.ds(pl.multiple_of(rows * span + r * 2 * local_len, local_len), 2 * local_len)
    q_tile = query[own_rows, cols]
    rel_tile = rel[own_rows, pl.ds(pl.multiple_of(g * 128, 128), 128)]
    side_key = keys[side_rows, cols].astype(jnp.float32)
    side_value = values[side_rows, cols].astype(jnp.float32)
    zero = jnp.zeros((local_len, 256), jnp.float32)
    scores = mm_back(heads_in(q_tile), keys[main_rows, cols])
    bias = skewed(mm(heads_in(rel_tile), hot), local_len)
    products = q_tile.astype(jnp.float32) * jnp.concatenate([zero, side_key], axis=0)
    own_dot = head_sums(products)
    rel_lane = lax.broadcasted_iota(jnp.int32, (mine, 128), 1)
    rel_wide = rel_tile.astype(jnp.float32)
    row = lax.broadcasted_iota(jnp.int32, (mine, span), 0)
    at = lax.broadcasted_iota(jnp.int32, (mine, span), 1)
    ahead = start + lax.rem(row, local_len) + jnp.where(row < local_len, 1, 0)
    kept = (at < ahead) & (at < lengths[r])
    first = lax.broadcasted_iota(jnp.int32, (mine, 1), 0) < local_len
    low, owns = [], []
    for h in range(4):
        part = slice(h * mine, (h + 1) * mine)
        score = jnp.where(kept, scores[part] + bias[part], NEG)
        near = jnp.sum(jnp.where(rel_lane == h * BUCKETS, rel_wide, 0.0), axis=1, keepdims=True)
        own = jnp.where(first, NEG, own_dot[h] + near)
        peak = jnp.maximum(jnp.max(score, axis=1, keepdims=True), own)
        power = jnp.exp(score - peak)
        own_power = jnp.exp(own - peak)
        share = 1.0 / (jnp.sum(power, axis=1, keepdims=True) + own_power)
        low.append((power * share).astype(jnp.bfloat16))
        owns.append(own_power * share)
    low = jnp.concatenate(low, axis=0)
    prob[step] = low
    spread = head_lanes(owns, 256)
    prob_own[own_rows, cols] = spread.astype(prob_own.dtype)
    total = heads_out(mm(low, values[main_rows, cols]))
    total = total + spread * jnp.concatenate([zero, side_value], axis=0)
    context[own_rows, cols] = total.astype(context.dtype)


def cross_step(
    r, g, step, mine, span, local_len, enc_lengths, cquery, ckeys, cvalues, cprob, ccontext
):
    cols = pl.ds(pl.multiple_of(g * 256, 256), 256)
    own_rows = pl.ds(pl.multiple_of(r * mine, local_len), mine)
    main_rows = pl.ds(pl.multiple_of(r * span, span), span)
    scores = mm_back(heads_in(cquery[own_rows, cols]), ckeys[main_rows, cols])
    at = lax.broadcasted_iota(jnp.int32, (mine, span), 1)
    kept = at < enc_lengths[r]
    low = []
    for h in range(4):
        score = jnp.where(kept, scores[h * mine : (h + 1) * mine], NEG)
        power = jnp.exp(score - jnp.max(score, axis=1, keepdims=True))
        share = 1.0 / jnp.sum(power, axis=1, keepdims=True)
        low.append((power * share).astype(jnp.bfloat16))
    low = jnp.concatenate(low, axis=0)
    cprob[step] = low
    ccontext[own_rows, cols] = heads_out(mm(low, cvalues[main_rows, cols])).astype(
        ccontext.dtype
    )


def forward_kernel(rows, local_len, *refs):
    (
        hidden,
        mains,
        states,
        lengths,
        enc_lengths,
        gains,
        *weights,
    ) = refs[:14]
    (hid, x_all, query, keys, values, prob, prob_own, context, ckeys, cvalues) = refs[14:24]
    (normal, normal_scale, normed_low, cquery, cprob, ccontext) = refs[24:30]
    rel, residual = refs[30:32]
    fetch = Fetch(weights, refs[32:40], refs[40])
    w_key, w_value, w_query, w_relative, w_ckey, w_cvalue, w_out, w_cquery = range(8)
    width = hid.shape[1]
    mine = 3 * local_len
    span = mains.shape[0] // rows
    start = lax.axis_index("seq") * local_len
    x_all[: rows * span] = mains[...]
    for r in range(rows):
        for j in range(3):
            tile = hidden[j, r]
            hid[r * mine + j * local_len : r * mine + (j + 1) * local_len] = tile
            if j:
                at = rows * span + (2 * r + j - 1) * local_len
                x_all[at : at + local_len] = tile

    def project(left, w, target, scale=None):
        weight = fetch[w]

        def body(cols):
            product = mm(left[...], weight[:, cols])
            if scale is not None:
                product = product * scale
            target[:, cols] = product.astype(target.dtype)

        tiles(target.shape[1], body)

    project(x_all, w_key, keys)
    project(x_all, w_value, values)
    project(hid, w_query, query, 0.125)
    project(hid, w_relative, rel)
    hot = hot_forward(start, span)

    def attend(step, carry):
        attend_step(
            step // 4, lax.rem(step, 4), step, start, mine, span, local_len, rows, lengths,
            query, rel, keys, values, prob, prob_own, context, hot,
        )
        return carry

    lax.fori_loop(0, 4 * rows, attend, 0)
    project(states, w_ckey, ckeys)
    project(states, w_cvalue, cvalues)
    weight_out = fetch[w_out]

    def out_body(cols):
        residual[:, cols] = hid[:, cols].astype(jnp.float32) + mm(context[...], weight_out[:, cols])

    tiles(width, out_body)

    def norm_body(part):
        normal[part], scale = norm_rows(residual[part])
        normal_scale[part] = jnp.broadcast_to(scale, (scale.shape[0], 128))
        normed_low[part] = (normal[part] * gains[0:1]).astype(jnp.bfloat16)

    row_tiles(hid.shape[0], norm_body)
    project(normed_low, w_cquery, cquery, 0.125)

    def cross(step, carry):
        cross_step(
            step // 4, lax.rem(step, 4), step, mine, span, local_len, enc_lengths,
            cquery, ckeys, cvalues, cprob, ccontext,
        )
        return carry

    lax.fori_loop(0, 4 * rows, cross, 0)


def middle_kernel(
    rows,
    local_len,
    normal,
    ccontext,
    gains,
    cotangent,
    any_cout,
    any_up,
    any_down,
    output,
    crossed_low,
    activated,
    last_low,
    up_back,
    cross_grad,
    cross_low,
    ccontext_back,
    gain_total,
    normal2,
    scale2,
    slope,
    residual,
    v_cout,
    v_up,
    v_down,
    sems,
):
    fetch = Fetch((any_cout, any_up, any_down), (v_cout, v_up, v_down), sems)
    tokens, width = normal.shape
    mine = 3 * local_len
    gain_total[...] = jnp.zeros_like(gain_total)
    weight_cout = fetch[0]

    def cross_body(cols):
        residual[:, cols] = normal[:, cols] * gains[0:1, cols] + mm(
            ccontext[...], weight_cout[:, cols]
        )

    tiles(width, cross_body)

    def norm_body(part):
        normal2[part], scale = norm_rows(residual[part])
        scale2[part] = jnp.broadcast_to(scale, (scale.shape[0], 128))
        crossed_low[part] = (normal2[part] * gains[1:2]).astype(jnp.bfloat16)

    row_tiles(tokens, norm_body)
    weight_up = fetch[1]

    def up_body(cols):
        value = mm(crossed_low[...], weight_up[:, cols])
        below = 0.5 + 0.5 * lax.erf(value * (0.5**0.5))
        activated[:, cols] = (value * below).astype(jnp.bfloat16)
        density = jnp.exp(-0.5 * value * value) * (1.0 / math.sqrt(2.0 * math.pi))
        slope[:, cols] = (below + value * density).astype(jnp.bfloat16)

    tiles(activated.shape[1], up_body)
    weight_down = fetch[2]

    def down_body(cols):
        residual[:, cols] = normal2[:, cols] * gains[1:2, cols] + mm(
            activated[...], weight_down[:, cols]
        )

    tiles(width, down_body)
    for r in range(rows):
        for j in range(3):
            at = r * mine + j * local_len
            part = slice(at, at + local_len)
            normal3, scale = norm_rows(residual[part])
            output[j, r] = (normal3 * gains[2:3]).astype(output.dtype)
            above = cotangent[j, r].astype(jnp.float32)
            add_rows(gain_total, 2, above * normal3)
            grad = norm_back(above, normal3, scale, gains[2:3])
            residual[part] = grad
            last_low[part] = grad.astype(jnp.bfloat16)

    def down_back(cols):
        product = mm_back(last_low[...], weight_down[cols, :])
        up_back[:, cols] = (product * slope[:, cols].astype(jnp.float32)).astype(jnp.bfloat16)

    tiles(activated.shape[1], down_back)

    def up_back_body(cols):
        residual[:, cols] = residual[:, cols] + mm_back(up_back[...], weight_up[cols, :])

    tiles(width, up_back_body)

    def cross_norm_back(part):
        above = residual[part]
        add_rows(gain_total, 1, above * normal2[part])
        grad = norm_back(above, normal2[part], scale2[part][:, 0:1], gains[1:2])
        cross_grad[part] = grad
        cross_low[part] = grad.astype(jnp.bfloat16)

    row_tiles(tokens, cross_norm_back)

    def cout_back(cols):
        ccontext_back[:, cols] = mm_back(cross_low[...], weight_cout[cols, :]).astype(jnp.bfloat16)

    tiles(width, cout_back)


def turning(span):
    return jnp.where(
        lax.broadcasted_iota(jnp.int32, (span, span), 0)
        + lax.broadcasted_iota(jnp.int32, (span, span), 1)
        == span - 1,
        1.0,
        0.0,
    ).astype(jnp.bfloat16)


def cross_back_step(
    r, g, step, mine, span, local_len, ccontext_back, cvalues, cprob, ckeys, cquery, cquery_back, ckey_back, cvalue_back
):
    cols = pl.ds(pl.multiple_of(g * 256, 256), 256)
    own_rows = pl.ds(pl.multiple_of(r * mine, local_len), mine)
    main_rows = pl.ds(pl.multiple_of(r * span, span), span)
    above = heads_in(ccontext_back[own_rows, cols])
    grads = mm_back(above, cvalues[main_rows, cols])
    low = []
    for h in range(4):
        part = slice(h * mine, (h + 1) * mine)
        share = cprob[step, part].astype(jnp.float32)
        weighted = share * grads[part]
        low.append(
            (weighted - share * jnp.sum(weighted, axis=1, keepdims=True)).astype(jnp.bfloat16)
        )
    low = jnp.concatenate(low, axis=0)
    back = heads_out(mm(low, ckeys[main_rows, cols])).astype(jnp.bfloat16)
    cquery_back[own_rows, cols] = back * jnp.bfloat16(0.125)
    ckey_back[main_rows, cols] = mm_grad(low, heads_in(cquery[own_rows, cols])).astype(
        jnp.bfloat16
    )
    cvalue_back[main_rows, cols] = mm_grad(cprob[step], above).astype(jnp.bfloat16)


def attend_back_step(
    r, g, step, mine, span, local_len, rows, context_back, query, keys, values, prob, prob_own,
    query_back, key_back, value_back, rel_back, hot, turn
):
    cols = pl.ds(pl.multiple_of(g * 256, 256), 256)
    own_rows = pl.ds(pl.multiple_of(r * mine, local_len), mine)
    main_rows = pl.ds(pl.multiple_of(r * span, span), span)
    side_rows = pl.ds(pl.multiple_of(rows * span + r * 2 * local_len, local_len), 2 * local_len)
    above_tile = context_back[own_rows, cols]
    above = heads_in(above_tile)
    above_wide = above_tile.astype(jnp.float32)
    q_tile = query[own_rows, cols]
    zero = jnp.zeros((local_len, 256), jnp.float32)
    side_key = jnp.concatenate([zero, keys[side_rows, cols].astype(jnp.float32)], axis=0)
    side_value = jnp.concatenate([zero, values[side_rows, cols].astype(jnp.float32)], axis=0)
    spread = prob_own[own_rows, cols].astype(jnp.float32)
    grads = mm_back(above, values[main_rows, cols])
    own_grads = head_sums(above_wide * side_value)
    low, own_low = [], []
    for h in range(4):
        part = slice(h * mine, (h + 1) * mine)
        share = prob[step, part].astype(jnp.float32)
        own_share = spread[:, h * 64 : h * 64 + 1]
        weighted = share * grads[part]
        delta = jnp.sum(weighted, axis=1, keepdims=True) + own_share * own_grads[h]
        low.append((weighted - share * delta).astype(jnp.bfloat16))
        own_low.append(own_share * (own_grads[h] - delta))
    low = jnp.concatenate(low, axis=0)
    own_spread = head_lanes(own_low, 256)
    back = heads_out(mm(low, keys[main_rows, cols])) + own_spread * side_key
    query_back[own_rows, cols] = back.astype(jnp.bfloat16) * jnp.bfloat16(0.125)
    key_back[main_rows, cols] = mm_grad(low, heads_in(q_tile)).astype(jnp.bfloat16)
    value_back[main_rows, cols] = mm_grad(prob[step], above).astype(jnp.bfloat16)
    key_back[side_rows, cols] = (own_spread * q_tile.astype(jnp.float32))[local_len:].astype(
        jnp.bfloat16
    )
    value_back[side_rows, cols] = (spread * above_wide)[local_len:].astype(jnp.bfloat16)
    turned_low = skewed(mm(low, turn), local_len).astype(jnp.bfloat16)
    rel_total = heads_out(mm(turned_low, hot))
    near = lax.rem(lax.broadcasted_iota(jnp.int32, rel_total.shape, 1), BUCKETS) == 0
    rel_total = rel_total + jnp.where(near, head_lanes(own_low, 128), 0.0)
    rel_back[own_rows, pl.ds(pl.multiple_of(g * 128, 128), 128)] = rel_total.astype(
        jnp.bfloat16
    )


def backward_kernel(rows, local_len, *refs):
    (
        ccontext_back,
        cross_grad,
        cquery,
        ckeys,
        cvalues,
        cprob,
        normal,
        normal_scale,
        gains,
        query,
        keys,
        values,
        prob,
        prob_own,
        *weights,
    ) = refs[:22]
    (cquery_back, ckey_back, cvalue_back, attn_low, query_back, key_back) = refs[22:28]
    (value_back, rel_back, hidden_own, main_part, states_part, gain_total) = refs[28:34]
    residual, context_back = refs[34:36]
    fetch = Fetch(weights, refs[36:44], refs[44])
    w_cquery, w_out, w_ckey, w_cvalue, w_query, w_relative, w_key, w_value = range(8)
    tokens, width = query.shape
    mine = 3 * local_len
    span = ckeys.shape[0] // rows
    start = lax.axis_index("seq") * local_len
    gain_total[...] = jnp.zeros_like(gain_total)

    def cross(step, carry):
        cross_back_step(
            step // 4, lax.rem(step, 4), step, mine, span, local_len, ccontext_back, cvalues,
            cprob, ckeys, cquery, cquery_back, ckey_back, cvalue_back,
        )
        return carry

    lax.fori_loop(0, 4 * rows, cross, 0)
    weight_cquery = fetch[w_cquery]

    def cquery_body(cols):
        residual[:, cols] = cross_grad[:, cols] + mm_back(cquery_back[...], weight_cquery[cols, :])

    tiles(width, cquery_body)

    def attn_norm_back(part):
        above = residual[part]
        add_rows(gain_total, 0, above * normal[part])
        grad = norm_back(above, normal[part], normal_scale[part][:, 0:1], gains[0:1])
        residual[part] = grad
        attn_low[part] = grad.astype(jnp.bfloat16)

    row_tiles(tokens, attn_norm_back)
    weight_out = fetch[w_out]

    def out_back(cols):
        context_back[:, cols] = mm_back(attn_low[...], weight_out[cols, :]).astype(jnp.bfloat16)

    tiles(width, out_back)
    hot = hot_backward(start, span)
    turn = turning(span)

    def attend(step, carry):
        attend_back_step(
            step // 4, lax.rem(step, 4), step, mine, span, local_len, rows, context_back, query,
            keys, values, prob, prob_own, query_back, key_back, value_back, rel_back, hot, turn,
        )
        return carry

    lax.fori_loop(0, 4 * rows, attend, 0)
    weight_ckey, weight_cvalue = fetch[w_ckey], fetch[w_cvalue]
    weight_query, weight_relative = fetch[w_query], fetch[w_relative]
    weight_key, weight_value = fetch[w_key], fetch[w_value]
    chips = rows * span // (rows * local_len)

    def states_body(cols):
        total = mm_back(ckey_back[...], weight_ckey[cols, :])
        total = total + mm_back(cvalue_back[...], weight_cvalue[cols, :])
        total = total.astype(jnp.bfloat16)
        for r in range(rows):
            for p in range(chips):
                at = r * span + p * local_len
                states_part[p, r, :, cols] = total[at : at + local_len]

    tiles(width, states_body)

    def hidden_body(cols):
        total = mm_back(key_back[...], weight_key[cols, :])
        total = total + mm_back(value_back[...], weight_value[cols, :])
        mains = total[: rows * span].astype(jnp.bfloat16)
        for r in range(rows):
            for p in range(chips):
                at = r * span + p * local_len
                main_part[p, r, :, cols] = mains[at : at + local_len]
        own = residual[:, cols] + mm_back(query_back[...], weight_query[cols, :])
        own = own + mm_back(rel_back[...], weight_relative[cols, :])
        for r in range(rows):
            for j in range(3):
                tile = own[r * mine + j * local_len : r * mine + (j + 1) * local_len]
                if j:
                    at = rows * span + (2 * r + j - 1) * local_len
                    tile = tile + total[at : at + local_len]
                hidden_own[j, r, :, cols] = tile

    tiles(width, hidden_body)


def gather_steps(sources, shards, planes, wholes, full_planes, nz, sems):
    local_sem, send, recv, plane_send, plane_recv, stage_sem = sems
    s, z, c, sx, sy = place()
    own = 2 * z + c
    core = (s, 2 * z + 1 - c)
    beside_x, beside_y = (sx, own), (sy, own)
    staged = [
        pltpu.make_async_copy(source, shard_ref, stage_sem.at[w])
        for w, (source, shard_ref) in enumerate(zip(sources, shards))
    ]
    for copy in staged:
        copy.start()
    awaited = set()
    greet(nz)
    started = {}

    def put(i, copy):
        copy.start()
        started.setdefault(i, []).append(copy)

    items = []
    for w, shard_ref in enumerate(shards):
        if shard_ref.shape[0] % 128:
            items.append((w, 0, 0, None))
            continue
        for row in range(0, shard_ref.shape[0], 128):
            wide = min(shard_ref.shape[1], 1024)
            for col in range(0, shard_ref.shape[1], wide):
                items.append((w, row, 128, pl.ds(col, wide)))
    count = len(items)
    split = [item[2] > 0 for item in items]

    def cut(ref, i, q=None, half=None):
        _, row, height, cols = items[i]
        if not height:
            return ref
        if q is not None:
            height = height // 4
            row = row + q * height
        if half is not None:
            height = height // 2
            row = row + half * height
        return ref.at[pl.ds(row, height), cols]

    def shard(i, q=None):
        return cut(shards[items[i][0]], i, q)

    def whole(i, block, q=None, half=None):
        return cut(wholes[items[i][0]].at[block], i, q, half)

    def every_block(i):
        w, row, height, cols = items[i]
        return wholes[w].at[:, pl.ds(row, height), cols] if height else wholes[w]

    def along_z(i):
        if items[i][0] not in awaited:
            awaited.add(items[i][0])
            staged[items[i][0]].wait()
        pltpu.make_async_copy(shard(i), whole(i, own), local_sem.at[i]).start()
        q = s if split[i] else None
        for dz in range(1, nz):
            to = (s, 2 * lax.rem(z + dz, nz) + c)
            put(i, remote(shard(i, q), whole(i, own, q), send.at[i, dz, 0], recv.at[i, dz, 0], to))
        put(i, remote(shard(i), whole(i, own), send.at[i, 0, 0], recv.at[i, 0, 0], core))

    def moved(i, dz, kind, q, half, to):
        part = whole(i, 2 * lax.rem(z + nz - dz, nz) + c, q if split[i] else None, half)
        return remote(part, part, send.at[i, dz, kind], recv.at[i, dz, kind], to)

    def core_copy(i, dz, of):
        part = whole(i, 2 * lax.rem(z + nz - dz, nz) + of)
        return remote(part, part, send.at[i, dz, 5], recv.at[i, dz, 5], core)

    def to_core(i, dz):
        put(i, core_copy(i, dz, c))

    def first(i, dz):
        moved(i, dz, 0, s, None, core).wait_recv()
        if split[i]:
            put(i, moved(i, dz, 1, s, None, beside_x))
            put(i, moved(i, dz, 2, s, None, beside_y))
        else:
            to_core(i, dz)

    def second(i, dz):
        moved(i, dz, 1, sx, None, core).wait_recv()
        put(i, moved(i, dz, 4, sx, 0, beside_y))
        moved(i, dz, 2, sy, None, core).wait_recv()
        put(i, moved(i, dz, 3, sy, 1, beside_x))

    def third(i, dz):
        moved(i, dz, 4, 3 - s, 0, core).wait_recv()
        moved(i, dz, 3, 3 - s, 1, core).wait_recv()
        to_core(i, dz)

    def arrive(i):
        other = 1 - c
        pltpu.make_async_copy(shard(i), whole(i, own), local_sem.at[i]).wait()
        block = whole(i, 2 * z + other)
        remote(block, block, send.at[i, 0, 0], recv.at[i, 0, 0], core).wait_recv()
        for dz in range(1, nz):
            core_copy(i, dz, other).wait_recv()

    def plane(i, kind, q, half, to):
        rows = full_planes[i].shape[0]
        part = full_planes[i].at[pl.ds(half * (rows // 2), rows // 2), q]
        return remote(part, part, plane_send.at[i, kind], plane_recv.at[i, kind], to)

    def plane_part(i):
        return planes[i].at[0] if len(planes[i].shape) == 4 else planes[i]

    def plane_whole(i, kind, q, to):
        return remote(
            plane_part(i), full_planes[i].at[:, q], plane_send.at[i, kind], plane_recv.at[i, kind], to
        )

    def plane_here(i):
        return pltpu.make_async_copy(
            plane_part(i), full_planes[i].at[:, s], local_sem.at[count + i]
        )

    def plane_first(i):
        plane_here(i).start()
        put(None, plane_whole(i, 0, s, beside_x))
        put(None, plane_whole(i, 1, s, beside_y))

    def plane_second(i):
        plane_whole(i, 0, sx, core).wait_recv()
        put(None, plane(i, 2, sx, 0, beside_y))
        plane_whole(i, 1, sy, core).wait_recv()
        put(None, plane(i, 3, sy, 1, beside_x))

    def plane_arrive(i):
        plane_here(i).wait()
        plane(i, 2, 3 - s, 0, core).wait_recv()
        plane(i, 3, 3 - s, 1, core).wait_recv()

    def sent(i):
        for copy in started.pop(i, ()):
            copy.wait_send()

    def settle():
        for i in list(started):
            sent(i)

    steps, ready = [], {}

    def step(call, *args):
        steps.append(lambda: call(*args))

    ahead = 5
    for i in range(2):
        plane_first(i)
    for i in range(min(ahead, count)):
        along_z(i)
    for i in range(count + 3):
        for dz in range(1, nz):
            if i < count:
                step(first, i, dz)
            if 1 <= i <= count and split[i - 1]:
                step(second, i - 1, dz)
            if 2 <= i < count + 2 and split[i - 2]:
                step(third, i - 2, dz)
        if ahead + i < count:
            step(along_z, ahead + i)
        if i >= 4:
            step(sent, i - 4)
        if i in (1, 2):
            step(plane_second, i - 1)
        if i == 3:
            ready["planes"] = len(steps)
        if i >= 3:
            ready[i - 3] = len(steps)
    return steps, ready, arrive, plane_arrive, every_block, settle


SLOTS = 8
LAYER_OUTS = 25


def layer_kernel(count, nz, rows, local_len, *refs):
    at = 0

    def take(n):
        nonlocal at
        at += n
        return refs[at - n : at]

    sources = take(count)
    hidden, encoder, cotangent, lengths, enc_lengths = take(5)
    wholes, outs = take(count), take(LAYER_OUTS)
    gains, residual = take(2)
    held = list(take(LAYER_OUTS - 1))
    held.insert(14, held[5])
    (hid, x_all, query, keys, values, prob, prob_own, context, ckeys, cvalues) = held[:10]
    (normal, normal_scale, normed_low, cquery, cprob, ccontext, output) = held[10:17]
    (crossed_low, activated, last_low, slope, gain_total, normal2, scale2) = held[17:24]
    states = held[24]
    land_gains, rel, pool, mains, hot_ref = take(5)
    shards = take(count)
    load_sems, out_sems = take(2)
    steps, ready, arrive, plane_arrive, every_block, settle = gather_steps(
        sources, shards, (hidden, encoder), wholes, (mains, states), nz, take(6)
    )
    tokens, width = hid.shape
    mine = 3 * local_len
    span = mains.shape[1] * local_len
    start = lax.axis_index("seq") * local_len
    emitted = []

    def leave(i):
        return pltpu.make_async_copy(held[i], outs[i], out_sems.at[i])

    def emit(*targets):
        for target in targets:
            i = next(i for i, ref in enumerate(held) if ref is target)
            leave(i).start()
            if target is not prob:
                emitted.append(leave(i))

    def emit_cross():
        leave(14).start()
        emitted.append(leave(14))

    order = list(range(1, 18))
    KEY, VALUE, QUERY, REL, CKEY, CVALUE, OUT, CQUERY, COUT, UP, DOWN = (*range(9), 9, 13)

    def slot_of(load):
        return load % SLOTS

    def load_copy(load):
        source = every_block(order[load])
        target = pool.at[slot_of(load)]
        if source.shape[2] < target.shape[2]:
            target = target.at[:, :, : source.shape[2]]
        return pltpu.make_async_copy(source, target, load_sems.at[load])

    def weight(load):
        return pool.at[slot_of(load)]

    def columns(load, cols):
        return pool[slot_of(load), :, :, cols].reshape(width, 256)

    def project(left, load, target, scale=None):
        def body(cols):
            product = mm(left[...], columns(load, cols))
            if scale is not None:
                product = product * scale
            target[:, cols] = product.astype(target.dtype)

        tiles(target.shape[1], body)

    def prepare():
        plane_arrive(0)
        plane_arrive(1)
        for r in range(rows):
            for j in range(3):
                tile = hidden[j, r]
                hid[r * mine + j * local_len : r * mine + (j + 1) * local_len] = tile
                if j:
                    to = rows * span + (2 * r + j - 1) * local_len
                    x_all[to : to + local_len] = tile
        x_all[: rows * span] = mains[...].reshape(rows * span, width)
        gain_total[...] = jnp.zeros_like(gain_total)
        hot_ref[...] = hot_forward(start, span)
        emit(hid, x_all, states)

    def take_gains():
        arrive(0)
        copy = pltpu.make_async_copy(wholes[0], land_gains, load_sems.at[len(order)])
        copy.start()
        copy.wait()
        for d in range(land_gains.shape[0]):
            gains[:, d * 128 : (d + 1) * 128] = land_gains[d].astype(jnp.float32)

    def attend(step, carry):
        r, g = step // 4, lax.rem(step, 4)
        attend_step(
            r, g, step, start, mine, span, local_len, rows, lengths, query, rel, keys, values,
            prob, prob_own, context, hot_ref[...],
        )
        return carry

    def cross(step, carry):
        r, g = step // 4, lax.rem(step, 4)
        cross_step(r, g, step, mine, span, local_len, enc_lengths, cquery, ckeys, cvalues, cprob, ccontext)
        return carry

    def out_body(cols):
        residual[:, cols] = hid[:, cols].astype(jnp.float32) + mm(context[...], columns(OUT, cols))

    def norm_body(part):
        normal[part], scale = norm_rows(residual[part])
        normal_scale[part] = jnp.broadcast_to(scale, (scale.shape[0], 128))
        normed_low[part] = (normal[part] * gains[0:1]).astype(jnp.bfloat16)

    def after_attention():
        tiles(width, out_body)
        row_tiles(tokens, norm_body)
        emit(context, normal, normal_scale, normed_low)

    def after_cross_query():
        project(normed_low, CQUERY, cquery, 0.125)
        emit(cquery)
        leave(5).wait()

    def cross_body(cols):
        residual[:, cols] = normal[:, cols] * gains[0:1, cols] + mm(ccontext[...], columns(COUT, cols))

    def cross_norm_body(part):
        normal2[part], scale = norm_rows(residual[part])
        scale2[part] = jnp.broadcast_to(scale, (scale.shape[0], 128))
        after = normal2[part] * gains[1:2]
        crossed_low[part] = after.astype(jnp.bfloat16)
        residual[part] = after

    def after_cross():
        tiles(width, cross_body)
        row_tiles(tokens, cross_norm_body)
        emit(ccontext, crossed_low, normal2, scale2)

    def up(k):
        def body(i, carry):
            cols = pl.ds(pl.multiple_of(i * 256, 256), 256)
            to = pl.ds(pl.multiple_of(k * width + i * 256, 256), 256)
            value = mm(crossed_low[...], columns(UP + k, cols))
            below = 0.5 + 0.5 * lax.erf(value * (0.5**0.5))
            activated[:, to] = (value * below).astype(jnp.bfloat16)
            density = jnp.exp(-0.5 * value * value) * (1.0 / math.sqrt(2.0 * math.pi))
            slope[:, to] = (below + value * density).astype(jnp.bfloat16)
            return carry

        lax.fori_loop(0, width // 256, body, 0)
        if k == 3:
            emit(activated, slope)

    blocks = pool.shape[1]

    def of_down(k, d):
        return d * 4 * 128 + k * 128

    def down(k):
        def body(cols):
            left = jnp.concatenate(
                [activated[:, of_down(k, d) : of_down(k, d) + 128] for d in range(blocks)], axis=1
            )
            residual[:, cols] += mm(left, columns(DOWN + k, cols))

        tiles(width, body)

    def last_norm():
        for r in range(rows):
            for j in range(3):
                part = slice(r * mine + j * local_len, r * mine + (j + 1) * local_len)
                normal3, scale = norm_rows(residual[part])
                output[j, r] = (normal3 * gains[2:3]).astype(output.dtype)
                above = cotangent[j, r].astype(jnp.float32)
                add_rows(gain_total, 2, above * normal3)
                grad = norm_back(above, normal3, scale, gains[2:3])
                residual[part] = grad
                last_low[part] = grad.astype(jnp.bfloat16)
        emit(output, last_low, gain_total)

    pieces = [("planes", 2, prepare)]
    pieces += [
        (KEY, 3, lambda: project(x_all, KEY, keys)),
        (VALUE, 3, lambda: project(x_all, VALUE, values)),
        (QUERY, 2, lambda: project(hid, QUERY, query, 0.125)),
        (REL, 1, lambda: project(hid, REL, rel)),
    ]
    half = 2
    for i in range(0, 4 * rows, half):
        pieces.append((REL, 5, lambda i=i: lax.fori_loop(i, i + half, attend, 0)))
    pieces += [
        (REL, 0, lambda: emit(query, keys, values, prob, prob_own)),
        (CKEY, 2, lambda: project_states(CKEY, ckeys)),
        (CVALUE, 2, lambda: project_states(CVALUE, cvalues)),
        (OUT, 0, take_gains),
        (OUT, 3, after_attention),
        (CQUERY, 2, after_cross_query),
    ]

    def project_states(load, target):
        def body(cols):
            left = states[...].reshape(rows * span, width)
            target[:, cols] = mm(left, columns(load, cols)).astype(target.dtype)

        tiles(width, body)
        emit(target)

    for i in range(0, 4 * rows, half):
        pieces.append((CQUERY, 3, lambda i=i: lax.fori_loop(i, i + half, cross, 0)))
    pieces += [(CQUERY, 0, emit_cross), (COUT, 3, after_cross)]
    pieces += [(UP + k, 3, functools.partial(up, k)) for k in range(4)]
    pieces += [(DOWN + k, 1, functools.partial(down, k)) for k in range(4)]
    pieces.append((DOWN + 3, 3, last_norm))

    last_use = {}
    for index, (need, _, _) in enumerate(pieces):
        last_use[need] = index
    state = {"step": 0, "load": 0}
    arrived, waited = set(), set()

    def run_to(n):
        while state["step"] < min(n, len(steps)):
            steps[state["step"]]()
            state["step"] += 1

    def free(load, done):
        return all(
            last_use[other] < done for other in range(load) if slot_of(other) == slot_of(load)
        )

    def begin_load():
        load = state["load"]
        if order[load] not in arrived:
            arrive(order[load])
            arrived.add(order[load])
        load_copy(load).start()
        state["load"] += 1

    rate = len(steps) / 130.0
    for index, (need, cost, call) in enumerate(pieces):
        if need == "planes":
            run_to(ready["planes"])
        else:
            while state["load"] <= need:
                run_to(ready[order[state["load"]]])
                begin_load()
            if need not in waited:
                waited.add(need)
                load_copy(need).wait()
        call()
        run_to(state["step"] + int(cost * rate + 0.5))
        while (
            state["load"] < len(order)
            and free(state["load"], index + 1)
            and ready[order[state["load"]]] <= state["step"]
        ):
            begin_load()
    run_to(len(steps))
    for copy in emitted:
        copy.wait()
    settle()


def layer(shards, hidden, encoder, cotangent, lengths, enc_lengths, ndp):
    nz = ndp // 2
    count = len(shards)
    low, wide = jnp.bfloat16, jnp.float32
    _, rows, local_len, width = hidden.shape
    tokens, span = 3 * rows * local_len, 4 * local_len
    every = rows * (span + 2 * local_len)
    ff = shards[-2].shape[1]
    steps = sum(max(1, w.size // (128 * 1024)) for w in shards)
    results = [
        ((tokens, width), low),
        ((every, width), low),
        ((tokens, width), low),
        ((every, width), low),
        ((every, width), low),
        ((4 * rows, 12 * local_len, span), low),
        ((tokens, width), low),
        ((tokens, width), low),
        ((rows * span, width), low),
        ((rows * span, width), low),
        ((tokens, width), wide),
        ((tokens, 128), wide),
        ((tokens, width), low),
        ((tokens, width), low),
        ((4 * rows, 12 * local_len, span), low),
        ((tokens, width), low),
        (hidden.shape, low),
        ((tokens, width), low),
        ((tokens, ff), low),
        ((tokens, width), low),
        ((tokens, ff), low),
        ((3, 8, width), wide),
        ((tokens, width), wide),
        ((tokens, 128), wide),
        ((rows, 4, local_len, width), low),
    ]
    more = [((16, width), wide), ((tokens, width), wide)]
    vmem = pl.BlockSpec(memory_space=pltpu.VMEM)
    smem = pl.BlockSpec(memory_space=pltpu.SMEM)
    anywhere = pl.BlockSpec(memory_space=pl.ANY)
    return pl.pallas_call(
        lambda *refs: layer_kernel(count, nz, rows, local_len, *refs),
        out_shape=[jax.ShapeDtypeStruct((ndp,) + w.shape, w.dtype) for w in shards]
        + [jax.ShapeDtypeStruct(*result) for result in results]
        + [jax.ShapeDtypeStruct(*result) for result in more],
        in_specs=[anywhere] * count + [vmem] * 3 + [smem] * 2,
        out_specs=[anywhere] * (count + len(results)) + [vmem] * 2,
        scratch_shapes=[pltpu.VMEM(*result) for i, result in enumerate(results) if i != 14]
        + [
            pltpu.VMEM((ndp,) + shards[0].shape, low),
            pltpu.VMEM((tokens, width // 2), low),
            pltpu.VMEM((SLOTS, ndp, 128, width), low),
            pltpu.VMEM((rows, 4, local_len, width), low),
            pltpu.VMEM((128, span), low),
        ]
        + [pltpu.VMEM(w.shape, w.dtype) for w in shards]
        + [
            pltpu.SemaphoreType.DMA((18,)),
            pltpu.SemaphoreType.DMA((len(results),)),
            pltpu.SemaphoreType.DMA((steps + 2,)),
            pltpu.SemaphoreType.DMA((steps, nz, 6)),
            pltpu.SemaphoreType.DMA((steps, nz, 6)),
            pltpu.SemaphoreType.DMA((2, 4)),
            pltpu.SemaphoreType.DMA((2, 4)),
            pltpu.SemaphoreType.DMA((count,)),
        ],
        compiler_params=pltpu.CompilerParams(
            collective_id=0, has_side_effects=True, vmem_limit_bytes=62 * 2**20
        ),
        name="layer",
    )(*shards, hidden, encoder, cotangent, lengths, enc_lengths)


RINGS = (5, 5)
SLACK = 0
LAGS = (4, 7, 10)
DEEP = ()
WIDE_RING = 8


def back_kernel(plan, nz, rows, local_len, n_out, *refs):
    at = 0

    def take(n):
        nonlocal at
        at += n
        return refs[at - n : at]

    (any_activated, any_last, any_grad, any_slope, any_crossed, any_normal2, any_scale2) = take(7)
    (any_normal, any_scale, any_ccontext, any_normed, any_context, any_hid, any_x_all) = take(7)
    (any_states, any_cquery, any_ckeys, any_cvalues, any_cprob, any_query, any_keys) = take(7)
    (any_values, any_prob, any_prob_own, any_gains, any_gain_total) = take(5)
    w_down, w_up, w_cout, w_cquery, w_out, w_ckey, w_cvalue, w_key, w_value, w_query, w_rel = take(11)
    outs = take(n_out)
    gain_out, states_sum, hidden_grad = take(3)
    (activated, last_low, residual, up_back, crossed_low, normal, scale, cross_low) = take(8)
    (ccontext_back, cquery, ckeys, cvalues, prob, query, keys, values, prob_own) = take(9)
    (gains, gain_total, cquery_back, ckey_back, cvalue_back, attn_low, query_back) = take(7)
    (key_back, value_back, rel_back, main_part, states_part, pool, hot_ref, turn_ref) = take(8)
    parts, held0s, held1s, held2s, held3s = take(2), take(3), take(3), take(3), take(3)
    gain_part, share1, share2, deep0, deep1, deep2 = take(6)
    load_sems, weight_sems, out_sems, send, recv, credit0, credit1, credit2 = take(8)
    shares = (main_part, states_part)
    context_back, slope = ccontext_back, up_back
    tokens, width = residual.shape
    mine = 3 * local_len
    span = ckeys.shape[0] // rows
    start = lax.axis_index("seq") * local_len
    s, z, c, sx, sy = place()
    own = 2 * z + c
    x, y = lax.rem(s, 2), s // 2
    core = (s, 2 * z + 1 - c)
    beside_x, beside_y = (sx, own), (sy, own)

    loads = []

    def load(source, target):
        copy = pltpu.make_async_copy(source, target, load_sems.at[len(loads)])
        loads.append(copy)
        copy.start()
        return copy

    begun = [
        load(any_activated, activated),
        load(any_last, last_low),
    ]
    first_loads = list(begun)
    ffn_loads = [
        load(any_slope, slope),
        load(any_grad, residual),
        load(any_crossed, crossed_low),
        load(any_normal2, normal),
        load(any_scale2, scale),
        load(any_gains, gains),
        load(any_gain_total, gain_total),
    ]
    cross_loads = [
        load(any_cquery, cquery),
        load(any_ckeys, ckeys),
        load(any_cvalues, cvalues),
        load(any_cprob.at[pl.ds(0, 4)], prob),
    ]
    attend_loads = [
        load(any_query, query),
        load(any_keys, keys),
        load(any_values, values),
        load(any_prob_own, prob_own),
    ]

    def await_all(copies):
        for copy in copies:
            copy.wait()
        copies.clear()

    blocks = [w_down.at[pl.ds(width * k, width)] for k in range(4)]
    blocks += [w_up.at[:, pl.ds(width * k, width)] for k in range(4)]
    blocks += [w_cout, w_cquery, w_out, w_ckey, w_cvalue, w_key, w_value, w_query, w_rel]
    DOWN, UP, COUT, CQUERY, OUT, CKEY, CVALUE, KEY, VALUE, QUERY, REL = (0, 4, *range(8, 17))

    def block_copy(i):
        target = pool.at[i % 2]
        if blocks[i].shape[1] < width:
            target = target.at[:, pl.ds(0, blocks[i].shape[1])]
        return pltpu.make_async_copy(blocks[i], target, weight_sems.at[i])

    started = []

    def need(i):
        while len(started) <= i:
            block_copy(len(started)).start()
            started.append(True)
        block_copy(i).wait()

    def release(i):
        if i + 2 < len(blocks) and len(started) <= i + 2:
            while len(started) <= i + 2:
                block_copy(len(started)).start()
                started.append(True)

    block_copy(0).start()
    block_copy(1).start()
    started += [True, True]
    greet(nz)
    gain_part[...] = jnp.zeros_like(gain_part)

    held = {}

    def buffers(k):
        kind, slot = plan[k][:2]
        sub = plan[k][5]
        if kind == 3:
            share = shares[slot // 2].at[:, :, slot % 2]
            return None, share, share1.at[slot], share2.at[slot], None
        if kind == 4:
            part, held0 = parts[0].at[slot % 2], held0s[0].at[slot % RINGS[0]]
            return part, held0, deep1.at[sub], deep2.at[sub], deep0.at[sub]
        if kind == 2:
            return (gain_part,) + tuple(h[2].at[0] for h in (held0s, held1s, held2s, held3s))
        ring = WIDE_RING if kind == 0 else held1s[1].shape[0]
        return (
            parts[kind].at[slot % 2],
            held0s[kind].at[slot % RINGS[kind]],
            held1s[kind].at[sub % ring],
            held2s[kind].at[sub % ring],
            held3s[kind].at[sub],
        )

    slots_of = [sum(p[0] in ((0, 4), (1,))[kind] for p in plan) for kind in range(2)]
    subs_of = sum(p[0] == 0 for p in plan)

    def even(k):
        return plan[k][5] % 2 == 0

    def core_copy(k):
        part, held0 = buffers(k)[:2]
        return remote(part.at[:, :, :, 1 - c], held0, send.at[k, 0], recv.at[k, 0], core)

    def first_copy(k):
        _, held0, held1 = buffers(k)[:3]
        if plan[k][0] == 4:
            held0 = buffers(k)[4].at[0]
        if even(k):
            return remote(held0.at[:, 1 - x], held1, send.at[k, 1], recv.at[k, 1], beside_x)
        return remote(held0.at[1 - y], held1, send.at[k, 1], recv.at[k, 1], beside_y)

    def second_copy(k):
        held1, held2 = buffers(k)[2:4]
        if even(k):
            return remote(held1.at[1 - y], held2, send.at[k, 2], recv.at[k, 2], beside_y)
        return remote(held1.at[1 - x], held2, send.at[k, 2], recv.at[k, 2], beside_x)

    def z_copy(k, dz):
        _, held0, _, held2, held3 = buffers(k)
        zt = lax.rem(z + dz, nz)
        source = held0.at[:, :, zt] if plan[k][0] == 4 else held2.at[zt]
        return remote(
            source, held3.at[dz - 1], send.at[k, 2 + dz], recv.at[k, 2 + dz], (s, 2 * zt + c)
        )

    def grant(semaphore, to):
        pl.semaphore_signal(semaphore, inc=1, device_id=to, device_id_type=MESH)

    def added(held, mine):
        held[...] = (held[...].astype(jnp.float32) + mine.astype(jnp.float32)).astype(held.dtype)

    half = rows * span // 2
    whole_rows = (0, tokens)

    def segments(pair, i):
        cols = pl.ds(256 * i, 256)
        if pair == 0:
            return [(activated[:, cols], whole_rows)]
        if pair == 1:
            return [(crossed_low[:, cols], whole_rows)]
        if pair <= 6:
            column = width * min(pair - 2, 3) + 256 * i
            return [(activated[:, pl.ds(column, 256)], whole_rows)]
        if pair <= 8:
            return [
                (up_back[:, pl.ds(width * n + 256 * i, 256)], (tokens * n, tokens)) for n in range(2)
            ]
        return [
            (up_back[:half, pl.ds(width * (2 + n) + 256 * i, 256)], (half * n, half))
            for n in range(2)
        ]

    rights = (
        last_low, up_back, cross_low, cquery_back, attn_low, query_back, rel_back,
        key_back, value_back, ckey_back, cvalue_back,
    )
    late_loads = []

    def reload():
        for n, source in enumerate((any_ccontext, any_normed, any_context, any_hid)):
            late_loads.append(load(source, activated.at[:, pl.ds(width * n, width)]))
        for n in range(2):
            late_loads.append(
                load(any_x_all.at[pl.ds(tokens * n, tokens)], up_back.at[:, pl.ds(width * n, width)])
            )
            late_loads.append(
                load(
                    any_states.at[pl.ds(half * n, half)],
                    up_back.at[pl.ds(0, half), pl.ds(width * (2 + n), width)],
                )
            )

    before, recent = {}, {}
    for k, entry in enumerate(plan):
        before[k] = recent.get((entry[0] % 4, entry[1] - 2))
        recent[entry[0] % 4, entry[1]] = k
    followed = set(v for v in before.values() if v is not None)
    pairs_before = max(k for k, entry in enumerate(plan) if entry[0] in (0, 1, 4) and entry[2] < 2)

    def make(k):
        kind, slot, pair, col, wide, _ = plan[k]
        if kind == 3:
            return
        if kind != 2:
            part = buffers(k)[0]
            block = part.shape[4]
            if pair == 0:
                await_all(first_loads)
            if pair >= 2:
                await_all(late_loads)
            if slot >= 2:
                core_copy(before[k]).wait_send()
            group = 256 // block
            for i in range(part.shape[0] * part.shape[1] * nz * 2 * block // 256):
                product = 0.0
                for left, (row, height) in segments(pair, i):
                    right = rights[pair][row : row + height, col : col + wide]
                    product = product + mm_grad(left, right)
                i_s, rest = divmod(i * group, 2 * nz)
                zs = rest // 2
                part[i_s // 2, i_s % 2, zs : zs + group // 2] = product.reshape(
                    group // 2, 2, block, wide
                ).astype(part.dtype)
            if k == pairs_before:
                reload()
            if slot >= RINGS[kind % 4]:
                pl.semaphore_wait(credit0.at[kind % 4], 1)
        else:
            lanes = width // (8 * nz)
            totals = jnp.concatenate(
                [jnp.sum(gain_total[g], axis=0, keepdims=True) for g in range(3)], axis=0
            )
            for b in range(8 * nz):
                i_s, rest = divmod(b, 2 * nz)
                gain_part[i_s // 2, i_s % 2, rest // 2, rest % 2, 0:3, 0:lanes] = totals[
                    :, b * lanes : (b + 1) * lanes
                ]
        core_copy(k).start()

    def after_core(k):
        part, held0 = buffers(k)[:2]
        kind, sub = plan[k][0], plan[k][5]
        if kind != 3:
            core_copy(k).wait_recv()
            added(held0, part[:, :, :, c])
        if kind == 4:
            for dz in range(1, nz):
                z_copy(k, dz).start()
            return
        if kind == 0 and sub >= WIDE_RING:
            pl.semaphore_wait(credit1.at[sub % 2], 1)
        first_copy(k).start()

    def over_z(k, mine_part):
        held3 = buffers(k)[4]
        total = mine_part.astype(jnp.float32)
        for dz in range(1, nz):
            z_copy(k, dz).wait_recv()
            total = total + held3[dz - 1].astype(jnp.float32)
        return total

    def sent_z(k):
        for dz in range(1, nz):
            z_copy(k, dz).wait_send()

    def after_first(k):
        _, held0, held1, _, held3 = buffers(k)
        kind, slot, sub = plan[k][0], plan[k][1], plan[k][5]
        if kind == 4:
            held3[0] = over_z(k, held0[:, :, z]).astype(held3.dtype)
            first_copy(k).start()
            sent_z(k)
        else:
            first_copy(k).wait_recv()
            added(held1, held0[:, x] if even(k) else held0[y])
            if kind == 0 and sub >= WIDE_RING:
                pl.semaphore_wait(credit2.at[sub % 2], 1)
            second_copy(k).start()
            first_copy(k).wait_send()
        if kind in (0, 1, 4) and slot + RINGS[kind % 4] < slots_of[kind % 4]:
            grant(credit0.at[kind % 4], core)

    def after_second(k):
        _, _, held1, held2, held3 = buffers(k)
        kind, slot, sub = plan[k][0], plan[k][1], plan[k][5]
        if kind == 4:
            first_copy(k).wait_recv()
            added(held1, held3[0, :, x] if even(k) else held3[0, y])
            second_copy(k).start()
            return
        second_copy(k).wait_recv()
        mine_part = held1[y] if even(k) else held1[x]
        if kind == 3:
            total = held2[...].astype(jnp.float32) + mine_part.astype(jnp.float32)
            r = slot % 2
            if slot < 2:
                residual[r * mine : r * mine + local_len] += total
                hidden_copy(0, r).start()
            else:
                states_sum[r] = total
            return
        added(held2, mine_part)
        for dz in range(1, nz):
            z_copy(k, dz).start()
        second_copy(k).wait_send()
        if kind == 0 and sub + WIDE_RING < subs_of:
            grant(credit1.at[sub % 2], beside_x if even(k) else beside_y)

    def finish_chunk(k):
        kind, _, pair, col, wide, sub = plan[k]
        if kind == 3:
            return
        _, _, held1, held2, _ = buffers(k)
        if kind == 4:
            second_copy(k).wait_recv()
            mine_part = (held1[y] if even(k) else held1[x]).astype(jnp.float32)
            outs[pair][:, col : col + wide] = held2[...].astype(jnp.float32) + mine_part
            first_copy(k).wait_send()
            second_copy(k).wait_send()
            return
        total = over_z(k, held2[z])
        if kind == 2:
            gain_out[...] = total
        else:
            outs[pair][:, col : col + wide] = total
        sent_z(k)
        if kind == 0 and sub + WIDE_RING < subs_of:
            grant(credit2.at[sub % 2], beside_y if even(k) else beside_x)

    count = len(plan)
    total_ticks = count + LAGS[2] + SLACK

    def tick(t):
        def at_lag(lag, call):
            if 0 <= t - lag < count:
                call(t - lag)

        at_lag(LAGS[2], finish_chunk)
        at_lag(LAGS[1], after_second)
        at_lag(LAGS[0], after_first)
        if t < count:
            make(t)
        if 1 <= t < count + 1:
            after_core(t - 1)

    def fours(body):
        def step(i, carry):
            body(pl.ds(pl.multiple_of(i * 256, 256), 256))
            return carry

        lax.fori_loop(0, width // 256, step, 0)

    def down_back(k):
        need(DOWN + k)
        if k == 0:
            await_all(ffn_loads)
        place_of = (DOWN + k) % 2

        def body(i, carry):
            to = pl.ds(pl.multiple_of(k * width + i * 256, 256), 256)
            product = mm_back(last_low[...], pool[place_of, pl.ds(pl.multiple_of(i * 256, 256), 256)])
            up_back[:, to] = (product * slope[:, to].astype(jnp.float32)).astype(jnp.bfloat16)
            return carry

        lax.fori_loop(0, width // 256, body, 0)
        release(DOWN + k)

    def up_again(k):
        need(UP + k)

        def body(cols):
            residual[:, cols] += mm_back(
                up_back[:, k * width : (k + 1) * width], pool[(UP + k) % 2, cols]
            )

        fours(body)
        release(UP + k)

    def cross_norm_back(part):
        above = residual[part]
        add_rows(gain_total, 1, above * normal[part])
        grad = norm_back(above, normal[part], scale[part][:, 0:1], gains[1:2])
        residual[part] = grad
        cross_low[part] = grad.astype(jnp.bfloat16)

    norm_loads = []

    def cout_back():
        row_tiles(tokens, cross_norm_back)
        norm_loads.append(load(any_normal, normal))
        norm_loads.append(load(any_scale, scale))
        need(COUT)

        def body(cols):
            ccontext_back[:, cols] = mm_back(cross_low[...], pool[COUT % 2, cols]).astype(
                jnp.bfloat16
            )

        fours(body)
        release(COUT)

    def cross(first, last):
        await_all(cross_loads)

        def step(i, carry):
            cross_back_step(
                i // 4, lax.rem(i, 4), lax.rem(i, 4), mine, span, local_len, ccontext_back, cvalues, prob,
                ckeys, cquery, cquery_back, ckey_back, cvalue_back,
            )
            return carry

        lax.fori_loop(first, last, step, 0)
        if last == 4 * rows:
            attend_loads.append(load(any_prob.at[pl.ds(0, 4)], prob))
        elif last % 4 == 0:
            cross_loads.append(load(any_cprob.at[pl.ds(last, 4)], prob))

    def attn_norm_back(part):
        above = residual[part]
        add_rows(gain_total, 0, above * normal[part])
        grad = norm_back(above, normal[part], scale[part][:, 0:1], gains[0:1])
        residual[part] = grad
        attn_low[part] = grad.astype(jnp.bfloat16)

    def cquery_again():
        need(CQUERY)

        def body(cols):
            residual[:, cols] += mm_back(cquery_back[...], pool[CQUERY % 2, cols])

        fours(body)
        release(CQUERY)
        await_all(norm_loads)
        row_tiles(tokens, attn_norm_back)

    def out_back():
        need(OUT)

        def body(cols):
            context_back[:, cols] = mm_back(attn_low[...], pool[OUT % 2, cols]).astype(jnp.bfloat16)

        fours(body)
        release(OUT)
        hot_ref[...] = hot_backward(start, span)
        turn_ref[...] = turning(span)

    def attend(first, last):
        await_all(attend_loads)

        def step(i, carry):
            attend_back_step(
                i // 4, lax.rem(i, 4), lax.rem(i, 4), mine, span, local_len, rows, context_back, query, keys,
                values, prob, prob_own, query_back, key_back, value_back, rel_back,
                hot_ref[...], turn_ref[...],
            )
            return carry

        lax.fori_loop(first, last, step, 0)
        if last < 4 * rows and last % 4 == 0:
            attend_loads.append(load(any_prob.at[pl.ds(last, 4)], prob))

    def into(share, total, cols):
        total = total.astype(jnp.bfloat16)
        for r in range(rows):
            for p in range(4):
                row = r * span + p * local_len
                share[p // 2, p % 2, r, :, cols] = total[row : row + local_len]

    def states_back():
        need(CKEY)
        need(CVALUE)

        def body(cols):
            total = mm_back(ckey_back[...], pool[CKEY % 2, cols])
            into(states_part, total + mm_back(cvalue_back[...], pool[CVALUE % 2, cols]), cols)

        fours(body)
        release(CKEY)
        release(CVALUE)

    def keys_again():
        need(KEY)
        need(VALUE)

        def body(cols):
            total = mm_back(key_back[...], pool[KEY % 2, cols])
            total = total + mm_back(value_back[...], pool[VALUE % 2, cols])
            into(main_part, total[: rows * span], cols)
            for r in range(rows):
                to = r * mine + local_len
                row = rows * span + 2 * r * local_len
                residual[to : to + 2 * local_len, cols] += total[row : row + 2 * local_len]

        fours(body)
        release(KEY)
        release(VALUE)

    def hidden_copy(j, r):
        row = r * mine + j * local_len
        return pltpu.make_async_copy(
            residual.at[pl.ds(row, local_len)], hidden_grad.at[j, r], out_sems.at[j, r]
        )

    def query_again():
        need(QUERY)
        need(REL)
        deep = rel_back.shape[1]

        def body(cols):
            total = mm_back(query_back[...], pool[QUERY % 2, cols])
            residual[:, cols] += total + mm_back(rel_back[...], pool[REL % 2, cols, :deep])

        fours(body)
        for r in range(rows):
            for j in (1, 2):
                hidden_copy(j, r).start()

    ends = {}
    for k, entry in enumerate(plan):
        ends[10 + entry[0] if entry[0] in (2, 3) else entry[2]] = k + 1
    steps_of = range(0, 4 * rows, 2)
    pieces = [(1, functools.partial(down_back, k), ends[0]) for k in range(4)]
    pieces += [(1, functools.partial(up_again, k), ends[1] - 1) for k in range(4)]
    pieces.append((3, cout_back, ends[2]))
    pieces += [(4, functools.partial(cross, i, i + 2), ends[2]) for i in steps_of]
    pieces[-1] = pieces[-1][:2] + (ends[10],)
    pieces.append((2, cquery_again, ends[12]))
    pieces.append((1, out_back, ends[12]))
    pieces += [(5, functools.partial(attend, i, i + 2), ends[12]) for i in steps_of]
    pieces.append((3, states_back, ends[8]))
    pieces.append((5, keys_again, ends[8]))
    pieces.append((2, query_again, count))
    done = {"tick": 0, "spent": 0.0}

    def ticks_to(limit, wanted):
        while done["tick"] < min(limit, wanted):
            tick(done["tick"])
            done["tick"] += 1

    tick(0)
    done["tick"] = 1
    for cost, call, limit in pieces:
        call()
        done["spent"] += cost
        ticks_to(limit, 1 + int(done["spent"] / 3.5))
    ticks_to(total_ticks, total_ticks)
    for k in range(count):
        if plan[k][0] != 3 and k not in followed:
            core_copy(k).wait_send()
        if plan[k][0] == 3:
            second_copy(k).wait_send()
    for j in range(3):
        for r in range(rows):
            hidden_copy(j, r).wait()


def back(values, weights, shape, ndp):
    nz = ndp // 2
    low, wide = jnp.bfloat16, jnp.float32
    rows, local_len, width = shape[1:]
    tokens, span = 3 * rows * local_len, 4 * local_len
    every = rows * (span + 2 * local_len)
    ff = weights[0].shape[0]
    ndev = 8 * nz
    heights = [ff, width, width, width, width, width, width, width, width, width, width]
    wides = [width, ff, width, width, width, width, width // 2, width, width, width, width]
    plan, slots, subs, at = [], [0, 0], [0, 0], 0
    for pair in (0, 1, 2, 3, 9, 10, 4, 5, 6, 7, 8):
        kind = int(heights[pair] > width)
        step = (512, 128)[kind]
        for col in range(0, wides[pair], step):
            if kind:
                plan.append((1, slots[1], pair, col, step, slots[1]))
            else:
                deep = at in DEEP
                plan.append((4 if deep else 0, slots[0], pair, col, step, subs[deep]))
                subs[deep] += 1
                at += 1
            slots[kind] += 1
        if pair == 4:
            plan.append((2, 0, 0, 0, 128, 0))
    plan += [(3, i, 0, 0, 0, i) for i in range(4)]
    n = len(plan)
    tails = [((width // ndev, 512), low), ((ff // ndev, 128), low), ((8, 128), wide)]
    counts = [
        (RINGS[0], WIDE_RING, WIDE_RING, subs[0]),
        (RINGS[1], slots[1], slots[1], slots[1]),
        (1, 1, 1, 1),
    ]
    leads = [(2, 2, nz), (2, nz), (nz,), (nz - 1,)]
    held = [
        pltpu.VMEM((counts[kind][stage],) + leads[stage] + tails[kind][0], tails[kind][1])
        for stage in range(4)
        for kind in range(3)
    ]
    parts = [pltpu.VMEM((2, 2, 2, nz, 2) + tails[kind][0], low) for kind in range(2)]
    share = (local_len, width)
    main = pltpu.VMEM((rows * span, width), low)
    token = pltpu.VMEM((tokens, width), low)
    fat = pltpu.VMEM((tokens, ff), low)
    all_rows = pltpu.VMEM((every, width), low)
    token_wide = pltpu.VMEM((tokens, width), wide)
    scratch = [fat, token, token_wide, fat, token, token_wide]
    scratch += [pltpu.VMEM((tokens, 128), wide), token, token, token, main, main]
    scratch += [pltpu.VMEM((4, 12 * local_len, span), low), token, all_rows, all_rows, token]
    scratch += [pltpu.VMEM((16, width), wide), pltpu.VMEM((3, 8, width), wide), token, main, main]
    scratch += [token, token, all_rows, all_rows, pltpu.VMEM((tokens, width // 2), low)]
    scratch += [pltpu.VMEM((2, 2, rows) + share, low)] * 2
    scratch += [pltpu.VMEM((2, width, width), low)]
    scratch += [pltpu.VMEM((span, 128), low), pltpu.VMEM((span, span), low)]
    scratch += parts + held
    scratch += [pltpu.VMEM((2, 2, nz, 2, 8, 128), wide)]
    scratch += [pltpu.VMEM((4, 2) + share, low), pltpu.VMEM((4,) + share, low)]
    scratch += [
        pltpu.VMEM((max(1, subs[1]),) + lead + tails[0][0], low) for lead in ((nz - 1, 2, 2), (2,), ())
    ]
    scratch += [
        pltpu.SemaphoreType.DMA((32,)),
        pltpu.SemaphoreType.DMA((17,)),
        pltpu.SemaphoreType.DMA((3, rows)),
        pltpu.SemaphoreType.DMA((n, 2 + nz)),
        pltpu.SemaphoreType.DMA((n, 2 + nz)),
        pltpu.SemaphoreType.REGULAR((2,)),
        pltpu.SemaphoreType.REGULAR((2,)),
        pltpu.SemaphoreType.REGULAR((2,)),
    ]
    anywhere = pl.BlockSpec(memory_space=pl.ANY)
    vmem = pl.BlockSpec(memory_space=pltpu.VMEM)
    outs = [jax.ShapeDtypeStruct((h // ndev, w), wide) for h, w in zip(heights, wides)]
    outs.append(jax.ShapeDtypeStruct((8, 128), wide))
    outs.append(jax.ShapeDtypeStruct((rows,) + share, wide))
    outs.append(jax.ShapeDtypeStruct(shape, wide))
    return pl.pallas_call(
        lambda *refs: back_kernel(plan, nz, rows, local_len, len(heights), *refs),
        out_shape=outs,
        in_specs=[anywhere] * (len(values) + len(weights)),
        out_specs=[vmem] * (len(outs) - 1) + [anywhere],
        scratch_shapes=scratch,
        compiler_params=pltpu.CompilerParams(
            collective_id=1, has_side_effects=True, vmem_limit_bytes=62 * 2**20
        ),
        name="back",
    )(*values, *weights)


def finish_kernel(count, *refs):
    sources, targets, held = refs[:count], refs[count : 2 * count], refs[2 * count : 3 * count]
    sems = refs[3 * count]
    ins = [pltpu.make_async_copy(sources[i], held[i], sems.at[0, i]) for i in range(count)]
    outs = [pltpu.make_async_copy(held[i], targets[i], sems.at[1, i]) for i in range(count)]
    for copy in ins:
        copy.start()
    for copy_in, copy_out in zip(ins, outs):
        copy_in.wait()
        copy_out.start()
    for copy in outs:
        copy.wait()


def finish(sums, hidden_grad, states_sum):
    arrays = (*sums, hidden_grad, states_sum)
    count = len(arrays)
    return pl.pallas_call(
        lambda *refs: finish_kernel(count, *refs),
        out_shape=[jax.ShapeDtypeStruct(a.shape, a.dtype) for a in arrays],
        in_specs=[pl.BlockSpec(memory_space=pl.ANY)] * count,
        out_specs=[pl.BlockSpec(memory_space=pl.ANY)] * count,
        scratch_shapes=[pltpu.VMEM(a.shape, a.dtype) for a in arrays]
        + [pltpu.SemaphoreType.DMA((2, count))],
        compiler_params=pltpu.CompilerParams(vmem_limit_bytes=62 * 2**20),
        name="finish",
    )(*arrays)


def plain_call(kernel, name, ins, spaces, outs, scratch, flops):
    space = {"v": pltpu.VMEM, "s": pltpu.SMEM, "a": pl.ANY}
    out_shape = [jax.ShapeDtypeStruct(shape, kind) for shape, kind in outs]
    moved = sum(a.size * a.dtype.itemsize for a in list(ins) + out_shape)
    return pl.pallas_call(
        kernel,
        out_shape=out_shape,
        in_specs=[pl.BlockSpec(memory_space=space[p]) for p in spaces],
        out_specs=[pl.BlockSpec(memory_space=pltpu.VMEM)] * len(outs),
        scratch_shapes=scratch,
        compiler_params=pltpu.CompilerParams(vmem_limit_bytes=62 * 2**20),
        cost_estimate=pl.CostEstimate(flops=flops, bytes_accessed=moved, transcendentals=0),
        name=name,
    )(*ins)


def copies_of(arrays):
    return [pltpu.VMEM(a.shape, a.dtype) for a in arrays] + [
        pltpu.SemaphoreType.DMA((len(arrays),))
    ]


def local(
    hidden,
    encoder,
    lengths,
    enc_lengths,
    w_query,
    w_key,
    w_value,
    w_attn_out,
    w_relative,
    w_cross_query,
    w_cross_key,
    w_cross_value,
    w_cross_out,
    w_up,
    w_down,
    gain_attn,
    gain_cross,
    gain_ffn,
    cotangent,
):
    ndp, chips = lax.axis_size("dp"), lax.axis_size("seq")
    devices = ndp * chips
    low, wide = jnp.bfloat16, jnp.float32
    _, rows, local_len, width = hidden.shape
    span, tokens = local_len * chips, 3 * rows * local_len
    weights = (
        w_key,
        w_value,
        w_query,
        w_relative,
        w_cross_key,
        w_cross_value,
        w_attn_out,
        w_cross_query,
        w_cross_out,
        w_up,
        w_down,
    )
    gains = jnp.stack([gain_attn, gain_cross, gain_ffn])
    every = rows * (span + 2 * local_len)
    kernels = chips == 4 and w_query.shape[0] == 128 and w_down.shape[0] == 512
    if kernels:
        gains = jnp.pad(gains, ((0, 13), (0, 0)))
        results = layer(
            (gains,) + weights, hidden, encoder, cotangent, lengths, enc_lengths, ndp
        )
        whole, results = results[1 : len(weights) + 1], results[len(weights) + 1 :]
        whole = [w.reshape(-1, w.shape[-1]) for w in whole]
        (hid, x_all, query, keys, values, prob, prob_own, context, ckeys, cvalues) = results[:10]
        (normal, normal_scale, normed_low, cquery, cprob, ccontext, output) = results[10:17]
        (crossed_low, activated, last_low, slope, gain_total, normal2, scale2) = results[17:24]
        (states, gains, grad) = results[24:]
        states = states.reshape(-1, width)
    else:
        gains = jnp.pad(gains, ((0, 5), (0, 0)))
        whole = [lax.all_gather(w, "dp", axis=0, tiled=True) for w in weights]
        gains = lax.all_gather(gains, "dp", axis=1, tiled=True).astype(wide)
        mains = lax.all_gather(hidden[0], "seq", axis=1).reshape(-1, width)
        states = lax.all_gather(encoder, "seq", axis=1).reshape(-1, width)
    (
        full_key,
        full_value,
        full_query,
        full_relative,
        full_ckey,
        full_cvalue,
        full_attn_out,
        full_cquery,
        full_cout,
        full_up,
        full_down,
    ) = whole
    if not kernels:
        ff = full_up.shape[1]
        fetched = (
            full_key,
            full_value,
            full_query,
            full_relative,
            full_ckey,
            full_cvalue,
            full_attn_out,
            full_cquery,
        )
        (
            hid,
            x_all,
            query,
            keys,
            values,
            prob,
            prob_own,
            context,
            ckeys,
            cvalues,
            normal,
            normal_scale,
            normed_low,
            cquery,
            cprob,
            ccontext,
        ) = plain_call(
            lambda *refs: forward_kernel(rows, local_len, *refs),
            "forward_attention",
            (hidden, mains, states, lengths, enc_lengths, gains) + fetched,
            "vvvssv" + "a" * len(fetched),
            [
                ((tokens, width), low),
                ((every, width), low),
                ((tokens, width), low),
                ((every, width), low),
                ((every, width), low),
                ((4 * rows, 12 * local_len, span), low),
                ((tokens, width), low),
                ((tokens, width), low),
                ((rows * span, width), low),
                ((rows * span, width), low),
                ((tokens, width), wide),
                ((tokens, 128), wide),
                ((tokens, width), low),
                ((tokens, width), low),
                ((4 * rows, 12 * local_len, span), low),
                ((tokens, width), low),
            ],
            [
                pltpu.VMEM((tokens, full_relative.shape[1]), low),
                pltpu.VMEM((tokens, width), wide),
            ]
            + copies_of(fetched),
            12 * 10**9,
        )
        fetched = (full_cout, full_up, full_down)
        (
            output,
            crossed_low,
            activated,
            last_low,
            up_back,
            cross_grad,
            cross_low,
            ccontext_back,
            gain_middle,
        ) = plain_call(
            lambda *refs: middle_kernel(rows, local_len, *refs),
            "feed_forward",
            (normal, ccontext, gains, cotangent) + fetched,
            "vvvv" + "a" * len(fetched),
            [
                (hidden.shape, low),
                ((tokens, width), low),
                ((tokens, ff), low),
                ((tokens, width), low),
                ((tokens, ff), low),
                ((tokens, width), wide),
                ((tokens, width), low),
                ((tokens, width), low),
                ((3, 8, width), wide),
            ],
            [
                pltpu.VMEM((tokens, width), wide),
                pltpu.VMEM((tokens, 128), wide),
                pltpu.VMEM((tokens, ff), low),
                pltpu.VMEM((tokens, width), wide),
            ]
            + copies_of(fetched),
            14 * 10**9,
        )
    if kernels:
        values_in = (
            activated, last_low, grad, slope, crossed_low, normal2, scale2, normal, normal_scale,
            ccontext, normed_low, context, hid, x_all, states, cquery, ckeys, cvalues, cprob,
            query, keys, values, prob, prob_own, gains, gain_total,
        )
        weights_in = (
            full_down, full_up, full_cout, full_cquery, full_attn_out, full_ckey, full_cvalue,
            full_key, full_value, full_query, full_relative,
        )
        *sums, gain_sums, states_sum, hidden_grad = back(values_in, weights_in, hidden.shape, ndp)
        gain_sums = gain_sums[:3, : width // devices]
        *sums, output, hidden_grad, states_sum = finish(sums + [output], hidden_grad, states_sum)
    else:
        fetched = (
            full_cquery,
            full_attn_out,
            full_ckey,
            full_cvalue,
            full_query,
            full_relative,
            full_key,
            full_value,
        )
        (
            cquery_back,
            ckey_back,
            cvalue_back,
            attn_low,
            query_back,
            key_back,
            value_back,
            rel_back,
            hidden_own,
            main_part,
            states_part,
            gain_back,
        ) = plain_call(
            lambda *refs: backward_kernel(rows, local_len, *refs),
            "backward_attention",
            (
                ccontext_back,
                cross_grad,
                cquery,
                ckeys,
                cvalues,
                cprob,
                normal,
                normal_scale,
                gains,
                query,
                keys,
                values,
                prob,
                prob_own,
            )
            + fetched,
            "v" * 14 + "a" * len(fetched),
            [
                ((tokens, width), low),
                ((rows * span, width), low),
                ((rows * span, width), low),
                ((tokens, width), low),
                ((tokens, width), low),
                ((every, width), low),
                ((every, width), low),
                ((tokens, full_relative.shape[1]), low),
                (hidden.shape, wide),
                ((chips, rows, local_len, width), low),
                ((chips, rows, local_len, width), low),
                ((3, 8, width), wide),
            ],
            [pltpu.VMEM((tokens, width), wide), pltpu.VMEM((tokens, width), low)] + copies_of(fetched),
            14 * 10**9,
        )
        xs = [activated, crossed_low, ccontext, normed_low, context, hid, x_all, states]
        gs = [
            last_low,
            up_back,
            cross_low,
            cquery_back,
            attn_low,
            query_back,
            rel_back,
            key_back,
            value_back,
            ckey_back,
            cvalue_back,
        ]
        pairs = [(0, 0), (1, 1), (2, 2), (3, 3), (4, 4), (5, 5), (5, 6), (6, 7), (6, 8), (7, 9), (7, 10)]
        gain_parts = jnp.sum(gain_middle + gain_back, axis=1)
        sums = [
            lax.psum_scatter(
                weight_grad(xs[i], gs[j]), ("seq", "dp"), scatter_dimension=0, tiled=True
            )
            for i, j in pairs
        ]
        gain_sums = lax.psum_scatter(gain_parts, ("seq", "dp"), scatter_dimension=1, tiled=True)
        main_sum, states_sum = (
            lax.psum_scatter(part, "seq", scatter_dimension=0).astype(wide)
            for part in (main_part, states_part)
        )
        hidden_grad = hidden_own.at[0].add(main_sum)
    gainattn_sum, gaincross_sum, gainffn_sum = gain_sums
    (
        down_sum,
        up_sum,
        cout_sum,
        cquery_sum,
        outproj_sum,
        query_sum,
        relative_sum,
        keyw_sum,
        valuew_sum,
        ckey_sum,
        cvalue_sum,
    ) = sums
    return (
        output,
        hidden_grad,
        states_sum,
        query_sum,
        keyw_sum,
        valuew_sum,
        outproj_sum,
        relative_sum,
        cquery_sum,
        ckey_sum,
        cvalue_sum,
        cout_sum,
        up_sum,
        down_sum,
        gainattn_sum,
        gaincross_sum,
        gainffn_sum,
    )


def solution(mesh):
    in_specs = (
        P(None, "dp", "seq", None),
        P("dp", "seq", None),
        P("dp"),
        P("dp"),
        P("dp", None),
        P("dp", None),
        P("dp", None),
        P("dp", None),
        P("dp", None),
        P("dp", None),
        P("dp", None),
        P("dp", None),
        P("dp", None),
        P("dp", None),
        P("dp", None),
        P("dp"),
        P("dp"),
        P("dp"),
        P(None, "dp", "seq", None),
    )
    out_specs = (
        P(None, "dp", "seq", None),
        P(None, "dp", "seq", None),
        P("dp", "seq", None),
        P(("seq", "dp"), None),
        P(("seq", "dp"), None),
        P(("seq", "dp"), None),
        P(("seq", "dp"), None),
        P(("seq", "dp"), None),
        P(("seq", "dp"), None),
        P(("seq", "dp"), None),
        P(("seq", "dp"), None),
        P(("seq", "dp"), None),
        P(("seq", "dp"), None),
        P(("seq", "dp"), None),
        P(("seq", "dp")),
        P(("seq", "dp")),
        P(("seq", "dp")),
    )
    return jax.shard_map(local, mesh=mesh, in_specs=in_specs, out_specs=out_specs, check_vma=False)
```

```python
import functools
import math

import jax
import jax.numpy as jnp
from jax import lax
from jax.experimental import pallas as pl
from jax.experimental.pallas import tpu as pltpu
from jax.sharding import PartitionSpec as P

MESH = pl.DeviceIdType.MESH

HEADS = 16
HEAD_DIM = 64
BUCKETS = 32


eps_norm = 1e-05
bucket_edges = [step_index for step_index in range(1, 16)] + [
    int(math.ceil(16 * 8 ** ((step_index - 16) / 16))) for step_index in range(16, 32)
]


def flatten_rows(array):
    return array.reshape(-1, array.shape[-1])


def weight_grad(array, grad_rows):
    return jnp.einsum(
        "nd,ne->de",
        flatten_rows(array),
        flatten_rows(grad_rows),
        preferred_element_type=jnp.float32,
    )


def remote(src, dst, send, recv, to):
    return pltpu.make_async_remote_copy(
        src_ref=src, dst_ref=dst, send_sem=send, recv_sem=recv, device_id=to, device_id_type=MESH
    )


def place():
    s = lax.axis_index("seq")
    d = lax.axis_index("dp")
    z, c = d // 2, lax.rem(d, 2)
    sx = s + 1 - 2 * lax.rem(s, 2)
    sy = lax.rem(s + 2, 4)
    return s, z, c, sx, sy


def greet(nz):
    s, z, c, sx, sy = place()
    barrier = pltpu.get_barrier_semaphore()
    dests = [(s, 2 * z + 1 - c), (sx, 2 * z + c), (sy, 2 * z + c)]
    for dz in range(1, nz):
        dests.append((s, 2 * lax.rem(z + dz, nz) + c))
    for dest in dests:
        pl.semaphore_signal(barrier, inc=1, device_id=dest, device_id_type=MESH)
    pl.semaphore_wait(barrier, len(dests))


NEG = -1000000000.0


def mm(left, right):
    return jnp.dot(left, right, preferred_element_type=jnp.float32)


def mm_back(left, right):
    return lax.dot_general(
        left, right, (((1,), (1,)), ((), ())), preferred_element_type=jnp.float32
    )


def mm_grad(left, right):
    return lax.dot_general(
        left, right, (((0,), (0,)), ((), ())), preferred_element_type=jnp.float32
    )


def tiles(width, body):
    def step(i, carry):
        body(pl.ds(pl.multiple_of(i * 256, 256), 256))
        return carry

    lax.fori_loop(0, width // 256, step, 0)


def row_tiles(rows, body, step_rows=64):
    def step(i, carry):
        body(pl.ds(pl.multiple_of(i * step_rows, step_rows), step_rows))
        return carry

    lax.fori_loop(0, rows // step_rows, step, 0)


def heads_in(tile):
    lane = lax.broadcasted_iota(jnp.int32, tile.shape, 1) // (tile.shape[1] // 4)
    return jnp.concatenate(
        [jnp.where(lane == h, tile, jnp.zeros_like(tile)) for h in range(4)], axis=0
    )


def heads_out(stacked):
    n, wide = stacked.shape[0] // 4, stacked.shape[1]
    lane = lax.broadcasted_iota(jnp.int32, (n, wide), 1) // (wide // 4)
    result = stacked[3 * n :]
    for h in (2, 1, 0):
        result = jnp.where(lane == h, stacked[h * n : (h + 1) * n], result)
    return result


def head_lanes(columns, wide):
    n = columns[0].shape[0]
    lane = lax.broadcasted_iota(jnp.int32, (n, wide), 1) // (wide // 4)
    result = jnp.broadcast_to(columns[3], (n, wide))
    for h in (2, 1, 0):
        result = jnp.where(lane == h, jnp.broadcast_to(columns[h], (n, wide)), result)
    return result


def head_sums(product):
    n, wide = product.shape
    lane = lax.broadcasted_iota(jnp.int32, (n, wide), 1) // (wide // 4)
    return [
        jnp.sum(jnp.where(lane == h, product, 0.0), axis=1, keepdims=True) for h in range(4)
    ]


def bucket_of(distance):
    total = jnp.zeros_like(distance)
    for edge in bucket_edges:
        total = total + (distance >= edge).astype(jnp.int32)
    return total


def hot_forward(start, span):
    lag = lax.broadcasted_iota(jnp.int32, (128, span), 1)
    row = lax.rem(lax.broadcasted_iota(jnp.int32, (128, span), 0), BUCKETS)
    distance = lax.rem(start - lag + span, span)
    return jnp.where(bucket_of(distance) == row, 1.0, 0.0).astype(jnp.bfloat16)


def hot_backward(start, span):
    lag = lax.broadcasted_iota(jnp.int32, (span, 128), 0)
    column = lax.rem(lax.broadcasted_iota(jnp.int32, (span, 128), 1), BUCKETS)
    distance = lax.rem(start + lag + 1, span)
    return jnp.where(bucket_of(distance) == column, 1.0, 0.0).astype(jnp.bfloat16)


def skewed(array, block):
    return jnp.concatenate(
        [
            pltpu.roll(array[i : i + block], 0, 1, stride=1, stride_axis=0)
            for i in range(0, array.shape[0], block)
        ],
        axis=0,
    )


def norm_rows(values):
    centred = values - jnp.mean(values, axis=1, keepdims=True)
    scale = lax.rsqrt(jnp.mean(centred * centred, axis=1, keepdims=True) + eps_norm)
    return centred * scale, scale


def norm_back(grad, normal, scale, gain):
    grad = grad * gain
    return scale * (
        grad
        - jnp.mean(grad, axis=1, keepdims=True)
        - normal * jnp.mean(grad * normal, axis=1, keepdims=True)
    )


def add_rows(total_ref, index, product):
    total_ref[index] += jnp.sum(product.reshape(-1, 8, product.shape[1]), axis=0)


class Fetch:
    def __init__(self, sources, targets, sems):
        self.copies = [
            pltpu.make_async_copy(src, dst, sems.at[i])
            for i, (src, dst) in enumerate(zip(sources, targets))
        ]
        self.targets = targets
        self.waited = set()
        for copy in self.copies:
            copy.start()

    def __getitem__(self, i):
        if i not in self.waited:
            self.waited.add(i)
            self.copies[i].wait()
        return self.targets[i]


def attend_step(
    r, g, step, start, mine, span, local_len, rows, lengths, query, rel, keys, values, prob, prob_own, context, hot
):
    cols = pl.ds(pl.multiple_of(g * 256, 256), 256)
    own_rows = pl.ds(pl.multiple_of(r * mine, local_len), mine)
    main_rows = pl.ds(pl.multiple_of(r * span, span), span)
    side_rows = pl.ds(pl.multiple_of(rows * span + r * 2 * local_len, local_len), 2 * local_len)
    q_tile = query[own_rows, cols]
    rel_tile = rel[own_rows, pl.ds(pl.multiple_of(g * 128, 128), 128)]
    side_key = keys[side_rows, cols].astype(jnp.float32)
    side_value = values[side_rows, cols].astype(jnp.float32)
    zero = jnp.zeros((local_len, 256), jnp.float32)
    scores = mm_back(heads_in(q_tile), keys[main_rows, cols])
    bias = skewed(mm(heads_in(rel_tile), hot), local_len)
    products = q_tile.astype(jnp.float32) * jnp.concatenate([zero, side_key], axis=0)
    own_dot = head_sums(products)
    rel_lane = lax.broadcasted_iota(jnp.int32, (mine, 128), 1)
    rel_wide = rel_tile.astype(jnp.float32)
    row = lax.broadcasted_iota(jnp.int32, (mine, span), 0)
    at = lax.broadcasted_iota(jnp.int32, (mine, span), 1)
    ahead = start + lax.rem(row, local_len) + jnp.where(row < local_len, 1, 0)
    kept = (at < ahead) & (at < lengths[r])
    first = lax.broadcasted_iota(jnp.int32, (mine, 1), 0) < local_len
    low, owns = [], []
    for h in range(4):
        part = slice(h * mine, (h + 1) * mine)
        score = jnp.where(kept, scores[part] + bias[part], NEG)
        near = jnp.sum(jnp.where(rel_lane == h * BUCKETS, rel_wide, 0.0), axis=1, keepdims=True)
        own = jnp.where(first, NEG, own_dot[h] + near)
        peak = jnp.maximum(jnp.max(score, axis=1, keepdims=True), own)
        power = jnp.exp(score - peak)
        own_power = jnp.exp(own - peak)
        share = 1.0 / (jnp.sum(power, axis=1, keepdims=True) + own_power)
        low.append((power * share).astype(jnp.bfloat16))
        owns.append(own_power * share)
    low = jnp.concatenate(low, axis=0)
    prob[step] = low
    spread = head_lanes(owns, 256)
    prob_own[own_rows, cols] = spread.astype(prob_own.dtype)
    total = heads_out(mm(low, values[main_rows, cols]))
    total = total + spread * jnp.concatenate([zero, side_value], axis=0)
    context[own_rows, cols] = total.astype(context.dtype)


def cross_step(
    r, g, step, mine, span, local_len, enc_lengths, cquery, ckeys, cvalues, cprob, ccontext
):
    cols = pl.ds(pl.multiple_of(g * 256, 256), 256)
    own_rows = pl.ds(pl.multiple_of(r * mine, local_len), mine)
    main_rows = pl.ds(pl.multiple_of(r * span, span), span)
    scores = mm_back(heads_in(cquery[own_rows, cols]), ckeys[main_rows, cols])
    at = lax.broadcasted_iota(jnp.int32, (mine, span), 1)
    kept = at < enc_lengths[r]
    low = []
    for h in range(4):
        score = jnp.where(kept, scores[h * mine : (h + 1) * mine], NEG)
        power = jnp.exp(score - jnp.max(score, axis=1, keepdims=True))
        share = 1.0 / jnp.sum(power, axis=1, keepdims=True)
        low.append((power * share).astype(jnp.bfloat16))
    low = jnp.concatenate(low, axis=0)
    cprob[step] = low
    ccontext[own_rows, cols] = heads_out(mm(low, cvalues[main_rows, cols])).astype(
        ccontext.dtype
    )


def forward_kernel(rows, local_len, *refs):
    (
        hidden,
        mains,
        states,
        lengths,
        enc_lengths,
        gains,
        *weights,
    ) = refs[:14]
    (hid, x_all, query, keys, values, prob, prob_own, context, ckeys, cvalues) = refs[14:24]
    (normal, normal_scale, normed_low, cquery, cprob, ccontext) = refs[24:30]
    rel, residual = refs[30:32]
    fetch = Fetch(weights, refs[32:40], refs[40])
    w_key, w_value, w_query, w_relative, w_ckey, w_cvalue, w_out, w_cquery = range(8)
    width = hid.shape[1]
    mine = 3 * local_len
    span = mains.shape[0] // rows
    start = lax.axis_index("seq") * local_len
    x_all[: rows * span] = mains[...]
    for r in range(rows):
        for j in range(3):
            tile = hidden[j, r]
            hid[r * mine + j * local_len : r * mine + (j + 1) * local_len] = tile
            if j:
                at = rows * span + (2 * r + j - 1) * local_len
                x_all[at : at + local_len] = tile

    def project(left, w, target, scale=None):
        weight = fetch[w]

        def body(cols):
            product = mm(left[...], weight[:, cols])
            if scale is not None:
                product = product * scale
            target[:, cols] = product.astype(target.dtype)

        tiles(target.shape[1], body)

    project(x_all, w_key, keys)
    project(x_all, w_value, values)
    project(hid, w_query, query, 0.125)
    project(hid, w_relative, rel)
    hot = hot_forward(start, span)

    def attend(step, carry):
        attend_step(
            step // 4, lax.rem(step, 4), step, start, mine, span, local_len, rows, lengths,
            query, rel, keys, values, prob, prob_own, context, hot,
        )
        return carry

    lax.fori_loop(0, 4 * rows, attend, 0)
    project(states, w_ckey, ckeys)
    project(states, w_cvalue, cvalues)
    weight_out = fetch[w_out]

    def out_body(cols):
        residual[:, cols] = hid[:, cols].astype(jnp.float32) + mm(context[...], weight_out[:, cols])

    tiles(width, out_body)

    def norm_body(part):
        normal[part], scale = norm_rows(residual[part])
        normal_scale[part] = jnp.broadcast_to(scale, (scale.shape[0], 128))
        normed_low[part] = (normal[part] * gains[0:1]).astype(jnp.bfloat16)

    row_tiles(hid.shape[0], norm_body)
    project(normed_low, w_cquery, cquery, 0.125)

    def cross(step, carry):
        cross_step(
            step // 4, lax.rem(step, 4), step, mine, span, local_len, enc_lengths,
            cquery, ckeys, cvalues, cprob, ccontext,
        )
        return carry

    lax.fori_loop(0, 4 * rows, cross, 0)


def middle_kernel(
    rows,
    local_len,
    normal,
    ccontext,
    gains,
    cotangent,
    any_cout,
    any_up,
    any_down,
    output,
    crossed_low,
    activated,
    last_low,
    up_back,
    cross_grad,
    cross_low,
    ccontext_back,
    gain_total,
    normal2,
    scale2,
    slope,
    residual,
    v_cout,
    v_up,
    v_down,
    sems,
):
    fetch = Fetch((any_cout, any_up, any_down), (v_cout, v_up, v_down), sems)
    tokens, width = normal.shape
    mine = 3 * local_len
    gain_total[...] = jnp.zeros_like(gain_total)
    weight_cout = fetch[0]

    def cross_body(cols):
        residual[:, cols] = normal[:, cols] * gains[0:1, cols] + mm(
            ccontext[...], weight_cout[:, cols]
        )

    tiles(width, cross_body)

    def norm_body(part):
        normal2[part], scale = norm_rows(residual[part])
        scale2[part] = jnp.broadcast_to(scale, (scale.shape[0], 128))
        crossed_low[part] = (normal2[part] * gains[1:2]).astype(jnp.bfloat16)

    row_tiles(tokens, norm_body)
    weight_up = fetch[1]

    def up_body(cols):
        value = mm(crossed_low[...], weight_up[:, cols])
        below = 0.5 + 0.5 * lax.erf(value * (0.5**0.5))
        activated[:, cols] = (value * below).astype(jnp.bfloat16)
        density = jnp.exp(-0.5 * value * value) * (1.0 / math.sqrt(2.0 * math.pi))
        slope[:, cols] = (below + value * density).astype(jnp.bfloat16)

    tiles(activated.shape[1], up_body)
    weight_down = fetch[2]

    def down_body(cols):
        residual[:, cols] = normal2[:, cols] * gains[1:2, cols] + mm(
            activated[...], weight_down[:, cols]
        )

    tiles(width, down_body)
    for r in range(rows):
        for j in range(3):
            at = r * mine + j * local_len
            part = slice(at, at + local_len)
            normal3, scale = norm_rows(residual[part])
            output[j, r] = (normal3 * gains[2:3]).astype(output.dtype)
            above = cotangent[j, r].astype(jnp.float32)
            add_rows(gain_total, 2, above * normal3)
            grad = norm_back(above, normal3, scale, gains[2:3])
            residual[part] = grad
            last_low[part] = grad.astype(jnp.bfloat16)

    def down_back(cols):
        product = mm_back(last_low[...], weight_down[cols, :])
        up_back[:, cols] = (product * slope[:, cols].astype(jnp.float32)).astype(jnp.bfloat16)

    tiles(activated.shape[1], down_back)

    def up_back_body(cols):
        residual[:, cols] = residual[:, cols] + mm_back(up_back[...], weight_up[cols, :])

    tiles(width, up_back_body)

    def cross_norm_back(part):
        above = residual[part]
        add_rows(gain_total, 1, above * normal2[part])
        grad = norm_back(above, normal2[part], scale2[part][:, 0:1], gains[1:2])
        cross_grad[part] = grad
        cross_low[part] = grad.astype(jnp.bfloat16)

    row_tiles(tokens, cross_norm_back)

    def cout_back(cols):
        ccontext_back[:, cols] = mm_back(cross_low[...], weight_cout[cols, :]).astype(jnp.bfloat16)

    tiles(width, cout_back)


def turning(span):
    return jnp.where(
        lax.broadcasted_iota(jnp.int32, (span, span), 0)
        + lax.broadcasted_iota(jnp.int32, (span, span), 1)
        == span - 1,
        1.0,
        0.0,
    ).astype(jnp.bfloat16)


def cross_back_step(
    r, g, step, mine, span, local_len, ccontext_back, cvalues, cprob, ckeys, cquery, cquery_back, ckey_back, cvalue_back
):
    cols = pl.ds(pl.multiple_of(g * 256, 256), 256)
    own_rows = pl.ds(pl.multiple_of(r * mine, local_len), mine)
    main_rows = pl.ds(pl.multiple_of(r * span, span), span)
    above = heads_in(ccontext_back[own_rows, cols])
    grads = mm_back(above, cvalues[main_rows, cols])
    low = []
    for h in range(4):
        part = slice(h * mine, (h + 1) * mine)
        share = cprob[step, part].astype(jnp.float32)
        weighted = share * grads[part]
        low.append(
            (weighted - share * jnp.sum(weighted, axis=1, keepdims=True)).astype(jnp.bfloat16)
        )
    low = jnp.concatenate(low, axis=0)
    back = heads_out(mm(low, ckeys[main_rows, cols])).astype(jnp.bfloat16)
    cquery_back[own_rows, cols] = back * jnp.bfloat16(0.125)
    ckey_back[main_rows, cols] = mm_grad(low, heads_in(cquery[own_rows, cols])).astype(
        jnp.bfloat16
    )
    cvalue_back[main_rows, cols] = mm_grad(cprob[step], above).astype(jnp.bfloat16)


def attend_back_step(
    r, g, step, mine, span, local_len, rows, context_back, query, keys, values, prob, prob_own,
    query_back, key_back, value_back, rel_back, hot, turn
):
    cols = pl.ds(pl.multiple_of(g * 256, 256), 256)
    own_rows = pl.ds(pl.multiple_of(r * mine, local_len), mine)
    main_rows = pl.ds(pl.multiple_of(r * span, span), span)
    side_rows = pl.ds(pl.multiple_of(rows * span + r * 2 * local_len, local_len), 2 * local_len)
    above_tile = context_back[own_rows, cols]
    above = heads_in(above_tile)
    above_wide = above_tile.astype(jnp.float32)
    q_tile = query[own_rows, cols]
    zero = jnp.zeros((local_len, 256), jnp.float32)
    side_key = jnp.concatenate([zero, keys[side_rows, cols].astype(jnp.float32)], axis=0)
    side_value = jnp.concatenate([zero, values[side_rows, cols].astype(jnp.float32)], axis=0)
    spread = prob_own[own_rows, cols].astype(jnp.float32)
    grads = mm_back(above, values[main_rows, cols])
    own_grads = head_sums(above_wide * side_value)
    low, own_low = [], []
    for h in range(4):
        part = slice(h * mine, (h + 1) * mine)
        share = prob[step, part].astype(jnp.float32)
        own_share = spread[:, h * 64 : h * 64 + 1]
        weighted = share * grads[part]
        delta = jnp.sum(weighted, axis=1, keepdims=True) + own_share * own_grads[h]
        low.append((weighted - share * delta).astype(jnp.bfloat16))
        own_low.append(own_share * (own_grads[h] - delta))
    low = jnp.concatenate(low, axis=0)
    own_spread = head_lanes(own_low, 256)
    back = heads_out(mm(low, keys[main_rows, cols])) + own_spread * side_key
    query_back[own_rows, cols] = back.astype(jnp.bfloat16) * jnp.bfloat16(0.125)
    key_back[main_rows, cols] = mm_grad(low, heads_in(q_tile)).astype(jnp.bfloat16)
    value_back[main_rows, cols] = mm_grad(prob[step], above).astype(jnp.bfloat16)
    key_back[side_rows, cols] = (own_spread * q_tile.astype(jnp.float32))[local_len:].astype(
        jnp.bfloat16
    )
    value_back[side_rows, cols] = (spread * above_wide)[local_len:].astype(jnp.bfloat16)
    turned_low = skewed(mm(low, turn), local_len).astype(jnp.bfloat16)
    rel_total = heads_out(mm(turned_low, hot))
    near = lax.rem(lax.broadcasted_iota(jnp.int32, rel_total.shape, 1), BUCKETS) == 0
    rel_total = rel_total + jnp.where(near, head_lanes(own_low, 128), 0.0)
    rel_back[own_rows, pl.ds(pl.multiple_of(g * 128, 128), 128)] = rel_total.astype(
        jnp.bfloat16
    )


def backward_kernel(rows, local_len, *refs):
    (
        ccontext_back,
        cross_grad,
        cquery,
        ckeys,
        cvalues,
        cprob,
        normal,
        normal_scale,
        gains,
        query,
        keys,
        values,
        prob,
        prob_own,
        *weights,
    ) = refs[:22]
    (cquery_back, ckey_back, cvalue_back, attn_low, query_back, key_back) = refs[22:28]
    (value_back, rel_back, hidden_own, main_part, states_part, gain_total) = refs[28:34]
    residual, context_back = refs[34:36]
    fetch = Fetch(weights, refs[36:44], refs[44])
    w_cquery, w_out, w_ckey, w_cvalue, w_query, w_relative, w_key, w_value = range(8)
    tokens, width = query.shape
    mine = 3 * local_len
    span = ckeys.shape[0] // rows
    start = lax.axis_index("seq") * local_len
    gain_total[...] = jnp.zeros_like(gain_total)

    def cross(step, carry):
        cross_back_step(
            step // 4, lax.rem(step, 4), step, mine, span, local_len, ccontext_back, cvalues,
            cprob, ckeys, cquery, cquery_back, ckey_back, cvalue_back,
        )
        return carry

    lax.fori_loop(0, 4 * rows, cross, 0)
    weight_cquery = fetch[w_cquery]

    def cquery_body(cols):
        residual[:, cols] = cross_grad[:, cols] + mm_back(cquery_back[...], weight_cquery[cols, :])

    tiles(width, cquery_body)

    def attn_norm_back(part):
        above = residual[part]
        add_rows(gain_total, 0, above * normal[part])
        grad = norm_back(above, normal[part], normal_scale[part][:, 0:1], gains[0:1])
        residual[part] = grad
        attn_low[part] = grad.astype(jnp.bfloat16)

    row_tiles(tokens, attn_norm_back)
    weight_out = fetch[w_out]

    def out_back(cols):
        context_back[:, cols] = mm_back(attn_low[...], weight_out[cols, :]).astype(jnp.bfloat16)

    tiles(width, out_back)
    hot = hot_backward(start, span)
    turn = turning(span)

    def attend(step, carry):
        attend_back_step(
            step // 4, lax.rem(step, 4), step, mine, span, local_len, rows, context_back, query,
            keys, values, prob, prob_own, query_back, key_back, value_back, rel_back, hot, turn,
        )
        return carry

    lax.fori_loop(0, 4 * rows, attend, 0)
    weight_ckey, weight_cvalue = fetch[w_ckey], fetch[w_cvalue]
    weight_query, weight_relative = fetch[w_query], fetch[w_relative]
    weight_key, weight_value = fetch[w_key], fetch[w_value]
    chips = rows * span // (rows * local_len)

    def states_body(cols):
        total = mm_back(ckey_back[...], weight_ckey[cols, :])
        total = total + mm_back(cvalue_back[...], weight_cvalue[cols, :])
        total = total.astype(jnp.bfloat16)
        for r in range(rows):
            for p in range(chips):
                at = r * span + p * local_len
                states_part[p, r, :, cols] = total[at : at + local_len]

    tiles(width, states_body)

    def hidden_body(cols):
        total = mm_back(key_back[...], weight_key[cols, :])
        total = total + mm_back(value_back[...], weight_value[cols, :])
        mains = total[: rows * span].astype(jnp.bfloat16)
        for r in range(rows):
            for p in range(chips):
                at = r * span + p * local_len
                main_part[p, r, :, cols] = mains[at : at + local_len]
        own = residual[:, cols] + mm_back(query_back[...], weight_query[cols, :])
        own = own + mm_back(rel_back[...], weight_relative[cols, :])
        for r in range(rows):
            for j in range(3):
                tile = own[r * mine + j * local_len : r * mine + (j + 1) * local_len]
                if j:
                    at = rows * span + (2 * r + j - 1) * local_len
                    tile = tile + total[at : at + local_len]
                hidden_own[j, r, :, cols] = tile

    tiles(width, hidden_body)


def gather_steps(sources, shards, planes, wholes, full_planes, nz, sems):
    local_sem, send, recv, plane_send, plane_recv, stage_sem = sems
    s, z, c, sx, sy = place()
    own = 2 * z + c
    core = (s, 2 * z + 1 - c)
    beside_x, beside_y = (sx, own), (sy, own)
    staged = [
        pltpu.make_async_copy(source, shard_ref, stage_sem.at[w]) if w else None
        for w, (source, shard_ref) in enumerate(zip(sources, shards))
    ]
    for copy in staged[1:]:
        copy.start()
    awaited = set([0])

    def across(dz):
        return (z + 1 - 2 * lax.rem(z, 2), lax.rem(z + 2, 4), 3 - z)[dz - 1]

    greet(nz)
    started = {}

    def put(i, copy):
        copy.start()
        started.setdefault(i, []).append(copy)

    items = []
    for w, shard_ref in enumerate(shards):
        if shard_ref.shape[0] % 128:
            items.append((w, 0, 0, None))
            continue
        high = min(shard_ref.shape[0], ITEM_ROWS)
        wide = min(shard_ref.shape[1], ITEM_COLUMNS)
        for row in range(0, shard_ref.shape[0], high):
            for col in range(0, shard_ref.shape[1], wide):
                items.append((w, row, high, pl.ds(col, wide)))
    count = len(items)
    split = [item[2] > 0 and i not in ALONG_Z for i, item in enumerate(items)]

    def cut(ref, i, q=None, half=None):
        _, row, height, cols = items[i]
        if not height:
            return ref
        if q is not None:
            height = height // 4
            row = row + q * height
        if half is not None:
            height = height // 2
            row = row + half * height
        return ref.at[pl.ds(row, height), cols]

    def shard(i, q=None):
        return cut(shards[items[i][0]], i, q)

    def whole(i, block, q=None, half=None):
        return cut(wholes[items[i][0]].at[block], i, q, half)

    def along_z(i):
        if items[i][0] not in awaited:
            awaited.add(items[i][0])
            staged[items[i][0]].wait()
        pltpu.make_async_copy(shard(i), whole(i, own), local_sem.at[i]).start()
        q = s if split[i] else None
        for dz in range(1, nz):
            to = (s, 2 * across(dz) + c)
            put(i, remote(shard(i, q), whole(i, own, q), send.at[i, dz, 0], recv.at[i, dz, 0], to))
        put(i, remote(shard(i), whole(i, own), send.at[i, 0, 0], recv.at[i, 0, 0], core))

    def moved(i, dz, kind, q, half, to):
        part = whole(i, 2 * across(dz) + c, q if split[i] else None, half)
        return remote(part, part, send.at[i, dz, kind], recv.at[i, dz, kind], to)

    def core_copy(i, dz, of):
        part = whole(i, 2 * across(dz) + of)
        return remote(part, part, send.at[i, dz, 5], recv.at[i, dz, 5], core)

    def to_core(i, dz):
        put(i, core_copy(i, dz, c))

    def first(i, dz):
        moved(i, dz, 0, s, None, core).wait_recv()
        if split[i]:
            put(i, moved(i, dz, 1, s, None, beside_x))
            put(i, moved(i, dz, 2, s, None, beside_y))
        else:
            to_core(i, dz)

    def second(i, dz):
        moved(i, dz, 1, sx, None, core).wait_recv()
        put(i, moved(i, dz, 4, sx, 0, beside_y))
        moved(i, dz, 2, sy, None, core).wait_recv()
        put(i, moved(i, dz, 3, sy, 1, beside_x))

    def third(i, dz):
        moved(i, dz, 4, 3 - s, 0, core).wait_recv()
        moved(i, dz, 3, 3 - s, 1, core).wait_recv()
        to_core(i, dz)

    def arrive(i):
        other = 1 - c
        pltpu.make_async_copy(shard(i), whole(i, own), local_sem.at[i]).wait()
        block = whole(i, 2 * z + other)
        remote(block, block, send.at[i, 0, 0], recv.at[i, 0, 0], core).wait_recv()
        for dz in range(1, nz):
            core_copy(i, dz, other).wait_recv()

    def plane(i, kind, q, half, to):
        rows = full_planes[i].shape[0]
        part = full_planes[i].at[pl.ds(half * (rows // 2), rows // 2), q]
        return remote(part, part, plane_send.at[i, kind], plane_recv.at[i, kind], to)

    def plane_part(i):
        return planes[i].at[0] if len(planes[i].shape) == 4 else planes[i]

    def plane_whole(i, kind, q, to):
        return remote(
            plane_part(i), full_planes[i].at[:, q], plane_send.at[i, kind], plane_recv.at[i, kind], to
        )

    def plane_here(i):
        return pltpu.make_async_copy(
            plane_part(i), full_planes[i].at[:, s], local_sem.at[count + i]
        )

    def plane_first(i):
        plane_here(i).start()
        put(None, plane_whole(i, 0, s, beside_x))
        put(None, plane_whole(i, 1, s, beside_y))

    def plane_second(i):
        plane_whole(i, 0, sx, core).wait_recv()
        put(None, plane(i, 2, sx, 0, beside_y))
        plane_whole(i, 1, sy, core).wait_recv()
        put(None, plane(i, 3, sy, 1, beside_x))

    def plane_arrive(i):
        plane_here(i).wait()
        plane(i, 2, 3 - s, 0, core).wait_recv()
        plane(i, 3, 3 - s, 1, core).wait_recv()

    def sent(i):
        for copy in started.pop(i, ()):
            copy.wait_send()

    def settle():
        for i in list(started):
            sent(i)

    steps, ready = [], {}

    def step(call, *args):
        steps.append(lambda: call(*args))

    ahead = 5
    for i in range(2):
        plane_first(i)
    for i in range(min(ahead, count)):
        along_z(i)
    for i in range(count + 3):
        for dz in range(1, nz):
            if i < count:
                step(first, i, dz)
            if 1 <= i <= count and split[i - 1]:
                step(second, i - 1, dz)
            if 2 <= i < count + 2 and split[i - 2]:
                step(third, i - 2, dz)
        if ahead + i < count:
            step(along_z, ahead + i)
        if i >= 4:
            step(sent, i - 4)
        if i in (1, 2):
            step(plane_second, i - 1)
        if i == 3:
            ready["planes"] = len(steps)
        if i >= 3:
            ready[i - 3] = len(steps)
    return steps, ready, arrive, plane_arrive, settle


SLOTS = 8
ITEM_ROWS, ITEM_COLUMNS = 128, 2048
ALONG_Z = ()
LAYER_OUTS = 25


def layer_kernel(count, nz, rows, local_len, *refs):
    at = 0

    def take(n):
        nonlocal at
        at += n
        return refs[at - n : at]

    sources = (None,) + take(count - 1)
    gain_rows = take(3)
    hidden, encoder, cotangent, lengths, enc_lengths = take(5)
    wholes, outs = take(count), take(LAYER_OUTS)
    gains, residual = take(2)
    held = list(take(LAYER_OUTS - 1))
    held.insert(14, held[5])
    (hid, x_all, query, keys, values, prob, prob_own, context, ckeys, cvalues) = held[:10]
    (normal, normal_scale, normed_low, cquery, cprob, ccontext, output) = held[10:17]
    (crossed_low, activated, last_low, slope, gain_total, normal2, scale2) = held[17:24]
    states = held[24]
    land_gains, rel, pool, mains, hot_ref = take(5)
    shards = take(count)
    load_sems, out_sems = take(2)
    gain_tile = [row[...].astype(jnp.float32) for row in gain_rows]
    gain_tile.append(jnp.zeros((13, gain_rows[0].shape[1]), jnp.float32))
    shards[0][...] = jnp.concatenate(gain_tile, axis=0).astype(jnp.bfloat16)
    steps, ready, arrive, plane_arrive, settle = gather_steps(
        sources, shards, (hidden, encoder), wholes, (mains, states), nz, take(6)
    )
    tokens, width = hid.shape
    mine = 3 * local_len
    span = mains.shape[1] * local_len
    start = lax.axis_index("seq") * local_len
    emitted = []

    def leave(i):
        return pltpu.make_async_copy(held[i], outs[i], out_sems.at[i])

    def emit(*targets):
        for target in targets:
            i = next(i for i, ref in enumerate(held) if ref is target)
            leave(i).start()
            if target is not prob:
                emitted.append(leave(i))

    def emit_cross():
        leave(14).start()
        emitted.append(leave(14))

    order, blocks_of = [], []
    item = 1
    for w in range(1, count):
        height, wide = shards[w].shape
        high, broad = min(height, ITEM_ROWS), min(wide, ITEM_COLUMNS)
        for row in range(0, height, 128):
            for col in range(0, wide, min(wide, 1024)):
                order.append(item + (row // high) * (wide // broad) + col // broad)
                blocks_of.append(
                    wholes[w].at[:, pl.ds(row, 128), pl.ds(col, min(wide, 1024))]
                )
        item = order[-1] + 1
    KEY, VALUE, QUERY, REL, CKEY, CVALUE, OUT, CQUERY, COUT, UP, DOWN = (*range(9), 9, 13)

    def slot_of(load):
        return load % SLOTS

    def load_copy(load):
        source = blocks_of[load]
        target = pool.at[slot_of(load)]
        if source.shape[2] < target.shape[2]:
            target = target.at[:, :, : source.shape[2]]
        return pltpu.make_async_copy(source, target, load_sems.at[load])

    def weight(load):
        return pool.at[slot_of(load)]

    def columns(load, cols):
        return pool[slot_of(load), :, :, cols].reshape(width, 256)

    def project(left, load, target, scale=None):
        def body(cols):
            product = mm(left[...], columns(load, cols))
            if scale is not None:
                product = product * scale
            target[:, cols] = product.astype(target.dtype)

        tiles(target.shape[1], body)

    def prepare():
        plane_arrive(0)
        plane_arrive(1)
        for r in range(rows):
            for j in range(3):
                tile = hidden[j, r]
                hid[r * mine + j * local_len : r * mine + (j + 1) * local_len] = tile
                if j:
                    to = rows * span + (2 * r + j - 1) * local_len
                    x_all[to : to + local_len] = tile
        x_all[: rows * span] = mains[...].reshape(rows * span, width)
        gain_total[...] = jnp.zeros_like(gain_total)
        hot_ref[...] = hot_forward(start, span)
        emit(hid, x_all, states)

    def take_gains():
        arrive(0)
        copy = pltpu.make_async_copy(wholes[0], land_gains, load_sems.at[len(order)])
        copy.start()
        copy.wait()
        for d in range(land_gains.shape[0]):
            gains[:, d * 128 : (d + 1) * 128] = land_gains[d].astype(jnp.float32)

    def attend(step, carry):
        r, g = step // 4, lax.rem(step, 4)
        attend_step(
            r, g, step, start, mine, span, local_len, rows, lengths, query, rel, keys, values,
            prob, prob_own, context, hot_ref[...],
        )
        return carry

    def cross(step, carry):
        r, g = step // 4, lax.rem(step, 4)
        cross_step(r, g, step, mine, span, local_len, enc_lengths, cquery, ckeys, cvalues, cprob, ccontext)
        return carry

    def out_body(cols):
        residual[:, cols] = hid[:, cols].astype(jnp.float32) + mm(context[...], columns(OUT, cols))

    def norm_body(part):
        normal[part], scale = norm_rows(residual[part])
        normal_scale[part] = jnp.broadcast_to(scale, (scale.shape[0], 128))
        normed_low[part] = (normal[part] * gains[0:1]).astype(jnp.bfloat16)

    def after_attention():
        tiles(width, out_body)
        row_tiles(tokens, norm_body)
        emit(context, normal, normal_scale, normed_low)

    def after_cross_query():
        project(normed_low, CQUERY, cquery, 0.125)
        emit(cquery)
        leave(5).wait()

    def cross_body(cols):
        residual[:, cols] = normal[:, cols] * gains[0:1, cols] + mm(ccontext[...], columns(COUT, cols))

    def cross_norm_body(part):
        normal2[part], scale = norm_rows(residual[part])
        scale2[part] = jnp.broadcast_to(scale, (scale.shape[0], 128))
        after = normal2[part] * gains[1:2]
        crossed_low[part] = after.astype(jnp.bfloat16)
        residual[part] = after

    def after_cross():
        tiles(width, cross_body)
        row_tiles(tokens, cross_norm_body)
        emit(ccontext, crossed_low, normal2, scale2)

    def up(k):
        def body(i, carry):
            cols = pl.ds(pl.multiple_of(i * 256, 256), 256)
            to = pl.ds(pl.multiple_of(k * width + i * 256, 256), 256)
            value = mm(crossed_low[...], columns(UP + k, cols))
            below = 0.5 + 0.5 * lax.erf(value * (0.5**0.5))
            activated[:, to] = (value * below).astype(jnp.bfloat16)
            density = jnp.exp(-0.5 * value * value) * (1.0 / math.sqrt(2.0 * math.pi))
            slope[:, to] = (below + value * density).astype(jnp.bfloat16)
            return carry

        lax.fori_loop(0, width // 256, body, 0)
        if k == 3:
            emit(activated, slope)

    blocks = pool.shape[1]

    def of_down(k, d):
        return d * 4 * 128 + k * 128

    def down(k):
        def body(cols):
            left = jnp.concatenate(
                [activated[:, of_down(k, d) : of_down(k, d) + 128] for d in range(blocks)], axis=1
            )
            residual[:, cols] += mm(left, columns(DOWN + k, cols))

        tiles(width, body)

    def last_norm():
        for r in range(rows):
            for j in range(3):
                part = slice(r * mine + j * local_len, r * mine + (j + 1) * local_len)
                normal3, scale = norm_rows(residual[part])
                output[j, r] = (normal3 * gains[2:3]).astype(output.dtype)
                above = cotangent[j, r].astype(jnp.float32)
                add_rows(gain_total, 2, above * normal3)
                grad = norm_back(above, normal3, scale, gains[2:3])
                residual[part] = grad
                last_low[part] = grad.astype(jnp.bfloat16)
        emit(output, last_low, gain_total)

    pieces = [("planes", 2, prepare)]
    pieces += [
        (KEY, 3, lambda: project(x_all, KEY, keys)),
        (VALUE, 3, lambda: project(x_all, VALUE, values)),
        (QUERY, 2, lambda: project(hid, QUERY, query, 0.125)),
        (REL, 1, lambda: project(hid, REL, rel)),
    ]
    half = 2
    for i in range(0, 4 * rows, half):
        pieces.append((REL, 5, lambda i=i: lax.fori_loop(i, i + half, attend, 0)))
    pieces += [
        (REL, 0, lambda: emit(query, keys, values, prob, prob_own)),
        (CKEY, 2, lambda: project_states(CKEY, ckeys)),
        (CVALUE, 2, lambda: project_states(CVALUE, cvalues)),
        (OUT, 0, take_gains),
        (OUT, 3, after_attention),
        (CQUERY, 2, after_cross_query),
    ]

    def project_states(load, target):
        def body(cols):
            left = states[...].reshape(rows * span, width)
            target[:, cols] = mm(left, columns(load, cols)).astype(target.dtype)

        tiles(width, body)
        emit(target)

    for i in range(0, 4 * rows, half):
        pieces.append((CQUERY, 3, lambda i=i: lax.fori_loop(i, i + half, cross, 0)))
    pieces += [(CQUERY, 0, emit_cross), (COUT, 3, after_cross)]
    pieces += [(UP + k, 3, functools.partial(up, k)) for k in range(4)]
    pieces += [(DOWN + k, 1, functools.partial(down, k)) for k in range(4)]
    pieces.append((DOWN + 3, 3, last_norm))

    last_use = {}
    for index, (need, _, _) in enumerate(pieces):
        last_use[need] = index
    state = {"step": 0, "load": 0}
    arrived, waited = set(), set()

    def run_to(n):
        while state["step"] < min(n, len(steps)):
            steps[state["step"]]()
            state["step"] += 1

    def free(load, done):
        return all(
            last_use[other] < done for other in range(load) if slot_of(other) == slot_of(load)
        )

    def begin_load():
        load = state["load"]
        if order[load] not in arrived:
            arrive(order[load])
            arrived.add(order[load])
        load_copy(load).start()
        state["load"] += 1

    rate = len(steps) / 130.0
    for index, (need, cost, call) in enumerate(pieces):
        if need == "planes":
            run_to(ready["planes"])
        else:
            while state["load"] <= need:
                run_to(ready[order[state["load"]]])
                begin_load()
            if need not in waited:
                waited.add(need)
                load_copy(need).wait()
        call()
        run_to(state["step"] + int(cost * rate + 0.5))
        while (
            state["load"] < len(order)
            and free(state["load"], index + 1)
            and ready[order[state["load"]]] <= state["step"]
        ):
            begin_load()
    run_to(len(steps))
    for copy in emitted:
        copy.wait()
    settle()


def layer(gains, shards, hidden, encoder, cotangent, lengths, enc_lengths, ndp):
    nz = ndp // 2
    shards = (jax.ShapeDtypeStruct((16, gains[0].shape[1]), jnp.bfloat16),) + shards
    count = len(shards)
    low, wide = jnp.bfloat16, jnp.float32
    _, rows, local_len, width = hidden.shape
    tokens, span = 3 * rows * local_len, 4 * local_len
    every = rows * (span + 2 * local_len)
    ff = shards[-2].shape[1]
    steps = sum(
        max(1, w.shape[0] // ITEM_ROWS) * max(1, w.shape[1] // ITEM_COLUMNS) for w in shards
    )
    results = [
        ((tokens, width), low),
        ((every, width), low),
        ((tokens, width), low),
        ((every, width), low),
        ((every, width), low),
        ((4 * rows, 12 * local_len, span), low),
        ((tokens, width), low),
        ((tokens, width), low),
        ((rows * span, width), low),
        ((rows * span, width), low),
        ((tokens, width), wide),
        ((tokens, 128), wide),
        ((tokens, width), low),
        ((tokens, width), low),
        ((4 * rows, 12 * local_len, span), low),
        ((tokens, width), low),
        (hidden.shape, low),
        ((tokens, width), low),
        ((tokens, ff), low),
        ((tokens, width), low),
        ((tokens, ff), low),
        ((3, 8, width), wide),
        ((tokens, width), wide),
        ((tokens, 128), wide),
        ((rows, 4, local_len, width), low),
    ]
    more = [((16, width), wide), ((tokens, width), wide)]
    vmem = pl.BlockSpec(memory_space=pltpu.VMEM)
    smem = pl.BlockSpec(memory_space=pltpu.SMEM)
    anywhere = pl.BlockSpec(memory_space=pl.ANY)
    return pl.pallas_call(
        lambda *refs: layer_kernel(count, nz, rows, local_len, *refs),
        out_shape=[jax.ShapeDtypeStruct((ndp,) + w.shape, w.dtype) for w in shards]
        + [jax.ShapeDtypeStruct(*result) for result in results]
        + [jax.ShapeDtypeStruct(*result) for result in more],
        in_specs=[anywhere] * (count - 1) + [vmem] * 6 + [smem] * 2,
        out_specs=[anywhere] * (count + len(results)) + [vmem] * 2,
        scratch_shapes=[pltpu.VMEM(*result) for i, result in enumerate(results) if i != 14]
        + [
            pltpu.VMEM((ndp,) + shards[0].shape, low),
            pltpu.VMEM((tokens, width // 2), low),
            pltpu.VMEM((SLOTS, ndp, 128, width), low),
            pltpu.VMEM((rows, 4, local_len, width), low),
            pltpu.VMEM((128, span), low),
        ]
        + [pltpu.VMEM(w.shape, w.dtype) for w in shards]
        + [
            pltpu.SemaphoreType.DMA((18,)),
            pltpu.SemaphoreType.DMA((len(results),)),
            pltpu.SemaphoreType.DMA((steps + 2,)),
            pltpu.SemaphoreType.DMA((steps, nz, 6)),
            pltpu.SemaphoreType.DMA((steps, nz, 6)),
            pltpu.SemaphoreType.DMA((2, 4)),
            pltpu.SemaphoreType.DMA((2, 4)),
            pltpu.SemaphoreType.DMA((count,)),
        ],
        compiler_params=pltpu.CompilerParams(
            collective_id=0, has_side_effects=True, vmem_limit_bytes=62 * 2**20
        ),
        name="layer",
    )(*shards[1:], *gains, hidden, encoder, cotangent, lengths, enc_lengths)


RINGS = (5, 5)
SLACK = 0
LAGS = (4, 7, 10)
DEEP = ()
WIDE_RING = 8


def back_kernel(plan, nz, rows, local_len, n_out, *refs):
    at = 0

    def take(n):
        nonlocal at
        at += n
        return refs[at - n : at]

    (any_activated, any_last, any_grad, any_slope, any_crossed, any_normal2, any_scale2) = take(7)
    (any_normal, any_scale, any_ccontext, any_normed, any_context, any_hid, any_x_all) = take(7)
    (any_states, any_cquery, any_ckeys, any_cvalues, any_cprob, any_query, any_keys) = take(7)
    (any_values, any_prob, any_prob_own, any_gains, any_gain_total) = take(5)
    w_down, w_up, w_cout, w_cquery, w_out, w_ckey, w_cvalue, w_key, w_value, w_query, w_rel = take(11)
    outs = take(n_out)
    gain_out, states_sum, hidden_grad = take(3)
    (activated, last_low, residual, up_back, crossed_low, normal, scale, cross_low) = take(8)
    (ccontext_back, cquery, ckeys, cvalues, prob, query, keys, values, prob_own) = take(9)
    (gains, gain_total, cquery_back, ckey_back, cvalue_back, attn_low, query_back) = take(7)
    (key_back, value_back, rel_back, main_part, states_part, pool, hot_ref, turn_ref) = take(8)
    parts, held0s, held1s, held2s, held3s = take(2), take(3), take(3), take(3), take(3)
    gain_part, share1, share2, deep0, deep1, deep2 = take(6)
    load_sems, weight_sems, out_sems, send, recv, credit0, credit1, credit2 = take(8)
    shares = (main_part, states_part)
    context_back, slope = ccontext_back, up_back
    tokens, width = residual.shape
    mine = 3 * local_len
    span = ckeys.shape[0] // rows
    start = lax.axis_index("seq") * local_len
    s, z, c, sx, sy = place()
    own = 2 * z + c
    x, y = lax.rem(s, 2), s // 2
    core = (s, 2 * z + 1 - c)
    beside_x, beside_y = (sx, own), (sy, own)

    loads = []

    def load(source, target):
        copy = pltpu.make_async_copy(source, target, load_sems.at[len(loads)])
        loads.append(copy)
        copy.start()
        return copy

    begun = [
        load(any_activated, activated),
        load(any_last, last_low),
    ]
    first_loads = list(begun)
    ffn_loads = [
        load(any_slope, slope),
        load(any_grad, residual),
        load(any_crossed, crossed_low),
        load(any_normal2, normal),
        load(any_scale2, scale),
        load(any_gains, gains),
        load(any_gain_total, gain_total),
    ]
    cross_loads = [
        load(any_cquery, cquery),
        load(any_ckeys, ckeys),
        load(any_cvalues, cvalues),
        load(any_cprob.at[pl.ds(0, 4)], prob),
    ]
    attend_loads = [
        load(any_query, query),
        load(any_keys, keys),
        load(any_values, values),
        load(any_prob_own, prob_own),
    ]

    def await_all(copies):
        for copy in copies:
            copy.wait()
        copies.clear()

    blocks = [w_down.at[pl.ds(width * k, width)] for k in range(4)]
    blocks += [w_up.at[:, pl.ds(width * k, width)] for k in range(4)]
    blocks += [w_cout, w_cquery, w_out, w_ckey, w_cvalue, w_key, w_value, w_query, w_rel]
    DOWN, UP, COUT, CQUERY, OUT, CKEY, CVALUE, KEY, VALUE, QUERY, REL = (0, 4, *range(8, 17))

    def block_copy(i):
        target = pool.at[i % 2]
        if blocks[i].shape[1] < width:
            target = target.at[:, pl.ds(0, blocks[i].shape[1])]
        return pltpu.make_async_copy(blocks[i], target, weight_sems.at[i])

    started = []

    def need(i):
        while len(started) <= i:
            block_copy(len(started)).start()
            started.append(True)
        block_copy(i).wait()

    def release(i):
        if i + 2 < len(blocks) and len(started) <= i + 2:
            while len(started) <= i + 2:
                block_copy(len(started)).start()
                started.append(True)

    block_copy(0).start()
    block_copy(1).start()
    started += [True, True]
    greet(nz)
    gain_part[...] = jnp.zeros_like(gain_part)

    held = {}

    def buffers(k):
        kind, slot = plan[k][:2]
        sub = plan[k][5]
        if kind == 3:
            share = shares[slot // 2].at[:, :, slot % 2]
            return None, share, share1.at[slot], share2.at[slot], None
        if kind == 4:
            part, held0 = parts[0].at[slot % 2], held0s[0].at[slot % RINGS[0]]
            return part, held0, deep1.at[sub], deep2.at[sub], deep0.at[sub]
        if kind == 2:
            return (gain_part,) + tuple(h[2].at[0] for h in (held0s, held1s, held2s, held3s))
        ring = WIDE_RING if kind == 0 else held1s[1].shape[0]
        return (
            parts[kind].at[slot % 2],
            held0s[kind].at[slot % RINGS[kind]],
            held1s[kind].at[sub % ring],
            held2s[kind].at[sub % ring],
            held3s[kind].at[sub],
        )

    slots_of = [sum(p[0] in ((0, 4), (1,))[kind] for p in plan) for kind in range(2)]
    subs_of = sum(p[0] == 0 for p in plan)

    def even(k):
        return plan[k][5] % 2 == 0

    def core_copy(k):
        part, held0 = buffers(k)[:2]
        return remote(part.at[:, :, :, 1 - c], held0, send.at[k, 0], recv.at[k, 0], core)

    def first_copy(k):
        _, held0, held1 = buffers(k)[:3]
        if plan[k][0] == 4:
            held0 = buffers(k)[4].at[0]
        if even(k):
            return remote(held0.at[:, 1 - x], held1, send.at[k, 1], recv.at[k, 1], beside_x)
        return remote(held0.at[1 - y], held1, send.at[k, 1], recv.at[k, 1], beside_y)

    def second_copy(k):
        held1, held2 = buffers(k)[2:4]
        if even(k):
            return remote(held1.at[1 - y], held2, send.at[k, 2], recv.at[k, 2], beside_y)
        return remote(held1.at[1 - x], held2, send.at[k, 2], recv.at[k, 2], beside_x)

    def z_copy(k, dz):
        _, held0, _, held2, held3 = buffers(k)
        zt = lax.rem(z + dz, nz)
        source = held0.at[:, :, zt] if plan[k][0] == 4 else held2.at[zt]
        return remote(
            source, held3.at[dz - 1], send.at[k, 2 + dz], recv.at[k, 2 + dz], (s, 2 * zt + c)
        )

    def grant(semaphore, to):
        pl.semaphore_signal(semaphore, inc=1, device_id=to, device_id_type=MESH)

    def added(held, mine):
        held[...] = (held[...].astype(jnp.float32) + mine.astype(jnp.float32)).astype(held.dtype)

    half = rows * span // 2
    whole_rows = (0, tokens)

    def segments(pair, i):
        cols = pl.ds(256 * i, 256)
        if pair == 0:
            return [(activated[:, cols], whole_rows)]
        if pair == 1:
            return [(crossed_low[:, cols], whole_rows)]
        if pair <= 6:
            column = width * min(pair - 2, 3) + 256 * i
            return [(activated[:, pl.ds(column, 256)], whole_rows)]
        if pair <= 8:
            return [
                (up_back[:, pl.ds(width * n + 256 * i, 256)], (tokens * n, tokens)) for n in range(2)
            ]
        return [
            (up_back[:half, pl.ds(width * (2 + n) + 256 * i, 256)], (half * n, half))
            for n in range(2)
        ]

    rights = (
        last_low, up_back, cross_low, cquery_back, attn_low, query_back, rel_back,
        key_back, value_back, ckey_back, cvalue_back,
    )
    late_loads = []

    def reload():
        for n, source in enumerate((any_ccontext, any_normed, any_context, any_hid)):
            late_loads.append(load(source, activated.at[:, pl.ds(width * n, width)]))
        for n in range(2):
            late_loads.append(
                load(any_x_all.at[pl.ds(tokens * n, tokens)], up_back.at[:, pl.ds(width * n, width)])
            )
            late_loads.append(
                load(
                    any_states.at[pl.ds(half * n, half)],
                    up_back.at[pl.ds(0, half), pl.ds(width * (2 + n), width)],
                )
            )

    before, recent = {}, {}
    for k, entry in enumerate(plan):
        before[k] = recent.get((entry[0] % 4, entry[1] - 2))
        recent[entry[0] % 4, entry[1]] = k
    followed = set(v for v in before.values() if v is not None)
    pairs_before = max(k for k, entry in enumerate(plan) if entry[0] in (0, 1, 4) and entry[2] < 2)

    def make(k):
        kind, slot, pair, col, wide, _ = plan[k]
        if kind == 3:
            return
        if kind != 2:
            part = buffers(k)[0]
            block = part.shape[4]
            if pair == 0:
                await_all(first_loads)
            if pair >= 2:
                await_all(late_loads)
            if slot >= 2:
                core_copy(before[k]).wait_send()
            group = 256 // block
            for i in range(part.shape[0] * part.shape[1] * nz * 2 * block // 256):
                product = 0.0
                for left, (row, height) in segments(pair, i):
                    right = rights[pair][row : row + height, col : col + wide]
                    product = product + mm_grad(left, right)
                i_s, rest = divmod(i * group, 2 * nz)
                zs = rest // 2
                part[i_s // 2, i_s % 2, zs : zs + group // 2] = product.reshape(
                    group // 2, 2, block, wide
                ).astype(part.dtype)
            if k == pairs_before:
                reload()
            if slot >= RINGS[kind % 4]:
                pl.semaphore_wait(credit0.at[kind % 4], 1)
        else:
            lanes = width // (8 * nz)
            totals = jnp.concatenate(
                [jnp.sum(gain_total[g], axis=0, keepdims=True) for g in range(3)], axis=0
            )
            for b in range(8 * nz):
                i_s, rest = divmod(b, 2 * nz)
                gain_part[i_s // 2, i_s % 2, rest // 2, rest % 2, 0:3, 0:lanes] = totals[
                    :, b * lanes : (b + 1) * lanes
                ]
        core_copy(k).start()

    def after_core(k):
        part, held0 = buffers(k)[:2]
        kind, sub = plan[k][0], plan[k][5]
        if kind != 3:
            core_copy(k).wait_recv()
            added(held0, part[:, :, :, c])
        if kind == 4:
            for dz in range(1, nz):
                z_copy(k, dz).start()
            return
        if kind == 0 and sub >= WIDE_RING:
            pl.semaphore_wait(credit1.at[sub % 2], 1)
        first_copy(k).start()

    def over_z(k, mine_part):
        held3 = buffers(k)[4]
        total = mine_part.astype(jnp.float32)
        for dz in range(1, nz):
            z_copy(k, dz).wait_recv()
            total = total + held3[dz - 1].astype(jnp.float32)
        return total

    def sent_z(k):
        for dz in range(1, nz):
            z_copy(k, dz).wait_send()

    def after_first(k):
        _, held0, held1, _, held3 = buffers(k)
        kind, slot, sub = plan[k][0], plan[k][1], plan[k][5]
        if kind == 4:
            held3[0] = over_z(k, held0[:, :, z]).astype(held3.dtype)
            first_copy(k).start()
            sent_z(k)
        else:
            first_copy(k).wait_recv()
            added(held1, held0[:, x] if even(k) else held0[y])
            if kind == 0 and sub >= WIDE_RING:
                pl.semaphore_wait(credit2.at[sub % 2], 1)
            second_copy(k).start()
            first_copy(k).wait_send()
        if kind in (0, 1, 4) and slot + RINGS[kind % 4] < slots_of[kind % 4]:
            grant(credit0.at[kind % 4], core)

    def after_second(k):
        _, _, held1, held2, held3 = buffers(k)
        kind, slot, sub = plan[k][0], plan[k][1], plan[k][5]
        if kind == 4:
            first_copy(k).wait_recv()
            added(held1, held3[0, :, x] if even(k) else held3[0, y])
            second_copy(k).start()
            return
        second_copy(k).wait_recv()
        mine_part = held1[y] if even(k) else held1[x]
        if kind == 3:
            total = held2[...].astype(jnp.float32) + mine_part.astype(jnp.float32)
            r = slot % 2
            if slot < 2:
                residual[r * mine : r * mine + local_len] += total
                hidden_copy(0, r).start()
            else:
                states_sum[r] = total
            return
        added(held2, mine_part)
        for dz in range(1, nz):
            z_copy(k, dz).start()
        second_copy(k).wait_send()
        if kind == 0 and sub + WIDE_RING < subs_of:
            grant(credit1.at[sub % 2], beside_x if even(k) else beside_y)

    def finish_chunk(k):
        kind, _, pair, col, wide, sub = plan[k]
        if kind == 3:
            return
        _, _, held1, held2, _ = buffers(k)
        if kind == 4:
            second_copy(k).wait_recv()
            mine_part = (held1[y] if even(k) else held1[x]).astype(jnp.float32)
            outs[pair][:, col : col + wide] = held2[...].astype(jnp.float32) + mine_part
            first_copy(k).wait_send()
            second_copy(k).wait_send()
            return
        total = over_z(k, held2[z])
        if kind == 2:
            gain_out[...] = total
        else:
            outs[pair][:, col : col + wide] = total
        sent_z(k)
        if kind == 0 and sub + WIDE_RING < subs_of:
            grant(credit2.at[sub % 2], beside_y if even(k) else beside_x)

    count = len(plan)
    total_ticks = count + LAGS[2] + SLACK

    def tick(t):
        def at_lag(lag, call):
            if 0 <= t - lag < count:
                call(t - lag)

        if 1 <= t < count + 1:
            after_core(t - 1)
        if t < count:
            make(t)
        at_lag(LAGS[0], after_first)
        at_lag(LAGS[1], after_second)
        at_lag(LAGS[2], finish_chunk)

    def fours(body):
        def step(i, carry):
            body(pl.ds(pl.multiple_of(i * 256, 256), 256))
            return carry

        lax.fori_loop(0, width // 256, step, 0)

    def down_back(k):
        need(DOWN + k)
        if k == 0:
            await_all(ffn_loads)
        place_of = (DOWN + k) % 2

        def body(i, carry):
            to = pl.ds(pl.multiple_of(k * width + i * 256, 256), 256)
            product = mm_back(last_low[...], pool[place_of, pl.ds(pl.multiple_of(i * 256, 256), 256)])
            up_back[:, to] = (product * slope[:, to].astype(jnp.float32)).astype(jnp.bfloat16)
            return carry

        lax.fori_loop(0, width // 256, body, 0)
        release(DOWN + k)

    def up_again(k):
        need(UP + k)

        def body(cols):
            residual[:, cols] += mm_back(
                up_back[:, k * width : (k + 1) * width], pool[(UP + k) % 2, cols]
            )

        fours(body)
        release(UP + k)

    def cross_norm_back(part):
        above = residual[part]
        add_rows(gain_total, 1, above * normal[part])
        grad = norm_back(above, normal[part], scale[part][:, 0:1], gains[1:2])
        residual[part] = grad
        cross_low[part] = grad.astype(jnp.bfloat16)

    norm_loads = []

    def cout_back():
        row_tiles(tokens, cross_norm_back)
        norm_loads.append(load(any_normal, normal))
        norm_loads.append(load(any_scale, scale))
        need(COUT)

        def body(cols):
            ccontext_back[:, cols] = mm_back(cross_low[...], pool[COUT % 2, cols]).astype(
                jnp.bfloat16
            )

        fours(body)
        release(COUT)

    def cross(first, last):
        await_all(cross_loads)

        def step(i, carry):
            cross_back_step(
                i // 4, lax.rem(i, 4), lax.rem(i, 4), mine, span, local_len, ccontext_back, cvalues, prob,
                ckeys, cquery, cquery_back, ckey_back, cvalue_back,
            )
            return carry

        lax.fori_loop(first, last, step, 0)
        if last == 4 * rows:
            attend_loads.append(load(any_prob.at[pl.ds(0, 4)], prob))
        elif last % 4 == 0:
            cross_loads.append(load(any_cprob.at[pl.ds(last, 4)], prob))

    def attn_norm_back(part):
        above = residual[part]
        add_rows(gain_total, 0, above * normal[part])
        grad = norm_back(above, normal[part], scale[part][:, 0:1], gains[0:1])
        residual[part] = grad
        attn_low[part] = grad.astype(jnp.bfloat16)

    def cquery_again():
        need(CQUERY)

        def body(cols):
            residual[:, cols] += mm_back(cquery_back[...], pool[CQUERY % 2, cols])

        fours(body)
        release(CQUERY)
        await_all(norm_loads)
        row_tiles(tokens, attn_norm_back)

    def out_back():
        need(OUT)

        def body(cols):
            context_back[:, cols] = mm_back(attn_low[...], pool[OUT % 2, cols]).astype(jnp.bfloat16)

        fours(body)
        release(OUT)
        hot_ref[...] = hot_backward(start, span)
        turn_ref[...] = turning(span)

    def attend(first, last):
        await_all(attend_loads)

        def step(i, carry):
            attend_back_step(
                i // 4, lax.rem(i, 4), lax.rem(i, 4), mine, span, local_len, rows, context_back, query, keys,
                values, prob, prob_own, query_back, key_back, value_back, rel_back,
                hot_ref[...], turn_ref[...],
            )
            return carry

        lax.fori_loop(first, last, step, 0)
        if last < 4 * rows and last % 4 == 0:
            attend_loads.append(load(any_prob.at[pl.ds(last, 4)], prob))

    def into(share, total, cols):
        total = total.astype(jnp.bfloat16)
        for r in range(rows):
            for p in range(4):
                row = r * span + p * local_len
                share[p // 2, p % 2, r, :, cols] = total[row : row + local_len]

    def states_back():
        need(CKEY)
        need(CVALUE)

        def body(cols):
            total = mm_back(ckey_back[...], pool[CKEY % 2, cols])
            into(states_part, total + mm_back(cvalue_back[...], pool[CVALUE % 2, cols]), cols)

        fours(body)
        release(CKEY)
        release(CVALUE)

    def keys_again():
        need(KEY)
        need(VALUE)

        def body(cols):
            total = mm_back(key_back[...], pool[KEY % 2, cols])
            total = total + mm_back(value_back[...], pool[VALUE % 2, cols])
            into(main_part, total[: rows * span], cols)
            for r in range(rows):
                to = r * mine + local_len
                row = rows * span + 2 * r * local_len
                residual[to : to + 2 * local_len, cols] += total[row : row + 2 * local_len]

        fours(body)
        release(KEY)
        release(VALUE)

    def hidden_copy(j, r):
        row = r * mine + j * local_len
        return pltpu.make_async_copy(
            residual.at[pl.ds(row, local_len)], hidden_grad.at[j, r], out_sems.at[j, r]
        )

    def query_again():
        need(QUERY)
        need(REL)
        deep = rel_back.shape[1]

        def body(cols):
            total = mm_back(query_back[...], pool[QUERY % 2, cols])
            residual[:, cols] += total + mm_back(rel_back[...], pool[REL % 2, cols, :deep])

        fours(body)
        for r in range(rows):
            for j in (1, 2):
                hidden_copy(j, r).start()

    ends = {}
    for k, entry in enumerate(plan):
        ends[10 + entry[0] if entry[0] in (2, 3) else entry[2]] = k + 1
    steps_of = range(0, 4 * rows, 2)
    pieces = [(1, functools.partial(down_back, k), ends[0]) for k in range(4)]
    pieces += [(1, functools.partial(up_again, k), ends[1] - 1) for k in range(4)]
    pieces.append((3, cout_back, ends[2]))
    pieces += [(4, functools.partial(cross, i, i + 2), ends[2]) for i in steps_of]
    pieces[-1] = pieces[-1][:2] + (ends[10],)
    pieces.append((2, cquery_again, ends[12]))
    pieces.append((1, out_back, ends[12]))
    pieces += [(5, functools.partial(attend, i, i + 2), ends[12]) for i in steps_of]
    pieces.append((3, states_back, ends[8]))
    pieces.append((5, keys_again, ends[8]))
    pieces.append((2, query_again, count))
    done = {"tick": 0, "spent": 0.0}

    def ticks_to(limit, wanted):
        while done["tick"] < min(limit, wanted):
            tick(done["tick"])
            done["tick"] += 1

    tick(0)
    done["tick"] = 1
    for cost, call, limit in pieces:
        call()
        done["spent"] += cost
        ticks_to(limit, 1 + int(done["spent"] / 3.5))
    ticks_to(total_ticks, total_ticks)
    for k in range(count):
        if plan[k][0] != 3 and k not in followed:
            core_copy(k).wait_send()
        if plan[k][0] == 3:
            second_copy(k).wait_send()
    for j in range(3):
        for r in range(rows):
            hidden_copy(j, r).wait()


def back(values, weights, shape, ndp):
    nz = ndp // 2
    low, wide = jnp.bfloat16, jnp.float32
    rows, local_len, width = shape[1:]
    tokens, span = 3 * rows * local_len, 4 * local_len
    every = rows * (span + 2 * local_len)
    ff = weights[0].shape[0]
    ndev = 8 * nz
    heights = [ff, width, width, width, width, width, width, width, width, width, width]
    wides = [width, ff, width, width, width, width, width // 2, width, width, width, width]
    plan, slots, subs, at = [], [0, 0], [0, 0], 0
    for pair in (0, 1, 2, 3, 9, 10, 4, 5, 6, 7, 8):
        kind = int(heights[pair] > width)
        step = (512, 128)[kind]
        for col in range(0, wides[pair], step):
            if kind:
                plan.append((1, slots[1], pair, col, step, slots[1]))
            else:
                deep = at in DEEP
                plan.append((4 if deep else 0, slots[0], pair, col, step, subs[deep]))
                subs[deep] += 1
                at += 1
            slots[kind] += 1
        if pair == 4:
            plan.append((2, 0, 0, 0, 128, 0))
    plan += [(3, i, 0, 0, 0, i) for i in range(4)]
    n = len(plan)
    tails = [((width // ndev, 512), low), ((ff // ndev, 128), low), ((8, 128), wide)]
    counts = [
        (RINGS[0], WIDE_RING, WIDE_RING, subs[0]),
        (RINGS[1], slots[1], slots[1], slots[1]),
        (1, 1, 1, 1),
    ]
    leads = [(2, 2, nz), (2, nz), (nz,), (nz - 1,)]
    held = [
        pltpu.VMEM((counts[kind][stage],) + leads[stage] + tails[kind][0], tails[kind][1])
        for stage in range(4)
        for kind in range(3)
    ]
    parts = [pltpu.VMEM((2, 2, 2, nz, 2) + tails[kind][0], low) for kind in range(2)]
    share = (local_len, width)
    main = pltpu.VMEM((rows * span, width), low)
    token = pltpu.VMEM((tokens, width), low)
    fat = pltpu.VMEM((tokens, ff), low)
    all_rows = pltpu.VMEM((every, width), low)
    token_wide = pltpu.VMEM((tokens, width), wide)
    scratch = [fat, token, token_wide, fat, token, token_wide]
    scratch += [pltpu.VMEM((tokens, 128), wide), token, token, token, main, main]
    scratch += [pltpu.VMEM((4, 12 * local_len, span), low), token, all_rows, all_rows, token]
    scratch += [pltpu.VMEM((16, width), wide), pltpu.VMEM((3, 8, width), wide), token, main, main]
    scratch += [token, token, all_rows, all_rows, pltpu.VMEM((tokens, width // 2), low)]
    scratch += [pltpu.VMEM((2, 2, rows) + share, low)] * 2
    scratch += [pltpu.VMEM((2, width, width), low)]
    scratch += [pltpu.VMEM((span, 128), low), pltpu.VMEM((span, span), low)]
    scratch += parts + held
    scratch += [pltpu.VMEM((2, 2, nz, 2, 8, 128), wide)]
    scratch += [pltpu.VMEM((4, 2) + share, low), pltpu.VMEM((4,) + share, low)]
    scratch += [
        pltpu.VMEM((max(1, subs[1]),) + lead + tails[0][0], low) for lead in ((nz - 1, 2, 2), (2,), ())
    ]
    scratch += [
        pltpu.SemaphoreType.DMA((32,)),
        pltpu.SemaphoreType.DMA((17,)),
        pltpu.SemaphoreType.DMA((3, rows)),
        pltpu.SemaphoreType.DMA((n, 2 + nz)),
        pltpu.SemaphoreType.DMA((n, 2 + nz)),
        pltpu.SemaphoreType.REGULAR((2,)),
        pltpu.SemaphoreType.REGULAR((2,)),
        pltpu.SemaphoreType.REGULAR((2,)),
    ]
    anywhere = pl.BlockSpec(memory_space=pl.ANY)
    vmem = pl.BlockSpec(memory_space=pltpu.VMEM)
    outs = [jax.ShapeDtypeStruct((h // ndev, w), wide) for h, w in zip(heights, wides)]
    outs.append(jax.ShapeDtypeStruct((8, 128), wide))
    outs.append(jax.ShapeDtypeStruct((rows,) + share, wide))
    outs.append(jax.ShapeDtypeStruct(shape, wide))
    return pl.pallas_call(
        lambda *refs: back_kernel(plan, nz, rows, local_len, len(heights), *refs),
        out_shape=outs,
        in_specs=[anywhere] * (len(values) + len(weights)),
        out_specs=[vmem] * (len(outs) - 1) + [anywhere],
        scratch_shapes=scratch,
        compiler_params=pltpu.CompilerParams(
            collective_id=1, has_side_effects=True, vmem_limit_bytes=62 * 2**20
        ),
        name="back",
    )(*values, *weights)


def finish_kernel(count, *refs):
    sources, gain_sums = refs[:count], refs[count]
    targets, gain_outs = refs[count + 1 : 2 * count + 1], refs[2 * count + 1 : 2 * count + 4]
    held, sems = refs[2 * count + 4 : 3 * count + 4], refs[3 * count + 4]
    ins = [pltpu.make_async_copy(sources[i], held[i], sems.at[0, i]) for i in range(count)]
    outs = [pltpu.make_async_copy(held[i], targets[i], sems.at[1, i]) for i in range(count)]
    for copy in ins:
        copy.start()
    for g, gain_out in enumerate(gain_outs):
        gain_out[...] = gain_sums[g : g + 1, : gain_out.shape[1]]
    for copy_in, copy_out in zip(ins, outs):
        copy_in.wait()
        copy_out.start()
    for copy in outs:
        copy.wait()


def finish(sums, hidden_grad, states_sum, gain_sums, lanes):
    arrays = (*sums, hidden_grad, states_sum)
    count = len(arrays)
    anywhere, vmem = pl.BlockSpec(memory_space=pl.ANY), pl.BlockSpec(memory_space=pltpu.VMEM)
    return pl.pallas_call(
        lambda *refs: finish_kernel(count, *refs),
        out_shape=[jax.ShapeDtypeStruct(a.shape, a.dtype) for a in arrays]
        + [jax.ShapeDtypeStruct((1, lanes), jnp.float32)] * 3,
        in_specs=[anywhere] * count + [vmem],
        out_specs=[anywhere] * count + [vmem] * 3,
        scratch_shapes=[pltpu.VMEM(a.shape, a.dtype) for a in arrays]
        + [pltpu.SemaphoreType.DMA((2, count))],
        compiler_params=pltpu.CompilerParams(vmem_limit_bytes=62 * 2**20),
        name="finish",
    )(*arrays, gain_sums)


def plain_call(kernel, name, ins, spaces, outs, scratch, flops):
    space = {"v": pltpu.VMEM, "s": pltpu.SMEM, "a": pl.ANY}
    out_shape = [jax.ShapeDtypeStruct(shape, kind) for shape, kind in outs]
    moved = sum(a.size * a.dtype.itemsize for a in list(ins) + out_shape)
    return pl.pallas_call(
        kernel,
        out_shape=out_shape,
        in_specs=[pl.BlockSpec(memory_space=space[p]) for p in spaces],
        out_specs=[pl.BlockSpec(memory_space=pltpu.VMEM)] * len(outs),
        scratch_shapes=scratch,
        compiler_params=pltpu.CompilerParams(vmem_limit_bytes=62 * 2**20),
        cost_estimate=pl.CostEstimate(flops=flops, bytes_accessed=moved, transcendentals=0),
        name=name,
    )(*ins)


def copies_of(arrays):
    return [pltpu.VMEM(a.shape, a.dtype) for a in arrays] + [
        pltpu.SemaphoreType.DMA((len(arrays),))
    ]


def local(
    hidden,
    encoder,
    lengths,
    enc_lengths,
    w_query,
    w_key,
    w_value,
    w_attn_out,
    w_relative,
    w_cross_query,
    w_cross_key,
    w_cross_value,
    w_cross_out,
    w_up,
    w_down,
    gain_attn,
    gain_cross,
    gain_ffn,
    cotangent,
):
    ndp, chips = lax.axis_size("dp"), lax.axis_size("seq")
    devices = ndp * chips
    low, wide = jnp.bfloat16, jnp.float32
    _, rows, local_len, width = hidden.shape
    span, tokens = local_len * chips, 3 * rows * local_len
    weights = (
        w_key,
        w_value,
        w_query,
        w_relative,
        w_cross_key,
        w_cross_value,
        w_attn_out,
        w_cross_query,
        w_cross_out,
        w_up,
        w_down,
    )
    gains = (gain_attn, gain_cross, gain_ffn)
    every = rows * (span + 2 * local_len)
    kernels = chips == 4 and w_query.shape[0] == 128 and w_down.shape[0] == 512
    if kernels:
        gains = [gain.reshape(1, -1) for gain in gains]
        results = layer(
            gains, weights, hidden, encoder, cotangent, lengths, enc_lengths, ndp
        )
        whole, results = results[1 : len(weights) + 1], results[len(weights) + 1 :]
        whole = [w.reshape(-1, w.shape[-1]) for w in whole]
        (hid, x_all, query, keys, values, prob, prob_own, context, ckeys, cvalues) = results[:10]
        (normal, normal_scale, normed_low, cquery, cprob, ccontext, output) = results[10:17]
        (crossed_low, activated, last_low, slope, gain_total, normal2, scale2) = results[17:24]
        (states, gains, grad) = results[24:]
        states = states.reshape(-1, width)
    else:
        gains = jnp.pad(jnp.stack(gains), ((0, 5), (0, 0)))
        whole = [lax.all_gather(w, "dp", axis=0, tiled=True) for w in weights]
        gains = lax.all_gather(gains, "dp", axis=1, tiled=True).astype(wide)
        mains = lax.all_gather(hidden[0], "seq", axis=1).reshape(-1, width)
        states = lax.all_gather(encoder, "seq", axis=1).reshape(-1, width)
    (
        full_key,
        full_value,
        full_query,
        full_relative,
        full_ckey,
        full_cvalue,
        full_attn_out,
        full_cquery,
        full_cout,
        full_up,
        full_down,
    ) = whole
    if not kernels:
        ff = full_up.shape[1]
        fetched = (
            full_key,
            full_value,
            full_query,
            full_relative,
            full_ckey,
            full_cvalue,
            full_attn_out,
            full_cquery,
        )
        (
            hid,
            x_all,
            query,
            keys,
            values,
            prob,
            prob_own,
            context,
            ckeys,
            cvalues,
            normal,
            normal_scale,
            normed_low,
            cquery,
            cprob,
            ccontext,
        ) = plain_call(
            lambda *refs: forward_kernel(rows, local_len, *refs),
            "forward_attention",
            (hidden, mains, states, lengths, enc_lengths, gains) + fetched,
            "vvvssv" + "a" * len(fetched),
            [
                ((tokens, width), low),
                ((every, width), low),
                ((tokens, width), low),
                ((every, width), low),
                ((every, width), low),
                ((4 * rows, 12 * local_len, span), low),
                ((tokens, width), low),
                ((tokens, width), low),
                ((rows * span, width), low),
                ((rows * span, width), low),
                ((tokens, width), wide),
                ((tokens, 128), wide),
                ((tokens, width), low),
                ((tokens, width), low),
                ((4 * rows, 12 * local_len, span), low),
                ((tokens, width), low),
            ],
            [
                pltpu.VMEM((tokens, full_relative.shape[1]), low),
                pltpu.VMEM((tokens, width), wide),
            ]
            + copies_of(fetched),
            12 * 10**9,
        )
        fetched = (full_cout, full_up, full_down)
        (
            output,
            crossed_low,
            activated,
            last_low,
            up_back,
            cross_grad,
            cross_low,
            ccontext_back,
            gain_middle,
        ) = plain_call(
            lambda *refs: middle_kernel(rows, local_len, *refs),
            "feed_forward",
            (normal, ccontext, gains, cotangent) + fetched,
            "vvvv" + "a" * len(fetched),
            [
                (hidden.shape, low),
                ((tokens, width), low),
                ((tokens, ff), low),
                ((tokens, width), low),
                ((tokens, ff), low),
                ((tokens, width), wide),
                ((tokens, width), low),
                ((tokens, width), low),
                ((3, 8, width), wide),
            ],
            [
                pltpu.VMEM((tokens, width), wide),
                pltpu.VMEM((tokens, 128), wide),
                pltpu.VMEM((tokens, ff), low),
                pltpu.VMEM((tokens, width), wide),
            ]
            + copies_of(fetched),
            14 * 10**9,
        )
    if kernels:
        values_in = (
            activated, last_low, grad, slope, crossed_low, normal2, scale2, normal, normal_scale,
            ccontext, normed_low, context, hid, x_all, states, cquery, ckeys, cvalues, cprob,
            query, keys, values, prob, prob_own, gains, gain_total,
        )
        weights_in = (
            full_down, full_up, full_cout, full_cquery, full_attn_out, full_ckey, full_cvalue,
            full_key, full_value, full_query, full_relative,
        )
        *sums, gain_sums, states_sum, hidden_grad = back(values_in, weights_in, hidden.shape, ndp)
        *sums, output, hidden_grad, states_sum, gain_a, gain_b, gain_c = finish(
            sums + [output], hidden_grad, states_sum, gain_sums, width // devices
        )
        gain_sums = [gain.reshape(-1) for gain in (gain_a, gain_b, gain_c)]
    else:
        fetched = (
            full_cquery,
            full_attn_out,
            full_ckey,
            full_cvalue,
            full_query,
            full_relative,
            full_key,
            full_value,
        )
        (
            cquery_back,
            ckey_back,
            cvalue_back,
            attn_low,
            query_back,
            key_back,
            value_back,
            rel_back,
            hidden_own,
            main_part,
            states_part,
            gain_back,
        ) = plain_call(
            lambda *refs: backward_kernel(rows, local_len, *refs),
            "backward_attention",
            (
                ccontext_back,
                cross_grad,
                cquery,
                ckeys,
                cvalues,
                cprob,
                normal,
                normal_scale,
                gains,
                query,
                keys,
                values,
                prob,
                prob_own,
            )
            + fetched,
            "v" * 14 + "a" * len(fetched),
            [
                ((tokens, width), low),
                ((rows * span, width), low),
                ((rows * span, width), low),
                ((tokens, width), low),
                ((tokens, width), low),
                ((every, width), low),
                ((every, width), low),
                ((tokens, full_relative.shape[1]), low),
                (hidden.shape, wide),
                ((chips, rows, local_len, width), low),
                ((chips, rows, local_len, width), low),
                ((3, 8, width), wide),
            ],
            [pltpu.VMEM((tokens, width), wide), pltpu.VMEM((tokens, width), low)] + copies_of(fetched),
            14 * 10**9,
        )
        xs = [activated, crossed_low, ccontext, normed_low, context, hid, x_all, states]
        gs = [
            last_low,
            up_back,
            cross_low,
            cquery_back,
            attn_low,
            query_back,
            rel_back,
            key_back,
            value_back,
            ckey_back,
            cvalue_back,
        ]
        pairs = [(0, 0), (1, 1), (2, 2), (3, 3), (4, 4), (5, 5), (5, 6), (6, 7), (6, 8), (7, 9), (7, 10)]
        gain_parts = jnp.sum(gain_middle + gain_back, axis=1)
        sums = [
            lax.psum_scatter(
                weight_grad(xs[i], gs[j]), ("seq", "dp"), scatter_dimension=0, tiled=True
            )
            for i, j in pairs
        ]
        gain_sums = lax.psum_scatter(gain_parts, ("seq", "dp"), scatter_dimension=1, tiled=True)
        main_sum, states_sum = (
            lax.psum_scatter(part, "seq", scatter_dimension=0).astype(wide)
            for part in (main_part, states_part)
        )
        hidden_grad = hidden_own.at[0].add(main_sum)
    gainattn_sum, gaincross_sum, gainffn_sum = gain_sums
    (
        down_sum,
        up_sum,
        cout_sum,
        cquery_sum,
        outproj_sum,
        query_sum,
        relative_sum,
        keyw_sum,
        valuew_sum,
        ckey_sum,
        cvalue_sum,
    ) = sums
    return (
        output,
        hidden_grad,
        states_sum,
        query_sum,
        keyw_sum,
        valuew_sum,
        outproj_sum,
        relative_sum,
        cquery_sum,
        ckey_sum,
        cvalue_sum,
        cout_sum,
        up_sum,
        down_sum,
        gainattn_sum,
        gaincross_sum,
        gainffn_sum,
    )


def solution(mesh):
    in_specs = (
        P(None, "dp", "seq", None),
        P("dp", "seq", None),
        P("dp"),
        P("dp"),
        P("dp", None),
        P("dp", None),
        P("dp", None),
        P("dp", None),
        P("dp", None),
        P("dp", None),
        P("dp", None),
        P("dp", None),
        P("dp", None),
        P("dp", None),
        P("dp", None),
        P("dp"),
        P("dp"),
        P("dp"),
        P(None, "dp", "seq", None),
    )
    out_specs = (
        P(None, "dp", "seq", None),
        P(None, "dp", "seq", None),
        P("dp", "seq", None),
        P(("seq", "dp"), None),
        P(("seq", "dp"), None),
        P(("seq", "dp"), None),
        P(("seq", "dp"), None),
        P(("seq", "dp"), None),
        P(("seq", "dp"), None),
        P(("seq", "dp"), None),
        P(("seq", "dp"), None),
        P(("seq", "dp"), None),
        P(("seq", "dp"), None),
        P(("seq", "dp"), None),
        P(("seq", "dp")),
        P(("seq", "dp")),
        P(("seq", "dp")),
    )
    return jax.shard_map(local, mesh=mesh, in_specs=in_specs, out_specs=out_specs, check_vma=False)
```

```python
import functools
import math

import jax
import jax.numpy as jnp
from jax import lax
from jax.experimental import pallas as pl
from jax.experimental.pallas import tpu as pltpu
from jax.sharding import PartitionSpec as P

MESH = pl.DeviceIdType.MESH

HEADS = 16
HEAD_DIM = 64
BUCKETS = 32


eps_norm = 1e-05
bucket_edges = [step_index for step_index in range(1, 16)] + [
    int(math.ceil(16 * 8 ** ((step_index - 16) / 16))) for step_index in range(16, 32)
]


def flatten_rows(array):
    return array.reshape(-1, array.shape[-1])


def weight_grad(array, grad_rows):
    return jnp.einsum(
        "nd,ne->de",
        flatten_rows(array),
        flatten_rows(grad_rows),
        preferred_element_type=jnp.float32,
    )


def remote(src, dst, send, recv, to):
    return pltpu.make_async_remote_copy(
        src_ref=src, dst_ref=dst, send_sem=send, recv_sem=recv, device_id=to, device_id_type=MESH
    )


def place():
    s = lax.axis_index("seq")
    d = lax.axis_index("dp")
    z, c = d // 2, lax.rem(d, 2)
    sx = s + 1 - 2 * lax.rem(s, 2)
    sy = lax.rem(s + 2, 4)
    return s, z, c, sx, sy


def greet(nz):
    s, z, c, sx, sy = place()
    barrier = pltpu.get_barrier_semaphore()
    dests = [(s, 2 * z + 1 - c), (sx, 2 * z + c), (sy, 2 * z + c)]
    for dz in range(1, nz):
        dests.append((s, 2 * lax.rem(z + dz, nz) + c))
    for dest in dests:
        pl.semaphore_signal(barrier, inc=1, device_id=dest, device_id_type=MESH)
    pl.semaphore_wait(barrier, len(dests))


NEG = -1000000000.0


def mm(left, right):
    return jnp.dot(left, right, preferred_element_type=jnp.float32)


def mm_back(left, right):
    return lax.dot_general(
        left, right, (((1,), (1,)), ((), ())), preferred_element_type=jnp.float32
    )


def mm_grad(left, right):
    return lax.dot_general(
        left, right, (((0,), (0,)), ((), ())), preferred_element_type=jnp.float32
    )


def tiles(width, body):
    def step(i, carry):
        body(pl.ds(pl.multiple_of(i * 256, 256), 256))
        return carry

    lax.fori_loop(0, width // 256, step, 0)


def row_tiles(rows, body, step_rows=64):
    def step(i, carry):
        body(pl.ds(pl.multiple_of(i * step_rows, step_rows), step_rows))
        return carry

    lax.fori_loop(0, rows // step_rows, step, 0)


def heads_in(tile):
    lane = lax.broadcasted_iota(jnp.int32, tile.shape, 1) // (tile.shape[1] // 4)
    return jnp.concatenate(
        [jnp.where(lane == h, tile, jnp.zeros_like(tile)) for h in range(4)], axis=0
    )


def heads_out(stacked):
    n, wide = stacked.shape[0] // 4, stacked.shape[1]
    lane = lax.broadcasted_iota(jnp.int32, (n, wide), 1) // (wide // 4)
    result = stacked[3 * n :]
    for h in (2, 1, 0):
        result = jnp.where(lane == h, stacked[h * n : (h + 1) * n], result)
    return result


def head_lanes(columns, wide):
    n = columns[0].shape[0]
    lane = lax.broadcasted_iota(jnp.int32, (n, wide), 1) // (wide // 4)
    result = jnp.broadcast_to(columns[3], (n, wide))
    for h in (2, 1, 0):
        result = jnp.where(lane == h, jnp.broadcast_to(columns[h], (n, wide)), result)
    return result


def head_sums(product):
    n, wide = product.shape
    lane = lax.broadcasted_iota(jnp.int32, (n, wide), 1) // (wide // 4)
    return [
        jnp.sum(jnp.where(lane == h, product, 0.0), axis=1, keepdims=True) for h in range(4)
    ]


def bucket_of(distance):
    total = jnp.zeros_like(distance)
    for edge in bucket_edges:
        total = total + (distance >= edge).astype(jnp.int32)
    return total


def hot_forward(start, span):
    lag = lax.broadcasted_iota(jnp.int32, (128, span), 1)
    row = lax.rem(lax.broadcasted_iota(jnp.int32, (128, span), 0), BUCKETS)
    distance = lax.rem(start - lag + span, span)
    return jnp.where(bucket_of(distance) == row, 1.0, 0.0).astype(jnp.bfloat16)


def hot_backward(start, span):
    lag = lax.broadcasted_iota(jnp.int32, (span, 128), 0)
    column = lax.rem(lax.broadcasted_iota(jnp.int32, (span, 128), 1), BUCKETS)
    distance = lax.rem(start + lag + 1, span)
    return jnp.where(bucket_of(distance) == column, 1.0, 0.0).astype(jnp.bfloat16)


def skewed(array, block):
    return jnp.concatenate(
        [
            pltpu.roll(array[i : i + block], 0, 1, stride=1, stride_axis=0)
            for i in range(0, array.shape[0], block)
        ],
        axis=0,
    )


def norm_rows(values):
    centred = values - jnp.mean(values, axis=1, keepdims=True)
    scale = lax.rsqrt(jnp.mean(centred * centred, axis=1, keepdims=True) + eps_norm)
    return centred * scale, scale


def norm_back(grad, normal, scale, gain):
    grad = grad * gain
    return scale * (
        grad
        - jnp.mean(grad, axis=1, keepdims=True)
        - normal * jnp.mean(grad * normal, axis=1, keepdims=True)
    )


def add_rows(total_ref, index, product):
    total_ref[index] += jnp.sum(product.reshape(-1, 8, product.shape[1]), axis=0)


class Fetch:
    def __init__(self, sources, targets, sems):
        self.copies = [
            pltpu.make_async_copy(src, dst, sems.at[i])
            for i, (src, dst) in enumerate(zip(sources, targets))
        ]
        self.targets = targets
        self.waited = set()
        for copy in self.copies:
            copy.start()

    def __getitem__(self, i):
        if i not in self.waited:
            self.waited.add(i)
            self.copies[i].wait()
        return self.targets[i]


def attend_step(
    r, g, step, start, mine, span, local_len, rows, lengths, query, rel, keys, values, prob, prob_own, context, hot
):
    cols = pl.ds(pl.multiple_of(g * 256, 256), 256)
    own_rows = pl.ds(pl.multiple_of(r * mine, local_len), mine)
    main_rows = pl.ds(pl.multiple_of(r * span, span), span)
    side_rows = pl.ds(pl.multiple_of(rows * span + r * 2 * local_len, local_len), 2 * local_len)
    q_tile = query[own_rows, cols]
    rel_tile = rel[own_rows, pl.ds(pl.multiple_of(g * 128, 128), 128)]
    side_key = keys[side_rows, cols].astype(jnp.float32)
    side_value = values[side_rows, cols].astype(jnp.float32)
    zero = jnp.zeros((local_len, 256), jnp.float32)
    scores = mm_back(heads_in(q_tile), keys[main_rows, cols])
    bias = skewed(mm(heads_in(rel_tile), hot), local_len)
    products = q_tile.astype(jnp.float32) * jnp.concatenate([zero, side_key], axis=0)
    own_dot = head_sums(products)
    rel_lane = lax.broadcasted_iota(jnp.int32, (mine, 128), 1)
    rel_wide = rel_tile.astype(jnp.float32)
    row = lax.broadcasted_iota(jnp.int32, (mine, span), 0)
    at = lax.broadcasted_iota(jnp.int32, (mine, span), 1)
    ahead = start + lax.rem(row, local_len) + jnp.where(row < local_len, 1, 0)
    kept = (at < ahead) & (at < lengths[r])
    first = lax.broadcasted_iota(jnp.int32, (mine, 1), 0) < local_len
    low, owns = [], []
    for h in range(4):
        part = slice(h * mine, (h + 1) * mine)
        score = jnp.where(kept, scores[part] + bias[part], NEG)
        near = jnp.sum(jnp.where(rel_lane == h * BUCKETS, rel_wide, 0.0), axis=1, keepdims=True)
        own = jnp.where(first, NEG, own_dot[h] + near)
        peak = jnp.maximum(jnp.max(score, axis=1, keepdims=True), own)
        power = jnp.exp(score - peak)
        own_power = jnp.exp(own - peak)
        share = 1.0 / (jnp.sum(power, axis=1, keepdims=True) + own_power)
        low.append((power * share).astype(jnp.bfloat16))
        owns.append(own_power * share)
    low = jnp.concatenate(low, axis=0)
    prob[step] = low
    spread = head_lanes(owns, 256)
    prob_own[own_rows, cols] = spread.astype(prob_own.dtype)
    total = heads_out(mm(low, values[main_rows, cols]))
    total = total + spread * jnp.concatenate([zero, side_value], axis=0)
    context[own_rows, cols] = total.astype(context.dtype)


def cross_step(
    r, g, step, mine, span, local_len, enc_lengths, cquery, ckeys, cvalues, cprob, ccontext
):
    cols = pl.ds(pl.multiple_of(g * 256, 256), 256)
    own_rows = pl.ds(pl.multiple_of(r * mine, local_len), mine)
    main_rows = pl.ds(pl.multiple_of(r * span, span), span)
    scores = mm_back(heads_in(cquery[own_rows, cols]), ckeys[main_rows, cols])
    at = lax.broadcasted_iota(jnp.int32, (mine, span), 1)
    kept = at < enc_lengths[r]
    low = []
    for h in range(4):
        score = jnp.where(kept, scores[h * mine : (h + 1) * mine], NEG)
        power = jnp.exp(score - jnp.max(score, axis=1, keepdims=True))
        share = 1.0 / jnp.sum(power, axis=1, keepdims=True)
        low.append((power * share).astype(jnp.bfloat16))
    low = jnp.concatenate(low, axis=0)
    cprob[step] = low
    ccontext[own_rows, cols] = heads_out(mm(low, cvalues[main_rows, cols])).astype(
        ccontext.dtype
    )


def forward_kernel(rows, local_len, *refs):
    (
        hidden,
        mains,
        states,
        lengths,
        enc_lengths,
        gains,
        *weights,
    ) = refs[:14]
    (hid, x_all, query, keys, values, prob, prob_own, context, ckeys, cvalues) = refs[14:24]
    (normal, normal_scale, normed_low, cquery, cprob, ccontext) = refs[24:30]
    rel, residual = refs[30:32]
    fetch = Fetch(weights, refs[32:40], refs[40])
    w_key, w_value, w_query, w_relative, w_ckey, w_cvalue, w_out, w_cquery = range(8)
    width = hid.shape[1]
    mine = 3 * local_len
    span = mains.shape[0] // rows
    start = lax.axis_index("seq") * local_len
    x_all[: rows * span] = mains[...]
    for r in range(rows):
        for j in range(3):
            tile = hidden[j, r]
            hid[r * mine + j * local_len : r * mine + (j + 1) * local_len] = tile
            if j:
                at = rows * span + (2 * r + j - 1) * local_len
                x_all[at : at + local_len] = tile

    def project(left, w, target, scale=None):
        weight = fetch[w]

        def body(cols):
            product = mm(left[...], weight[:, cols])
            if scale is not None:
                product = product * scale
            target[:, cols] = product.astype(target.dtype)

        tiles(target.shape[1], body)

    project(x_all, w_key, keys)
    project(x_all, w_value, values)
    project(hid, w_query, query, 0.125)
    project(hid, w_relative, rel)
    hot = hot_forward(start, span)

    def attend(step, carry):
        attend_step(
            step // 4, lax.rem(step, 4), step, start, mine, span, local_len, rows, lengths,
            query, rel, keys, values, prob, prob_own, context, hot,
        )
        return carry

    lax.fori_loop(0, 4 * rows, attend, 0)
    project(states, w_ckey, ckeys)
    project(states, w_cvalue, cvalues)
    weight_out = fetch[w_out]

    def out_body(cols):
        residual[:, cols] = hid[:, cols].astype(jnp.float32) + mm(context[...], weight_out[:, cols])

    tiles(width, out_body)

    def norm_body(part):
        normal[part], scale = norm_rows(residual[part])
        normal_scale[part] = jnp.broadcast_to(scale, (scale.shape[0], 128))
        normed_low[part] = (normal[part] * gains[0:1]).astype(jnp.bfloat16)

    row_tiles(hid.shape[0], norm_body)
    project(normed_low, w_cquery, cquery, 0.125)

    def cross(step, carry):
        cross_step(
            step // 4, lax.rem(step, 4), step, mine, span, local_len, enc_lengths,
            cquery, ckeys, cvalues, cprob, ccontext,
        )
        return carry

    lax.fori_loop(0, 4 * rows, cross, 0)


def middle_kernel(
    rows,
    local_len,
    normal,
    ccontext,
    gains,
    cotangent,
    any_cout,
    any_up,
    any_down,
    output,
    crossed_low,
    activated,
    last_low,
    up_back,
    cross_grad,
    cross_low,
    ccontext_back,
    gain_total,
    normal2,
    scale2,
    slope,
    residual,
    v_cout,
    v_up,
    v_down,
    sems,
):
    fetch = Fetch((any_cout, any_up, any_down), (v_cout, v_up, v_down), sems)
    tokens, width = normal.shape
    mine = 3 * local_len
    gain_total[...] = jnp.zeros_like(gain_total)
    weight_cout = fetch[0]

    def cross_body(cols):
        residual[:, cols] = normal[:, cols] * gains[0:1, cols] + mm(
            ccontext[...], weight_cout[:, cols]
        )

    tiles(width, cross_body)

    def norm_body(part):
        normal2[part], scale = norm_rows(residual[part])
        scale2[part] = jnp.broadcast_to(scale, (scale.shape[0], 128))
        crossed_low[part] = (normal2[part] * gains[1:2]).astype(jnp.bfloat16)

    row_tiles(tokens, norm_body)
    weight_up = fetch[1]

    def up_body(cols):
        value = mm(crossed_low[...], weight_up[:, cols])
        below = 0.5 + 0.5 * lax.erf(value * (0.5**0.5))
        activated[:, cols] = (value * below).astype(jnp.bfloat16)
        density = jnp.exp(-0.5 * value * value) * (1.0 / math.sqrt(2.0 * math.pi))
        slope[:, cols] = (below + value * density).astype(jnp.bfloat16)

    tiles(activated.shape[1], up_body)
    weight_down = fetch[2]

    def down_body(cols):
        residual[:, cols] = normal2[:, cols] * gains[1:2, cols] + mm(
            activated[...], weight_down[:, cols]
        )

    tiles(width, down_body)
    for r in range(rows):
        for j in range(3):
            at = r * mine + j * local_len
            part = slice(at, at + local_len)
            normal3, scale = norm_rows(residual[part])
            output[j, r] = (normal3 * gains[2:3]).astype(output.dtype)
            above = cotangent[j, r].astype(jnp.float32)
            add_rows(gain_total, 2, above * normal3)
            grad = norm_back(above, normal3, scale, gains[2:3])
            residual[part] = grad
            last_low[part] = grad.astype(jnp.bfloat16)

    def down_back(cols):
        product = mm_back(last_low[...], weight_down[cols, :])
        up_back[:, cols] = (product * slope[:, cols].astype(jnp.float32)).astype(jnp.bfloat16)

    tiles(activated.shape[1], down_back)

    def up_back_body(cols):
        residual[:, cols] = residual[:, cols] + mm_back(up_back[...], weight_up[cols, :])

    tiles(width, up_back_body)

    def cross_norm_back(part):
        above = residual[part]
        add_rows(gain_total, 1, above * normal2[part])
        grad = norm_back(above, normal2[part], scale2[part][:, 0:1], gains[1:2])
        cross_grad[part] = grad
        cross_low[part] = grad.astype(jnp.bfloat16)

    row_tiles(tokens, cross_norm_back)

    def cout_back(cols):
        ccontext_back[:, cols] = mm_back(cross_low[...], weight_cout[cols, :]).astype(jnp.bfloat16)

    tiles(width, cout_back)


def turning(span):
    return jnp.where(
        lax.broadcasted_iota(jnp.int32, (span, span), 0)
        + lax.broadcasted_iota(jnp.int32, (span, span), 1)
        == span - 1,
        1.0,
        0.0,
    ).astype(jnp.bfloat16)


def cross_back_step(
    r, g, step, mine, span, local_len, ccontext_back, cvalues, cprob, ckeys, cquery, cquery_back, ckey_back, cvalue_back
):
    cols = pl.ds(pl.multiple_of(g * 256, 256), 256)
    own_rows = pl.ds(pl.multiple_of(r * mine, local_len), mine)
    main_rows = pl.ds(pl.multiple_of(r * span, span), span)
    above = heads_in(ccontext_back[own_rows, cols])
    grads = mm_back(above, cvalues[main_rows, cols])
    low = []
    for h in range(4):
        part = slice(h * mine, (h + 1) * mine)
        share = cprob[step, part].astype(jnp.float32)
        weighted = share * grads[part]
        low.append(
            (weighted - share * jnp.sum(weighted, axis=1, keepdims=True)).astype(jnp.bfloat16)
        )
    low = jnp.concatenate(low, axis=0)
    back = heads_out(mm(low, ckeys[main_rows, cols])).astype(jnp.bfloat16)
    cquery_back[own_rows, cols] = back * jnp.bfloat16(0.125)
    ckey_back[main_rows, cols] = mm_grad(low, heads_in(cquery[own_rows, cols])).astype(
        jnp.bfloat16
    )
    cvalue_back[main_rows, cols] = mm_grad(cprob[step], above).astype(jnp.bfloat16)


def attend_back_step(
    r, g, step, mine, span, local_len, rows, context_back, query, keys, values, prob, prob_own,
    query_back, key_back, value_back, rel_back, hot, turn
):
    cols = pl.ds(pl.multiple_of(g * 256, 256), 256)
    own_rows = pl.ds(pl.multiple_of(r * mine, local_len), mine)
    main_rows = pl.ds(pl.multiple_of(r * span, span), span)
    side_rows = pl.ds(pl.multiple_of(rows * span + r * 2 * local_len, local_len), 2 * local_len)
    above_tile = context_back[own_rows, cols]
    above = heads_in(above_tile)
    above_wide = above_tile.astype(jnp.float32)
    q_tile = query[own_rows, cols]
    zero = jnp.zeros((local_len, 256), jnp.float32)
    side_key = jnp.concatenate([zero, keys[side_rows, cols].astype(jnp.float32)], axis=0)
    side_value = jnp.concatenate([zero, values[side_rows, cols].astype(jnp.float32)], axis=0)
    spread = prob_own[own_rows, cols].astype(jnp.float32)
    grads = mm_back(above, values[main_rows, cols])
    own_grads = head_sums(above_wide * side_value)
    low, own_low = [], []
    for h in range(4):
        part = slice(h * mine, (h + 1) * mine)
        share = prob[step, part].astype(jnp.float32)
        own_share = spread[:, h * 64 : h * 64 + 1]
        weighted = share * grads[part]
        delta = jnp.sum(weighted, axis=1, keepdims=True) + own_share * own_grads[h]
        low.append((weighted - share * delta).astype(jnp.bfloat16))
        own_low.append(own_share * (own_grads[h] - delta))
    low = jnp.concatenate(low, axis=0)
    own_spread = head_lanes(own_low, 256)
    back = heads_out(mm(low, keys[main_rows, cols])) + own_spread * side_key
    query_back[own_rows, cols] = back.astype(jnp.bfloat16) * jnp.bfloat16(0.125)
    key_back[main_rows, cols] = mm_grad(low, heads_in(q_tile)).astype(jnp.bfloat16)
    value_back[main_rows, cols] = mm_grad(prob[step], above).astype(jnp.bfloat16)
    key_back[side_rows, cols] = (own_spread * q_tile.astype(jnp.float32))[local_len:].astype(
        jnp.bfloat16
    )
    value_back[side_rows, cols] = (spread * above_wide)[local_len:].astype(jnp.bfloat16)
    turned_low = skewed(mm(low, turn), local_len).astype(jnp.bfloat16)
    rel_total = heads_out(mm(turned_low, hot))
    near = lax.rem(lax.broadcasted_iota(jnp.int32, rel_total.shape, 1), BUCKETS) == 0
    rel_total = rel_total + jnp.where(near, head_lanes(own_low, 128), 0.0)
    rel_back[own_rows, pl.ds(pl.multiple_of(g * 128, 128), 128)] = rel_total.astype(
        jnp.bfloat16
    )


def backward_kernel(rows, local_len, *refs):
    (
        ccontext_back,
        cross_grad,
        cquery,
        ckeys,
        cvalues,
        cprob,
        normal,
        normal_scale,
        gains,
        query,
        keys,
        values,
        prob,
        prob_own,
        *weights,
    ) = refs[:22]
    (cquery_back, ckey_back, cvalue_back, attn_low, query_back, key_back) = refs[22:28]
    (value_back, rel_back, hidden_own, main_part, states_part, gain_total) = refs[28:34]
    residual, context_back = refs[34:36]
    fetch = Fetch(weights, refs[36:44], refs[44])
    w_cquery, w_out, w_ckey, w_cvalue, w_query, w_relative, w_key, w_value = range(8)
    tokens, width = query.shape
    mine = 3 * local_len
    span = ckeys.shape[0] // rows
    start = lax.axis_index("seq") * local_len
    gain_total[...] = jnp.zeros_like(gain_total)

    def cross(step, carry):
        cross_back_step(
            step // 4, lax.rem(step, 4), step, mine, span, local_len, ccontext_back, cvalues,
            cprob, ckeys, cquery, cquery_back, ckey_back, cvalue_back,
        )
        return carry

    lax.fori_loop(0, 4 * rows, cross, 0)
    weight_cquery = fetch[w_cquery]

    def cquery_body(cols):
        residual[:, cols] = cross_grad[:, cols] + mm_back(cquery_back[...], weight_cquery[cols, :])

    tiles(width, cquery_body)

    def attn_norm_back(part):
        above = residual[part]
        add_rows(gain_total, 0, above * normal[part])
        grad = norm_back(above, normal[part], normal_scale[part][:, 0:1], gains[0:1])
        residual[part] = grad
        attn_low[part] = grad.astype(jnp.bfloat16)

    row_tiles(tokens, attn_norm_back)
    weight_out = fetch[w_out]

    def out_back(cols):
        context_back[:, cols] = mm_back(attn_low[...], weight_out[cols, :]).astype(jnp.bfloat16)

    tiles(width, out_back)
    hot = hot_backward(start, span)
    turn = turning(span)

    def attend(step, carry):
        attend_back_step(
            step // 4, lax.rem(step, 4), step, mine, span, local_len, rows, context_back, query,
            keys, values, prob, prob_own, query_back, key_back, value_back, rel_back, hot, turn,
        )
        return carry

    lax.fori_loop(0, 4 * rows, attend, 0)
    weight_ckey, weight_cvalue = fetch[w_ckey], fetch[w_cvalue]
    weight_query, weight_relative = fetch[w_query], fetch[w_relative]
    weight_key, weight_value = fetch[w_key], fetch[w_value]
    chips = rows * span // (rows * local_len)

    def states_body(cols):
        total = mm_back(ckey_back[...], weight_ckey[cols, :])
        total = total + mm_back(cvalue_back[...], weight_cvalue[cols, :])
        total = total.astype(jnp.bfloat16)
        for r in range(rows):
            for p in range(chips):
                at = r * span + p * local_len
                states_part[p, r, :, cols] = total[at : at + local_len]

    tiles(width, states_body)

    def hidden_body(cols):
        total = mm_back(key_back[...], weight_key[cols, :])
        total = total + mm_back(value_back[...], weight_value[cols, :])
        mains = total[: rows * span].astype(jnp.bfloat16)
        for r in range(rows):
            for p in range(chips):
                at = r * span + p * local_len
                main_part[p, r, :, cols] = mains[at : at + local_len]
        own = residual[:, cols] + mm_back(query_back[...], weight_query[cols, :])
        own = own + mm_back(rel_back[...], weight_relative[cols, :])
        for r in range(rows):
            for j in range(3):
                tile = own[r * mine + j * local_len : r * mine + (j + 1) * local_len]
                if j:
                    at = rows * span + (2 * r + j - 1) * local_len
                    tile = tile + total[at : at + local_len]
                hidden_own[j, r, :, cols] = tile

    tiles(width, hidden_body)


def gather_steps(sources, shards, planes, wholes, full_planes, nz, sems):
    local_sem, send, recv, plane_send, plane_recv, stage_sem = sems
    s, z, c, sx, sy = place()
    own = 2 * z + c
    core = (s, 2 * z + 1 - c)
    beside_x, beside_y = (sx, own), (sy, own)
    staged = [
        pltpu.make_async_copy(source, shard_ref, stage_sem.at[w]) if w else None
        for w, (source, shard_ref) in enumerate(zip(sources, shards))
    ]
    for copy in staged[1:]:
        copy.start()
    awaited = set([0])

    def across(dz):
        return (z + 1 - 2 * lax.rem(z, 2), lax.rem(z + 2, 4), 3 - z)[dz - 1]

    greet(nz)
    started = {}

    def put(i, copy):
        copy.start()
        started.setdefault(i, []).append(copy)

    items = []
    for w, shard_ref in enumerate(shards):
        if shard_ref.shape[0] % 128:
            items.append((w, 0, 0, None))
            continue
        high = min(shard_ref.shape[0], ITEM_ROWS)
        wide = min(shard_ref.shape[1], ITEM_COLUMNS)
        for row in range(0, shard_ref.shape[0], high):
            for col in range(0, shard_ref.shape[1], wide):
                items.append((w, row, high, pl.ds(col, wide)))
    count = len(items)
    split = [item[2] > 0 and i not in ALONG_Z for i, item in enumerate(items)]

    def cut(ref, i, q=None, half=None):
        _, row, height, cols = items[i]
        if not height:
            return ref
        if q is not None:
            height = height // 4
            row = row + q * height
        if half is not None:
            height = height // 2
            row = row + half * height
        return ref.at[pl.ds(row, height), cols]

    def shard(i, q=None):
        return cut(shards[items[i][0]], i, q)

    def whole(i, block, q=None, half=None):
        return cut(wholes[items[i][0]].at[block], i, q, half)

    def along_z(i):
        if items[i][0] not in awaited:
            awaited.add(items[i][0])
            staged[items[i][0]].wait()
        pltpu.make_async_copy(shard(i), whole(i, own), local_sem.at[i]).start()
        q = s if split[i] else None
        for dz in range(1, nz):
            to = (s, 2 * across(dz) + c)
            put(i, remote(shard(i, q), whole(i, own, q), send.at[i, dz, 0], recv.at[i, dz, 0], to))
        put(i, remote(shard(i), whole(i, own), send.at[i, 0, 0], recv.at[i, 0, 0], core))

    def moved(i, dz, kind, q, half, to):
        part = whole(i, 2 * across(dz) + c, q if split[i] else None, half)
        return remote(part, part, send.at[i, dz, kind], recv.at[i, dz, kind], to)

    def core_copy(i, dz, of):
        part = whole(i, 2 * across(dz) + of)
        return remote(part, part, send.at[i, dz, 5], recv.at[i, dz, 5], core)

    def to_core(i, dz):
        put(i, core_copy(i, dz, c))

    def first(i, dz):
        moved(i, dz, 0, s, None, core).wait_recv()
        if split[i]:
            put(i, moved(i, dz, 1, s, None, beside_x))
            put(i, moved(i, dz, 2, s, None, beside_y))
        else:
            to_core(i, dz)

    def second(i, dz):
        moved(i, dz, 1, sx, None, core).wait_recv()
        put(i, moved(i, dz, 4, sx, 0, beside_y))
        moved(i, dz, 2, sy, None, core).wait_recv()
        put(i, moved(i, dz, 3, sy, 1, beside_x))

    def third(i, dz):
        moved(i, dz, 4, 3 - s, 0, core).wait_recv()
        moved(i, dz, 3, 3 - s, 1, core).wait_recv()
        to_core(i, dz)

    def arrive(i):
        other = 1 - c
        pltpu.make_async_copy(shard(i), whole(i, own), local_sem.at[i]).wait()
        block = whole(i, 2 * z + other)
        remote(block, block, send.at[i, 0, 0], recv.at[i, 0, 0], core).wait_recv()
        for dz in range(1, nz):
            core_copy(i, dz, other).wait_recv()

    def plane(i, kind, q, half, to):
        rows = full_planes[i].shape[0]
        part = full_planes[i].at[pl.ds(half * (rows // 2), rows // 2), q]
        return remote(part, part, plane_send.at[i, kind], plane_recv.at[i, kind], to)

    def plane_part(i):
        return planes[i].at[0] if len(planes[i].shape) == 4 else planes[i]

    def plane_whole(i, kind, q, to):
        return remote(
            plane_part(i), full_planes[i].at[:, q], plane_send.at[i, kind], plane_recv.at[i, kind], to
        )

    def plane_here(i):
        return pltpu.make_async_copy(
            plane_part(i), full_planes[i].at[:, s], local_sem.at[count + i]
        )

    def plane_first(i):
        plane_here(i).start()
        put(None, plane_whole(i, 0, s, beside_x))
        put(None, plane_whole(i, 1, s, beside_y))

    def plane_second(i):
        plane_whole(i, 0, sx, core).wait_recv()
        put(None, plane(i, 2, sx, 0, beside_y))
        plane_whole(i, 1, sy, core).wait_recv()
        put(None, plane(i, 3, sy, 1, beside_x))

    def plane_arrive(i):
        plane_here(i).wait()
        plane(i, 2, 3 - s, 0, core).wait_recv()
        plane(i, 3, 3 - s, 1, core).wait_recv()

    def sent(i):
        for copy in started.pop(i, ()):
            copy.wait_send()

    def settle():
        for i in list(started):
            sent(i)

    steps, ready = [], {}

    def step(call, *args):
        steps.append(lambda: call(*args))

    ahead = 5
    for i in range(2):
        plane_first(i)
    for i in range(min(ahead, count)):
        along_z(i)
    for i in range(count + 3):
        for dz in range(1, nz):
            if i < count:
                step(first, i, dz)
            if 1 <= i <= count and split[i - 1]:
                step(second, i - 1, dz)
            if 2 <= i < count + 2 and split[i - 2]:
                step(third, i - 2, dz)
        if ahead + i < count:
            step(along_z, ahead + i)
        if i >= 4:
            step(sent, i - 4)
        if i in (1, 2):
            step(plane_second, i - 1)
        if i == 3:
            ready["planes"] = len(steps)
        if i >= 3:
            ready[i - 3] = len(steps)
    return steps, ready, arrive, plane_arrive, settle


SLOTS = 8
ITEM_ROWS, ITEM_COLUMNS = 128, 2048
ALONG_Z = ()
LAYER_OUTS = 25


def layer_kernel(count, nz, rows, local_len, *refs):
    at = 0

    def take(n):
        nonlocal at
        at += n
        return refs[at - n : at]

    sources = (None,) + take(count - 1)
    gain_rows = take(3)
    hidden, encoder, cotangent, lengths, enc_lengths = take(5)
    wholes, outs = take(count), take(LAYER_OUTS)
    gains, residual = take(2)
    held = list(take(LAYER_OUTS - 1))
    held.insert(14, held[5])
    (hid, x_all, query, keys, values, prob, prob_own, context, ckeys, cvalues) = held[:10]
    (normal, normal_scale, normed_low, cquery, cprob, ccontext, output) = held[10:17]
    (crossed_low, activated, last_low, slope, gain_total, normal2, scale2) = held[17:24]
    states = held[24]
    land_gains, rel, pool, mains, hot_ref = take(5)
    shards = take(count)
    load_sems, out_sems = take(2)
    gain_tile = [row[...].astype(jnp.float32) for row in gain_rows]
    gain_tile.append(jnp.zeros((13, gain_rows[0].shape[1]), jnp.float32))
    shards[0][...] = jnp.concatenate(gain_tile, axis=0).astype(jnp.bfloat16)
    steps, ready, arrive, plane_arrive, settle = gather_steps(
        sources, shards, (hidden, encoder), wholes, (mains, states), nz, take(6)
    )
    tokens, width = hid.shape
    mine = 3 * local_len
    span = mains.shape[1] * local_len
    start = lax.axis_index("seq") * local_len
    emitted = []

    def leave(i):
        return pltpu.make_async_copy(held[i], outs[i], out_sems.at[i])

    def emit(*targets):
        for target in targets:
            i = next(i for i, ref in enumerate(held) if ref is target)
            leave(i).start()
            if target is not prob:
                emitted.append(leave(i))

    def emit_cross():
        leave(14).start()
        emitted.append(leave(14))

    order, blocks_of = [], []
    item = 1
    for w in range(1, count):
        height, wide = shards[w].shape
        high, broad = min(height, ITEM_ROWS), min(wide, ITEM_COLUMNS)
        for row in range(0, height, 128):
            for col in range(0, wide, min(wide, 1024)):
                order.append(item + (row // high) * (wide // broad) + col // broad)
                blocks_of.append(
                    wholes[w].at[:, pl.ds(row, 128), pl.ds(col, min(wide, 1024))]
                )
        item = order[-1] + 1
    KEY, VALUE, QUERY, REL, CKEY, CVALUE, OUT, CQUERY, COUT, UP, DOWN = (*range(9), 9, 13)

    def slot_of(load):
        return load % SLOTS

    def load_copy(load):
        source = blocks_of[load]
        target = pool.at[slot_of(load)]
        if source.shape[2] < target.shape[2]:
            target = target.at[:, :, : source.shape[2]]
        return pltpu.make_async_copy(source, target, load_sems.at[load])

    def weight(load):
        return pool.at[slot_of(load)]

    def columns(load, cols):
        return pool[slot_of(load), :, :, cols].reshape(width, 256)

    def project(left, load, target, scale=None):
        def body(cols):
            product = mm(left[...], columns(load, cols))
            if scale is not None:
                product = product * scale
            target[:, cols] = product.astype(target.dtype)

        tiles(target.shape[1], body)

    def prepare():
        plane_arrive(0)
        plane_arrive(1)
        for r in range(rows):
            for j in range(3):
                tile = hidden[j, r]
                hid[r * mine + j * local_len : r * mine + (j + 1) * local_len] = tile
                if j:
                    to = rows * span + (2 * r + j - 1) * local_len
                    x_all[to : to + local_len] = tile
        x_all[: rows * span] = mains[...].reshape(rows * span, width)
        gain_total[...] = jnp.zeros_like(gain_total)
        hot_ref[...] = hot_forward(start, span)
        emit(hid, x_all, states)

    def take_gains():
        arrive(0)
        copy = pltpu.make_async_copy(wholes[0], land_gains, load_sems.at[len(order)])
        copy.start()
        copy.wait()
        for d in range(land_gains.shape[0]):
            gains[:, d * 128 : (d + 1) * 128] = land_gains[d].astype(jnp.float32)

    def attend(step, carry):
        r, g = step // 4, lax.rem(step, 4)
        attend_step(
            r, g, step, start, mine, span, local_len, rows, lengths, query, rel, keys, values,
            prob, prob_own, context, hot_ref[...],
        )
        return carry

    def cross(step, carry):
        r, g = step // 4, lax.rem(step, 4)
        cross_step(r, g, step, mine, span, local_len, enc_lengths, cquery, ckeys, cvalues, cprob, ccontext)
        return carry

    def out_body(cols):
        residual[:, cols] = hid[:, cols].astype(jnp.float32) + mm(context[...], columns(OUT, cols))

    def norm_body(part):
        normal[part], scale = norm_rows(residual[part])
        normal_scale[part] = jnp.broadcast_to(scale, (scale.shape[0], 128))
        normed_low[part] = (normal[part] * gains[0:1]).astype(jnp.bfloat16)

    def after_attention():
        tiles(width, out_body)
        row_tiles(tokens, norm_body)
        emit(context, normal, normal_scale, normed_low)

    def after_cross_query():
        project(normed_low, CQUERY, cquery, 0.125)
        emit(cquery)
        leave(5).wait()

    def cross_body(cols):
        residual[:, cols] = normal[:, cols] * gains[0:1, cols] + mm(ccontext[...], columns(COUT, cols))

    def cross_norm_body(part):
        normal2[part], scale = norm_rows(residual[part])
        scale2[part] = jnp.broadcast_to(scale, (scale.shape[0], 128))
        after = normal2[part] * gains[1:2]
        crossed_low[part] = after.astype(jnp.bfloat16)
        residual[part] = after

    def after_cross():
        tiles(width, cross_body)
        row_tiles(tokens, cross_norm_body)
        emit(ccontext, crossed_low, normal2, scale2)

    def up(k):
        def body(i, carry):
            cols = pl.ds(pl.multiple_of(i * 256, 256), 256)
            to = pl.ds(pl.multiple_of(k * width + i * 256, 256), 256)
            value = mm(crossed_low[...], columns(UP + k, cols))
            below = 0.5 + 0.5 * lax.erf(value * (0.5**0.5))
            activated[:, to] = (value * below).astype(jnp.bfloat16)
            density = jnp.exp(-0.5 * value * value) * (1.0 / math.sqrt(2.0 * math.pi))
            slope[:, to] = (below + value * density).astype(jnp.bfloat16)
            return carry

        lax.fori_loop(0, width // 256, body, 0)
        if k == 3:
            emit(activated, slope)

    blocks = pool.shape[1]

    def of_down(k, d):
        return d * 4 * 128 + k * 128

    def down(k):
        def body(cols):
            left = jnp.concatenate(
                [activated[:, of_down(k, d) : of_down(k, d) + 128] for d in range(blocks)], axis=1
            )
            residual[:, cols] += mm(left, columns(DOWN + k, cols))

        tiles(width, body)

    def last_norm():
        for r in range(rows):
            for j in range(3):
                part = slice(r * mine + j * local_len, r * mine + (j + 1) * local_len)
                normal3, scale = norm_rows(residual[part])
                output[j, r] = (normal3 * gains[2:3]).astype(output.dtype)
                above = cotangent[j, r].astype(jnp.float32)
                add_rows(gain_total, 2, above * normal3)
                grad = norm_back(above, normal3, scale, gains[2:3])
                residual[part] = grad
                last_low[part] = grad.astype(jnp.bfloat16)
        emit(output, last_low, gain_total)

    pieces = [("planes", 2, prepare)]
    pieces += [
        (KEY, 3, lambda: project(x_all, KEY, keys)),
        (VALUE, 3, lambda: project(x_all, VALUE, values)),
        (QUERY, 2, lambda: project(hid, QUERY, query, 0.125)),
        (REL, 1, lambda: project(hid, REL, rel)),
    ]
    half = 2
    for i in range(0, 4 * rows, half):
        pieces.append((REL, 5, lambda i=i: lax.fori_loop(i, i + half, attend, 0)))
    pieces += [
        (REL, 0, lambda: emit(query, keys, values, prob, prob_own)),
        (CKEY, 2, lambda: project_states(CKEY, ckeys)),
        (CVALUE, 2, lambda: project_states(CVALUE, cvalues)),
        (OUT, 0, take_gains),
        (OUT, 3, after_attention),
        (CQUERY, 2, after_cross_query),
    ]

    def project_states(load, target):
        def body(cols):
            left = states[...].reshape(rows * span, width)
            target[:, cols] = mm(left, columns(load, cols)).astype(target.dtype)

        tiles(width, body)
        emit(target)

    for i in range(0, 4 * rows, half):
        pieces.append((CQUERY, 3, lambda i=i: lax.fori_loop(i, i + half, cross, 0)))
    pieces += [(CQUERY, 0, emit_cross), (COUT, 3, after_cross)]
    pieces += [(UP + k, 3, functools.partial(up, k)) for k in range(4)]
    pieces += [(DOWN + k, 1, functools.partial(down, k)) for k in range(4)]
    pieces.append((DOWN + 3, 3, last_norm))

    last_use = {}
    for index, (need, _, _) in enumerate(pieces):
        last_use[need] = index
    state = {"step": 0, "load": 0}
    arrived, waited = set(), set()

    def run_to(n):
        while state["step"] < min(n, len(steps)):
            steps[state["step"]]()
            state["step"] += 1

    def free(load, done):
        return all(
            last_use[other] < done for other in range(load) if slot_of(other) == slot_of(load)
        )

    def begin_load():
        load = state["load"]
        if order[load] not in arrived:
            arrive(order[load])
            arrived.add(order[load])
        load_copy(load).start()
        state["load"] += 1

    rate = len(steps) / 130.0
    for index, (need, cost, call) in enumerate(pieces):
        if need == "planes":
            run_to(ready["planes"])
        else:
            while state["load"] <= need:
                run_to(ready[order[state["load"]]])
                begin_load()
            if need not in waited:
                waited.add(need)
                load_copy(need).wait()
        call()
        run_to(state["step"] + int(cost * rate + 0.5))
        while (
            state["load"] < len(order)
            and free(state["load"], index + 1)
            and ready[order[state["load"]]] <= state["step"]
        ):
            begin_load()
    run_to(len(steps))
    for copy in emitted:
        copy.wait()
    settle()


def layer(gains, shards, hidden, encoder, cotangent, lengths, enc_lengths, ndp):
    nz = ndp // 2
    shards = (jax.ShapeDtypeStruct((16, gains[0].shape[1]), jnp.bfloat16),) + shards
    count = len(shards)
    low, wide = jnp.bfloat16, jnp.float32
    _, rows, local_len, width = hidden.shape
    tokens, span = 3 * rows * local_len, 4 * local_len
    every = rows * (span + 2 * local_len)
    ff = shards[-2].shape[1]
    steps = sum(
        max(1, w.shape[0] // ITEM_ROWS) * max(1, w.shape[1] // ITEM_COLUMNS) for w in shards
    )
    results = [
        ((tokens, width), low),
        ((every, width), low),
        ((tokens, width), low),
        ((every, width), low),
        ((every, width), low),
        ((4 * rows, 12 * local_len, span), low),
        ((tokens, width), low),
        ((tokens, width), low),
        ((rows * span, width), low),
        ((rows * span, width), low),
        ((tokens, width), wide),
        ((tokens, 128), wide),
        ((tokens, width), low),
        ((tokens, width), low),
        ((4 * rows, 12 * local_len, span), low),
        ((tokens, width), low),
        (hidden.shape, low),
        ((tokens, width), low),
        ((tokens, ff), low),
        ((tokens, width), low),
        ((tokens, ff), low),
        ((3, 8, width), wide),
        ((tokens, width), wide),
        ((tokens, 128), wide),
        ((rows, 4, local_len, width), low),
    ]
    more = [((16, width), wide), ((tokens, width), wide)]
    vmem = pl.BlockSpec(memory_space=pltpu.VMEM)
    smem = pl.BlockSpec(memory_space=pltpu.SMEM)
    anywhere = pl.BlockSpec(memory_space=pl.ANY)
    return pl.pallas_call(
        lambda *refs: layer_kernel(count, nz, rows, local_len, *refs),
        out_shape=[jax.ShapeDtypeStruct((ndp,) + w.shape, w.dtype) for w in shards]
        + [jax.ShapeDtypeStruct(*result) for result in results]
        + [jax.ShapeDtypeStruct(*result) for result in more],
        in_specs=[anywhere] * (count - 1) + [vmem] * 6 + [smem] * 2,
        out_specs=[anywhere] * (count + len(results)) + [vmem] * 2,
        scratch_shapes=[pltpu.VMEM(*result) for i, result in enumerate(results) if i != 14]
        + [
            pltpu.VMEM((ndp,) + shards[0].shape, low),
            pltpu.VMEM((tokens, width // 2), low),
            pltpu.VMEM((SLOTS, ndp, 128, width), low),
            pltpu.VMEM((rows, 4, local_len, width), low),
            pltpu.VMEM((128, span), low),
        ]
        + [pltpu.VMEM(w.shape, w.dtype) for w in shards]
        + [
            pltpu.SemaphoreType.DMA((18,)),
            pltpu.SemaphoreType.DMA((len(results),)),
            pltpu.SemaphoreType.DMA((steps + 2,)),
            pltpu.SemaphoreType.DMA((steps, nz, 6)),
            pltpu.SemaphoreType.DMA((steps, nz, 6)),
            pltpu.SemaphoreType.DMA((2, 4)),
            pltpu.SemaphoreType.DMA((2, 4)),
            pltpu.SemaphoreType.DMA((count,)),
        ],
        compiler_params=pltpu.CompilerParams(
            collective_id=0, has_side_effects=True, vmem_limit_bytes=62 * 2**20
        ),
        name="layer",
    )(*shards[1:], *gains, hidden, encoder, cotangent, lengths, enc_lengths)


RINGS = (5, 5)
SLACK = 0
LAGS = (4, 7, 10)
DEEP = ()
WIDE_RING = 8


def back_kernel(plan, nz, rows, local_len, n_out, *refs):
    at = 0

    def take(n):
        nonlocal at
        at += n
        return refs[at - n : at]

    (any_activated, any_last, any_grad, any_slope, any_crossed, any_normal2, any_scale2) = take(7)
    (any_normal, any_scale, any_ccontext, any_normed, any_context, any_hid, any_x_all) = take(7)
    (any_states, any_cquery, any_ckeys, any_cvalues, any_cprob, any_query, any_keys) = take(7)
    (any_values, any_prob, any_prob_own, any_gains, any_gain_total) = take(5)
    w_down, w_up, w_cout, w_cquery, w_out, w_ckey, w_cvalue, w_key, w_value, w_query, w_rel = take(11)
    outs = take(n_out)
    gain_out, states_sum, hidden_grad = take(3)
    (activated, last_low, residual, up_back, crossed_low, normal, scale, cross_low) = take(8)
    (ccontext_back, cquery, ckeys, cvalues, prob, query, keys, values, prob_own) = take(9)
    (gains, gain_total, cquery_back, ckey_back, cvalue_back, attn_low, query_back) = take(7)
    (key_back, value_back, rel_back, main_part, states_part, pool, hot_ref, turn_ref) = take(8)
    parts, held0s, held1s, held2s, held3s = take(2), take(3), take(3), take(3), take(3)
    gain_part, share1, share2, deep0, deep1, deep2 = take(6)
    load_sems, weight_sems, out_sems, send, recv, credit0, credit1, credit2 = take(8)
    shares = (main_part, states_part)
    context_back, slope = ccontext_back, up_back
    tokens, width = residual.shape
    mine = 3 * local_len
    span = ckeys.shape[0] // rows
    start = lax.axis_index("seq") * local_len
    s, z, c, sx, sy = place()
    own = 2 * z + c
    x, y = lax.rem(s, 2), s // 2
    core = (s, 2 * z + 1 - c)
    beside_x, beside_y = (sx, own), (sy, own)

    loads = []

    def load(source, target):
        copy = pltpu.make_async_copy(source, target, load_sems.at[len(loads)])
        loads.append(copy)
        copy.start()
        return copy

    begun = [
        load(any_activated, activated),
        load(any_last, last_low),
    ]
    first_loads = list(begun)
    ffn_loads = [
        load(any_slope, slope),
        load(any_grad, residual),
        load(any_crossed, crossed_low),
        load(any_normal2, normal),
        load(any_scale2, scale),
        load(any_gains, gains),
        load(any_gain_total, gain_total),
    ]
    cross_loads = [
        load(any_cquery, cquery),
        load(any_ckeys, ckeys),
        load(any_cvalues, cvalues),
        load(any_cprob.at[pl.ds(0, 4)], prob),
    ]
    attend_loads = [
        load(any_query, query),
        load(any_keys, keys),
        load(any_values, values),
        load(any_prob_own, prob_own),
    ]

    def await_all(copies):
        for copy in copies:
            copy.wait()
        copies.clear()

    blocks = [w_down.at[pl.ds(width * k, width)] for k in range(4)]
    blocks += [w_up.at[:, pl.ds(width * k, width)] for k in range(4)]
    blocks += [w_cout, w_cquery, w_out, w_ckey, w_cvalue, w_key, w_value, w_query, w_rel]
    DOWN, UP, COUT, CQUERY, OUT, CKEY, CVALUE, KEY, VALUE, QUERY, REL = (0, 4, *range(8, 17))

    def block_copy(i):
        target = pool.at[i % 2]
        if blocks[i].shape[1] < width:
            target = target.at[:, pl.ds(0, blocks[i].shape[1])]
        return pltpu.make_async_copy(blocks[i], target, weight_sems.at[i])

    started = []

    def need(i):
        while len(started) <= i:
            block_copy(len(started)).start()
            started.append(True)
        block_copy(i).wait()

    def release(i):
        if i + 2 < len(blocks) and len(started) <= i + 2:
            while len(started) <= i + 2:
                block_copy(len(started)).start()
                started.append(True)

    block_copy(0).start()
    block_copy(1).start()
    started += [True, True]
    greet(nz)
    gain_part[...] = jnp.zeros_like(gain_part)

    held = {}

    def buffers(k):
        kind, slot = plan[k][:2]
        sub = plan[k][5]
        if kind == 3:
            share = shares[slot // 2].at[:, :, slot % 2]
            return None, share, share1.at[slot], share2.at[slot], None
        if kind == 4:
            part, held0 = parts[0].at[slot % 2], held0s[0].at[slot % RINGS[0]]
            return part, held0, deep1.at[sub], deep2.at[sub], deep0.at[sub]
        if kind == 2:
            return (gain_part,) + tuple(h[2].at[0] for h in (held0s, held1s, held2s, held3s))
        ring = WIDE_RING if kind == 0 else held1s[1].shape[0]
        return (
            parts[kind].at[slot % 2],
            held0s[kind].at[slot % RINGS[kind]],
            held1s[kind].at[sub % ring],
            held2s[kind].at[sub % ring],
            held3s[kind].at[sub],
        )

    slots_of = [sum(p[0] in ((0, 4), (1,))[kind] for p in plan) for kind in range(2)]
    subs_of = sum(p[0] == 0 for p in plan)

    def even(k):
        return plan[k][5] % 2 == 0

    def core_copy(k):
        part, held0 = buffers(k)[:2]
        return remote(part.at[:, :, :, 1 - c], held0, send.at[k, 0], recv.at[k, 0], core)

    def first_copy(k):
        _, held0, held1 = buffers(k)[:3]
        if plan[k][0] == 4:
            held0 = buffers(k)[4].at[0]
        if even(k):
            return remote(held0.at[:, 1 - x], held1, send.at[k, 1], recv.at[k, 1], beside_x)
        return remote(held0.at[1 - y], held1, send.at[k, 1], recv.at[k, 1], beside_y)

    def second_copy(k):
        held1, held2 = buffers(k)[2:4]
        if even(k):
            return remote(held1.at[1 - y], held2, send.at[k, 2], recv.at[k, 2], beside_y)
        return remote(held1.at[1 - x], held2, send.at[k, 2], recv.at[k, 2], beside_x)

    def z_copy(k, dz):
        _, held0, _, held2, held3 = buffers(k)
        zt = lax.rem(z + dz, nz)
        source = held0.at[:, :, zt] if plan[k][0] == 4 else held2.at[zt]
        return remote(
            source, held3.at[dz - 1], send.at[k, 2 + dz], recv.at[k, 2 + dz], (s, 2 * zt + c)
        )

    def grant(semaphore, to):
        pl.semaphore_signal(semaphore, inc=1, device_id=to, device_id_type=MESH)

    def added(held, mine):
        held[...] = (held[...].astype(jnp.float32) + mine.astype(jnp.float32)).astype(held.dtype)

    half = rows * span // 2
    whole_rows = (0, tokens)

    def segments(pair, i):
        cols = pl.ds(256 * i, 256)
        if pair == 0:
            return [(activated[:, cols], whole_rows)]
        if pair == 1:
            return [(crossed_low[:, cols], whole_rows)]
        if pair <= 6:
            column = width * min(pair - 2, 3) + 256 * i
            return [(activated[:, pl.ds(column, 256)], whole_rows)]
        if pair <= 8:
            return [
                (up_back[:, pl.ds(width * n + 256 * i, 256)], (tokens * n, tokens)) for n in range(2)
            ]
        return [
            (up_back[:half, pl.ds(width * (2 + n) + 256 * i, 256)], (half * n, half))
            for n in range(2)
        ]

    rights = (
        last_low, up_back, cross_low, cquery_back, attn_low, query_back, rel_back,
        key_back, value_back, ckey_back, cvalue_back,
    )
    late_loads = []

    def reload():
        for n, source in enumerate((any_ccontext, any_normed, any_context, any_hid)):
            late_loads.append(load(source, activated.at[:, pl.ds(width * n, width)]))
        for n in range(2):
            late_loads.append(
                load(any_x_all.at[pl.ds(tokens * n, tokens)], up_back.at[:, pl.ds(width * n, width)])
            )
            late_loads.append(
                load(
                    any_states.at[pl.ds(half * n, half)],
                    up_back.at[pl.ds(0, half), pl.ds(width * (2 + n), width)],
                )
            )

    before, recent = {}, {}
    for k, entry in enumerate(plan):
        before[k] = recent.get((entry[0] % 4, entry[1] - 2))
        recent[entry[0] % 4, entry[1]] = k
    followed = set(v for v in before.values() if v is not None)
    pairs_before = max(k for k, entry in enumerate(plan) if entry[0] in (0, 1, 4) and entry[2] < 2)

    def make(k):
        kind, slot, pair, col, wide, _ = plan[k]
        if kind == 3:
            return
        if kind != 2:
            part = buffers(k)[0]
            block = part.shape[4]
            if pair == 0:
                await_all(first_loads)
            if pair >= 2:
                await_all(late_loads)
            if slot >= 2:
                core_copy(before[k]).wait_send()
            group = 256 // block
            for i in range(part.shape[0] * part.shape[1] * nz * 2 * block // 256):
                product = 0.0
                for left, (row, height) in segments(pair, i):
                    right = rights[pair][row : row + height, col : col + wide]
                    product = product + mm_grad(left, right)
                i_s, rest = divmod(i * group, 2 * nz)
                zs = rest // 2
                part[i_s // 2, i_s % 2, zs : zs + group // 2] = product.reshape(
                    group // 2, 2, block, wide
                ).astype(part.dtype)
            if k == pairs_before:
                reload()
            if slot >= RINGS[kind % 4]:
                pl.semaphore_wait(credit0.at[kind % 4], 1)
        else:
            lanes = width // (8 * nz)
            totals = jnp.concatenate(
                [jnp.sum(gain_total[g], axis=0, keepdims=True) for g in range(3)], axis=0
            )
            for b in range(8 * nz):
                i_s, rest = divmod(b, 2 * nz)
                gain_part[i_s // 2, i_s % 2, rest // 2, rest % 2, 0:3, 0:lanes] = totals[
                    :, b * lanes : (b + 1) * lanes
                ]
        core_copy(k).start()

    def after_core(k):
        part, held0 = buffers(k)[:2]
        kind, sub = plan[k][0], plan[k][5]
        if kind != 3:
            core_copy(k).wait_recv()
            added(held0, part[:, :, :, c])
        if kind == 4:
            for dz in range(1, nz):
                z_copy(k, dz).start()
            return
        if kind == 0 and sub >= WIDE_RING:
            pl.semaphore_wait(credit1.at[sub % 2], 1)
        first_copy(k).start()

    def over_z(k, mine_part):
        held3 = buffers(k)[4]
        total = mine_part.astype(jnp.float32)
        for dz in range(1, nz):
            z_copy(k, dz).wait_recv()
            total = total + held3[dz - 1].astype(jnp.float32)
        return total

    def sent_z(k):
        for dz in range(1, nz):
            z_copy(k, dz).wait_send()

    def after_first(k):
        _, held0, held1, _, held3 = buffers(k)
        kind, slot, sub = plan[k][0], plan[k][1], plan[k][5]
        if kind == 4:
            held3[0] = over_z(k, held0[:, :, z]).astype(held3.dtype)
            first_copy(k).start()
            sent_z(k)
        else:
            first_copy(k).wait_recv()
            added(held1, held0[:, x] if even(k) else held0[y])
            if kind == 0 and sub >= WIDE_RING:
                pl.semaphore_wait(credit2.at[sub % 2], 1)
            second_copy(k).start()
            first_copy(k).wait_send()
        if kind in (0, 1, 4) and slot + RINGS[kind % 4] < slots_of[kind % 4]:
            grant(credit0.at[kind % 4], core)

    def after_second(k):
        _, _, held1, held2, held3 = buffers(k)
        kind, slot, sub = plan[k][0], plan[k][1], plan[k][5]
        if kind == 4:
            first_copy(k).wait_recv()
            added(held1, held3[0, :, x] if even(k) else held3[0, y])
            second_copy(k).start()
            return
        second_copy(k).wait_recv()
        mine_part = held1[y] if even(k) else held1[x]
        if kind == 3:
            total = held2[...].astype(jnp.float32) + mine_part.astype(jnp.float32)
            r = slot % 2
            if slot < 2:
                residual[r * mine : r * mine + local_len] += total
                hidden_copy(0, r).start()
            else:
                states_sum[r] = total
            return
        added(held2, mine_part)
        for dz in range(1, nz):
            z_copy(k, dz).start()
        second_copy(k).wait_send()
        if kind == 0 and sub + WIDE_RING < subs_of:
            grant(credit1.at[sub % 2], beside_x if even(k) else beside_y)

    def finish_chunk(k):
        kind, _, pair, col, wide, sub = plan[k]
        if kind == 3:
            return
        _, _, held1, held2, _ = buffers(k)
        if kind == 4:
            second_copy(k).wait_recv()
            mine_part = (held1[y] if even(k) else held1[x]).astype(jnp.float32)
            outs[pair][:, col : col + wide] = held2[...].astype(jnp.float32) + mine_part
            first_copy(k).wait_send()
            second_copy(k).wait_send()
            return
        total = over_z(k, held2[z])
        if kind == 2:
            gain_out[...] = total
        else:
            outs[pair][:, col : col + wide] = total
        sent_z(k)
        if kind == 0 and sub + WIDE_RING < subs_of:
            grant(credit2.at[sub % 2], beside_y if even(k) else beside_x)

    count = len(plan)
    total_ticks = count + LAGS[2] + SLACK

    def tick(t):
        def at_lag(lag, call):
            if 0 <= t - lag < count:
                call(t - lag)

        if 1 <= t < count + 1:
            after_core(t - 1)
        if t < count:
            make(t)
        at_lag(LAGS[0], after_first)
        at_lag(LAGS[1], after_second)
        at_lag(LAGS[2], finish_chunk)

    def fours(body):
        def step(i, carry):
            body(pl.ds(pl.multiple_of(i * 256, 256), 256))
            return carry

        lax.fori_loop(0, width // 256, step, 0)

    def down_back(k):
        need(DOWN + k)
        if k == 0:
            await_all(ffn_loads)
        place_of = (DOWN + k) % 2

        def body(i, carry):
            to = pl.ds(pl.multiple_of(k * width + i * 256, 256), 256)
            product = mm_back(last_low[...], pool[place_of, pl.ds(pl.multiple_of(i * 256, 256), 256)])
            up_back[:, to] = (product * slope[:, to].astype(jnp.float32)).astype(jnp.bfloat16)
            return carry

        lax.fori_loop(0, width // 256, body, 0)
        release(DOWN + k)

    def up_again(k):
        need(UP + k)

        def body(cols):
            residual[:, cols] += mm_back(
                up_back[:, k * width : (k + 1) * width], pool[(UP + k) % 2, cols]
            )

        fours(body)
        release(UP + k)

    def cross_norm_back(part):
        above = residual[part]
        add_rows(gain_total, 1, above * normal[part])
        grad = norm_back(above, normal[part], scale[part][:, 0:1], gains[1:2])
        residual[part] = grad
        cross_low[part] = grad.astype(jnp.bfloat16)

    norm_loads = []

    def cout_back():
        row_tiles(tokens, cross_norm_back)
        norm_loads.append(load(any_normal, normal))
        norm_loads.append(load(any_scale, scale))
        need(COUT)

        def body(cols):
            ccontext_back[:, cols] = mm_back(cross_low[...], pool[COUT % 2, cols]).astype(
                jnp.bfloat16
            )

        fours(body)
        release(COUT)

    def cross(first, last):
        await_all(cross_loads)

        def step(i, carry):
            cross_back_step(
                i // 4, lax.rem(i, 4), lax.rem(i, 4), mine, span, local_len, ccontext_back, cvalues, prob,
                ckeys, cquery, cquery_back, ckey_back, cvalue_back,
            )
            return carry

        lax.fori_loop(first, last, step, 0)
        if last == 4 * rows:
            attend_loads.append(load(any_prob.at[pl.ds(0, 4)], prob))
        elif last % 4 == 0:
            cross_loads.append(load(any_cprob.at[pl.ds(last, 4)], prob))

    def attn_norm_back(part):
        above = residual[part]
        add_rows(gain_total, 0, above * normal[part])
        grad = norm_back(above, normal[part], scale[part][:, 0:1], gains[0:1])
        residual[part] = grad
        attn_low[part] = grad.astype(jnp.bfloat16)

    def cquery_again():
        need(CQUERY)

        def body(cols):
            residual[:, cols] += mm_back(cquery_back[...], pool[CQUERY % 2, cols])

        fours(body)
        release(CQUERY)
        await_all(norm_loads)
        row_tiles(tokens, attn_norm_back)

    def out_back():
        need(OUT)

        def body(cols):
            context_back[:, cols] = mm_back(attn_low[...], pool[OUT % 2, cols]).astype(jnp.bfloat16)

        fours(body)
        release(OUT)
        hot_ref[...] = hot_backward(start, span)
        turn_ref[...] = turning(span)

    def attend(first, last):
        await_all(attend_loads)

        def step(i, carry):
            attend_back_step(
                i // 4, lax.rem(i, 4), lax.rem(i, 4), mine, span, local_len, rows, context_back, query, keys,
                values, prob, prob_own, query_back, key_back, value_back, rel_back,
                hot_ref[...], turn_ref[...],
            )
            return carry

        lax.fori_loop(first, last, step, 0)
        if last < 4 * rows and last % 4 == 0:
            attend_loads.append(load(any_prob.at[pl.ds(last, 4)], prob))

    def into(share, total, cols):
        total = total.astype(jnp.bfloat16)
        for r in range(rows):
            for p in range(4):
                row = r * span + p * local_len
                share[p // 2, p % 2, r, :, cols] = total[row : row + local_len]

    def states_back():
        need(CKEY)
        need(CVALUE)

        def body(cols):
            total = mm_back(ckey_back[...], pool[CKEY % 2, cols])
            into(states_part, total + mm_back(cvalue_back[...], pool[CVALUE % 2, cols]), cols)

        fours(body)
        release(CKEY)
        release(CVALUE)

    def keys_again():
        need(KEY)
        need(VALUE)

        def body(cols):
            total = mm_back(key_back[...], pool[KEY % 2, cols])
            total = total + mm_back(value_back[...], pool[VALUE % 2, cols])
            into(main_part, total[: rows * span], cols)
            for r in range(rows):
                to = r * mine + local_len
                row = rows * span + 2 * r * local_len
                residual[to : to + 2 * local_len, cols] += total[row : row + 2 * local_len]

        fours(body)
        release(KEY)
        release(VALUE)

    def hidden_copy(j, r):
        row = r * mine + j * local_len
        return pltpu.make_async_copy(
            residual.at[pl.ds(row, local_len)], hidden_grad.at[j, r], out_sems.at[j, r]
        )

    def query_again():
        need(QUERY)
        need(REL)
        deep = rel_back.shape[1]

        def body(cols):
            total = mm_back(query_back[...], pool[QUERY % 2, cols])
            residual[:, cols] += total + mm_back(rel_back[...], pool[REL % 2, cols, :deep])

        fours(body)
        for r in range(rows):
            for j in (1, 2):
                hidden_copy(j, r).start()

    ends = {}
    for k, entry in enumerate(plan):
        ends[10 + entry[0] if entry[0] in (2, 3) else entry[2]] = k + 1
    steps_of = range(0, 4 * rows, 2)
    pieces = [(1, functools.partial(down_back, k), ends[0]) for k in range(4)]
    pieces += [(1, functools.partial(up_again, k), ends[1] - 1) for k in range(4)]
    pieces.append((3, cout_back, ends[2]))
    pieces += [(4, functools.partial(cross, i, i + 2), ends[2]) for i in steps_of]
    pieces[-1] = pieces[-1][:2] + (ends[10],)
    pieces.append((2, cquery_again, ends[12]))
    pieces.append((1, out_back, ends[12]))
    pieces += [(5, functools.partial(attend, i, i + 2), ends[12]) for i in steps_of]
    pieces.append((3, states_back, ends[8]))
    pieces.append((5, keys_again, ends[8]))
    pieces.append((2, query_again, count))
    done = {"tick": 0, "spent": 0.0}

    def ticks_to(limit, wanted):
        while done["tick"] < min(limit, wanted):
            tick(done["tick"])
            done["tick"] += 1

    tick(0)
    done["tick"] = 1
    for cost, call, limit in pieces:
        call()
        done["spent"] += cost
        ticks_to(limit, 1 + int(done["spent"] / 2.5))
    ticks_to(total_ticks, total_ticks)
    for k in range(count):
        if plan[k][0] != 3 and k not in followed:
            core_copy(k).wait_send()
        if plan[k][0] == 3:
            second_copy(k).wait_send()
    for j in range(3):
        for r in range(rows):
            hidden_copy(j, r).wait()


def back(values, weights, shape, ndp):
    nz = ndp // 2
    low, wide = jnp.bfloat16, jnp.float32
    rows, local_len, width = shape[1:]
    tokens, span = 3 * rows * local_len, 4 * local_len
    every = rows * (span + 2 * local_len)
    ff = weights[0].shape[0]
    ndev = 8 * nz
    heights = [ff, width, width, width, width, width, width, width, width, width, width]
    wides = [width, ff, width, width, width, width, width // 2, width, width, width, width]
    plan, slots, subs, at = [], [0, 0], [0, 0], 0
    for pair in (0, 1, 2, 3, 9, 10, 4, 5, 6, 7, 8):
        kind = int(heights[pair] > width)
        step = (512, 128)[kind]
        for col in range(0, wides[pair], step):
            if kind:
                plan.append((1, slots[1], pair, col, step, slots[1]))
            else:
                deep = at in DEEP
                plan.append((4 if deep else 0, slots[0], pair, col, step, subs[deep]))
                subs[deep] += 1
                at += 1
            slots[kind] += 1
        if pair == 4:
            plan.append((2, 0, 0, 0, 128, 0))
    plan += [(3, i, 0, 0, 0, i) for i in range(4)]
    n = len(plan)
    tails = [((width // ndev, 512), low), ((ff // ndev, 128), low), ((8, 128), wide)]
    counts = [
        (RINGS[0], WIDE_RING, WIDE_RING, subs[0]),
        (RINGS[1], slots[1], slots[1], slots[1]),
        (1, 1, 1, 1),
    ]
    leads = [(2, 2, nz), (2, nz), (nz,), (nz - 1,)]
    held = [
        pltpu.VMEM((counts[kind][stage],) + leads[stage] + tails[kind][0], tails[kind][1])
        for stage in range(4)
        for kind in range(3)
    ]
    parts = [pltpu.VMEM((2, 2, 2, nz, 2) + tails[kind][0], low) for kind in range(2)]
    share = (local_len, width)
    main = pltpu.VMEM((rows * span, width), low)
    token = pltpu.VMEM((tokens, width), low)
    fat = pltpu.VMEM((tokens, ff), low)
    all_rows = pltpu.VMEM((every, width), low)
    token_wide = pltpu.VMEM((tokens, width), wide)
    scratch = [fat, token, token_wide, fat, token, token_wide]
    scratch += [pltpu.VMEM((tokens, 128), wide), token, token, token, main, main]
    scratch += [pltpu.VMEM((4, 12 * local_len, span), low), token, all_rows, all_rows, token]
    scratch += [pltpu.VMEM((16, width), wide), pltpu.VMEM((3, 8, width), wide), token, main, main]
    scratch += [token, token, all_rows, all_rows, pltpu.VMEM((tokens, width // 2), low)]
    scratch += [pltpu.VMEM((2, 2, rows) + share, low)] * 2
    scratch += [pltpu.VMEM((2, width, width), low)]
    scratch += [pltpu.VMEM((span, 128), low), pltpu.VMEM((span, span), low)]
    scratch += parts + held
    scratch += [pltpu.VMEM((2, 2, nz, 2, 8, 128), wide)]
    scratch += [pltpu.VMEM((4, 2) + share, low), pltpu.VMEM((4,) + share, low)]
    scratch += [
        pltpu.VMEM((max(1, subs[1]),) + lead + tails[0][0], low) for lead in ((nz - 1, 2, 2), (2,), ())
    ]
    scratch += [
        pltpu.SemaphoreType.DMA((32,)),
        pltpu.SemaphoreType.DMA((17,)),
        pltpu.SemaphoreType.DMA((3, rows)),
        pltpu.SemaphoreType.DMA((n, 2 + nz)),
        pltpu.SemaphoreType.DMA((n, 2 + nz)),
        pltpu.SemaphoreType.REGULAR((2,)),
        pltpu.SemaphoreType.REGULAR((2,)),
        pltpu.SemaphoreType.REGULAR((2,)),
    ]
    anywhere = pl.BlockSpec(memory_space=pl.ANY)
    vmem = pl.BlockSpec(memory_space=pltpu.VMEM)
    outs = [jax.ShapeDtypeStruct((h // ndev, w), wide) for h, w in zip(heights, wides)]
    outs.append(jax.ShapeDtypeStruct((8, 128), wide))
    outs.append(jax.ShapeDtypeStruct((rows,) + share, wide))
    outs.append(jax.ShapeDtypeStruct(shape, wide))
    return pl.pallas_call(
        lambda *refs: back_kernel(plan, nz, rows, local_len, len(heights), *refs),
        out_shape=outs,
        in_specs=[anywhere] * (len(values) + len(weights)),
        out_specs=[vmem] * (len(outs) - 1) + [anywhere],
        scratch_shapes=scratch,
        compiler_params=pltpu.CompilerParams(
            collective_id=1, has_side_effects=True, vmem_limit_bytes=62 * 2**20
        ),
        name="back",
    )(*values, *weights)


def finish_kernel(count, *refs):
    sources, gain_sums = refs[:count], refs[count]
    targets, gain_outs = refs[count + 1 : 2 * count + 1], refs[2 * count + 1 : 2 * count + 4]
    held, sems = refs[2 * count + 4 : 3 * count + 4], refs[3 * count + 4]
    ins = [pltpu.make_async_copy(sources[i], held[i], sems.at[0, i]) for i in range(count)]
    outs = [pltpu.make_async_copy(held[i], targets[i], sems.at[1, i]) for i in range(count)]
    for copy in ins:
        copy.start()
    for g, gain_out in enumerate(gain_outs):
        gain_out[...] = gain_sums[g : g + 1, : gain_out.shape[1]]
    for copy_in, copy_out in zip(ins, outs):
        copy_in.wait()
        copy_out.start()
    for copy in outs:
        copy.wait()


def finish(sums, hidden_grad, states_sum, gain_sums, lanes):
    arrays = (*sums, hidden_grad, states_sum)
    count = len(arrays)
    anywhere, vmem = pl.BlockSpec(memory_space=pl.ANY), pl.BlockSpec(memory_space=pltpu.VMEM)
    return pl.pallas_call(
        lambda *refs: finish_kernel(count, *refs),
        out_shape=[jax.ShapeDtypeStruct(a.shape, a.dtype) for a in arrays]
        + [jax.ShapeDtypeStruct((1, lanes), jnp.float32)] * 3,
        in_specs=[anywhere] * count + [vmem],
        out_specs=[anywhere] * count + [vmem] * 3,
        scratch_shapes=[pltpu.VMEM(a.shape, a.dtype) for a in arrays]
        + [pltpu.SemaphoreType.DMA((2, count))],
        compiler_params=pltpu.CompilerParams(vmem_limit_bytes=62 * 2**20),
        name="finish",
    )(*arrays, gain_sums)


def plain_call(kernel, name, ins, spaces, outs, scratch, flops):
    space = {"v": pltpu.VMEM, "s": pltpu.SMEM, "a": pl.ANY}
    out_shape = [jax.ShapeDtypeStruct(shape, kind) for shape, kind in outs]
    moved = sum(a.size * a.dtype.itemsize for a in list(ins) + out_shape)
    return pl.pallas_call(
        kernel,
        out_shape=out_shape,
        in_specs=[pl.BlockSpec(memory_space=space[p]) for p in spaces],
        out_specs=[pl.BlockSpec(memory_space=pltpu.VMEM)] * len(outs),
        scratch_shapes=scratch,
        compiler_params=pltpu.CompilerParams(vmem_limit_bytes=62 * 2**20),
        cost_estimate=pl.CostEstimate(flops=flops, bytes_accessed=moved, transcendentals=0),
        name=name,
    )(*ins)


def copies_of(arrays):
    return [pltpu.VMEM(a.shape, a.dtype) for a in arrays] + [
        pltpu.SemaphoreType.DMA((len(arrays),))
    ]


def local(
    hidden,
    encoder,
    lengths,
    enc_lengths,
    w_query,
    w_key,
    w_value,
    w_attn_out,
    w_relative,
    w_cross_query,
    w_cross_key,
    w_cross_value,
    w_cross_out,
    w_up,
    w_down,
    gain_attn,
    gain_cross,
    gain_ffn,
    cotangent,
):
    ndp, chips = lax.axis_size("dp"), lax.axis_size("seq")
    devices = ndp * chips
    low, wide = jnp.bfloat16, jnp.float32
    _, rows, local_len, width = hidden.shape
    span, tokens = local_len * chips, 3 * rows * local_len
    weights = (
        w_key,
        w_value,
        w_query,
        w_relative,
        w_cross_key,
        w_cross_value,
        w_attn_out,
        w_cross_query,
        w_cross_out,
        w_up,
        w_down,
    )
    gains = (gain_attn, gain_cross, gain_ffn)
    every = rows * (span + 2 * local_len)
    kernels = chips == 4 and w_query.shape[0] == 128 and w_down.shape[0] == 512
    if kernels:
        gains = [gain.reshape(1, -1) for gain in gains]
        results = layer(
            gains, weights, hidden, encoder, cotangent, lengths, enc_lengths, ndp
        )
        whole, results = results[1 : len(weights) + 1], results[len(weights) + 1 :]
        whole = [w.reshape(-1, w.shape[-1]) for w in whole]
        (hid, x_all, query, keys, values, prob, prob_own, context, ckeys, cvalues) = results[:10]
        (normal, normal_scale, normed_low, cquery, cprob, ccontext, output) = results[10:17]
        (crossed_low, activated, last_low, slope, gain_total, normal2, scale2) = results[17:24]
        (states, gains, grad) = results[24:]
        states = states.reshape(-1, width)
    else:
        gains = jnp.pad(jnp.stack(gains), ((0, 5), (0, 0)))
        whole = [lax.all_gather(w, "dp", axis=0, tiled=True) for w in weights]
        gains = lax.all_gather(gains, "dp", axis=1, tiled=True).astype(wide)
        mains = lax.all_gather(hidden[0], "seq", axis=1).reshape(-1, width)
        states = lax.all_gather(encoder, "seq", axis=1).reshape(-1, width)
    (
        full_key,
        full_value,
        full_query,
        full_relative,
        full_ckey,
        full_cvalue,
        full_attn_out,
        full_cquery,
        full_cout,
        full_up,
        full_down,
    ) = whole
    if not kernels:
        ff = full_up.shape[1]
        fetched = (
            full_key,
            full_value,
            full_query,
            full_relative,
            full_ckey,
            full_cvalue,
            full_attn_out,
            full_cquery,
        )
        (
            hid,
            x_all,
            query,
            keys,
            values,
            prob,
            prob_own,
            context,
            ckeys,
            cvalues,
            normal,
            normal_scale,
            normed_low,
            cquery,
            cprob,
            ccontext,
        ) = plain_call(
            lambda *refs: forward_kernel(rows, local_len, *refs),
            "forward_attention",
            (hidden, mains, states, lengths, enc_lengths, gains) + fetched,
            "vvvssv" + "a" * len(fetched),
            [
                ((tokens, width), low),
                ((every, width), low),
                ((tokens, width), low),
                ((every, width), low),
                ((every, width), low),
                ((4 * rows, 12 * local_len, span), low),
                ((tokens, width), low),
                ((tokens, width), low),
                ((rows * span, width), low),
                ((rows * span, width), low),
                ((tokens, width), wide),
                ((tokens, 128), wide),
                ((tokens, width), low),
                ((tokens, width), low),
                ((4 * rows, 12 * local_len, span), low),
                ((tokens, width), low),
            ],
            [
                pltpu.VMEM((tokens, full_relative.shape[1]), low),
                pltpu.VMEM((tokens, width), wide),
            ]
            + copies_of(fetched),
            12 * 10**9,
        )
        fetched = (full_cout, full_up, full_down)
        (
            output,
            crossed_low,
            activated,
            last_low,
            up_back,
            cross_grad,
            cross_low,
            ccontext_back,
            gain_middle,
        ) = plain_call(
            lambda *refs: middle_kernel(rows, local_len, *refs),
            "feed_forward",
            (normal, ccontext, gains, cotangent) + fetched,
            "vvvv" + "a" * len(fetched),
            [
                (hidden.shape, low),
                ((tokens, width), low),
                ((tokens, ff), low),
                ((tokens, width), low),
                ((tokens, ff), low),
                ((tokens, width), wide),
                ((tokens, width), low),
                ((tokens, width), low),
                ((3, 8, width), wide),
            ],
            [
                pltpu.VMEM((tokens, width), wide),
                pltpu.VMEM((tokens, 128), wide),
                pltpu.VMEM((tokens, ff), low),
                pltpu.VMEM((tokens, width), wide),
            ]
            + copies_of(fetched),
            14 * 10**9,
        )
    if kernels:
        values_in = (
            activated, last_low, grad, slope, crossed_low, normal2, scale2, normal, normal_scale,
            ccontext, normed_low, context, hid, x_all, states, cquery, ckeys, cvalues, cprob,
            query, keys, values, prob, prob_own, gains, gain_total,
        )
        weights_in = (
            full_down, full_up, full_cout, full_cquery, full_attn_out, full_ckey, full_cvalue,
            full_key, full_value, full_query, full_relative,
        )
        *sums, gain_sums, states_sum, hidden_grad = back(values_in, weights_in, hidden.shape, ndp)
        *sums, output, hidden_grad, states_sum, gain_a, gain_b, gain_c = finish(
            sums + [output], hidden_grad, states_sum, gain_sums, width // devices
        )
        gain_sums = [gain.reshape(-1) for gain in (gain_a, gain_b, gain_c)]
    else:
        fetched = (
            full_cquery,
            full_attn_out,
            full_ckey,
            full_cvalue,
            full_query,
            full_relative,
            full_key,
            full_value,
        )
        (
            cquery_back,
            ckey_back,
            cvalue_back,
            attn_low,
            query_back,
            key_back,
            value_back,
            rel_back,
            hidden_own,
            main_part,
            states_part,
            gain_back,
        ) = plain_call(
            lambda *refs: backward_kernel(rows, local_len, *refs),
            "backward_attention",
            (
                ccontext_back,
                cross_grad,
                cquery,
                ckeys,
                cvalues,
                cprob,
                normal,
                normal_scale,
                gains,
                query,
                keys,
                values,
                prob,
                prob_own,
            )
            + fetched,
            "v" * 14 + "a" * len(fetched),
            [
                ((tokens, width), low),
                ((rows * span, width), low),
                ((rows * span, width), low),
                ((tokens, width), low),
                ((tokens, width), low),
                ((every, width), low),
                ((every, width), low),
                ((tokens, full_relative.shape[1]), low),
                (hidden.shape, wide),
                ((chips, rows, local_len, width), low),
                ((chips, rows, local_len, width), low),
                ((3, 8, width), wide),
            ],
            [pltpu.VMEM((tokens, width), wide), pltpu.VMEM((tokens, width), low)] + copies_of(fetched),
            14 * 10**9,
        )
        xs = [activated, crossed_low, ccontext, normed_low, context, hid, x_all, states]
        gs = [
            last_low,
            up_back,
            cross_low,
            cquery_back,
            attn_low,
            query_back,
            rel_back,
            key_back,
            value_back,
            ckey_back,
            cvalue_back,
        ]
        pairs = [(0, 0), (1, 1), (2, 2), (3, 3), (4, 4), (5, 5), (5, 6), (6, 7), (6, 8), (7, 9), (7, 10)]
        gain_parts = jnp.sum(gain_middle + gain_back, axis=1)
        sums = [
            lax.psum_scatter(
                weight_grad(xs[i], gs[j]), ("seq", "dp"), scatter_dimension=0, tiled=True
            )
            for i, j in pairs
        ]
        gain_sums = lax.psum_scatter(gain_parts, ("seq", "dp"), scatter_dimension=1, tiled=True)
        main_sum, states_sum = (
            lax.psum_scatter(part, "seq", scatter_dimension=0).astype(wide)
            for part in (main_part, states_part)
        )
        hidden_grad = hidden_own.at[0].add(main_sum)
    gainattn_sum, gaincross_sum, gainffn_sum = gain_sums
    (
        down_sum,
        up_sum,
        cout_sum,
        cquery_sum,
        outproj_sum,
        query_sum,
        relative_sum,
        keyw_sum,
        valuew_sum,
        ckey_sum,
        cvalue_sum,
    ) = sums
    return (
        output,
        hidden_grad,
        states_sum,
        query_sum,
        keyw_sum,
        valuew_sum,
        outproj_sum,
        relative_sum,
        cquery_sum,
        ckey_sum,
        cvalue_sum,
        cout_sum,
        up_sum,
        down_sum,
        gainattn_sum,
        gaincross_sum,
        gainffn_sum,
    )


def solution(mesh):
    in_specs = (
        P(None, "dp", "seq", None),
        P("dp", "seq", None),
        P("dp"),
        P("dp"),
        P("dp", None),
        P("dp", None),
        P("dp", None),
        P("dp", None),
        P("dp", None),
        P("dp", None),
        P("dp", None),
        P("dp", None),
        P("dp", None),
        P("dp", None),
        P("dp", None),
        P("dp"),
        P("dp"),
        P("dp"),
        P(None, "dp", "seq", None),
    )
    out_specs = (
        P(None, "dp", "seq", None),
        P(None, "dp", "seq", None),
        P("dp", "seq", None),
        P(("seq", "dp"), None),
        P(("seq", "dp"), None),
        P(("seq", "dp"), None),
        P(("seq", "dp"), None),
        P(("seq", "dp"), None),
        P(("seq", "dp"), None),
        P(("seq", "dp"), None),
        P(("seq", "dp"), None),
        P(("seq", "dp"), None),
        P(("seq", "dp"), None),
        P(("seq", "dp"), None),
        P(("seq", "dp")),
        P(("seq", "dp")),
        P(("seq", "dp")),
    )
    return jax.shard_map(local, mesh=mesh, in_specs=in_specs, out_specs=out_specs, check_vma=False)
```
